32 devices in a mesh: fsdp: 16 (over z, y, x), dp: 2 (over core).
Axes of the slice: x: 2, y: 2, z: 4, core: 2. Of those that a mesh axis runs over, the one named last changes fastest.
Arguments:
- codons: int32 [16384], P(('fsdp', 'dp')), may hold values from 0 to 68
- masked: int32 [16384], P(('fsdp', 'dp')), may hold values from 0 to 1
- segments: int32 [16384], P(('fsdp', 'dp')), may hold values from 0 to 127, never falling along the last dimension, each value on 1 to 256 neighbouring positions
- inward: float32 [2, 768, 2304], P(None, 'fsdp'), may hold values from -0.21875 to 0.21875
- outward: float32 [2, 768, 768], P(None, 'fsdp'), may hold values from -0.875 to 0.875
- expand: float32 [2, 768, 3072], P(None, 'fsdp'), may hold values from -0.21875 to 0.21875
- shrink: float32 [2, 3072, 768], P(None, 'fsdp'), may hold values from -0.109375 to 0.109375
- codon_table: float32 [70, 768], P(None, 'fsdp'), may hold values from -0.21875 to 0.21875
- norm_params: float32 [5, 2, 768], P(None, None, 'fsdp'), may hold values from -0.9 to 2.5
- inward_first: float32 [2, 768, 2304], P(None, 'fsdp'), may hold values from -9.536743e-06 to 9.536743e-06
- inward_second: float32 [2, 768, 2304], P(None, 'fsdp'), may hold values from 9.143844e-12 to 3.7278746e-11
- outward_first: float32 [2, 768, 768], P(None, 'fsdp'), may hold values from -9.536743e-06 to 9.536743e-06
- outward_second: float32 [2, 768, 768], P(None, 'fsdp'), may hold values from 9.143844e-12 to 3.7278746e-11
- expand_first: float32 [2, 768, 3072], P(None, 'fsdp'), may hold values from -9.536743e-06 to 9.536743e-06
- expand_second: float32 [2, 768, 3072], P(None, 'fsdp'), may hold values from 9.143844e-12 to 3.7278746e-11
- shrink_first: float32 [2, 3072, 768], P(None, 'fsdp'), may hold values from -9.536743e-06 to 9.536743e-06
- shrink_second: float32 [2, 3072, 768], P(None, 'fsdp'), may hold values from 9.143844e-12 to 3.7278746e-11
- table_first: float32 [70, 768], P(None, 'fsdp'), may hold values from -9.536743e-06 to 9.536743e-06
- table_second: float32 [70, 768], P(None, 'fsdp'), may hold values from 9.143844e-12 to 3.7278746e-11
- norm_first: float32 [5, 2, 768], P(None, None, 'fsdp'), may hold values from -3.8146973e-05 to 3.8146973e-05
- norm_second: float32 [5, 2, 768], P(None, None, 'fsdp'), may hold values from 1.4770825e-10 to 5.978667e-10
Outputs:
- loss_sum: float32 [], replicated
- mask_count: float32 [], replicated
- grad_norm: float32 [], replicated
- inward_new: float32 [2, 768, 2304], P(None, 'fsdp')
- inward_moment: float32 [2, 768, 2304], P(None, 'fsdp')
- inward_square: float32 [2, 768, 2304], P(None, 'fsdp')
- outward_new: float32 [2, 768, 768], P(None, 'fsdp')
- outward_moment: float32 [2, 768, 768], P(None, 'fsdp')
- outward_square: float32 [2, 768, 768], P(None, 'fsdp')
- expand_new: float32 [2, 768, 3072], P(None, 'fsdp')
- expand_moment: float32 [2, 768, 3072], P(None, 'fsdp')
- expand_square: float32 [2, 768, 3072], P(None, 'fsdp')
- shrink_new: float32 [2, 3072, 768], P(None, 'fsdp')
- shrink_moment: float32 [2, 3072, 768], P(None, 'fsdp')
- shrink_square: float32 [2, 3072, 768], P(None, 'fsdp')
- table_new: float32 [70, 768], P(None, 'fsdp')
- table_moment: float32 [70, 768], P(None, 'fsdp')
- table_square: float32 [70, 768], P(None, 'fsdp')
- norm_new: float32 [5, 2, 768], P(None, None, 'fsdp')
- norm_moment: float32 [5, 2, 768], P(None, None, 'fsdp')
- norm_square: float32 [5, 2, 768], P(None, None, 'fsdp')
The draws below stay inside these ranges and needn't reach their ends.
All inputs are finite; a program needn't handle non-finite values.
Results may differ from the reference program's by a relative error of at most 0.012.
The reference program's roundings to bfloat16 on the way count: a program that leaves them out, or rounds other values in their place, can miss the bound.
Values may be sent and summed in bfloat16 or wider, within the bound.
No kernel may reach another device: no remote copies, remote signals or barrier semaphores. Data moves between devices by JAX's collectives and lax.ppermute only.
A program may use at most 192 MiB of HBM per device.

```python
import math
import jax
import jax.numpy as jnp
import numpy as np
from jax import lax

H = 12
HD = 64
D = 768
FF = 3072
V = 70
LAYERS = 2
STEP = 10
TOK_DEV = 512
TOKENS = 16384
NORMS = 5
PARAMS = 14217216


def draw_masked(key, part):
    key = jax.random.fold_in(key, 7)
    rows = jnp.arange(TOKENS, dtype=jnp.int32)
    device = rows // TOK_DEV
    span = max(TOKENS // TOK_DEV // 2 - 1, 1)
    outer = device // 2
    inner = device % 2
    per_mille = (50 * span + 100 * outer) * (1 + 2 * inner) // span
    picks = jax.random.randint(key, (TOKENS,), 0, 1000)
    return (picks < per_mille).astype(jnp.int32)


def draw_norm_params(key, part):
    key = jax.random.fold_in(key, 11)
    first_key, second_key = jax.random.split(key)
    ramp = jnp.arange(D, dtype=jnp.float32) / (D - 1)
    spread = jnp.clip(jax.random.normal(first_key, (NORMS, D), jnp.float32), -3.0, 3.0)
    gains = 0.6 * 3.0 ** ramp * jnp.exp(0.1 * spread)
    biases = jnp.clip(0.3 * jax.random.normal(second_key, (NORMS, D), jnp.float32), -0.9, 0.9)
    return jnp.stack([gains, biases], 1)


def touch_ends(array, key, low, largest):
    place = [jax.random.randint(jax.random.fold_in(key, axis), (), 0, length) for axis, length in enumerate(array.shape)]
    main_axis = array.shape.index(max(array.shape))
    next_to = place[:main_axis] + [(place[main_axis] + 1) % array.shape[main_axis]] + place[main_axis + 1:]
    return array.at[tuple(place)].set(low).at[tuple(next_to)].set(largest)


def block_scale(own_key, dims, cuts, smallest, high):
    factor_of, own = 1.0, jax.random.fold_in(own_key, 6)
    for dim, parts in cuts:
        draws = jnp.exp(jax.random.uniform(jax.random.fold_in(own, dim), (parts,), jnp.float32, smallest / len(cuts), high / len(cuts)))
        factor_of = factor_of * jnp.repeat(draws, dims[dim] // parts).reshape([-1 if axis == dim else 1 for axis in range(len(dims))])
    return factor_of


def split_up(number_of, total, most, skew):
    loads = [(1 << 20) // math.isqrt(grade ** skew) + 1 for grade in range(2, number_of + 1)]
    rest, holding = total - most - (number_of - 1), [1] * (number_of - 1)
    while rest > 0:
        candidates = [i for i in range(number_of - 1) if holding[i] < most]
        whole, budget = sum([loads[i] for i in candidates]), rest
        for i in candidates:
            extra = min(most - holding[i], max(1, budget * loads[i] // whole), rest)
            holding[i] = holding[i] + extra
            rest = rest - extra
    return np.array([most] + holding)


def ragged_sizes(own_key, amount, total, limit, slope):
    if amount == 2:
        one = jax.random.randint(own_key, (), max(1, total - limit), min(limit, total - 1) + 1)
        return jnp.stack([one, total - one])
    lengths = jnp.asarray(split_up(amount, total, limit, slope), jnp.int32)
    twos = (amount - 1) // 2
    donor, taker = lengths[1:1 + 2 * twos:2], lengths[2:2 + 2 * twos:2]
    margin = jnp.minimum(donor - 1, limit - taker)
    shifted = jax.random.randint(jax.random.fold_in(own_key, 1), (twos,), 0, 1 << 20) % (margin + 1)
    lengths = lengths.at[1:1 + 2 * twos:2].set(donor - shifted).at[2:2 + 2 * twos:2].set(taker + shifted)
    return lengths[jax.random.permutation(jax.random.fold_in(own_key, 2), amount)]


def normal_values(stream_key, shape, scale, bound, cuts=(), kind=jnp.bfloat16):
    entries = jax.random.normal(stream_key, shape, jnp.float32) * scale
    if len(cuts) > 0:
        entries = block_scale(stream_key, shape, cuts, -0.22, 0.18) * entries
    return jnp.clip(entries, min=-bound, max=bound).astype(kind)


def setup_inputs(seed: int = 0) -> dict:
    arg_keys = jax.random.split(jax.random.key(seed), 22)
    codons = touch_ends(jax.random.randint(arg_keys[0], (TOKENS,), 0, V - 1), jax.random.fold_in(arg_keys[0], 1), 0, (V - 1) - 1).astype(jnp.int32)
    masked = draw_masked(jax.random.fold_in(arg_keys[21], 71), 0)
    segments = jnp.searchsorted(jnp.cumsum(ragged_sizes(arg_keys[2], TOKENS // 128, TOKENS, 256, 1)), jnp.arange(TOKENS), side="right").astype(jnp.int32)
    inward = normal_values(arg_keys[3], (LAYERS, D, 3 * D), D ** -0.5, 0.21875, ((1, 16),), jnp.float32)
    outward = normal_values(arg_keys[4], (LAYERS, D, D), (D // 16) ** -0.5, 0.875, ((1, 16),), jnp.float32)
    expand = normal_values(arg_keys[5], (LAYERS, D, FF), D ** -0.5, 0.21875, ((1, 16),), jnp.float32)
    shrink = normal_values(arg_keys[6], (LAYERS, FF, D), FF ** -0.5, 0.109375, ((1, 16),), jnp.float32)
    codon_table = normal_values(arg_keys[7], (V, D), D ** -0.5, 0.21875, ((1, 16),), jnp.float32)
    norm_params = draw_norm_params(jax.random.fold_in(arg_keys[21], 71), 0)
    inward_first = normal_values(arg_keys[9], (LAYERS, D, 3 * D), (0.00555 * PARAMS ** -0.5), 9.5367431640625e-06, ((1, 16),), jnp.float32)
    inward_second = jnp.clip(jnp.exp(math.log(3.7278746062296975e-11) - 1.40534252 * jax.random.uniform(arg_keys[10], (LAYERS, D, 3 * D), jnp.float32) ** block_scale(arg_keys[10], (LAYERS, D, 3 * D), ((1, 16),), -0.2, 0.2)), 9.14384366834664e-12, 3.7278746062296975e-11)
    outward_first = normal_values(arg_keys[11], (LAYERS, D, D), (0.00555 * PARAMS ** -0.5), 9.5367431640625e-06, ((1, 16),), jnp.float32)
    outward_second = jnp.clip(jnp.exp(math.log(3.7278746062296975e-11) - 1.40534252 * jax.random.uniform(arg_keys[12], (LAYERS, D, D), jnp.float32) ** block_scale(arg_keys[12], (LAYERS, D, D), ((1, 16),), -0.2, 0.2)), 9.14384366834664e-12, 3.7278746062296975e-11)
    expand_first = normal_values(arg_keys[13], (LAYERS, D, FF), (0.00555 * PARAMS ** -0.5), 9.5367431640625e-06, ((1, 16),), jnp.float32)
    expand_second = jnp.clip(jnp.exp(math.log(3.7278746062296975e-11) - 1.40534252 * jax.random.uniform(arg_keys[14], (LAYERS, D, FF), jnp.float32) ** block_scale(arg_keys[14], (LAYERS, D, FF), ((1, 16),), -0.2, 0.2)), 9.14384366834664e-12, 3.7278746062296975e-11)
    shrink_first = normal_values(arg_keys[15], (LAYERS, FF, D), (0.00555 * PARAMS ** -0.5), 9.5367431640625e-06, ((1, 16),), jnp.float32)
    shrink_second = jnp.clip(jnp.exp(math.log(3.7278746062296975e-11) - 1.40534252 * jax.random.uniform(arg_keys[16], (LAYERS, FF, D), jnp.float32) ** block_scale(arg_keys[16], (LAYERS, FF, D), ((1, 16),), -0.2, 0.2)), 9.14384366834664e-12, 3.7278746062296975e-11)
    table_first = normal_values(arg_keys[17], (V, D), (0.00555 * PARAMS ** -0.5), 9.5367431640625e-06, ((1, 16),), jnp.float32)
    table_second = jnp.clip(jnp.exp(math.log(3.7278746062296975e-11) - 1.40534252 * jax.random.uniform(arg_keys[18], (V, D), jnp.float32) ** block_scale(arg_keys[18], (V, D), ((1, 16),), -0.2, 0.2)), 9.14384366834664e-12, 3.7278746062296975e-11)
    norm_first = normal_values(arg_keys[19], (NORMS, 2, D), (0.0222 * PARAMS ** -0.5), 3.814697265625e-05, ((2, 16),), jnp.float32)
    norm_second = jnp.clip(jnp.exp(math.log(5.978667005912541e-10) - 1.3981288 * jax.random.uniform(arg_keys[20], (NORMS, 2, D), jnp.float32) ** block_scale(arg_keys[20], (NORMS, 2, D), ((2, 16),), -0.2, 0.2)), 1.4770824841026098e-10, 5.978667005912541e-10)
    return dict(codons=codons, masked=masked, segments=segments, inward=inward, outward=outward, expand=expand, shrink=shrink, codon_table=codon_table, norm_params=norm_params, inward_first=inward_first, inward_second=inward_second, outward_first=outward_first, outward_second=outward_second, expand_first=expand_first, expand_second=expand_second, shrink_first=shrink_first, shrink_second=shrink_second, table_first=table_first, table_second=table_second, norm_first=norm_first, norm_second=norm_second)


NORM_EPS = 1e-05
HIGH = lax.Precision.HIGHEST
BETA_ONE = 0.9
BETA_TWO = 0.95
ADAM_EPS = 1e-08
DECAY = 0.1
RATE_MATRIX = 0.05
RATE_VECTOR = 0.3
CLIP = 0.05

@jax.custom_vjp
def low(v):
    return lax.optimization_barrier(v.astype(jnp.bfloat16)).astype(jnp.float32)

@jax.custom_vjp
def low_back(v):
    return v

def low_keep(v):
    return (low(v), None)

def low_pass(kept, grad):
    return (grad,)

def back_keep(v):
    return (v, None)

def back_low(kept, grad):
    return (low(grad),)
low.defvjp(low_keep, low_pass)
low_back.defvjp(back_keep, back_low)

def layer_norm(value, gain, bias):
    mean = lax.optimization_barrier(jnp.mean(value, -1, keepdims=True))
    centred = value - mean
    inverse = lax.rsqrt(lax.optimization_barrier(jnp.mean(centred * centred, -1, keepdims=True)) + NORM_EPS)
    return centred * inverse * gain + bias

def rotary_tables(length, size):
    freq = 10000.0 ** (-jnp.arange(size // 2, dtype=jnp.float32) * 2.0 / size)
    angle = jnp.arange(length, dtype=jnp.float32)[:, None] * freq[None, :]
    return (jnp.cos(angle)[:, None, :], jnp.sin(angle)[:, None, :])

def rotate(value, cosine, sine):
    half = value.shape[-1] // 2
    first = value[..., :half]
    second = value[..., half:]
    return jnp.concatenate([first * cosine - second * sine, second * cosine + first * sine], -1)

def forward(params, inputs, targets, weights_mask, segs):
    inward, outward, expand, shrink, table, norms = [low(p) for p in params]
    groups, length = inputs.shape
    vocab_ids = jnp.arange(V, dtype=jnp.int32)
    chosen = (inputs[..., None] == vocab_ids).astype(jnp.float32)
    resid = low_back(jnp.einsum('gsv,vd->gsd', chosen, table, precision=HIGH))
    cosine, sine = rotary_tables(length, HD)
    same = segs[:, :, None] == segs[:, None, :]
    scale = HD ** (-0.5)
    for layer in range(LAYERS):
        normed = low(layer_norm(resid, norms[2 * layer, 0], norms[2 * layer, 1]))
        mixed = low_back(jnp.einsum('gsd,de->gse', normed, inward[layer], precision=HIGH))
        mixed = mixed.reshape(groups, length, 3, H, HD)
        query = low(rotate(mixed[:, :, 0], cosine, sine))
        keys = low(rotate(mixed[:, :, 1], cosine, sine))
        values = low(mixed[:, :, 2])
        scores = jnp.einsum('gqhe,gkhe->ghqk', query, keys, precision=HIGH) * scale
        scores = low_back(jnp.where(same[:, None], scores, -1000000000.0))
        top = lax.optimization_barrier(jnp.max(scores, -1, keepdims=True))
        expo = jnp.exp(scores - top)
        probs = low(expo / lax.optimization_barrier(jnp.sum(expo, -1, keepdims=True)))
        attended = jnp.einsum('ghqk,gkhe->gqhe', probs, values, precision=HIGH)
        attended = low(low_back(attended)).reshape(groups, length, H * HD)
        resid = resid + low_back(jnp.einsum('gsd,de->gse', attended, outward[layer], precision=HIGH))
        normed_mid = low(layer_norm(resid, norms[2 * layer + 1, 0], norms[2 * layer + 1, 1]))
        hidden = low_back(jnp.einsum('gsd,df->gsf', normed_mid, expand[layer], precision=HIGH))
        active = low(jax.nn.gelu(hidden))
        resid = resid + low_back(jnp.einsum('gsf,fd->gsd', active, shrink[layer], precision=HIGH))
    head_in = low(layer_norm(resid, norms[2 * LAYERS, 0], norms[2 * LAYERS, 1]))
    logits = low_back(jnp.einsum('gsd,vd->gsv', head_in, table, precision=HIGH))
    top = lax.optimization_barrier(jnp.max(logits, -1, keepdims=True))
    lse = top[..., 0] + jnp.log(lax.optimization_barrier(jnp.sum(jnp.exp(logits - top), -1)))
    picked = lax.optimization_barrier(jnp.sum(logits * (targets[..., None] == vocab_ids).astype(jnp.float32), -1))
    return jnp.sum((lse - picked) * weights_mask)

def adam_step(master, grad, first, second, rate, decay):
    first = BETA_ONE * first + (1.0 - BETA_ONE) * grad
    second = BETA_TWO * second + (1.0 - BETA_TWO) * grad * grad
    fix_one = 1.0 - BETA_ONE ** STEP
    fix_two = 1.0 - BETA_TWO ** STEP
    update = first / fix_one / (jnp.sqrt(second / fix_two) + ADAM_EPS) + decay * master
    return (master - rate * update, first, second)

def reference(codons, masked, segments, inward, outward, expand, shrink, codon_table, norm_params, inward_first, inward_second, outward_first, outward_second, expand_first, expand_second, shrink_first, shrink_second, table_first, table_second, norm_first, norm_second):
    params = (inward, outward, expand, shrink, codon_table, norm_params)
    rows = min(TOKENS, 4096)
    blocks = TOKENS // rows
    seqs = rows // TOK_DEV
    inputs = jnp.where(masked == 1, V - 1, codons).astype(jnp.int32)

    def shape(arr):
        return arr.reshape(blocks, seqs, TOK_DEV)

    def step(carry, block):
        total, sums = carry
        inp, tgt, msk, seg = block
        value, pull = jax.vjp(lambda p: forward(p, inp, tgt, msk.astype(inward.dtype), seg), params)
        delta, = pull(jnp.ones((), value.dtype))
        return ((total + value, jax.tree.map(jnp.add, sums, delta)), None)
    zeros = jax.tree.map(jnp.zeros_like, params)
    start = (jnp.zeros((), inward.dtype), zeros)
    (loss_sum, sums), _ = lax.scan(step, start, (shape(inputs), shape(codons), shape(masked), shape(segments)))
    mask_count = jnp.sum(masked.astype(inward.dtype))
    grads = [g / mask_count for g in sums]
    squares = jnp.zeros((), inward.dtype)
    for g in grads:
        squares = squares + jnp.sum(g * g)
    grad_norm = jnp.sqrt(squares)
    factor = CLIP / jnp.maximum(grad_norm, CLIP)
    firsts = (inward_first, outward_first, expand_first, shrink_first, table_first, norm_first)
    seconds = (inward_second, outward_second, expand_second, shrink_second, table_second, norm_second)
    result = [loss_sum, mask_count, grad_norm]
    for index in range(6):
        rate = RATE_VECTOR if index == 5 else RATE_MATRIX
        decay = 0.0 if index == 5 else DECAY
        result.extend(adam_step(params[index], grads[index] * factor, firsts[index], seconds[index], rate, decay))
    return (result[0], result[1], result[2], result[3], result[4], result[5], result[6], result[7], result[8], result[9], result[10], result[11], result[12], result[13], result[14], result[15], result[16], result[17], result[18], result[19], result[20])
```

```python
import functools

import jax
import jax.numpy as jnp
from jax import lax
from jax.sharding import PartitionSpec as P

HD = 64
V = 70
STEP = 10


NORM_EPS = 1e-05
BETA_ONE = 0.9
BETA_TWO = 0.95
ADAM_EPS = 1e-08
DECAY = 0.1
RATE_MATRIX = 0.05
RATE_VECTOR = 0.3
CLIP = 0.05


def rotary_tables(length, size):
    freq = 10000.0 ** (-jnp.arange(size // 2, dtype=jnp.float32) * 2.0 / size)
    angle = jnp.arange(length, dtype=jnp.float32)[:, None] * freq[None, :]
    return (jnp.cos(angle)[:, None, :], jnp.sin(angle)[:, None, :])


def rotate(value, cosine, sine):
    half = value.shape[-1] // 2
    first = value[..., :half]
    second = value[..., half:]
    return jnp.concatenate([first * cosine - second * sine, second * cosine + first * sine], -1)


def normalize(resid, gain, bias):
    mean = jnp.mean(resid, -1, keepdims=True)
    centred = resid - mean
    inverse = lax.rsqrt(jnp.mean(centred * centred, -1, keepdims=True) + NORM_EPS)
    unit = centred * inverse
    return (unit * gain + bias, unit, inverse)


def normalize_back(grad, unit, inverse, gain):
    scaled = grad * gain
    across = (
        scaled
        - jnp.mean(scaled, -1, keepdims=True)
        - unit * jnp.mean(scaled * unit, -1, keepdims=True)
    )
    return (across * inverse, jnp.sum(grad * unit, 0), jnp.sum(grad, 0))


def layer_forward(resid, weights, cosine, sine, same):
    w_in, w_out, w_up, w_down, gains = weights
    length = resid.shape[0]
    width = w_out.shape[0]
    heads = width // HD
    normed, unit_in, inverse_in = normalize(resid, gains[0, 0], gains[0, 1])
    normed_low = normed.astype(jnp.bfloat16)
    mixed = dots(normed_low, w_in).reshape(length, 3, heads, HD)
    query = rotate(mixed[:, 0], cosine, sine).astype(jnp.bfloat16)
    keys = rotate(mixed[:, 1], cosine, sine).astype(jnp.bfloat16)
    values = mixed[:, 2].astype(jnp.bfloat16)
    scores = jnp.einsum("qhe,khe->hqk", query, keys, preferred_element_type=jnp.float32) * HD ** (
        -0.5
    )
    scores = jnp.where(same[None], scores, -1000000000.0)
    top = jnp.max(scores, -1, keepdims=True)
    expo = jnp.exp(scores - top)
    total = jnp.sum(expo, -1, keepdims=True)
    probs = expo / total
    probs_low = probs.astype(jnp.bfloat16)
    attended = jnp.einsum("hqk,khe->qhe", probs_low, values, preferred_element_type=jnp.float32)
    attended = attended.astype(jnp.bfloat16).reshape(length, width)
    middle = resid + dots(attended, [w_out])
    normed_mid, unit_mid, inverse_mid = normalize(middle, gains[1, 0], gains[1, 1])
    normed_mid_low = normed_mid.astype(jnp.bfloat16)
    hidden = dots(normed_mid_low, w_up)
    active = jax.nn.gelu(hidden).astype(jnp.bfloat16)
    output = middle
    width = w_down[0].shape[0]
    for part, w_part in enumerate(w_down):
        output = output + jnp.dot(
            active[:, part * width : (part + 1) * width],
            w_part,
            preferred_element_type=jnp.float32,
        )
    saved = (
        normed_low,
        unit_in,
        inverse_in,
        query,
        keys,
        values,
        probs,
        probs_low,
        attended,
        unit_mid,
        inverse_mid,
        normed_mid_low,
        hidden,
        active,
    )
    return (output, saved)


def dots(value, weights):
    return jnp.concatenate(
        [jnp.dot(value, w, preferred_element_type=jnp.float32) for w in weights], 1
    )


def dots_back(grad, weights):
    total, at = 0.0, 0
    for w in weights:
        part = grad[:, at : at + w.shape[1]]
        total = total + jnp.dot(part, w.T, preferred_element_type=jnp.float32)
        at += w.shape[1]
    return total


def layer_back(saved, weights, cosine, sine, grad_out):
    (
        normed_low,
        unit_in,
        inverse_in,
        query,
        keys,
        values,
        probs,
        probs_low,
        attended,
        unit_mid,
        inverse_mid,
        normed_mid_low,
        hidden,
        active,
    ) = saved
    w_in, w_out, w_up, w_down, gains = weights
    length = grad_out.shape[0]
    width = w_out.shape[0]
    heads = width // HD
    branch_grad = grad_out.astype(jnp.bfloat16)
    grad_down = jnp.dot(active.T, branch_grad, preferred_element_type=jnp.float32)
    grad_active = jnp.concatenate(
        [jnp.dot(branch_grad, w.T, preferred_element_type=jnp.float32) for w in w_down], 1
    )
    _, gelu_back = jax.vjp(jax.nn.gelu, hidden)
    grad_hidden = gelu_back(grad_active)[0].astype(jnp.bfloat16)
    grad_up = jnp.dot(normed_mid_low.T, grad_hidden, preferred_element_type=jnp.float32)
    grad_normed_mid = dots_back(grad_hidden, w_up)
    grad_middle, gain_mid, bias_mid = normalize_back(
        grad_normed_mid, unit_mid, inverse_mid, gains[1, 0]
    )
    grad_middle = grad_middle + grad_out
    attn_grad = grad_middle.astype(jnp.bfloat16)
    grad_wout = jnp.dot(attended.T, attn_grad, preferred_element_type=jnp.float32)
    grad_attended = jnp.dot(attn_grad, w_out.T, preferred_element_type=jnp.float32)
    grad_attended = grad_attended.astype(jnp.bfloat16).reshape(length, heads, HD)
    grad_probs = jnp.einsum(
        "qhe,khe->hqk", grad_attended, values, preferred_element_type=jnp.float32
    )
    grad_scores = probs * (grad_probs - jnp.sum(probs * grad_probs, -1, keepdims=True))
    grad_scores = grad_scores.astype(jnp.bfloat16)
    scale = HD ** (-0.5)
    grad_query = (
        jnp.einsum("hqk,khe->qhe", grad_scores, keys, preferred_element_type=jnp.float32) * scale
    )
    grad_keys = (
        jnp.einsum("hqk,qhe->khe", grad_scores, query, preferred_element_type=jnp.float32) * scale
    )
    grad_values = jnp.einsum(
        "hqk,qhe->khe", probs_low, grad_attended, preferred_element_type=jnp.float32
    )
    grad_mixed = jnp.stack(
        [rotate(grad_query, cosine, -sine), rotate(grad_keys, cosine, -sine), grad_values], 1
    )
    grad_mixed = grad_mixed.reshape(length, 3 * width).astype(jnp.bfloat16)
    grad_in = jnp.dot(normed_low.T, grad_mixed, preferred_element_type=jnp.float32)
    grad_normed = dots_back(grad_mixed, w_in)
    grad_resid, gain_in, bias_in = normalize_back(grad_normed, unit_in, inverse_in, gains[0, 0])
    grad_gains = [gain_in, bias_in, gain_mid, bias_mid]
    return (grad_resid + grad_middle, grad_in, grad_wout, grad_up, grad_down, grad_gains)


def adam_step(master, grad, first, second, rate, decay):
    first = BETA_ONE * first + (1.0 - BETA_ONE) * grad
    second = BETA_TWO * second + (1.0 - BETA_TWO) * grad * grad
    fix_one = 1.0 - BETA_ONE**STEP
    fix_two = 1.0 - BETA_TWO**STEP
    update = first / fix_one / (jnp.sqrt(second / fix_two) + ADAM_EPS) + decay * master
    return (master - rate * update, first, second)


def bits_of(size, swap):
    order = list(range(size.bit_length() - 1))
    if swap and len(order) > 1:
        order[0], order[1] = order[1], order[0]
    return order


def exchange(value, axis, size, bit=0):
    return lax.ppermute(value, axis, [(i, i ^ (1 << bit)) for i in range(size)])


def total_of(value, sizes):
    for axis, size in sizes:
        for bit in bits_of(size, False):
            value = value + exchange(value, axis, size, bit)
    return value


def scatter_sum(value, size, low, swap):
    levels = size.bit_length() - 1
    me = lax.axis_index("fsdp")
    rows, columns = value.shape[0] // size, value.shape[1]
    value = value.reshape((2,) * levels + (rows, columns))
    left = list(range(levels))[::-1]
    for bit in bits_of(size, swap):
        place = left.index(bit)
        left.remove(bit)
        mine = lax.rem(lax.div(me, 1 << bit), 2)
        send = lax.dynamic_index_in_dim(value, 1 - mine, place, keepdims=False)
        keep = lax.dynamic_index_in_dim(value, mine, place, keepdims=False)
        value = keep + exchange(send.astype(low), "fsdp", size, bit).astype(jnp.float32)
    return value


def reduce_matrix(grad, size, swap):
    core = lax.axis_index("dp")
    half = grad.shape[1] // 2
    send = lax.dynamic_slice_in_dim(grad, (1 - core) * half, half, 1)
    keep = lax.dynamic_slice_in_dim(grad, core * half, half, 1)
    grad = keep + exchange(send.astype(jnp.bfloat16), "dp", 2).astype(jnp.float32)
    return scatter_sum(grad, size, jnp.bfloat16, swap)


def both_halves(part):
    other = exchange(part, "dp", 2)
    first = lax.axis_index("dp") == 0
    return jnp.concatenate(
        [jnp.where(first, part, other), jnp.where(first, other, part)], 1
    )


def gather_halves(first, second):
    own = jnp.where(lax.axis_index("dp") == 0, first, second)
    own = lax.all_gather(own, "fsdp", axis=0, tiled=True)
    return lax.all_gather(own, "dp", axis=0, tiled=False)


def down_to_rows(shrink_shard, rows):
    return jnp.concatenate(
        [shrink_shard[at : at + rows] for at in range(0, shrink_shard.shape[0], rows)], 1
    )


def up_to_parts(expand_shard, size, rows, parts):
    r = expand_shard.shape[0]
    return expand_shard.reshape(r, size, parts, rows).transpose(0, 2, 1, 3).reshape(r, -1)


def up_from_parts(expand_shard, size, rows, parts):
    r = expand_shard.shape[0]
    return expand_shard.reshape(r, parts, size, rows).transpose(0, 2, 1, 3).reshape(r, -1)


def body(
    fsdp,
    codons,
    masked,
    segments,
    inward,
    outward,
    expand,
    shrink,
    codon_table,
    norm_params,
    inward_first,
    inward_second,
    outward_first,
    outward_second,
    expand_first,
    expand_second,
    shrink_first,
    shrink_second,
    table_first,
    table_second,
    norm_first,
    norm_second,
):
    layers = inward.shape[0]
    length = codons.shape[0]
    rows = inward.shape[1]
    width = rows * fsdp
    parts = shrink.shape[1] // rows
    low = jnp.bfloat16
    sizes = (("dp", 2), ("fsdp", fsdp))
    weight = masked.astype(jnp.float32)
    inputs = jnp.where(masked == 1, V - 1, codons)

    norms = norm_params.shape[0] * 2
    small = jnp.concatenate(
        [codon_table.astype(low), norm_params.astype(low).reshape(norms, rows)], 0
    ).T
    small = jnp.pad(small, ((0, 0), (0, -small.shape[1] % 128)))
    w_in, w_out = inward.astype(low), outward.astype(low)
    w_up = [up_to_parts(expand[l].astype(low), fsdp, rows, parts) for l in range(layers)]
    w_down = [down_to_rows(shrink[l].astype(low), rows) for l in range(layers)]
    half = (3 * width + width) // 2
    mixer = [jnp.concatenate([w_in[l], w_out[l]], 1) for l in range(layers)]
    whole = []
    first = gather_halves(
        jnp.concatenate([mixer[0][:, :half], small], 1),
        jnp.concatenate([mixer[0][:, half:], small], 1),
    )
    second = gather_halves(w_up[0], w_down[0])
    small = first[0, :, half:]
    whole.append((first[0, :, :half], first[1, :, :half], second[0], second[1]))
    for l in range(1, layers):
        cut = parts * width // 2
        later = gather_halves(
            jnp.concatenate([mixer[l], w_up[l][:, :cut]], 1),
            jnp.concatenate([w_up[l][:, cut:], w_down[l]], 1),
        )
        whole.append(
            (
                later[0, :, :half],
                later[0, :, half : 2 * half],
                jnp.concatenate([later[0, :, 2 * half :], later[1, :, :cut]], 1),
                later[1, :, cut:],
            )
        )
    table_low = small[:, :V].T
    gains = small[:, V : V + norms].T.astype(jnp.float32).reshape(-1, 2, width)
    weights = []
    for l in range(layers):
        left, right, up, down = whole[l]
        weights.append(
            (
                [left, right[:, : 3 * width - half]],
                right[:, 3 * width - half :],
                [up],
                [down[:, p * width : (p + 1) * width] for p in range(parts)],
                gains[2 * l : 2 * l + 2],
            )
        )

    cosine, sine = rotary_tables(length, HD)
    same = segments[:, None] == segments[None, :]
    vocab_ids = jnp.arange(V, dtype=jnp.int32)
    chosen = (inputs[:, None] == vocab_ids[None, :]).astype(low)
    resid = jnp.dot(chosen, table_low, preferred_element_type=jnp.float32)
    kept = []
    for l in range(layers):
        resid, saved = layer_forward(resid, weights[l], cosine, sine, same)
        kept.append(saved)
    final_gain = gains[2 * layers]
    normed_out, unit_out, inverse_out = normalize(resid, final_gain[0], final_gain[1])
    head_in = normed_out.astype(low)
    logits = jnp.einsum("sd,vd->sv", head_in, table_low, preferred_element_type=jnp.float32)
    top = jnp.max(logits, -1, keepdims=True)
    lse_head = top + jnp.log(jnp.sum(jnp.exp(logits - top), -1, keepdims=True))
    targets = (codons[:, None] == vocab_ids[None, :]).astype(jnp.float32)
    picked = jnp.sum(logits * targets, -1)
    loss_local = jnp.sum((lse_head[:, 0] - picked) * weight)
    scalars = total_of(jnp.stack([loss_local, jnp.sum(weight)])[None], sizes)
    loss_sum, count = scalars[0, 0], scalars[0, 1]
    grad_logits = ((jnp.exp(logits - lse_head) - targets) * weight[:, None]).astype(low)
    grad_table = jnp.einsum("sv,sd->vd", grad_logits, head_in, preferred_element_type=jnp.float32)
    grad_head = jnp.dot(grad_logits, table_low, preferred_element_type=jnp.float32)
    grad, grad_final_gain, grad_final_bias = normalize_back(
        grad_head, unit_out, inverse_out, final_gain[0]
    )
    grad_norms = [grad_final_gain, grad_final_bias]
    shares = [[None] * layers for _ in range(4)]
    for l in reversed(range(layers)):
        grad, grad_in, grad_wout, grad_up, grad_down, grad_gains = layer_back(
            kept[l], weights[l], cosine, sine, grad
        )
        grad_norms = grad_gains + grad_norms
        grad_down = jnp.concatenate(
            [grad_down[p * width : (p + 1) * width] for p in range(parts)], 1
        )
        for index, (value, swap) in enumerate(
            ((grad_in, False), (grad_wout, True), (grad_up, True), (grad_down, False))
        ):
            shares[index][l] = reduce_matrix(value, fsdp, swap)
    grad_table = grad_table + jnp.einsum(
        "sv,sd->vd", chosen, grad.astype(low), preferred_element_type=jnp.float32
    )
    grad_small = jnp.concatenate([grad_table, jnp.stack(grad_norms)], 0)
    grad_small = grad_small + exchange(grad_small, "dp", 2)
    grad_small = grad_small.reshape(V + norms, fsdp, rows).transpose(1, 0, 2)
    share_small = scatter_sum(grad_small.reshape(-1, rows), fsdp, jnp.float32, False)

    squares = jnp.zeros((), jnp.float32)
    for value in sum(shares, []):
        squares = squares + jnp.sum(value * value)
    squares = squares + 0.5 * jnp.sum(share_small * share_small)
    square_total = total_of(squares.reshape(1, 1), sizes)[0, 0]
    shares = [[both_halves(value) for value in group] for group in shares]
    share_in, share_out, share_up, share_down = shares
    share_up = [up_from_parts(value, fsdp, rows, parts) for value in share_up]
    share_down = [
        jnp.concatenate([value[:, p * width : (p + 1) * width] for p in range(parts)], 0)
        for value in share_down
    ]
    group = (
        jnp.stack(share_in),
        jnp.stack(share_out),
        jnp.stack(share_up),
        jnp.stack(share_down),
        share_small[:V],
        share_small[V:].reshape(-1, 2, rows),
    )
    grad_norm = jnp.sqrt(square_total) / count
    factor = CLIP / jnp.maximum(grad_norm, CLIP)
    masters = (inward, outward, expand, shrink, codon_table, norm_params)
    firsts = (inward_first, outward_first, expand_first, shrink_first, table_first, norm_first)
    seconds = (
        inward_second,
        outward_second,
        expand_second,
        shrink_second,
        table_second,
        norm_second,
    )
    result = [loss_sum, count, grad_norm]
    for index in range(6):
        rate = RATE_VECTOR if index == 5 else RATE_MATRIX
        decay = 0.0 if index == 5 else DECAY
        clipped = group[index] / count * factor
        result.extend(
            adam_step(masters[index], clipped, firsts[index], seconds[index], rate, decay)
        )
    return tuple(result)


def solution(mesh):
    in_specs = (
        P(("fsdp", "dp")),
        P(("fsdp", "dp")),
        P(("fsdp", "dp")),
        P(None, "fsdp", None),
        P(None, "fsdp", None),
        P(None, "fsdp", None),
        P(None, "fsdp", None),
        P(None, "fsdp"),
        P(None, None, "fsdp"),
        P(None, "fsdp", None),
        P(None, "fsdp", None),
        P(None, "fsdp", None),
        P(None, "fsdp", None),
        P(None, "fsdp", None),
        P(None, "fsdp", None),
        P(None, "fsdp", None),
        P(None, "fsdp", None),
        P(None, "fsdp"),
        P(None, "fsdp"),
        P(None, None, "fsdp"),
        P(None, None, "fsdp"),
    )
    out_specs = (
        P(),
        P(),
        P(),
        P(None, "fsdp", None),
        P(None, "fsdp", None),
        P(None, "fsdp", None),
        P(None, "fsdp", None),
        P(None, "fsdp", None),
        P(None, "fsdp", None),
        P(None, "fsdp", None),
        P(None, "fsdp", None),
        P(None, "fsdp", None),
        P(None, "fsdp", None),
        P(None, "fsdp", None),
        P(None, "fsdp", None),
        P(None, "fsdp"),
        P(None, "fsdp"),
        P(None, "fsdp"),
        P(None, None, "fsdp"),
        P(None, None, "fsdp"),
        P(None, None, "fsdp"),
    )
    step = functools.partial(body, mesh.shape["fsdp"])
    return jax.shard_map(step, mesh=mesh, in_specs=in_specs, out_specs=out_specs, check_vma=False)
```

```python
import functools

import jax
import jax.numpy as jnp
from jax import lax
from jax.sharding import PartitionSpec as P

HD = 64
V = 70
STEP = 10


NORM_EPS = 1e-05
BETA_ONE = 0.9
BETA_TWO = 0.95
ADAM_EPS = 1e-08
DECAY = 0.1
RATE_MATRIX = 0.05
RATE_VECTOR = 0.3
CLIP = 0.05


def rotary_tables(length, size):
    freq = 10000.0 ** (-jnp.arange(size // 2, dtype=jnp.float32) * 2.0 / size)
    angle = jnp.arange(length, dtype=jnp.float32)[:, None] * freq[None, :]
    return (jnp.cos(angle)[:, None, :], jnp.sin(angle)[:, None, :])


def rotate(value, cosine, sine):
    half = value.shape[-1] // 2
    first = value[..., :half]
    second = value[..., half:]
    return jnp.concatenate([first * cosine - second * sine, second * cosine + first * sine], -1)


def normalize(resid, gain, bias):
    mean = jnp.mean(resid, -1, keepdims=True)
    centred = resid - mean
    inverse = lax.rsqrt(jnp.mean(centred * centred, -1, keepdims=True) + NORM_EPS)
    unit = centred * inverse
    return (unit * gain + bias, unit, inverse)


def normalize_back(grad, unit, inverse, gain):
    scaled = grad * gain
    across = (
        scaled
        - jnp.mean(scaled, -1, keepdims=True)
        - unit * jnp.mean(scaled * unit, -1, keepdims=True)
    )
    return (across * inverse, jnp.sum(grad * unit, 0), jnp.sum(grad, 0))


def dot(left, right):
    return jnp.dot(left, right, preferred_element_type=jnp.float32)


def cross(left, right):
    return jnp.dot(left.T, right, preferred_element_type=jnp.float32)


def in_order(own, other):
    first = lax.axis_index("dp") == 0
    return jnp.concatenate(
        [jnp.where(first, own, other), jnp.where(first, other, own)], 1
    )


def half_of(value, core):
    half = value.shape[1] // 2
    return lax.dynamic_slice_in_dim(value, core * half, half, 1)


def attention_forward(resid, mixer, gains, cosine, sine, same):
    (own_a, other_a), (own_b, other_b) = mixer
    length, width = resid.shape
    heads = width // HD
    half = width // 2
    w_query = in_order(own_a[:, :half], other_a[:, :half])
    w_keys = in_order(own_a[:, half:], other_a[:, half:])
    w_values = in_order(own_b[:, :half], other_b[:, :half])
    w_out = in_order(own_b[:, half:], other_b[:, half:])
    normed, unit_in, inverse_in = normalize(resid, gains[0, 0], gains[0, 1])
    normed_low = normed.astype(jnp.bfloat16)
    shape = (length, heads, HD)
    query = rotate(dot(normed_low, w_query).reshape(shape), cosine, sine).astype(jnp.bfloat16)
    keys = rotate(dot(normed_low, w_keys).reshape(shape), cosine, sine).astype(jnp.bfloat16)
    values = dot(normed_low, w_values).reshape(shape).astype(jnp.bfloat16)
    scores = jnp.einsum("qhe,khe->hqk", query, keys, preferred_element_type=jnp.float32) * HD ** (
        -0.5
    )
    scores = jnp.where(same[None], scores, -1000000000.0)
    top = jnp.max(scores, -1, keepdims=True)
    expo = jnp.exp(scores - top)
    total = jnp.sum(expo, -1, keepdims=True)
    probs = expo / total
    probs_low = probs.astype(jnp.bfloat16)
    attended = jnp.einsum("hqk,khe->qhe", probs_low, values, preferred_element_type=jnp.float32)
    attended = attended.astype(jnp.bfloat16).reshape(length, width)
    middle = resid + dot(attended, w_out)
    kept = (
        (w_query, w_keys, w_values, w_out),
        normed_low,
        unit_in,
        inverse_in,
        query,
        keys,
        values,
        probs,
        probs_low,
        attended,
    )
    return middle, kept


def hidden_forward(middle, ups, downs, gains):
    normed_mid, unit_mid, inverse_mid = normalize(middle, gains[1, 0], gains[1, 1])
    normed_mid_low = normed_mid.astype(jnp.bfloat16)
    hidden = [dot(normed_mid_low, w) for w in ups]
    active = [jax.nn.gelu(h).astype(jnp.bfloat16) for h in hidden]
    output = middle
    for a, w in zip(active, downs):
        output = output + dot(a, w)
    return output, (unit_mid, inverse_mid, normed_mid_low, hidden, active)


def adam_step(master, grad, first, second, rate, decay):
    first = BETA_ONE * first + (1.0 - BETA_ONE) * grad
    second = BETA_TWO * second + (1.0 - BETA_TWO) * grad * grad
    fix_one = 1.0 - BETA_ONE**STEP
    fix_two = 1.0 - BETA_TWO**STEP
    update = first / fix_one / (jnp.sqrt(second / fix_two) + ADAM_EPS) + decay * master
    return (master - rate * update, first, second)


def bits_of(size, swap):
    order = list(range(size.bit_length() - 1))
    if swap and len(order) > 1:
        order[0], order[1] = order[1], order[0]
    return order


def my_bit(bit):
    return lax.rem(lax.div(lax.axis_index("fsdp"), 1 << bit), 2)


class Links:
    def __init__(self, size):
        self.size = size
        self.live = []
        self.flying = []

    def add(self, stream):
        box = []
        link, rows = next(stream)
        self.live.append((stream, box, link, rows))
        return box

    def start(self):
        groups = {}
        for item in self.live:
            key = (str(item[2]), str(item[3].dtype), item[3].shape[1])
            groups.setdefault(key, []).append(item)
        self.flying = []
        for items in groups.values():
            link = items[0][2]
            rows = [item[3] for item in items]
            rows = rows[0] if len(rows) == 1 else jnp.concatenate(rows, 0)
            if link == "dp":
                got = lax.ppermute(rows, "dp", [(0, 1), (1, 0)])
            else:
                pairs = [(i, i ^ (1 << link)) for i in range(self.size)]
                got = lax.ppermute(rows, "fsdp", pairs)
            self.flying.append((items, got))

    def finish(self, tied=()):
        got, tied = lax.optimization_barrier(([g for _, g in self.flying], tied))
        self.live = []
        for (items, _), rows in zip(self.flying, got):
            at = 0
            for stream, box, _, sent in items:
                part = rows if len(items) == 1 else rows[at : at + sent.shape[0]]
                at += sent.shape[0]
                try:
                    link, following = stream.send(part)
                    self.live.append((stream, box, link, following))
                except StopIteration as end:
                    box.append(end.value)
        return tied

    def drain(self):
        while self.live:
            self.start()
            self.finish()


def gather_stream(shard, size, swap):
    columns = shard.shape[1]
    value, held = shard, []
    for bit in reversed(bits_of(size, swap)):
        got = yield bit, value.reshape(-1, columns)
        got = got.reshape(value.shape)
        low = my_bit(bit) == 0
        place = len([b for b in held if b > bit])
        held.append(bit)
        value = jnp.stack(
            [jnp.where(low, value, got), jnp.where(low, got, value)], place
        )
    value = value.reshape(-1, columns)
    other = yield "dp", value
    return value, other


def swap_stream(value):
    other = yield "dp", value
    return value, other


def scatter_steps(value, size, low, swap):
    levels = size.bit_length() - 1
    rows, columns = value.shape[0] // size, value.shape[1]
    value = value.reshape((2,) * levels + (rows, columns))
    left = list(range(levels))[::-1]
    for bit in bits_of(size, swap):
        place = left.index(bit)
        left.remove(bit)
        mine = my_bit(bit)
        send = lax.dynamic_index_in_dim(value, 1 - mine, place, keepdims=False)
        keep = lax.dynamic_index_in_dim(value, mine, place, keepdims=False)
        got = yield bit, send.astype(low).reshape(-1, columns)
        value = keep + got.reshape(keep.shape).astype(jnp.float32)
    return value


def tile_stream(send, keep, size, swap):
    got = yield "dp", send
    return (yield from scatter_steps(keep() + got.astype(jnp.float32), size, jnp.bfloat16, swap))


def small_stream(value, size, rows):
    got = yield "dp", value
    value = (value + got).reshape(-1, size, rows).transpose(1, 0, 2).reshape(-1, rows)
    return (yield from scatter_steps(value, size, jnp.float32, False))


def total_stream(value, size):
    for link in ["dp"] + bits_of(size, False):
        got = yield link, value
        value = value + got
    return value


def up_to_parts(expand_shard, size, rows, parts):
    r = expand_shard.shape[0]
    return expand_shard.reshape(r, size, parts, rows).transpose(0, 2, 1, 3).reshape(r, -1)


def up_from_parts(expand_shard, size, rows, parts):
    r = expand_shard.shape[0]
    return expand_shard.reshape(r, parts, size, rows).transpose(0, 2, 1, 3).reshape(r, -1)


def body(
    fsdp,
    codons,
    masked,
    segments,
    inward,
    outward,
    expand,
    shrink,
    codon_table,
    norm_params,
    inward_first,
    inward_second,
    outward_first,
    outward_second,
    expand_first,
    expand_second,
    shrink_first,
    shrink_second,
    table_first,
    table_second,
    norm_first,
    norm_second,
):
    layers = inward.shape[0]
    length = codons.shape[0]
    rows = inward.shape[1]
    width = rows * fsdp
    half = width // 2
    parts = shrink.shape[1] // rows
    low = jnp.bfloat16
    core = lax.axis_index("dp")
    weight = masked.astype(jnp.float32)
    inputs = jnp.where(masked == 1, V - 1, codons)
    links = Links(fsdp)

    norms = norm_params.shape[0] * 2
    small = jnp.concatenate(
        [codon_table.astype(low), norm_params.astype(low).reshape(norms, rows)], 0
    ).reshape(-1)
    small_size = small.shape[0]
    small = jnp.pad(small, (0, -small_size % (16 * width))).reshape(-1, width)

    def mixer_of(l):
        w_in, w_out = inward[l].astype(low), outward[l].astype(low)
        pieces = [half_of(w_in[:, p * width : (p + 1) * width], core) for p in range(3)]
        pieces.append(half_of(w_out, core))
        return jnp.concatenate(pieces[:2], 1), jnp.concatenate(pieces[2:], 1)

    def up_of(l):
        own = half_of(up_to_parts(expand[l].astype(low), fsdp, rows, parts), core)
        return own[:, :width], own[:, width:]

    def down_of(l):
        own = lax.dynamic_slice_in_dim(shrink[l].astype(low), core * 2 * rows, 2 * rows, 0)
        return own[:rows], own[rows:]

    def gather(pair):
        return [links.add(gather_stream(v, fsdp, swap)) for v, swap in zip(pair, (False, True))]

    late = jnp.concatenate(up_of(layers - 1) + down_of(layers - 1), 1)
    late = lax.all_gather(late, "fsdp", axis=0, tiled=True)
    mixers, ups, downs = [None] * layers, [None] * layers, [None] * layers
    table_box = links.add(gather_stream(small, fsdp, False))
    for l in range(layers):
        mixers[l] = gather(mixer_of(l))
        links.start()
        links.finish()
        if l < layers - 1:
            ups[l] = gather(up_of(l))
            links.start()
            links.finish()
            downs[l] = gather(down_of(l))
            links.start()
            links.finish()
    links.drain()
    late_box = links.add(swap_stream(late))
    links.drain()
    late, late_other = late_box[0]
    cut = lambda v, p: v[:, p * width : (p + 1) * width]
    ups[-1] = [[(cut(late, p), cut(late_other, p))] for p in (0, 1)]
    downs[-1] = [[(cut(late, p), cut(late_other, p))] for p in (2, 3)]
    pairs = lambda boxes: (boxes[0][0], boxes[1][0])
    own_first = lambda boxes: [b[0][0] for b in boxes] + [b[0][1] for b in boxes]
    small = table_box[0][0].reshape(fsdp, -1)[:, :small_size]
    small = small.reshape(fsdp, V + norms, rows).transpose(1, 0, 2).reshape(V + norms, width)
    table_low = small[:V]
    gains = small[V:].astype(jnp.float32).reshape(-1, 2, width)

    cosine, sine = rotary_tables(length, HD)
    same = segments[:, None] == segments[None, :]
    vocab_ids = jnp.arange(V, dtype=jnp.int32)
    chosen = (inputs[:, None] == vocab_ids[None, :]).astype(low)
    resid = dot(chosen, table_low)
    kept = []
    for l in range(layers):
        gain = gains[2 * l : 2 * l + 2]
        middle, kept_mixer = attention_forward(resid, pairs(mixers[l]), gain, cosine, sine, same)
        resid, kept_hidden = hidden_forward(middle, own_first(ups[l]), own_first(downs[l]), gain)
        kept.append((kept_mixer, kept_hidden))
    final_gain = gains[2 * layers]
    normed_out, unit_out, inverse_out = normalize(resid, final_gain[0], final_gain[1])
    head_in = normed_out.astype(low)
    logits = jnp.einsum("sd,vd->sv", head_in, table_low, preferred_element_type=jnp.float32)
    top = jnp.max(logits, -1, keepdims=True)
    lse_head = top + jnp.log(jnp.sum(jnp.exp(logits - top), -1, keepdims=True))
    targets = (codons[:, None] == vocab_ids[None, :]).astype(jnp.float32)
    picked = jnp.sum(logits * targets, -1)
    loss_local = jnp.sum((lse_head[:, 0] - picked) * weight)
    scalars = jnp.stack([loss_local, jnp.sum(weight)])
    scalars_box = links.add(total_stream(jnp.pad(scalars, (0, 126))[None], fsdp))
    grad_logits = ((jnp.exp(logits - lse_head) - targets) * weight[:, None]).astype(low)
    grad_table = cross(grad_logits, head_in)
    grad_head = dot(grad_logits, table_low)
    grad, grad_final_gain, grad_final_bias = normalize_back(
        grad_head, unit_out, inverse_out, final_gain[0]
    )

    def scatter(tiles):
        boxes = []
        for (theirs, own), swap in zip(tiles, (False, True)):
            make = lambda pairs: jnp.concatenate([cross(a, b) for a, b in pairs], 1)
            send = make(theirs).astype(low)
            keep = functools.partial(make, own)
            boxes.append(links.add(tile_stream(send, keep, fsdp, swap)))
        return boxes

    grad_norms = [grad_final_gain, grad_final_bias]
    shares = [[None] * layers for _ in range(3)]
    for l in reversed(range(layers)):
        (w_mix, normed_low, unit_in, inverse_in, query, keys, values, probs, probs_low, attended), (
            unit_mid, inverse_mid, normed_mid_low, hidden, active,
        ) = kept[l]
        up_tiles, down_tiles = own_first(ups[l]), own_first(downs[l])
        gain = gains[2 * l : 2 * l + 2]
        heads = width // HD
        branch = grad.astype(low)
        links.start()
        grad_hidden = []
        for h, w in zip(hidden, down_tiles):
            _, gelu_back = jax.vjp(jax.nn.gelu, h)
            grad_active = jnp.einsum("sd,fd->sf", branch, w, preferred_element_type=jnp.float32)
            grad_hidden.append(gelu_back(grad_active)[0].astype(low))
        grad_hidden, branch = links.finish((grad_hidden, branch))
        shares[2][l] = scatter(
            [([(active[2 + s], branch)], [(active[s], branch)]) for s in range(2)]
        )
        links.start()
        grad_normed = 0.0
        for g, w in zip(grad_hidden, up_tiles):
            grad_normed = grad_normed + jnp.einsum(
                "sf,df->sd", g, w, preferred_element_type=jnp.float32
            )
        grad_middle, gain_mid, bias_mid = normalize_back(
            grad_normed, unit_mid, inverse_mid, gain[1, 0]
        )
        grad_middle = grad_middle + grad
        grad_middle, grad_hidden = links.finish((grad_middle, grad_hidden))
        shares[1][l] = scatter(
            [
                ([(normed_mid_low, grad_hidden[2 + s])], [(normed_mid_low, grad_hidden[s])])
                for s in range(2)
            ]
        )
        links.start()
        attn_grad = grad_middle.astype(low)
        w_query, w_keys, w_values, w_out = w_mix
        grad_attended = jnp.einsum(
            "sd,ed->se", attn_grad, w_out, preferred_element_type=jnp.float32
        )
        grad_attended = grad_attended.astype(low).reshape(length, heads, HD)
        grad_probs = jnp.einsum(
            "qhe,khe->hqk", grad_attended, values, preferred_element_type=jnp.float32
        )
        grad_scores = probs * (grad_probs - jnp.sum(probs * grad_probs, -1, keepdims=True))
        grad_scores = grad_scores.astype(low)
        grad_scores, grad_attended, attn_grad = links.finish(
            (grad_scores, grad_attended, attn_grad)
        )
        links.start()
        scale = HD ** (-0.5)
        grad_query = (
            jnp.einsum("hqk,khe->qhe", grad_scores, keys, preferred_element_type=jnp.float32)
            * scale
        )
        grad_keys = (
            jnp.einsum("hqk,qhe->khe", grad_scores, query, preferred_element_type=jnp.float32)
            * scale
        )
        grad_values = jnp.einsum(
            "hqk,qhe->khe", probs_low, grad_attended, preferred_element_type=jnp.float32
        )
        flat = lambda v: v.reshape(length, width).astype(low)
        grad_query = flat(rotate(grad_query, cosine, -sine))
        grad_keys = flat(rotate(grad_keys, cosine, -sine))
        grad_values = flat(grad_values)
        grad_query, grad_keys, grad_values, attn_grad = links.finish(
            (grad_query, grad_keys, grad_values, attn_grad)
        )
        tiles = [([], []), ([], [])]
        for place, c in enumerate((1 - core, core)):
            g_q, g_k, g_v, g_o = (
                half_of(v, c) for v in (grad_query, grad_keys, grad_values, attn_grad)
            )
            tiles[0][place].append((normed_low, jnp.concatenate([g_q, g_k], 1)))
            tiles[1][place].extend([(normed_low, g_v), (attended, g_o)])
        shares[0][l] = scatter(tiles)
        links.start()
        grad_normed = 0.0
        for g, w in ((grad_query, w_query), (grad_keys, w_keys), (grad_values, w_values)):
            grad_normed = grad_normed + jnp.einsum(
                "se,de->sd", g, w, preferred_element_type=jnp.float32
            )
        grad_resid, gain_in, bias_in = normalize_back(
            grad_normed, unit_in, inverse_in, gain[0, 0]
        )
        grad = grad_resid + grad_middle
        grad_norms = [gain_in, bias_in, gain_mid, bias_mid] + grad_norms
        if l == 0:
            grad_table = grad_table + cross(chosen, grad.astype(low))
        grad, grad_table = links.finish((grad, grad_table))
    grad_small = jnp.concatenate([grad_table, jnp.stack(grad_norms)], 0)
    small_box = links.add(small_stream(grad_small, fsdp, rows))
    links.drain()

    share_small = small_box[0]
    shares = [[[box[0] for box in pair] for pair in group] for group in shares]
    squares = 0.5 * jnp.sum(share_small * share_small)
    for value in sum(sum(shares, []), []):
        squares = squares + jnp.sum(value * value)
    squares = jnp.pad(squares.reshape(1, 1), ((0, 0), (0, 127)))
    total_box = links.add(total_stream(squares, fsdp))
    swapped = [
        [links.add(swap_stream(jnp.concatenate(pair, 0))) for pair in group] for group in shares
    ]
    links.drain()
    square_total = total_box[0][0, 0]
    loss_sum, count = scalars_box[0][0, 0], scalars_box[0][0, 1]

    def tiles_of(box):
        own, other = box[0]
        first = core == 0
        ordered = (jnp.where(first, own, other), jnp.where(first, other, own))
        return [v[s * rows : (s + 1) * rows] for v in ordered for s in range(2)]

    share_in, share_out, share_up, share_down = [], [], [], []
    for l in range(layers):
        a_0, b_0, a_1, b_1 = tiles_of(swapped[0][l])
        side = lambda x, y: jnp.concatenate([x, y], 1)
        share_in.append(
            jnp.concatenate(
                [a_0[:, :half], a_1[:, :half], a_0[:, half:], a_1[:, half:], b_0[:, :half], b_1[:, :half]], 1
            )
        )
        share_out.append(side(b_0[:, half:], b_1[:, half:]))
        up = jnp.concatenate(tiles_of(swapped[1][l]), 1)
        share_up.append(up_from_parts(up, fsdp, rows, parts))
        share_down.append(jnp.concatenate(tiles_of(swapped[2][l]), 0))
    group = (
        jnp.stack(share_in),
        jnp.stack(share_out),
        jnp.stack(share_up),
        jnp.stack(share_down),
        share_small[:V],
        share_small[V:].reshape(-1, 2, rows),
    )
    grad_norm = jnp.sqrt(square_total) / count
    factor = CLIP / jnp.maximum(grad_norm, CLIP)
    masters = (inward, outward, expand, shrink, codon_table, norm_params)
    firsts = (inward_first, outward_first, expand_first, shrink_first, table_first, norm_first)
    seconds = (
        inward_second,
        outward_second,
        expand_second,
        shrink_second,
        table_second,
        norm_second,
    )
    result = [loss_sum, count, grad_norm]
    for index in range(6):
        rate = RATE_VECTOR if index == 5 else RATE_MATRIX
        decay = 0.0 if index == 5 else DECAY
        clipped = group[index] / count * factor
        result.extend(
            adam_step(masters[index], clipped, firsts[index], seconds[index], rate, decay)
        )
    return tuple(result)


def solution(mesh):
    in_specs = (
        P(("fsdp", "dp")),
        P(("fsdp", "dp")),
        P(("fsdp", "dp")),
        P(None, "fsdp", None),
        P(None, "fsdp", None),
        P(None, "fsdp", None),
        P(None, "fsdp", None),
        P(None, "fsdp"),
        P(None, None, "fsdp"),
        P(None, "fsdp", None),
        P(None, "fsdp", None),
        P(None, "fsdp", None),
        P(None, "fsdp", None),
        P(None, "fsdp", None),
        P(None, "fsdp", None),
        P(None, "fsdp", None),
        P(None, "fsdp", None),
        P(None, "fsdp"),
        P(None, "fsdp"),
        P(None, None, "fsdp"),
        P(None, None, "fsdp"),
    )
    out_specs = (
        P(),
        P(),
        P(),
        P(None, "fsdp", None),
        P(None, "fsdp", None),
        P(None, "fsdp", None),
        P(None, "fsdp", None),
        P(None, "fsdp", None),
        P(None, "fsdp", None),
        P(None, "fsdp", None),
        P(None, "fsdp", None),
        P(None, "fsdp", None),
        P(None, "fsdp", None),
        P(None, "fsdp", None),
        P(None, "fsdp", None),
        P(None, "fsdp"),
        P(None, "fsdp"),
        P(None, "fsdp"),
        P(None, None, "fsdp"),
        P(None, None, "fsdp"),
        P(None, None, "fsdp"),
    )
    step = functools.partial(body, mesh.shape["fsdp"])
    return jax.shard_map(step, mesh=mesh, in_specs=in_specs, out_specs=out_specs, check_vma=False)
```

```python
import functools

import jax
import jax.numpy as jnp
from jax import lax
from jax.experimental import pallas as pl
from jax.experimental.pallas import tpu as pltpu
from jax.sharding import PartitionSpec as P

HD = 64
V = 70
STEP = 10


NORM_EPS = 1e-05
BETA_ONE = 0.9
BETA_TWO = 0.95
ADAM_EPS = 1e-08
DECAY = 0.1
RATE_MATRIX = 0.05
RATE_VECTOR = 0.3
CLIP = 0.05


def rotary_tables(length):
    freq = 10000.0 ** (-jnp.arange(HD // 2, dtype=jnp.float32) * 2.0 / HD)
    angle = jnp.arange(length, dtype=jnp.float32)[:, None] * freq[None, :]
    cosine, sine = jnp.cos(angle), jnp.sin(angle)
    return (
        jnp.concatenate([cosine] * 4, 1),
        jnp.concatenate([-sine, sine] * 2, 1),
    )


def normalize(resid, gain, bias):
    mean = jnp.mean(resid, -1, keepdims=True)
    centred = resid - mean
    inverse = lax.rsqrt(jnp.mean(centred * centred, -1, keepdims=True) + NORM_EPS)
    unit = centred * inverse
    return (unit * gain + bias, unit, inverse)


def normalize_back(grad, unit, inverse, gain):
    scaled = grad * gain
    across = (
        scaled
        - jnp.mean(scaled, -1, keepdims=True)
        - unit * jnp.mean(scaled * unit, -1, keepdims=True)
    )
    return (across * inverse, jnp.sum(grad * unit, 0, keepdims=True), jnp.sum(grad, 0, keepdims=True))


def dot(left, right):
    return jnp.dot(left, right, preferred_element_type=jnp.float32)


def dot_nt(left, right):
    return lax.dot_general(
        left, right, (((1,), (1,)), ((), ())), preferred_element_type=jnp.float32
    )


def cross(left, right):
    return lax.dot_general(
        left, right, (((0,), (0,)), ((), ())), preferred_element_type=jnp.float32
    )


VMEM_LIMIT = 56 * 1024 * 1024


def call(kernel, out_shapes, ins, anys, scratch, flops, outs_any=0):
    whole = pl.BlockSpec(memory_space=pltpu.VMEM)
    left = pl.BlockSpec(memory_space=pl.ANY)
    n = len(out_shapes)
    return pl.pallas_call(
        kernel,
        out_shape=[jax.ShapeDtypeStruct(s, t) for s, t in out_shapes],
        in_specs=[pl.BlockSpec(memory_space=pltpu.SMEM)]
        + [whole] * len(ins)
        + [left] * len(anys),
        out_specs=[whole] * (n - outs_any) + [left] * outs_any,
        scratch_shapes=scratch,
        compiler_params=pltpu.CompilerParams(vmem_limit_bytes=VMEM_LIMIT),
        cost_estimate=pl.CostEstimate(
            flops=flops,
            bytes_accessed=sum(x.size * x.dtype.itemsize for x in ins + anys),
            transcendentals=0,
        ),
    )(lax.axis_index("dp").reshape(1).astype(jnp.int32), *ins, *anys)


def fetch(sources, targets, sems):
    copies = [pltpu.make_async_copy(s, t, sems.at[i]) for i, (s, t) in enumerate(zip(sources, targets))]
    for c in copies:
        c.start()
    return copies


def swap_halves(value):
    lane = lax.broadcasted_iota(jnp.int32, value.shape, 1)
    return jnp.where(
        lax.rem(lane, HD) < HD // 2,
        pltpu.roll(value, 128 - HD // 2, 1),
        pltpu.roll(value, HD // 2, 1),
    )


def ordered(first, own, other):
    return jnp.concatenate([jnp.where(first, own, other), jnp.where(first, other, own)], 1)


def head_mask(shape, head):
    lane = lax.broadcasted_iota(jnp.int32, shape, 1)
    return (lane < HD) if head == 0 else (lane >= HD)


def attention_forward_kernel(
    core, resid, seg_col, seg_row, cosine, sine, gains, a_own, a_other, b_own, b_other,
    middle, normed_low, query, keys, values, attended, lse,
    w_a, w_b, mixed, same, sems,
):
    copies = fetch(
        [a_own, a_other, b_own, b_other], [w_a.at[0], w_a.at[1], w_b.at[0], w_b.at[1]], sems
    )
    first = core[0] == 0
    half = resid.shape[1] // 2
    normed, _, _ = normalize(resid[...], gains[0:1], gains[1:2])
    normed_low[...] = normed.astype(jnp.bfloat16)
    same[...] = jnp.where(seg_col[...] == seg_row[...], 0.0, 1.0)
    for place in range(2):
        copies[place].wait()
        mixed[...] = dot(normed_low[...], w_a[place])
        for p in range(half // 128):
            for part, target in ((0, query), (1, keys)):
                x = mixed[:, part * half + p * 128 : part * half + (p + 1) * 128]
                x = x * cosine[...] + swap_halves(x) * sine[...]
                target[:, place * half + p * 128 : place * half + (p + 1) * 128] = x.astype(jnp.bfloat16)
    for place in range(2):
        copies[2 + place].wait()
        values[:, place * half : (place + 1) * half] = dot(
            normed_low[...], w_b[place, :, :half]
        ).astype(jnp.bfloat16)

    lse[...] = jnp.zeros_like(lse)

    def pair(p, _):
        columns = pl.ds(pl.multiple_of(p * 128, 128), 128)
        q, k, v = query[:, columns], keys[:, columns], values[:, columns]
        out = []
        for head in range(2):
            masked_q = jnp.where(head_mask(q.shape, head), q, jnp.zeros_like(q))
            scores = dot_nt(masked_q, k) * HD ** (-0.5)
            scores = jnp.where(same[...] > 0.5, -1000000000.0, scores)
            top = jnp.max(scores, -1, keepdims=True)
            expo = jnp.exp(scores - top)
            total = jnp.sum(expo, -1, keepdims=True)
            probs = (expo / total).astype(jnp.bfloat16)
            out.append(dot(probs, v))
            lane = lax.broadcasted_iota(jnp.int32, lse.shape, 1)
            lse[...] = jnp.where(lane == 2 * p + head, top + jnp.log(total), lse[...])
        attended[:, columns] = jnp.where(head_mask(out[0].shape, 0), out[0], out[1]).astype(jnp.bfloat16)
        return 0

    lax.fori_loop(0, resid.shape[1] // 128, pair, 0)
    attended[...] = ordered(first, attended[:, :half], attended[:, half:])
    out = ordered(
        first, dot(attended[...], w_b[0, :, half:]), dot(attended[...], w_b[1, :, half:])
    )
    middle[...] = resid[...] + out


def attention_forward(resid, mixer, gains, cosine, sine, segments):
    (a_own, a_other), (b_own, b_other) = mixer
    length, width = resid.shape
    low, full = jnp.bfloat16, jnp.float32
    ins = [resid, segments[:, None], segments[None, :], cosine, sine, gains]
    outs = [((length, width), full)] + [((length, width), low)] * 5 + [((length, 128), full)]
    return call(
        attention_forward_kernel,
        outs,
        ins,
        [a_own, a_other, b_own, b_other],
        [
            pltpu.VMEM((2, width, width), low),
            pltpu.VMEM((2, width, width), low),
            pltpu.VMEM((length, width), full),
            pltpu.VMEM((length, length), full),
            pltpu.SemaphoreType.DMA((4,)),
        ],
        8 * length * width * width + 4 * length * length * width,
    )


GELU_SCALE = 0.7978845608028654
GELU_CUBE = 0.044715


def hidden_forward_kernel(
    core, middle, gains, u0, u1, u2, u3, d0, d1, d2, d3,
    output, normed_low, hidden, active, ups, downs, hidden_here, active_here, sems, out_sems,
):
    ins = fetch(
        [u0, d0, u1, d1, u2, d2, u3, d3],
        [w.at[t] for t in range(4) for w in (ups, downs)],
        sems,
    )
    normed, _, _ = normalize(middle[...], gains[0:1], gains[1:2])
    normed_low[...] = normed.astype(jnp.bfloat16)
    outs = []
    for t in range(4):
        ins[2 * t].wait()
        x = dot(normed_low[...], ups[t])
        hidden_here[t] = x
        inner = jnp.tanh(GELU_SCALE * (x + GELU_CUBE * (x * x * x)))
        active_here[t] = (x * (0.5 * (1.0 + inner))).astype(jnp.bfloat16)
        for here, there in ((hidden_here, hidden), (active_here, active)):
            out = pltpu.make_async_copy(here.at[t], there.at[t], out_sems.at[len(outs)])
            out.start()
            outs.append(out)
        ins[2 * t + 1].wait()
        product = dot(active_here[t], downs[t])
        output[...] = (middle[...] if t == 0 else output[...]) + product
    for out in outs:
        out.wait()


def hidden_forward(middle, ups, downs, gains):
    length, width = middle.shape
    low, full = jnp.bfloat16, jnp.float32
    many = (4, length, width)
    outs = [((length, width), full), ((length, width), low), (many, full), (many, low)]
    return call(
        hidden_forward_kernel,
        outs,
        [middle, gains],
        ups + downs,
        [
            pltpu.VMEM((4, width, width), low),
            pltpu.VMEM((4, width, width), low),
            pltpu.VMEM(many, full),
            pltpu.VMEM(many, low),
            pltpu.SemaphoreType.DMA((8,)),
            pltpu.SemaphoreType.DMA((8,)),
        ],
        16 * length * width * width,
        outs_any=2,
    )


def hidden_back_kernel(
    core, grad, middle, gains, hidden, u0, u1, u2, u3, d0, d1, d2, d3,
    grad_middle, grad_gains, grad_hidden, ups, downs, hidden_here, grad_here, total, sems, out_sems,
):
    ins = fetch(
        [r for t, d, u in ((0, d0, u0), (1, d1, u1), (2, d2, u2), (3, d3, u3)) for r in (d, hidden.at[t], u)],
        [w.at[t] for t in range(4) for w in (downs, hidden_here, ups)],
        sems,
    )
    branch = grad[...].astype(jnp.bfloat16)
    outs = []
    for t in range(4):
        ins[3 * t].wait()
        grad_active = dot_nt(branch, downs[t])
        ins[3 * t + 1].wait()
        x = hidden_here[t]
        inner = jnp.tanh(GELU_SCALE * (x + GELU_CUBE * (x * x * x)))
        slope = 0.5 * (1.0 + inner) + (0.5 * GELU_SCALE) * x * (1.0 - inner * inner) * (
            1.0 + (3.0 * GELU_CUBE) * (x * x)
        )
        grad_here[t] = (grad_active * slope).astype(jnp.bfloat16)
        out = pltpu.make_async_copy(grad_here.at[t], grad_hidden.at[t], out_sems.at[t])
        out.start()
        outs.append(out)
        ins[3 * t + 2].wait()
        product = dot_nt(grad_here[t], ups[t])
        total[...] = product if t == 0 else total[...] + product
    _, unit, inverse = normalize(middle[...], gains[0:1], gains[1:2])
    back, gain, bias = normalize_back(total[...], unit, inverse, gains[0:1])
    grad_middle[...] = grad[...] + back
    grad_gains[0:1] = gain
    grad_gains[1:2] = bias
    for out in outs:
        out.wait()


def hidden_back(grad, middle, hidden, ups, downs, gains):
    length, width = middle.shape
    low, full = jnp.bfloat16, jnp.float32
    many = (4, length, width)
    outs = [((length, width), full), ((2, width), full), (many, low)]
    return call(
        hidden_back_kernel,
        outs,
        [grad, middle, gains],
        [hidden] + ups + downs,
        [
            pltpu.VMEM((4, width, width), low),
            pltpu.VMEM((4, width, width), low),
            pltpu.VMEM(many, full),
            pltpu.VMEM(many, low),
            pltpu.VMEM((length, width), full),
            pltpu.SemaphoreType.DMA((12,)),
            pltpu.SemaphoreType.DMA((4,)),
        ],
        16 * length * width * width,
        outs_any=1,
    )


def attention_back_kernel(
    core, grad_middle, resid, seg_col, seg_row, cosine, sine, gains, query, keys, values, lse,
    a_own, a_other, b_own, b_other,
    grad, grad_gains, grad_a, grad_b,
    w_a, w_b, same, ga, gq, gk, gv, sems,
):
    copies = fetch(
        [b_own, b_other, a_own, a_other], [w_b.at[0], w_b.at[1], w_a.at[0], w_a.at[1]], sems
    )
    low = jnp.bfloat16
    first = core[0] == 0
    width = resid.shape[1]
    half = width // 2
    scale = HD ** (-0.5)
    same[...] = jnp.where(seg_col[...] == seg_row[...], 0.0, 1.0)
    attn_grad = grad_middle[...].astype(low)
    left, right = attn_grad[:, :half], attn_grad[:, half:]
    grad_b[0, :, half:] = jnp.where(first, left, right)
    grad_b[1, :, half:] = jnp.where(first, right, left)
    copies[0].wait()
    copies[1].wait()
    natural = dot_nt(grad_b[0, :, half:], w_b[0, :, half:]) + dot_nt(
        grad_b[1, :, half:], w_b[1, :, half:]
    )
    natural = natural.astype(low)
    ga[:, :half] = jnp.where(first, natural[:, :half], natural[:, half:])
    ga[:, half:] = jnp.where(first, natural[:, half:], natural[:, :half])

    def pair(p, _):
        columns = pl.ds(pl.multiple_of(p * 128, 128), 128)
        q, k, v, g = query[:, columns], keys[:, columns], values[:, columns], ga[:, columns]
        out_q, out_k, out_v = [], [], []
        for head in range(2):
            mask = head_mask(q.shape, head)
            zero = jnp.zeros_like(q)
            scores = dot_nt(k, jnp.where(mask, q, zero)) * scale
            scores = jnp.where(same[...] > 0.5, -1000000000.0, scores)
            probs = jnp.exp(scores - lse[pl.ds(2 * p + head, 1), :])
            grad_probs = dot_nt(v, jnp.where(mask, g, zero))
            across = jnp.sum(probs * grad_probs, 0, keepdims=True)
            grad_scores = (probs * (grad_probs - across)).astype(low)
            out_k.append(dot(grad_scores, q))
            out_q.append(cross(grad_scores, k))
            out_v.append(dot(probs.astype(low), g))
        for out, target in ((out_q, gq), (out_k, gk)):
            x = jnp.where(head_mask(out[0].shape, 0), out[0], out[1]) * scale
            x = x * cosine[...] - swap_halves(x) * sine[...]
            target[:, columns] = x.astype(low)
        gv[:, columns] = jnp.where(head_mask(out_v[0].shape, 0), out_v[0], out_v[1]).astype(low)
        return 0

    lax.fori_loop(0, width // 128, pair, 0)
    for place in range(2):
        columns = slice(place * half, (place + 1) * half)
        grad_a[place, :, :half] = gq[:, columns]
        grad_a[place, :, half:] = gk[:, columns]
        grad_b[place, :, :half] = gv[:, columns]
    copies[2].wait()
    copies[3].wait()
    total = dot_nt(grad_a[0], w_a[0]) + dot_nt(grad_a[1], w_a[1])
    total = total + dot_nt(grad_b[0, :, :half], w_b[0, :, :half])
    total = total + dot_nt(grad_b[1, :, :half], w_b[1, :, :half])
    _, unit, inverse = normalize(resid[...], gains[0:1], gains[1:2])
    back, gain, bias = normalize_back(total, unit, inverse, gains[0:1])
    grad[...] = grad_middle[...] + back
    grad_gains[0:1] = gain
    grad_gains[1:2] = bias


def attention_back(grad_middle, resid, mixer, gains, cosine, sine, segments, query, keys, values, lse):
    (a_own, a_other), (b_own, b_other) = mixer
    length, width = resid.shape
    low, full = jnp.bfloat16, jnp.float32
    outs = [((length, width), full), ((2, width), full)] + [((2, length, width), low)] * 2
    ins = [grad_middle, resid, segments[:, None], segments[None, :], cosine, sine, gains]
    ins += [query, keys, values, lse.T[: width // HD]]
    return call(
        attention_back_kernel,
        outs,
        ins,
        [a_own, a_other, b_own, b_other],
        [
            pltpu.VMEM((2, width, width), low),
            pltpu.VMEM((2, width, width), low),
            pltpu.VMEM((length, length), full),
        ]
        + [pltpu.VMEM((length, width), low)] * 4
        + [pltpu.SemaphoreType.DMA((4,))],
        8 * length * width * width + 10 * length * length * width,
    )


def adam_step(master, grad, first, second, rate, decay):
    first = BETA_ONE * first + (1.0 - BETA_ONE) * grad
    second = BETA_TWO * second + (1.0 - BETA_TWO) * grad * grad
    fix_one = 1.0 - BETA_ONE**STEP
    fix_two = 1.0 - BETA_TWO**STEP
    update = first / fix_one / (jnp.sqrt(second / fix_two) + ADAM_EPS) + decay * master
    return (master - rate * update, first, second)


def bits_of(size, swap):
    order = list(range(size.bit_length() - 1))
    if swap and len(order) > 1:
        order[0], order[1] = order[1], order[0]
    return order


def my_bit(bit):
    return lax.rem(lax.div(lax.axis_index("fsdp"), 1 << bit), 2)


class Links:
    def __init__(self, size):
        self.size = size
        self.live = []
        self.flying = []

    def add(self, stream):
        box = []
        link, rows = next(stream)
        self.live.append((stream, box, link, rows))
        return box

    def start(self):
        groups = {}
        for item in self.live:
            key = (str(item[2]), str(item[3].dtype), item[3].shape[1])
            groups.setdefault(key, []).append(item)
        self.flying = []
        for items in groups.values():
            link = items[0][2]
            rows = [item[3] for item in items]
            rows = rows[0] if len(rows) == 1 else jnp.concatenate(rows, 0)
            if link == "dp":
                got = lax.ppermute(rows, "dp", [(0, 1), (1, 0)])
            else:
                pairs = [(i, i ^ (1 << link)) for i in range(self.size)]
                got = lax.ppermute(rows, "fsdp", pairs)
            self.flying.append((items, got))

    def finish(self, tied=()):
        got, tied = lax.optimization_barrier(([g for _, g in self.flying], tied))
        self.live = []
        for (items, _), rows in zip(self.flying, got):
            at = 0
            for stream, box, _, sent in items:
                part = rows if len(items) == 1 else rows[at : at + sent.shape[0]]
                at += sent.shape[0]
                try:
                    link, following = stream.send(part)
                    self.live.append((stream, box, link, following))
                except StopIteration as end:
                    box.append(end.value)
        return tied

    def drain(self):
        while self.live:
            self.start()
            self.finish()


def gather_stream(shard, size, swap):
    columns = shard.shape[1]
    value, held = shard, []
    for bit in reversed(bits_of(size, swap)):
        got = yield bit, value.reshape(-1, columns)
        got = got.reshape(value.shape)
        low = my_bit(bit) == 0
        place = len([b for b in held if b > bit])
        held.append(bit)
        value = jnp.stack(
            [jnp.where(low, value, got), jnp.where(low, got, value)], place
        )
    value = value.reshape(-1, columns)
    other = yield "dp", value
    return value, other


def swap_stream(value):
    other = yield "dp", value
    return value, other


def scatter_steps(value, size, low, swap):
    levels = size.bit_length() - 1
    rows, columns = value.shape[0] // size, value.shape[1]
    value = value.reshape((2,) * levels + (rows, columns))
    left = list(range(levels))[::-1]
    for bit in bits_of(size, swap):
        place = left.index(bit)
        left.remove(bit)
        mine = my_bit(bit)
        send = lax.dynamic_index_in_dim(value, 1 - mine, place, keepdims=False)
        keep = lax.dynamic_index_in_dim(value, mine, place, keepdims=False)
        got = yield bit, send.astype(low).reshape(-1, columns)
        value = keep + got.reshape(keep.shape).astype(jnp.float32)
    return value


def tile_stream(send, keep, size, swap):
    got = yield "dp", send
    return (yield from scatter_steps(keep() + got.astype(jnp.float32), size, jnp.bfloat16, swap))


def small_stream(value, size, rows):
    got = yield "dp", value
    value = (value + got).reshape(-1, size, rows).transpose(1, 0, 2).reshape(-1, rows)
    return (yield from scatter_steps(value, size, jnp.float32, False))


def total_stream(value, size):
    for link in ["dp"] + bits_of(size, False):
        got = yield link, value
        value = value + got
    return value


def half_of(value, core):
    half = value.shape[1] // 2
    return lax.dynamic_slice_in_dim(value, core * half, half, 1)


def up_to_parts(expand_shard, size, rows, parts):
    r = expand_shard.shape[0]
    return expand_shard.reshape(r, size, parts, rows).transpose(0, 2, 1, 3).reshape(r, -1)


def up_from_parts(expand_shard, size, rows, parts):
    r = expand_shard.shape[0]
    return expand_shard.reshape(r, parts, size, rows).transpose(0, 2, 1, 3).reshape(r, -1)


def body(
    fsdp,
    codons,
    masked,
    segments,
    inward,
    outward,
    expand,
    shrink,
    codon_table,
    norm_params,
    inward_first,
    inward_second,
    outward_first,
    outward_second,
    expand_first,
    expand_second,
    shrink_first,
    shrink_second,
    table_first,
    table_second,
    norm_first,
    norm_second,
):
    layers = inward.shape[0]
    length = codons.shape[0]
    rows = inward.shape[1]
    width = rows * fsdp
    half = width // 2
    parts = shrink.shape[1] // rows
    low = jnp.bfloat16
    core = lax.axis_index("dp")
    weight = masked.astype(jnp.float32)
    inputs = jnp.where(masked == 1, V - 1, codons)
    links = Links(fsdp)

    norms = norm_params.shape[0] * 2
    small = jnp.concatenate(
        [codon_table.astype(low), norm_params.astype(low).reshape(norms, rows)], 0
    ).reshape(-1)
    small_size = small.shape[0]
    small = jnp.pad(small, (0, -small_size % (16 * width))).reshape(-1, width)

    def mixer_of(l):
        w_in, w_out = inward[l].astype(low), outward[l].astype(low)
        pieces = [half_of(w_in[:, p * width : (p + 1) * width], core) for p in range(3)]
        pieces.append(half_of(w_out, core))
        return jnp.concatenate(pieces[:2], 1), jnp.concatenate(pieces[2:], 1)

    def up_of(l):
        own = half_of(up_to_parts(expand[l].astype(low), fsdp, rows, parts), core)
        return own[:, :width], own[:, width:]

    def down_of(l):
        own = lax.dynamic_slice_in_dim(shrink[l].astype(low), core * 2 * rows, 2 * rows, 0)
        return own[:rows], own[rows:]

    def gather(pair):
        return [links.add(gather_stream(v, fsdp, swap)) for v, swap in zip(pair, (False, True))]

    late = jnp.concatenate(up_of(layers - 1) + down_of(layers - 1), 1)
    late = lax.all_gather(late, "fsdp", axis=0, tiled=True)
    mixers, ups, downs = [None] * layers, [None] * layers, [None] * layers
    table_box = links.add(gather_stream(small, fsdp, False))
    for l in range(layers):
        mixers[l] = gather(mixer_of(l))
        links.start()
        links.finish()
        if l < layers - 1:
            ups[l] = gather(up_of(l))
            links.start()
            links.finish()
            downs[l] = gather(down_of(l))
            links.start()
            links.finish()
    links.drain()
    late_box = links.add(swap_stream(late))
    links.drain()
    late, late_other = late_box[0]
    cut = lambda v, p: v[:, p * width : (p + 1) * width]
    ups[-1] = [[(cut(late, p), cut(late_other, p))] for p in (0, 1)]
    downs[-1] = [[(cut(late, p), cut(late_other, p))] for p in (2, 3)]
    pairs = lambda boxes: (boxes[0][0], boxes[1][0])
    own_first = lambda boxes: [b[0][0] for b in boxes] + [b[0][1] for b in boxes]
    small = table_box[0][0].reshape(fsdp, -1)[:, :small_size]
    small = small.reshape(fsdp, V + norms, rows).transpose(1, 0, 2).reshape(V + norms, width)
    table_low = small[:V]
    gains = small[V:].astype(jnp.float32).reshape(-1, 2, width)

    cosine, sine = rotary_tables(length)
    vocab_ids = jnp.arange(V, dtype=jnp.int32)
    chosen = (inputs[:, None] == vocab_ids[None, :]).astype(low)
    resid = dot(chosen, table_low)
    kept = []
    for l in range(layers):
        gain = gains[2 * l : 2 * l + 2]
        middle, *saved = attention_forward(
            resid, pairs(mixers[l]), gain[0], cosine, sine, segments
        )
        output, *saved_mid = hidden_forward(
            middle, own_first(ups[l]), own_first(downs[l]), gain[1]
        )
        kept.append((resid, saved, middle, saved_mid))
        resid = output
    final_gain = gains[2 * layers]
    normed_out, unit_out, inverse_out = normalize(resid, final_gain[0], final_gain[1])
    head_in = normed_out.astype(low)
    logits = jnp.einsum("sd,vd->sv", head_in, table_low, preferred_element_type=jnp.float32)
    top = jnp.max(logits, -1, keepdims=True)
    lse_head = top + jnp.log(jnp.sum(jnp.exp(logits - top), -1, keepdims=True))
    targets = (codons[:, None] == vocab_ids[None, :]).astype(jnp.float32)
    picked = jnp.sum(logits * targets, -1)
    loss_local = jnp.sum((lse_head[:, 0] - picked) * weight)
    scalars = jnp.stack([loss_local, jnp.sum(weight)])
    scalars_box = links.add(total_stream(jnp.pad(scalars, (0, 126))[None], fsdp))
    grad_logits = ((jnp.exp(logits - lse_head) - targets) * weight[:, None]).astype(low)
    grad_table = cross(grad_logits, head_in)
    grad_head = dot(grad_logits, table_low)
    grad, grad_final_gain, grad_final_bias = normalize_back(
        grad_head, unit_out, inverse_out, final_gain[0]
    )

    def scatter(tiles):
        boxes = []
        for (theirs, own), swap in zip(tiles, (False, True)):
            make = lambda pairs: jnp.concatenate([cross(a, b) for a, b in pairs], 1)
            send = make(theirs).astype(low)
            keep = functools.partial(make, own)
            boxes.append(links.add(tile_stream(send, keep, fsdp, swap)))
        return boxes

    grad_norms = [jnp.concatenate([grad_final_gain, grad_final_bias], 0)]
    shares = [[None] * layers for _ in range(3)]
    for l in reversed(range(layers)):
        resid, (normed_low, query, keys, values, attended, lse), middle, saved_mid = kept[l]
        normed_mid_low, hidden, active = saved_mid
        gain = gains[2 * l : 2 * l + 2]
        branch = grad.astype(low)
        shares[2][l] = scatter(
            [([(active[2 + s], branch)], [(active[s], branch)]) for s in range(2)]
        )
        links.start()
        grad_middle, gains_mid, grad_hidden = hidden_back(
            grad, middle, hidden, own_first(ups[l]), own_first(downs[l]), gain[1]
        )
        grad_middle, grad_hidden = links.finish((grad_middle, grad_hidden))
        shares[1][l] = scatter(
            [
                ([(normed_mid_low, grad_hidden[2 + s])], [(normed_mid_low, grad_hidden[s])])
                for s in range(2)
            ]
        )
        links.start()
        links.finish()
        links.start()
        grad, gains_in, grad_a, grad_b = attention_back(
            grad_middle, resid, pairs(mixers[l]), gain[0], cosine, sine, segments,
            query, keys, values, lse,
        )
        grad_norms = [gains_in, gains_mid] + grad_norms
        if l == 0:
            grad_table = grad_table + cross(chosen, grad.astype(low))
        grad, grad_a, grad_b, grad_table = links.finish((grad, grad_a, grad_b, grad_table))
        split = lambda g: (normed_low, g[:, : width // 2])
        outer = lambda g: (attended, g[:, width // 2 :])
        shares[0][l] = scatter(
            [
                ([(normed_low, grad_a[1])], [(normed_low, grad_a[0])]),
                ([split(grad_b[1]), outer(grad_b[1])], [split(grad_b[0]), outer(grad_b[0])]),
            ]
        )
    grad_small = jnp.concatenate([grad_table] + grad_norms, 0)
    small_box = links.add(small_stream(grad_small, fsdp, rows))
    links.drain()

    share_small = small_box[0]
    shares = [[[box[0] for box in pair] for pair in group] for group in shares]
    squares = 0.5 * jnp.sum(share_small * share_small)
    for value in sum(sum(shares, []), []):
        squares = squares + jnp.sum(value * value)
    squares = jnp.pad(squares.reshape(1, 1), ((0, 0), (0, 127)))
    total_box = links.add(total_stream(squares, fsdp))
    swapped = [
        [links.add(swap_stream(jnp.concatenate(pair, 0))) for pair in group] for group in shares
    ]
    links.drain()
    square_total = total_box[0][0, 0]
    loss_sum, count = scalars_box[0][0, 0], scalars_box[0][0, 1]

    def tiles_of(box):
        own, other = box[0]
        first = core == 0
        ordered = (jnp.where(first, own, other), jnp.where(first, other, own))
        return [v[s * rows : (s + 1) * rows] for v in ordered for s in range(2)]

    share_in, share_out, share_up, share_down = [], [], [], []
    for l in range(layers):
        a_0, b_0, a_1, b_1 = tiles_of(swapped[0][l])
        side = lambda x, y: jnp.concatenate([x, y], 1)
        share_in.append(
            jnp.concatenate(
                [a_0[:, :half], a_1[:, :half], a_0[:, half:], a_1[:, half:], b_0[:, :half], b_1[:, :half]], 1
            )
        )
        share_out.append(side(b_0[:, half:], b_1[:, half:]))
        up = jnp.concatenate(tiles_of(swapped[1][l]), 1)
        share_up.append(up_from_parts(up, fsdp, rows, parts))
        share_down.append(jnp.concatenate(tiles_of(swapped[2][l]), 0))
    group = (
        jnp.stack(share_in),
        jnp.stack(share_out),
        jnp.stack(share_up),
        jnp.stack(share_down),
        share_small[:V],
        share_small[V:].reshape(-1, 2, rows),
    )
    grad_norm = jnp.sqrt(square_total) / count
    factor = CLIP / jnp.maximum(grad_norm, CLIP)
    masters = (inward, outward, expand, shrink, codon_table, norm_params)
    firsts = (inward_first, outward_first, expand_first, shrink_first, table_first, norm_first)
    seconds = (
        inward_second,
        outward_second,
        expand_second,
        shrink_second,
        table_second,
        norm_second,
    )
    result = [loss_sum, count, grad_norm]
    for index in range(6):
        rate = RATE_VECTOR if index == 5 else RATE_MATRIX
        decay = 0.0 if index == 5 else DECAY
        clipped = group[index] / count * factor
        result.extend(
            adam_step(masters[index], clipped, firsts[index], seconds[index], rate, decay)
        )
    return tuple(result)


def solution(mesh):
    in_specs = (
        P(("fsdp", "dp")),
        P(("fsdp", "dp")),
        P(("fsdp", "dp")),
        P(None, "fsdp", None),
        P(None, "fsdp", None),
        P(None, "fsdp", None),
        P(None, "fsdp", None),
        P(None, "fsdp"),
        P(None, None, "fsdp"),
        P(None, "fsdp", None),
        P(None, "fsdp", None),
        P(None, "fsdp", None),
        P(None, "fsdp", None),
        P(None, "fsdp", None),
        P(None, "fsdp", None),
        P(None, "fsdp", None),
        P(None, "fsdp", None),
        P(None, "fsdp"),
        P(None, "fsdp"),
        P(None, None, "fsdp"),
        P(None, None, "fsdp"),
    )
    out_specs = (
        P(),
        P(),
        P(),
        P(None, "fsdp", None),
        P(None, "fsdp", None),
        P(None, "fsdp", None),
        P(None, "fsdp", None),
        P(None, "fsdp", None),
        P(None, "fsdp", None),
        P(None, "fsdp", None),
        P(None, "fsdp", None),
        P(None, "fsdp", None),
        P(None, "fsdp", None),
        P(None, "fsdp", None),
        P(None, "fsdp", None),
        P(None, "fsdp"),
        P(None, "fsdp"),
        P(None, "fsdp"),
        P(None, None, "fsdp"),
        P(None, None, "fsdp"),
        P(None, None, "fsdp"),
    )
    step = functools.partial(body, mesh.shape["fsdp"])
    return jax.shard_map(step, mesh=mesh, in_specs=in_specs, out_specs=out_specs, check_vma=False)
```

```python
import functools

import jax
import jax.numpy as jnp
from jax import lax
from jax.experimental import pallas as pl
from jax.experimental.pallas import tpu as pltpu
from jax.sharding import PartitionSpec as P

HD = 64
V = 70
STEP = 10


NORM_EPS = 1e-05
BETA_ONE = 0.9
BETA_TWO = 0.95
ADAM_EPS = 1e-08
DECAY = 0.1
RATE_MATRIX = 0.05
RATE_VECTOR = 0.3
CLIP = 0.05


def rotary_tables(length):
    freq = 10000.0 ** (-jnp.arange(HD // 2, dtype=jnp.float32) * 2.0 / HD)
    angle = jnp.arange(length, dtype=jnp.float32)[:, None] * freq[None, :]
    cosine, sine = jnp.cos(angle), jnp.sin(angle)
    return (
        jnp.concatenate([cosine] * 4, 1),
        jnp.concatenate([-sine, sine] * 2, 1),
    )


def normalize(resid, gain, bias):
    mean = jnp.mean(resid, -1, keepdims=True)
    centred = resid - mean
    inverse = lax.rsqrt(jnp.mean(centred * centred, -1, keepdims=True) + NORM_EPS)
    unit = centred * inverse
    return (unit * gain + bias, unit, inverse)


def normalize_back(grad, unit, inverse, gain):
    scaled = grad * gain
    across = (
        scaled
        - jnp.mean(scaled, -1, keepdims=True)
        - unit * jnp.mean(scaled * unit, -1, keepdims=True)
    )
    return (across * inverse, jnp.sum(grad * unit, 0, keepdims=True), jnp.sum(grad, 0, keepdims=True))


def dot(left, right):
    return jnp.dot(left, right, preferred_element_type=jnp.float32)


def dot_nt(left, right):
    return lax.dot_general(
        left, right, (((1,), (1,)), ((), ())), preferred_element_type=jnp.float32
    )


def cross(left, right):
    return lax.dot_general(
        left, right, (((0,), (0,)), ((), ())), preferred_element_type=jnp.float32
    )


VMEM_LIMIT = 56 * 1024 * 1024
LOW, FULL = jnp.bfloat16, jnp.float32


def call(kernel, scalars, out_shapes, ins, anys, scratch, flops, outs_any=0):
    whole = pl.BlockSpec(memory_space=pltpu.VMEM)
    left = pl.BlockSpec(memory_space=pl.ANY)
    n = len(out_shapes)
    return pl.pallas_call(
        kernel,
        out_shape=[jax.ShapeDtypeStruct(s, t) for s, t in out_shapes],
        in_specs=[pl.BlockSpec(memory_space=pltpu.SMEM)]
        + [whole] * len(ins)
        + [left] * len(anys),
        out_specs=[whole] * (n - outs_any) + [left] * outs_any,
        scratch_shapes=scratch,
        compiler_params=pltpu.CompilerParams(vmem_limit_bytes=VMEM_LIMIT),
        cost_estimate=pl.CostEstimate(
            flops=flops,
            bytes_accessed=sum(x.size * x.dtype.itemsize for x in ins + anys),
            transcendentals=0,
        ),
    )(scalars, *ins, *anys)


def fetch(sources, targets, sems):
    copies = [
        pltpu.make_async_copy(s, t, sems.at[i]) for i, (s, t) in enumerate(zip(sources, targets))
    ]
    for c in copies:
        c.start()
    return copies


def tile_of(ref, t, width):
    return ref.at[t] if len(ref.shape) == 3 else ref.at[:, t * width : (t + 1) * width]


def swap_halves(value):
    lane = lax.broadcasted_iota(jnp.int32, value.shape, 1)
    return jnp.where(
        lax.rem(lane, HD) < HD // 2,
        pltpu.roll(value, 128 - HD // 2, 1),
        pltpu.roll(value, HD // 2, 1),
    )


def ordered(first, own, other):
    return jnp.concatenate([jnp.where(first, own, other), jnp.where(first, other, own)], 1)


def head_mask(shape, head):
    lane = lax.broadcasted_iota(jnp.int32, shape, 1)
    return (lane < HD) if head == 0 else (lane >= HD)


def attention_forward_kernel(
    place_of, resid, seg_col, seg_row, cosine, sine, gains, own, other,
    middle, query, keys, values, lse, pack,
    w_a, w_b, mixed, same, sems,
):
    width = resid.shape[1]
    half = width // 2
    copies = fetch(
        [tile_of(r, t, width) for t in range(2) for r in (own, other)],
        [w.at[place] for w in (w_a, w_b) for place in range(2)],
        sems,
    )
    first = place_of[0] == 0
    normed, _, _ = normalize(resid[...], gains[0:1], gains[1:2])
    normed_low, attended = pack.at[0], pack.at[1]
    normed_low[...] = normed.astype(LOW)
    same[...] = jnp.where(seg_col[...] == seg_row[...], 0.0, 1.0)
    for place in range(2):
        copies[place].wait()
        mixed[...] = dot(normed_low[...], w_a[place])
        for p in range(half // 128):
            for part, target in ((0, query), (1, keys)):
                x = mixed[:, part * half + p * 128 : part * half + (p + 1) * 128]
                x = x * cosine[...] + swap_halves(x) * sine[...]
                target[:, place * half + p * 128 : place * half + (p + 1) * 128] = x.astype(LOW)
    for place in range(2):
        copies[2 + place].wait()
        values[:, place * half : (place + 1) * half] = dot(
            normed_low[...], w_b[place, :, :half]
        ).astype(LOW)

    lse[...] = jnp.zeros_like(lse)

    def pair(p, _):
        columns = pl.ds(pl.multiple_of(p * 128, 128), 128)
        q, k, v = query[:, columns], keys[:, columns], values[:, columns]
        out = []
        for head in range(2):
            masked_q = jnp.where(head_mask(q.shape, head), q, jnp.zeros_like(q))
            scores = dot_nt(masked_q, k) * HD ** (-0.5)
            scores = jnp.where(same[...] > 0.5, -1000000000.0, scores)
            top = jnp.max(scores, -1, keepdims=True)
            expo = jnp.exp(scores - top)
            total = jnp.sum(expo, -1, keepdims=True)
            probs = (expo / total).astype(LOW)
            out.append(dot(probs, v))
            lane = lax.broadcasted_iota(jnp.int32, lse.shape, 1)
            lse[...] = jnp.where(lane == 2 * p + head, top + jnp.log(total), lse[...])
        attended[:, columns] = jnp.where(head_mask(out[0].shape, 0), out[0], out[1]).astype(LOW)
        return 0

    lax.fori_loop(0, width // 128, pair, 0)
    attended[...] = ordered(first, attended[:, :half], attended[:, half:])
    out = ordered(
        first, dot(attended[...], w_b[0, :, half:]), dot(attended[...], w_b[1, :, half:])
    )
    middle[...] = resid[...] + out


def attention_forward(place, resid, mixer, gains, cosine, sine, segments):
    length, width = resid.shape
    one = (length, width)
    outs = [(one, FULL)] + [(one, LOW)] * 3 + [((length, 128), FULL), ((2,) + one, LOW)]
    return call(
        attention_forward_kernel,
        place,
        outs,
        [resid, segments[:, None], segments[None, :], cosine, sine, gains],
        list(mixer),
        [
            pltpu.VMEM((2, width, width), LOW),
            pltpu.VMEM((2, width, width), LOW),
            pltpu.VMEM(one, FULL),
            pltpu.VMEM((length, length), FULL),
            pltpu.SemaphoreType.DMA((4,)),
        ],
        8 * length * width * width + 4 * length * length * width,
    )


GELU_SCALE = 0.7978845608028654
GELU_CUBE = 0.044715


def hidden_tiles(own, other, width):
    ups = [tile_of(r, t, width) for r in (own, other) for t in (0, 1)]
    downs = [tile_of(r, t, width) for r in (own, other) for t in (2, 3)]
    return ups, downs


def hidden_forward_kernel(
    place_of, middle, gains, own, other,
    output, active, pack, hidden, ups, downs, hidden_here, sems, out_sems,
):
    u, d = hidden_tiles(own, other, middle.shape[1])
    ins = fetch(
        [r for t in range(4) for r in (u[t], d[t])],
        [w.at[t] for t in range(4) for w in (ups, downs)],
        sems,
    )
    normed, _, _ = normalize(middle[...], gains[0:1], gains[1:2])
    pack[0] = normed.astype(LOW)
    outs = []
    for t in range(4):
        ins[2 * t].wait()
        x = dot(pack[0], ups[t])
        hidden_here[t] = x
        out = pltpu.make_async_copy(hidden_here.at[t], hidden.at[t], out_sems.at[t])
        out.start()
        outs.append(out)
        inner = jnp.tanh(GELU_SCALE * (x + GELU_CUBE * (x * x * x)))
        target = active.at[t] if t < 2 else pack.at[t - 1]
        target[...] = (x * (0.5 * (1.0 + inner))).astype(LOW)
        ins[2 * t + 1].wait()
        product = dot(target[...], downs[t])
        output[...] = (middle[...] if t == 0 else output[...]) + product
    for out in outs:
        out.wait()


def hidden_forward(place, middle, pair, gains):
    length, width = middle.shape
    one = (length, width)
    outs = [(one, FULL), ((2,) + one, LOW), ((3,) + one, LOW), ((4,) + one, FULL)]
    return call(
        hidden_forward_kernel,
        place,
        outs,
        [middle, gains],
        list(pair),
        [
            pltpu.VMEM((4, width, width), LOW),
            pltpu.VMEM((4, width, width), LOW),
            pltpu.VMEM((4,) + one, FULL),
            pltpu.SemaphoreType.DMA((8,)),
            pltpu.SemaphoreType.DMA((4,)),
        ],
        16 * length * width * width,
        outs_any=1,
    )


def hidden_back_kernel(
    place_of, grad, branch, middle, gains, hidden, own, other,
    grad_middle, grad_gains, grad_own, grad_other, ups, downs, hidden_here, total, sems,
):
    u, d = hidden_tiles(own, other, middle.shape[1])
    ins = fetch(
        [r for t in range(4) for r in (d[t], hidden.at[t], u[t])],
        [w.at[t] for t in range(4) for w in (downs, hidden_here, ups)],
        sems,
    )
    for t in range(4):
        ins[3 * t].wait()
        grad_active = dot_nt(branch[...], downs[t])
        ins[3 * t + 1].wait()
        x = hidden_here[t]
        inner = jnp.tanh(GELU_SCALE * (x + GELU_CUBE * (x * x * x)))
        slope = 0.5 * (1.0 + inner) + (0.5 * GELU_SCALE) * x * (1.0 - inner * inner) * (
            1.0 + (3.0 * GELU_CUBE) * (x * x)
        )
        target = grad_own.at[t] if t < 2 else grad_other.at[t - 2]
        target[...] = (grad_active * slope).astype(LOW)
        ins[3 * t + 2].wait()
        product = dot_nt(target[...], ups[t])
        total[...] = product if t == 0 else total[...] + product
    _, unit, inverse = normalize(middle[...], gains[0:1], gains[1:2])
    back, gain, bias = normalize_back(total[...], unit, inverse, gains[0:1])
    grad_middle[...] = grad[...] + back
    grad_gains[0:1] = gain
    grad_gains[1:2] = bias


def hidden_back(place, grad, branch, middle, hidden, pair, gains):
    length, width = middle.shape
    one = (length, width)
    outs = [(one, FULL), ((2, width), FULL), ((2,) + one, LOW), ((2,) + one, LOW)]
    return call(
        hidden_back_kernel,
        place,
        outs,
        [grad, branch, middle, gains],
        [hidden] + list(pair),
        [
            pltpu.VMEM((4, width, width), LOW),
            pltpu.VMEM((4, width, width), LOW),
            pltpu.VMEM((4,) + one, FULL),
            pltpu.VMEM(one, FULL),
            pltpu.SemaphoreType.DMA((12,)),
        ],
        16 * length * width * width,
    )


def attention_back_kernel(
    place_of, grad_middle, resid, seg_col, seg_row, cosine, sine, gains, query, keys, values, lse,
    own, other,
    grad, branch, grad_gains, grad_own, grad_other,
    w_a, w_b, same, ga, gq, gk, gv, sems,
):
    width = resid.shape[1]
    half = width // 2
    copies = fetch(
        [tile_of(r, t, width) for t in (1, 0) for r in (own, other)],
        [w.at[place] for w in (w_b, w_a) for place in range(2)],
        sems,
    )
    first = place_of[0] == 0
    scale = HD ** (-0.5)
    grads = (grad_own, grad_other)
    same[...] = jnp.where(seg_col[...] == seg_row[...], 0.0, 1.0)
    attn_grad = grad_middle[...].astype(LOW)
    left, right = attn_grad[:, :half], attn_grad[:, half:]
    grad_own[1, :, half:] = jnp.where(first, left, right)
    grad_other[1, :, half:] = jnp.where(first, right, left)
    copies[0].wait()
    copies[1].wait()
    natural = dot_nt(grad_own[1, :, half:], w_b[0, :, half:]) + dot_nt(
        grad_other[1, :, half:], w_b[1, :, half:]
    )
    natural = natural.astype(LOW)
    ga[:, :half] = jnp.where(first, natural[:, :half], natural[:, half:])
    ga[:, half:] = jnp.where(first, natural[:, half:], natural[:, :half])

    def pair(p, _):
        columns = pl.ds(pl.multiple_of(p * 128, 128), 128)
        q, k, v, g = query[:, columns], keys[:, columns], values[:, columns], ga[:, columns]
        out_q, out_k, out_v = [], [], []
        for head in range(2):
            mask = head_mask(q.shape, head)
            zero = jnp.zeros_like(q)
            scores = dot_nt(k, jnp.where(mask, q, zero)) * scale
            scores = jnp.where(same[...] > 0.5, -1000000000.0, scores)
            probs = jnp.exp(scores - lse[pl.ds(2 * p + head, 1), :])
            grad_probs = dot_nt(v, jnp.where(mask, g, zero))
            across = jnp.sum(probs * grad_probs, 0, keepdims=True)
            grad_scores = (probs * (grad_probs - across)).astype(LOW)
            out_k.append(dot(grad_scores, q))
            out_q.append(cross(grad_scores, k))
            out_v.append(dot(probs.astype(LOW), g))
        for out, target in ((out_q, gq), (out_k, gk)):
            x = jnp.where(head_mask(out[0].shape, 0), out[0], out[1]) * scale
            x = x * cosine[...] - swap_halves(x) * sine[...]
            target[:, columns] = x.astype(LOW)
        gv[:, columns] = jnp.where(head_mask(out_v[0].shape, 0), out_v[0], out_v[1]).astype(LOW)
        return 0

    lax.fori_loop(0, width // 128, pair, 0)
    for place in range(2):
        columns = slice(place * half, (place + 1) * half)
        grads[place][0, :, :half] = gq[:, columns]
        grads[place][0, :, half:] = gk[:, columns]
        grads[place][1, :, :half] = gv[:, columns]
    copies[2].wait()
    copies[3].wait()
    total = dot_nt(grad_own[0], w_a[0]) + dot_nt(grad_other[0], w_a[1])
    total = total + dot_nt(grad_own[1, :, :half], w_b[0, :, :half])
    total = total + dot_nt(grad_other[1, :, :half], w_b[1, :, :half])
    _, unit, inverse = normalize(resid[...], gains[0:1], gains[1:2])
    back, gain, bias = normalize_back(total, unit, inverse, gains[0:1])
    back = grad_middle[...] + back
    grad[...] = back
    branch[...] = back.astype(LOW)
    grad_gains[0:1] = gain
    grad_gains[1:2] = bias


def attention_back(place, grad_middle, resid, mixer, gains, cosine, sine, segments, query, keys, values, lse):
    length, width = resid.shape
    one = (length, width)
    outs = [(one, FULL), (one, LOW), ((2, width), FULL)] + [((2,) + one, LOW)] * 2
    ins = [grad_middle, resid, segments[:, None], segments[None, :], cosine, sine, gains]
    ins += [query, keys, values, lse.T[: width // HD]]
    return call(
        attention_back_kernel,
        place,
        outs,
        ins,
        list(mixer),
        [
            pltpu.VMEM((2, width, width), LOW),
            pltpu.VMEM((2, width, width), LOW),
            pltpu.VMEM((length, length), FULL),
        ]
        + [pltpu.VMEM(one, LOW)] * 4
        + [pltpu.SemaphoreType.DMA((4,))],
        8 * length * width * width + 10 * length * length * width,
    )


def adam_step(master, grad, first, second, rate, decay):
    first = BETA_ONE * first + (1.0 - BETA_ONE) * grad
    second = BETA_TWO * second + (1.0 - BETA_TWO) * grad * grad
    fix_one = 1.0 - BETA_ONE**STEP
    fix_two = 1.0 - BETA_TWO**STEP
    update = first / fix_one / (jnp.sqrt(second / fix_two) + ADAM_EPS) + decay * master
    return (master - rate * update, first, second)


def swap_cores(value):
    return lax.ppermute(value, "dp", [(0, 1), (1, 0)])


def across(value, mask, size):
    return lax.ppermute(value, "fsdp", [(i, i ^ mask) for i in range(size)])


def tie(*values):
    return lax.optimization_barrier(values)


def total_of(value, size):
    value = value + swap_cores(value)
    for bit in range(size.bit_length() - 1):
        value = value + across(value, 1 << bit, size)
    return value


X, Y = 1, 2
Z = (4, 8, 12)


def place_kernel(parts, place_of, quarter, from_x, from_y, far_a, far_b, mixer, hidden, small, sems):
    x, y, z = place_of[1], place_of[2], place_of[3]
    rows = (parts[0] - parts[2]) // 3
    for xor_z in range(4):
        for xor_y in range(2):
            for xor_x in range(2):
                index = (z ^ xor_z) * 4 + (y ^ xor_y) * 2 + (x ^ xor_x)
                for h in range(2):
                    at = xor_z * parts[h]
                    if xor_x and xor_y:
                        source = (far_a, far_b)[h]
                    else:
                        source = from_x if xor_x else from_y if xor_y else quarter
                        at += h * 4 * parts[0]
                    for j in range(3):
                        target = mixer.at[h] if j == 0 else hidden.at[2 * (j - 1) + h]
                        pltpu.make_async_copy(
                            source.at[pl.ds(at + j * rows, rows)],
                            target.at[pl.ds(pl.multiple_of(index * rows, 16), rows)],
                            sems.at[h * 3 + j],
                        ).start()
                    if h == 0:
                        pltpu.make_async_copy(
                            source.at[pl.ds(at + 3 * rows, parts[2])],
                            small.at[pl.ds(pl.multiple_of(index * parts[2], 16), parts[2])],
                            sems.at[6],
                        ).start()
    for h in range(2):
        for j in range(3):
            target = mixer.at[h] if j == 0 else hidden.at[2 * (j - 1) + h]
            pltpu.make_async_copy(target, target, sems.at[h * 3 + j]).wait()
    pltpu.make_async_copy(small, small, sems.at[6]).wait()


def gather_blocks(place, shard_a, shard_b, small, size):
    rows, width = shard_a.shape[0] // 3, shard_a.shape[1]
    shard_a = jnp.concatenate([shard_a, small], 0)
    parts = (shard_a.shape[0], shard_b.shape[0], small.shape[0])
    shard = jnp.concatenate([shard_a, shard_b], 0)
    got = [across(shard, mask, size) for mask in Z]
    (got,) = tie(got)
    got = [shard] + got
    quarter = jnp.concatenate([g[: parts[0]] for g in got] + [g[parts[0] :] for g in got], 0)
    from_x, from_y = tie(across(quarter, X, size), across(quarter, Y, size))
    cut = 4 * parts[0]
    far_a, far_b = tie(across(from_y[:cut], X, size), across(from_x[cut:], Y, size))
    return call(
        functools.partial(place_kernel, parts),
        place,
        [
            ((2, width, width), LOW),
            ((4, width, width), LOW),
            ((size * parts[2], width), LOW),
        ],
        [],
        [quarter, from_x, from_y, far_a, far_b],
        [pltpu.SemaphoreType.DMA((7,))],
        0,
        outs_any=3,
    )


def round_kernel(jobs, n_ins, counts, *refs):
    new, once, twice, done = counts
    place_of, ins = refs[0], refs[1 : 1 + n_ins]
    rest = list(refs[1 + n_ins :])
    pop = lambda present, n=1: [rest.pop(0) for _ in range(n)] if present else [None] * n
    (keep_once,), (keep_twice,) = pop(once), pop(twice)
    from_x, from_y = pop(once or twice, 2)
    keep_done, *from_z = pop(done, 4)
    to_x, to_y = pop(new or once, 2)
    (out_once,), (out_twice,) = pop(new), pop(once)
    out_done, *to_z = pop(twice, 4)
    share, squares = pop(done, 2)
    (tile,) = pop(new)
    rows = (out_once if new else out_twice if once else out_done if twice else share).shape[-2]
    rows = rows // (8 if new else 4 if once else 1)
    bits, z = (place_of[1], place_of[2]), place_of[3]
    to, came = (to_x, to_y), (from_x, from_y)

    def block(index):
        if isinstance(index, int):
            return pl.ds(index * rows, rows)
        return pl.ds(pl.multiple_of(index * rows, 16), rows)

    def factor(spec):
        which, index, low, high = spec
        ref = ins[which] if index is None else ins[which].at[index]
        return ref[...] if low is None else ref[:, low:high]

    for p in range(new):
        for s in range(2):
            for low, high, products in jobs[2 * p + s]:
                total = None
                for left, right in products:
                    product = cross(factor(left), factor(right))
                    total = product if total is None else total + product
                tile[:, low:high] = total
            for zz in range(4):
                for other in range(2):
                    at = zz * 2 + other
                    index = lambda bit: zz * 4 + (other * 2 + bit if s == 0 else bit * 2 + other)
                    to[s][block(p * 8 + at), :] = tile[block(index(1 - bits[s])), :].astype(LOW)
                    out_once[p, s, block(at), :] = tile[block(index(bits[s])), :]
    for p in range(once):
        for s in range(2):
            for zz in range(4):
                for bit in range(2):
                    at = zz * 2 + (bits[1 - s] if bit else 1 - bits[1 - s])
                    value = keep_once[p, s, block(at), :] + came[s][block(p * 8 + at), :].astype(FULL)
                    if bit:
                        out_twice[p, s, block(zz), :] = value
                    else:
                        to[1 - s][block(new * 8 + p * 4 + zz), :] = value.astype(LOW)
    for p in range(twice):
        for s in range(2):
            for xor in range(4):
                at = jnp.bitwise_xor(z, xor)
                value = keep_twice[p, s, block(at), :] + came[1 - s][
                    block(once * 8 + p * 4 + at), :
                ].astype(FULL)
                if xor == 0:
                    out_done[p, s] = value
                else:
                    to_z[xor - 1][block(2 * p + s), :] = value.astype(LOW)
    if done:
        squares[...] = jnp.zeros_like(squares)
    for p in range(done):
        for s in range(2):
            value = keep_done[p, s]
            for f in from_z:
                value = value + f[block(2 * p + s), :].astype(FULL)
            share[p, s] = value
            squares[...] += jnp.sum(value * value, 0, keepdims=True)


class Rounds:
    def __init__(self, place, rows, width):
        self.place, self.rows, self.width = place, rows, width
        self.counts = (0, 0, 0, 0)
        self.kept = [None] * 3
        self.came = None
        self.came_z = None
        self.shares, self.squares = [], []
        self.flying = []

    def step(self, chunk):
        rows, width = self.rows, self.width
        new, once, twice, done = counts = (len(chunk),) + self.counts[:3]
        arrays, jobs = [], []

        def number(spec):
            array, *place = spec
            for i, known in enumerate(arrays):
                if known is array:
                    return (i, *place)
            arrays.append(array)
            return (len(arrays) - 1, *place)

        for pair in chunk:
            for tile in pair:
                jobs.append(
                    [(a, b, [(number(l), number(r)) for l, r in ps]) for a, b, ps in tile]
                )
        ins = list(arrays)
        if once:
            ins.append(self.kept[0])
        if twice:
            ins.append(self.kept[1])
        if once or twice:
            ins += self.came
        if done:
            ins += [self.kept[2]] + self.came_z
        outs = []
        if new or once:
            outs += [(((new * 8 + once * 4) * rows, width), LOW)] * 2
        if new:
            outs.append(((new, 2, 8 * rows, width), FULL))
        if once:
            outs.append(((once, 2, 4 * rows, width), FULL))
        if twice:
            outs.append(((twice, 2, rows, width), FULL))
            outs += [((twice * 2 * rows, width), LOW)] * 3
        if done:
            outs += [((done, 2, rows, width), FULL), ((1, width), FULL)]
        length = 2 * arrays[0].shape[-2] if new else 0
        got = call(
            functools.partial(round_kernel, jobs, len(arrays), counts),
            self.place,
            outs,
            ins,
            [],
            [pltpu.VMEM((16 * rows, width), FULL)] if new else [],
            4 * new * length * width * width,
        )
        got = list(got)
        self.flying, self.kept, self.counts = [], [None] * 3, counts
        if new or once:
            self.flying += [across(got.pop(0), X, 16), across(got.pop(0), Y, 16)]
        if new:
            self.kept[0] = got.pop(0)
        if once:
            self.kept[1] = got.pop(0)
        if twice:
            self.kept[2] = got.pop(0)
            self.flying += [across(got.pop(0), mask, 16) for mask in Z]
        if done:
            self.shares.append(got[0])
            self.squares.append(got[1])

    def finish(self, *ties):
        flying, ties = tie(self.flying, ties)
        self.came = self.came_z = None
        if self.counts[0] or self.counts[1]:
            self.came, flying = flying[:2], flying[2:]
        if self.counts[2]:
            self.came_z = flying
        return ties

    def left(self):
        return any(self.counts[:3])


class PlainRounds:
    def __init__(self):
        self.shares, self.squares = [], []

    def step(self, chunk):
        def factor(spec):
            array, index, low, high = spec
            array = array if index is None else array[index]
            return array if low is None else array[:, low:high]

        def summed(tile):
            parts = [sum(cross(factor(l), factor(r)) for l, r in ps) for _, _, ps in tile]
            return lax.psum_scatter(
                jnp.concatenate(parts, 1), "fsdp", scatter_dimension=0, tiled=True
            )

        share = jnp.stack([jnp.stack([summed(tile) for tile in pair]) for pair in chunk])
        self.shares.append(share)
        self.squares.append(jnp.sum(share * share, (0, 1, 2))[None])

    def finish(self, *ties):
        return ties

    def left(self):
        return False


def small_steps(value, place, size, rows):
    (got,) = yield [swap_cores(value)]
    value = (value + got).reshape(-1, 4, 2, 2, rows).transpose(1, 2, 3, 0, 4)
    for bit in range(2):
        axis = 2 - bit
        send = lax.dynamic_index_in_dim(value, 1 - place[1 + bit], axis, keepdims=False)
        keep = lax.dynamic_index_in_dim(value, place[1 + bit], axis, keepdims=False)
        (got,) = yield [across(send, 1 << bit, size)]
        value = keep + got
    take = lambda xor: lax.dynamic_index_in_dim(value, place[3] ^ xor, 0, keepdims=False)
    got = yield [across(take(mask // 4), mask, size) for mask in Z]
    return take(0) + (got[0] + (got[1] + got[2]))


def up_to_parts(expand_shard, size, rows, parts):
    r = expand_shard.shape[0]
    return expand_shard.reshape(r, size, parts, rows).transpose(0, 2, 1, 3).reshape(r, -1)


def up_from_parts(expand_shard, size, rows, parts):
    r = expand_shard.shape[0]
    return expand_shard.reshape(r, parts, size, rows).transpose(0, 2, 1, 3).reshape(r, -1)


def half_of(value, core):
    half = value.shape[1] // 2
    return lax.dynamic_slice_in_dim(value, core * half, half, 1)


def body(
    fsdp,
    codons,
    masked,
    segments,
    inward,
    outward,
    expand,
    shrink,
    codon_table,
    norm_params,
    inward_first,
    inward_second,
    outward_first,
    outward_second,
    expand_first,
    expand_second,
    shrink_first,
    shrink_second,
    table_first,
    table_second,
    norm_first,
    norm_second,
):
    layers = inward.shape[0]
    length = codons.shape[0]
    rows = inward.shape[1]
    width = rows * fsdp
    half = width // 2
    parts = shrink.shape[1] // rows
    fast = fsdp == 16 and rows % 16 == 0
    core, index = lax.axis_index("dp"), lax.axis_index("fsdp")
    bit = lambda b: lax.rem(lax.div(index, b), 2)
    place = jnp.stack([core, bit(1), bit(2), lax.div(index, 4)]).astype(jnp.int32)
    weight = masked.astype(FULL)
    inputs = jnp.where(masked == 1, V - 1, codons)

    def tiles_of(l):
        w_in, w_out = inward[l].astype(LOW), outward[l].astype(LOW)
        pieces = [half_of(w_in[:, p * width : (p + 1) * width], core) for p in range(3)]
        pieces.append(half_of(w_out, core))
        mixer = [jnp.concatenate(pieces[:2], 1), jnp.concatenate(pieces[2:], 1)]
        up = half_of(up_to_parts(expand[l].astype(LOW), fsdp, rows, parts), core)
        down = lax.dynamic_slice_in_dim(shrink[l].astype(LOW), core * 2 * rows, 2 * rows, 0)
        return mixer + [up[:, :width], up[:, width:], down[:rows], down[rows:]]

    norms = norm_params.shape[0] * 2
    small = jnp.concatenate(
        [codon_table.astype(LOW), norm_params.astype(LOW).reshape(norms, rows)], 0
    )
    mixers, hiddens = [None] * layers, [None] * layers
    plain = list(range(1, layers)) if fast else list(range(layers))
    sides = [jnp.concatenate(tiles_of(l), 1) for l in plain]
    if fast:
        tiles = tiles_of(0)
        flat = small.reshape(-1)
        flat = jnp.pad(flat, (0, -flat.shape[0] % (16 * width))).reshape(-1, width)
        shard_a = jnp.concatenate(tiles[0::2], 0)
        shard_b = jnp.concatenate(tiles[1::2], 0)
        sides, shard_a = tie(sides, shard_a)
    for l, side in zip(plain, sides):
        own = lax.all_gather(side, "fsdp", axis=0, tiled=True)
        mixers[l], hiddens[l] = own[:, : 2 * width], own[:, 2 * width :]
    if fast:
        mixers[0], hiddens[0], blocks = gather_blocks(place, shard_a, shard_b, flat, fsdp)
        blocks = blocks.reshape(fsdp, -1)[:, : small.size].reshape(fsdp, V + norms, rows)
        small = blocks.transpose(1, 0, 2).reshape(V + norms, width)
    else:
        small = lax.all_gather(small, "fsdp", axis=1, tiled=True)
    mixers = [(own, swap_cores(own)) for own in mixers]
    hiddens = [(own, swap_cores(own)) for own in hiddens]
    table_low = small[:V]
    gains = small[V:].astype(FULL).reshape(-1, 2, width)

    cosine, sine = rotary_tables(length)
    vocab_ids = jnp.arange(V, dtype=jnp.int32)
    chosen = (inputs[:, None] == vocab_ids[None, :]).astype(LOW)
    resid = dot(chosen, table_low)
    kept = []
    for l in range(layers):
        gain = gains[2 * l : 2 * l + 2]
        middle, query, keys, values, lse, pack = attention_forward(
            place, resid, mixers[l], gain[0], cosine, sine, segments
        )
        if l > 0:
            middle, came = tie(middle, kept[-1][-1])
            kept[-1] = kept[-1][:-1] + (came,)
        pack_came = swap_cores(pack)
        output, active, pack_mid, hidden = hidden_forward(place, middle, hiddens[l], gain[1])
        output, pack_came = tie(output, pack_came)
        kept.append(
            (resid, query, keys, values, lse, pack, pack_came, middle, hidden, active, pack_mid)
            + (swap_cores(pack_mid),)
        )
        resid = output
    final_gain = gains[2 * layers]
    normed_out, unit_out, inverse_out = normalize(resid, final_gain[0], final_gain[1])
    head_in = normed_out.astype(LOW)
    logits = jnp.einsum("sd,vd->sv", head_in, table_low, preferred_element_type=FULL)
    top = jnp.max(logits, -1, keepdims=True)
    lse_head = top + jnp.log(jnp.sum(jnp.exp(logits - top), -1, keepdims=True))
    targets = (codons[:, None] == vocab_ids[None, :]).astype(FULL)
    picked = jnp.sum(logits * targets, -1)
    loss_local = jnp.sum((lse_head[:, 0] - picked) * weight)
    grad_logits = ((jnp.exp(logits - lse_head) - targets) * weight[:, None]).astype(LOW)
    grad_table = cross(grad_logits, head_in)
    grad_head = dot(grad_logits, table_low)
    grad, grad_final_gain, grad_final_bias = normalize_back(
        grad_head, unit_out, inverse_out, final_gain[0]
    )
    branch = grad.astype(LOW)
    grad_norms = [grad_final_gain, grad_final_bias]
    grad, branch, came = tie(grad, branch, kept[-1][-1])
    kept[-1] = kept[-1][:-1] + (came,)

    rounds = Rounds(place, rows, width) if fast else PlainRounds()
    whole = lambda array, i=None: (array, i, None, None)
    tile = lambda left, right, other_left, other_right: [
        (0, width, [(left, right), (other_left, other_right)])
    ]
    chunk = []
    for l in reversed(range(layers)):
        (resid, query, keys, values, lse, pack, pack_came, middle, hidden, active, pack_mid, mid_came) = kept[l]
        gain = gains[2 * l : 2 * l + 2]
        branch_came = swap_cores(branch)
        chunk.append(
            [
                tile(
                    whole(active, s), whole(branch), whole(mid_came, 1 + s), whole(branch_came)
                )
                for s in range(2)
            ]
        )
        rounds.step(chunk)
        grad_middle, gains_mid, up_own, up_other = hidden_back(
            place, grad, branch, middle, hidden, hiddens[l], gain[1]
        )
        grad_middle, up_own, up_came = rounds.finish(grad_middle, up_own, swap_cores(up_other))
        rounds.step(
            [
                [
                    tile(
                        whole(pack_mid, 0), whole(up_own, s), whole(mid_came, 0), whole(up_came, s)
                    )
                    for s in range(2)
                ]
            ]
        )
        grad, branch, gains_in, mix_own, mix_other = attention_back(
            place, grad_middle, resid, mixers[l], gain[0], cosine, sine, segments,
            query, keys, values, lse,
        )
        grad_norms = [gains_in, gains_mid] + grad_norms
        grad, branch, mix_own, mix_came = rounds.finish(
            grad, branch, mix_own, swap_cores(mix_other)
        )
        products = lambda i, a, b: [
            ((pack, i, None, None), (mix_own, 1, a, b)),
            ((pack_came, i, None, None), (mix_came, 1, a, b)),
        ]
        chunk = [
            [
                tile(whole(pack, 0), whole(mix_own, 0), whole(pack_came, 0), whole(mix_came, 0)),
                [(0, half, products(0, 0, half)), (half, width, products(1, half, width))],
            ]
        ]
    grad_table = grad_table + cross(chosen, branch)
    grad_small = jnp.concatenate([grad_table] + grad_norms, 0)
    if fast:
        steps = small_steps(grad_small, place, fsdp, rows)
        messages = steps.send(next(steps))
        rounds.step(chunk)
        share_small = None
        while rounds.left() or share_small is None:
            ((messages,),) = (rounds.finish(messages),)
            try:
                messages = steps.send(messages) if share_small is None else []
            except StopIteration as end:
                share_small, messages = end.value, []
            if rounds.left():
                rounds.step([])
    else:
        rounds.step(chunk)
        share_small = lax.psum_scatter(
            grad_small + swap_cores(grad_small), "fsdp", scatter_dimension=1, tiled=True
        )

    squares = 0.5 * jnp.sum(share_small * share_small)
    for value in rounds.squares:
        squares = squares + jnp.sum(value)
    totals = jnp.stack([loss_local, jnp.sum(weight), squares])
    totals = total_of(jnp.pad(totals, (0, 125))[None], fsdp)
    loss_sum, count, square_total = totals[0, 0], totals[0, 1], totals[0, 2]

    both = []
    for share in rounds.shares:
        other = swap_cores(share)
        first = core == 0
        both.append((jnp.where(first, share, other), jnp.where(first, other, share)))
    share_in, share_out, share_up, share_down = ([None] * layers for _ in range(4))
    side = lambda *values: jnp.concatenate(values, 1)
    for l in range(layers):
        at = 2 * (layers - 1 - l)
        down, up, mix = (at, at and 1), (at + 1, 0), (at + 2, 0)
        tiles = lambda where: [both[where[0]][c][where[1], s] for c in range(2) for s in range(2)]
        a_0, b_0, a_1, b_1 = tiles(mix)
        share_in[l] = side(
            a_0[:, :half], a_1[:, :half], a_0[:, half:], a_1[:, half:], b_0[:, :half], b_1[:, :half]
        )
        share_out[l] = side(b_0[:, half:], b_1[:, half:])
        share_up[l] = up_from_parts(side(*tiles(up)), fsdp, rows, parts)
        share_down[l] = jnp.concatenate(tiles(down), 0)
    group = (
        jnp.stack(share_in),
        jnp.stack(share_out),
        jnp.stack(share_up),
        jnp.stack(share_down),
        share_small[:V],
        share_small[V:].reshape(-1, 2, rows),
    )
    grad_norm = jnp.sqrt(square_total) / count
    factor = CLIP / jnp.maximum(grad_norm, CLIP)
    masters = (inward, outward, expand, shrink, codon_table, norm_params)
    firsts = (inward_first, outward_first, expand_first, shrink_first, table_first, norm_first)
    seconds = (
        inward_second,
        outward_second,
        expand_second,
        shrink_second,
        table_second,
        norm_second,
    )
    result = [loss_sum, count, grad_norm]
    for index in range(6):
        rate = RATE_VECTOR if index == 5 else RATE_MATRIX
        decay = 0.0 if index == 5 else DECAY
        clipped = group[index] / count * factor
        result.extend(
            adam_step(masters[index], clipped, firsts[index], seconds[index], rate, decay)
        )
    return tuple(result)


def solution(mesh):
    in_specs = (
        P(("fsdp", "dp")),
        P(("fsdp", "dp")),
        P(("fsdp", "dp")),
        P(None, "fsdp", None),
        P(None, "fsdp", None),
        P(None, "fsdp", None),
        P(None, "fsdp", None),
        P(None, "fsdp"),
        P(None, None, "fsdp"),
        P(None, "fsdp", None),
        P(None, "fsdp", None),
        P(None, "fsdp", None),
        P(None, "fsdp", None),
        P(None, "fsdp", None),
        P(None, "fsdp", None),
        P(None, "fsdp", None),
        P(None, "fsdp", None),
        P(None, "fsdp"),
        P(None, "fsdp"),
        P(None, None, "fsdp"),
        P(None, None, "fsdp"),
    )
    out_specs = (
        P(),
        P(),
        P(),
        P(None, "fsdp", None),
        P(None, "fsdp", None),
        P(None, "fsdp", None),
        P(None, "fsdp", None),
        P(None, "fsdp", None),
        P(None, "fsdp", None),
        P(None, "fsdp", None),
        P(None, "fsdp", None),
        P(None, "fsdp", None),
        P(None, "fsdp", None),
        P(None, "fsdp", None),
        P(None, "fsdp", None),
        P(None, "fsdp"),
        P(None, "fsdp"),
        P(None, "fsdp"),
        P(None, None, "fsdp"),
        P(None, None, "fsdp"),
        P(None, None, "fsdp"),
    )
    step = functools.partial(body, mesh.shape["fsdp"])
    return jax.shard_map(step, mesh=mesh, in_specs=in_specs, out_specs=out_specs, check_vma=False)
```

```python
import functools

import jax
import jax.numpy as jnp
from jax import lax
from jax.experimental import pallas as pl
from jax.experimental.pallas import tpu as pltpu
from jax.sharding import PartitionSpec as P

HD = 64
V = 70
STEP = 10


NORM_EPS = 1e-05
BETA_ONE = 0.9
BETA_TWO = 0.95
ADAM_EPS = 1e-08
DECAY = 0.1
RATE_MATRIX = 0.05
RATE_VECTOR = 0.3
CLIP = 0.05


def rotary_tables(length):
    freq = 10000.0 ** (-jnp.arange(HD // 2, dtype=jnp.float32) * 2.0 / HD)
    angle = jnp.arange(length, dtype=jnp.float32)[:, None] * freq[None, :]
    cosine, sine = jnp.cos(angle), jnp.sin(angle)
    return (
        jnp.concatenate([cosine] * 4, 1),
        jnp.concatenate([-sine, sine] * 2, 1),
    )


def normalize(resid, gain, bias):
    mean = jnp.mean(resid, -1, keepdims=True)
    centred = resid - mean
    inverse = lax.rsqrt(jnp.mean(centred * centred, -1, keepdims=True) + NORM_EPS)
    unit = centred * inverse
    return (unit * gain + bias, unit, inverse)


def normalize_back(grad, unit, inverse, gain):
    scaled = grad * gain
    across = (
        scaled
        - jnp.mean(scaled, -1, keepdims=True)
        - unit * jnp.mean(scaled * unit, -1, keepdims=True)
    )
    return (across * inverse, jnp.sum(grad * unit, 0, keepdims=True), jnp.sum(grad, 0, keepdims=True))


def dot(left, right):
    return jnp.dot(left, right, preferred_element_type=jnp.float32)


def dot_nt(left, right):
    return lax.dot_general(
        left, right, (((1,), (1,)), ((), ())), preferred_element_type=jnp.float32
    )


def cross(left, right):
    return lax.dot_general(
        left, right, (((0,), (0,)), ((), ())), preferred_element_type=jnp.float32
    )


VMEM_LIMIT = 56 * 1024 * 1024
LOW, FULL = jnp.bfloat16, jnp.float32


def call(kernel, scalars, out_shapes, ins, anys, scratch, flops, outs_any=0):
    whole = pl.BlockSpec(memory_space=pltpu.VMEM)
    left = pl.BlockSpec(memory_space=pl.ANY)
    n = len(out_shapes)
    return pl.pallas_call(
        kernel,
        out_shape=[jax.ShapeDtypeStruct(s, t) for s, t in out_shapes],
        in_specs=[pl.BlockSpec(memory_space=pltpu.SMEM)]
        + [whole] * len(ins)
        + [left] * len(anys),
        out_specs=[whole] * (n - outs_any) + [left] * outs_any,
        scratch_shapes=scratch,
        compiler_params=pltpu.CompilerParams(vmem_limit_bytes=VMEM_LIMIT),
        cost_estimate=pl.CostEstimate(
            flops=flops,
            bytes_accessed=sum(x.size * x.dtype.itemsize for x in ins + anys),
            transcendentals=0,
        ),
    )(scalars, *ins, *anys)


def fetch(sources, targets, sems):
    copies = [
        pltpu.make_async_copy(s, t, sems.at[i]) for i, (s, t) in enumerate(zip(sources, targets))
    ]
    for c in copies:
        c.start()
    return copies


def tile_of(ref, t, width):
    return ref.at[t] if len(ref.shape) == 3 else ref.at[:, t * width : (t + 1) * width]


def swap_halves(value):
    lane = lax.broadcasted_iota(jnp.int32, value.shape, 1)
    return jnp.where(
        lax.rem(lane, HD) < HD // 2,
        pltpu.roll(value, 128 - HD // 2, 1),
        pltpu.roll(value, HD // 2, 1),
    )


def ordered(first, own, other):
    return jnp.concatenate([jnp.where(first, own, other), jnp.where(first, other, own)], 1)


def head_mask(shape, head):
    lane = lax.broadcasted_iota(jnp.int32, shape, 1)
    return (lane < HD) if head == 0 else (lane >= HD)


def attention_forward_kernel(
    place_of, resid, seg_col, seg_row, cosine, sine, gains, own, other,
    middle, query, keys, values, lse, pack,
    w_a, w_b, mixed, same, sems,
):
    width = resid.shape[1]
    half = width // 2
    copies = fetch(
        [tile_of(r, t, width) for t in range(2) for r in (own, other)],
        [w.at[place] for w in (w_a, w_b) for place in range(2)],
        sems,
    )
    first = place_of[0] == 0
    normed, _, _ = normalize(resid[...], gains[0:1], gains[1:2])
    normed_low, attended = pack.at[0], pack.at[1]
    normed_low[...] = normed.astype(LOW)
    same[...] = jnp.where(seg_col[...] == seg_row[...], 0.0, 1.0)
    for place in range(2):
        copies[place].wait()
        mixed[...] = dot(normed_low[...], w_a[place])
        for p in range(half // 128):
            for part, target in ((0, query), (1, keys)):
                x = mixed[:, part * half + p * 128 : part * half + (p + 1) * 128]
                x = x * cosine[...] + swap_halves(x) * sine[...]
                target[:, place * half + p * 128 : place * half + (p + 1) * 128] = x.astype(LOW)
    for place in range(2):
        copies[2 + place].wait()
        values[:, place * half : (place + 1) * half] = dot(
            normed_low[...], w_b[place, :, :half]
        ).astype(LOW)

    lse[...] = jnp.zeros_like(lse)

    def pair(p, _):
        columns = pl.ds(pl.multiple_of(p * 128, 128), 128)
        q, k, v = query[:, columns], keys[:, columns], values[:, columns]
        out = []
        for head in range(2):
            masked_q = jnp.where(head_mask(q.shape, head), q, jnp.zeros_like(q))
            scores = dot_nt(masked_q, k) * HD ** (-0.5)
            scores = jnp.where(same[...] > 0.5, -1000000000.0, scores)
            top = jnp.max(scores, -1, keepdims=True)
            expo = jnp.exp(scores - top)
            total = jnp.sum(expo, -1, keepdims=True)
            probs = (expo / total).astype(LOW)
            out.append(dot(probs, v))
            lane = lax.broadcasted_iota(jnp.int32, lse.shape, 1)
            lse[...] = jnp.where(lane == 2 * p + head, top + jnp.log(total), lse[...])
        attended[:, columns] = jnp.where(head_mask(out[0].shape, 0), out[0], out[1]).astype(LOW)
        return 0

    lax.fori_loop(0, width // 128, pair, 0)
    attended[...] = ordered(first, attended[:, :half], attended[:, half:])
    out = ordered(
        first, dot(attended[...], w_b[0, :, half:]), dot(attended[...], w_b[1, :, half:])
    )
    middle[...] = resid[...] + out


def attention_forward(place, resid, mixer, gains, cosine, sine, segments):
    length, width = resid.shape
    one = (length, width)
    outs = [(one, FULL)] + [(one, LOW)] * 3 + [((length, 128), FULL), ((2,) + one, LOW)]
    return call(
        attention_forward_kernel,
        place,
        outs,
        [resid, segments[:, None], segments[None, :], cosine, sine, gains],
        list(mixer),
        [
            pltpu.VMEM((2, width, width), LOW),
            pltpu.VMEM((2, width, width), LOW),
            pltpu.VMEM(one, FULL),
            pltpu.VMEM((length, length), FULL),
            pltpu.SemaphoreType.DMA((4,)),
        ],
        8 * length * width * width + 4 * length * length * width,
    )


GELU_SCALE = 0.7978845608028654
GELU_CUBE = 0.044715


def hidden_tiles(own, other, width):
    ups = [tile_of(r, t, width) for r in (own, other) for t in (0, 1)]
    downs = [tile_of(r, t, width) for r in (own, other) for t in (2, 3)]
    return ups, downs


def hidden_forward_kernel(
    place_of, middle, gains, own, other,
    output, active, pack, hidden, ups, downs, hidden_here, sems, out_sems,
):
    u, d = hidden_tiles(own, other, middle.shape[1])
    ins = fetch(
        [r for t in range(4) for r in (u[t], d[t])],
        [w.at[t] for t in range(4) for w in (ups, downs)],
        sems,
    )
    normed, _, _ = normalize(middle[...], gains[0:1], gains[1:2])
    pack[0] = normed.astype(LOW)
    outs = []
    for t in range(4):
        ins[2 * t].wait()
        x = dot(pack[0], ups[t])
        hidden_here[t] = x
        out = pltpu.make_async_copy(hidden_here.at[t], hidden.at[t], out_sems.at[t])
        out.start()
        outs.append(out)
        inner = jnp.tanh(GELU_SCALE * (x + GELU_CUBE * (x * x * x)))
        target = active.at[t] if t < 2 else pack.at[t - 1]
        target[...] = (x * (0.5 * (1.0 + inner))).astype(LOW)
        ins[2 * t + 1].wait()
        product = dot(target[...], downs[t])
        output[...] = (middle[...] if t == 0 else output[...]) + product
    for out in outs:
        out.wait()


def hidden_forward(place, middle, pair, gains):
    length, width = middle.shape
    one = (length, width)
    outs = [(one, FULL), ((2,) + one, LOW), ((3,) + one, LOW), ((4,) + one, FULL)]
    return call(
        hidden_forward_kernel,
        place,
        outs,
        [middle, gains],
        list(pair),
        [
            pltpu.VMEM((4, width, width), LOW),
            pltpu.VMEM((4, width, width), LOW),
            pltpu.VMEM((4,) + one, FULL),
            pltpu.SemaphoreType.DMA((8,)),
            pltpu.SemaphoreType.DMA((4,)),
        ],
        16 * length * width * width,
        outs_any=1,
    )


def hidden_back_kernel(
    place_of, grad, branch, middle, gains, hidden, own, other,
    grad_middle, grad_gains, grad_own, grad_other, ups, downs, hidden_here, total, sems,
):
    u, d = hidden_tiles(own, other, middle.shape[1])
    ins = fetch(
        [r for t in range(4) for r in (d[t], hidden.at[t], u[t])],
        [w.at[t] for t in range(4) for w in (downs, hidden_here, ups)],
        sems,
    )
    for t in range(4):
        ins[3 * t].wait()
        grad_active = dot_nt(branch[...], downs[t])
        ins[3 * t + 1].wait()
        x = hidden_here[t]
        inner = jnp.tanh(GELU_SCALE * (x + GELU_CUBE * (x * x * x)))
        slope = 0.5 * (1.0 + inner) + (0.5 * GELU_SCALE) * x * (1.0 - inner * inner) * (
            1.0 + (3.0 * GELU_CUBE) * (x * x)
        )
        target = grad_own.at[t] if t < 2 else grad_other.at[t - 2]
        target[...] = (grad_active * slope).astype(LOW)
        ins[3 * t + 2].wait()
        product = dot_nt(target[...], ups[t])
        total[...] = product if t == 0 else total[...] + product
    _, unit, inverse = normalize(middle[...], gains[0:1], gains[1:2])
    back, gain, bias = normalize_back(total[...], unit, inverse, gains[0:1])
    grad_middle[...] = grad[...] + back
    grad_gains[0:1] = gain
    grad_gains[1:2] = bias


def hidden_back(place, grad, branch, middle, hidden, pair, gains):
    length, width = middle.shape
    one = (length, width)
    outs = [(one, FULL), ((2, width), FULL), ((2,) + one, LOW), ((2,) + one, LOW)]
    return call(
        hidden_back_kernel,
        place,
        outs,
        [grad, branch, middle, gains],
        [hidden] + list(pair),
        [
            pltpu.VMEM((4, width, width), LOW),
            pltpu.VMEM((4, width, width), LOW),
            pltpu.VMEM((4,) + one, FULL),
            pltpu.VMEM(one, FULL),
            pltpu.SemaphoreType.DMA((12,)),
        ],
        16 * length * width * width,
    )


def attention_back_kernel(
    place_of, grad_middle, resid, seg_col, seg_row, cosine, sine, gains, query, keys, values, lse,
    own, other,
    grad, branch, grad_gains, grad_own, grad_other,
    w_a, w_b, same, ga, gq, gk, gv, sems,
):
    width = resid.shape[1]
    half = width // 2
    copies = fetch(
        [tile_of(r, t, width) for t in (1, 0) for r in (own, other)],
        [w.at[place] for w in (w_b, w_a) for place in range(2)],
        sems,
    )
    first = place_of[0] == 0
    scale = HD ** (-0.5)
    grads = (grad_own, grad_other)
    same[...] = jnp.where(seg_col[...] == seg_row[...], 0.0, 1.0)
    attn_grad = grad_middle[...].astype(LOW)
    left, right = attn_grad[:, :half], attn_grad[:, half:]
    grad_own[1, :, half:] = jnp.where(first, left, right)
    grad_other[1, :, half:] = jnp.where(first, right, left)
    copies[0].wait()
    copies[1].wait()
    natural = dot_nt(grad_own[1, :, half:], w_b[0, :, half:]) + dot_nt(
        grad_other[1, :, half:], w_b[1, :, half:]
    )
    natural = natural.astype(LOW)
    ga[:, :half] = jnp.where(first, natural[:, :half], natural[:, half:])
    ga[:, half:] = jnp.where(first, natural[:, half:], natural[:, :half])

    def pair(p, _):
        columns = pl.ds(pl.multiple_of(p * 128, 128), 128)
        q, k, v, g = query[:, columns], keys[:, columns], values[:, columns], ga[:, columns]
        out_q, out_k, out_v = [], [], []
        for head in range(2):
            mask = head_mask(q.shape, head)
            zero = jnp.zeros_like(q)
            scores = dot_nt(k, jnp.where(mask, q, zero)) * scale
            scores = jnp.where(same[...] > 0.5, -1000000000.0, scores)
            probs = jnp.exp(scores - lse[pl.ds(2 * p + head, 1), :])
            grad_probs = dot_nt(v, jnp.where(mask, g, zero))
            across = jnp.sum(probs * grad_probs, 0, keepdims=True)
            grad_scores = (probs * (grad_probs - across)).astype(LOW)
            out_k.append(dot(grad_scores, q))
            out_q.append(cross(grad_scores, k))
            out_v.append(dot(probs.astype(LOW), g))
        for out, target in ((out_q, gq), (out_k, gk)):
            x = jnp.where(head_mask(out[0].shape, 0), out[0], out[1]) * scale
            x = x * cosine[...] - swap_halves(x) * sine[...]
            target[:, columns] = x.astype(LOW)
        gv[:, columns] = jnp.where(head_mask(out_v[0].shape, 0), out_v[0], out_v[1]).astype(LOW)
        return 0

    lax.fori_loop(0, width // 128, pair, 0)
    for place in range(2):
        columns = slice(place * half, (place + 1) * half)
        grads[place][0, :, :half] = gq[:, columns]
        grads[place][0, :, half:] = gk[:, columns]
        grads[place][1, :, :half] = gv[:, columns]
    copies[2].wait()
    copies[3].wait()
    total = dot_nt(grad_own[0], w_a[0]) + dot_nt(grad_other[0], w_a[1])
    total = total + dot_nt(grad_own[1, :, :half], w_b[0, :, :half])
    total = total + dot_nt(grad_other[1, :, :half], w_b[1, :, :half])
    _, unit, inverse = normalize(resid[...], gains[0:1], gains[1:2])
    back, gain, bias = normalize_back(total, unit, inverse, gains[0:1])
    back = grad_middle[...] + back
    grad[...] = back
    branch[...] = back.astype(LOW)
    grad_gains[0:1] = gain
    grad_gains[1:2] = bias


def attention_back(place, grad_middle, resid, mixer, gains, cosine, sine, segments, query, keys, values, lse):
    length, width = resid.shape
    one = (length, width)
    outs = [(one, FULL), (one, LOW), ((2, width), FULL)] + [((2,) + one, LOW)] * 2
    ins = [grad_middle, resid, segments[:, None], segments[None, :], cosine, sine, gains]
    ins += [query, keys, values, lse.T[: width // HD]]
    return call(
        attention_back_kernel,
        place,
        outs,
        ins,
        list(mixer),
        [
            pltpu.VMEM((2, width, width), LOW),
            pltpu.VMEM((2, width, width), LOW),
            pltpu.VMEM((length, length), FULL),
        ]
        + [pltpu.VMEM(one, LOW)] * 4
        + [pltpu.SemaphoreType.DMA((4,))],
        8 * length * width * width + 10 * length * length * width,
    )


def adam_step(master, grad, first, second, rate, decay):
    first = BETA_ONE * first + (1.0 - BETA_ONE) * grad
    second = BETA_TWO * second + (1.0 - BETA_TWO) * grad * grad
    fix_one = 1.0 - BETA_ONE**STEP
    fix_two = 1.0 - BETA_TWO**STEP
    update = first / fix_one / (jnp.sqrt(second / fix_two) + ADAM_EPS) + decay * master
    return (master - rate * update, first, second)


def swap_cores(value):
    return lax.ppermute(value, "dp", [(0, 1), (1, 0)])


def across(value, mask, size):
    return lax.ppermute(value, "fsdp", [(i, i ^ mask) for i in range(size)])


def tie(*values):
    return lax.optimization_barrier(values)


def total_of(value, size):
    value = value + swap_cores(value)
    for bit in range(size.bit_length() - 1):
        value = value + across(value, 1 << bit, size)
    return value


X, Y = 1, 2
Z = (4, 8, 12)


def round_kernel(jobs, n_ins, counts, *refs):
    new, once, twice, done = counts
    place_of, ins = refs[0], refs[1 : 1 + n_ins]
    rest = list(refs[1 + n_ins :])
    pop = lambda present, n=1: [rest.pop(0) for _ in range(n)] if present else [None] * n
    (keep_once,), (keep_twice,) = pop(once), pop(twice)
    from_x, from_y = pop(once or twice, 2)
    keep_done, *from_z = pop(done, 4)
    to_x, to_y = pop(new or once, 2)
    (out_once,), (out_twice,) = pop(new), pop(once)
    out_done, *to_z = pop(twice, 4)
    share, squares = pop(done, 2)
    (tile,) = pop(new)
    rows = (out_once if new else out_twice if once else out_done if twice else share).shape[-2]
    rows = rows // (8 if new else 4 if once else 1)
    bits, z = (place_of[1], place_of[2]), place_of[3]
    to, came = (to_x, to_y), (from_x, from_y)

    def block(index):
        if isinstance(index, int):
            return pl.ds(index * rows, rows)
        return pl.ds(pl.multiple_of(index * rows, 16), rows)

    def factor(spec):
        which, index, low, high = spec
        ref = ins[which] if index is None else ins[which].at[index]
        return ref[...] if low is None else ref[:, low:high]

    for p in range(new):
        for s in range(2):
            for low, high, products in jobs[2 * p + s]:
                total = None
                for left, right in products:
                    product = cross(factor(left), factor(right))
                    total = product if total is None else total + product
                tile[:, low:high] = total
            for zz in range(4):
                for other in range(2):
                    at = zz * 2 + other
                    index = lambda bit: zz * 4 + (other * 2 + bit if s == 0 else bit * 2 + other)
                    to[s][block(p * 8 + at), :] = tile[block(index(1 - bits[s])), :].astype(LOW)
                    out_once[p, s, block(at), :] = tile[block(index(bits[s])), :]
    for p in range(once):
        for s in range(2):
            for zz in range(4):
                for bit in range(2):
                    at = zz * 2 + (bits[1 - s] if bit else 1 - bits[1 - s])
                    value = keep_once[p, s, block(at), :] + came[s][block(p * 8 + at), :].astype(FULL)
                    if bit:
                        out_twice[p, s, block(zz), :] = value
                    else:
                        to[1 - s][block(new * 8 + p * 4 + zz), :] = value.astype(LOW)
    for p in range(twice):
        for s in range(2):
            for xor in range(4):
                at = jnp.bitwise_xor(z, xor)
                value = keep_twice[p, s, block(at), :] + came[1 - s][
                    block(once * 8 + p * 4 + at), :
                ].astype(FULL)
                if xor == 0:
                    out_done[p, s] = value
                else:
                    to_z[xor - 1][block(2 * p + s), :] = value.astype(LOW)
    if done:
        squares[...] = jnp.zeros_like(squares)
    for p in range(done):
        for s in range(2):
            value = keep_done[p, s]
            for f in from_z:
                value = value + f[block(2 * p + s), :].astype(FULL)
            share[p, s] = value
            squares[...] += jnp.sum(value * value, 0, keepdims=True)


class Rounds:
    def __init__(self, place, rows, width):
        self.place, self.rows, self.width = place, rows, width
        self.counts = (0, 0, 0, 0)
        self.kept = [None] * 3
        self.came = None
        self.came_z = None
        self.shares, self.squares = [], []
        self.flying = []

    def step(self, chunk, *ties):
        rows, width = self.rows, self.width
        new, once, twice, done = counts = (len(chunk),) + self.counts[:3]
        arrays, jobs = [], []

        def number(spec):
            array, *place = spec
            for i, known in enumerate(arrays):
                if known is array:
                    return (i, *place)
            arrays.append(array)
            return (len(arrays) - 1, *place)

        for pair in chunk:
            for tile in pair:
                jobs.append(
                    [(a, b, [(number(l), number(r)) for l, r in ps]) for a, b, ps in tile]
                )
        ins = list(arrays)
        if once:
            ins.append(self.kept[0])
        if twice:
            ins.append(self.kept[1])
        if once or twice:
            ins += self.came
        if done:
            ins += [self.kept[2]] + self.came_z
        outs = []
        if new or once:
            outs += [(((new * 8 + once * 4) * rows, width), LOW)] * 2
        if new:
            outs.append(((new, 2, 8 * rows, width), FULL))
        if once:
            outs.append(((once, 2, 4 * rows, width), FULL))
        if twice:
            outs.append(((twice, 2, rows, width), FULL))
            outs += [((twice * 2 * rows, width), LOW)] * 3
        if done:
            outs += [((done, 2, rows, width), FULL), ((1, width), FULL)]
        length = 2 * arrays[0].shape[-2] if new else 0
        got = call(
            functools.partial(round_kernel, jobs, len(arrays), counts),
            self.place,
            outs,
            ins,
            [],
            [pltpu.VMEM((16 * rows, width), FULL)] if new else [],
            4 * new * length * width * width,
        )
        self.flying, self.kept, self.counts = [], [None] * 3, counts
        if done:
            *got, share, square = got
            self.squares.append(square)
        if not (new or once or twice):
            self.shares.append((share, swap_cores(share)))
            return ties
        got, ties = tie(list(got), ties)
        if new or once:
            self.flying += [across(got.pop(0), X, 16), across(got.pop(0), Y, 16)]
        if new:
            self.kept[0] = got.pop(0)
        if once:
            self.kept[1] = got.pop(0)
        if twice:
            self.kept[2] = got.pop(0)
            self.flying += [across(got.pop(0), mask, 16) for mask in Z]
        if done:
            self.shares.append((share, swap_cores(share)))
        return ties

    def finish(self, *ties):
        if self.counts[3]:
            share, other = self.shares[-1]
            self.flying.append(other)
        flying, ties = tie(self.flying, ties)
        if self.counts[3]:
            self.shares[-1] = (share, flying.pop())
        self.came = self.came_z = None
        if self.counts[0] or self.counts[1]:
            self.came, flying = flying[:2], flying[2:]
        if self.counts[2]:
            self.came_z = flying
        return ties

    def left(self):
        return any(self.counts[:3])


class PlainRounds:
    def __init__(self):
        self.shares, self.squares = [], []

    def step(self, chunk, *ties):
        def factor(spec):
            array, index, low, high = spec
            array = array if index is None else array[index]
            return array if low is None else array[:, low:high]

        def summed(tile):
            parts = [sum(cross(factor(l), factor(r)) for l, r in ps) for _, _, ps in tile]
            return lax.psum_scatter(
                jnp.concatenate(parts, 1), "fsdp", scatter_dimension=0, tiled=True
            )

        share = jnp.stack([jnp.stack([summed(tile) for tile in pair]) for pair in chunk])
        self.shares.append((share, swap_cores(share)))
        self.squares.append(jnp.sum(share * share, (0, 1, 2))[None])
        return ties

    def finish(self, *ties):
        return ties

    def left(self):
        return False


def small_steps(value, place, size, rows):
    (got,) = yield [swap_cores(value)]
    value = (value + got).reshape(-1, 4, 2, 2, rows).transpose(1, 2, 3, 0, 4)
    for bit in range(2):
        axis = 2 - bit
        send = lax.dynamic_index_in_dim(value, 1 - place[1 + bit], axis, keepdims=False)
        keep = lax.dynamic_index_in_dim(value, place[1 + bit], axis, keepdims=False)
        (got,) = yield [across(send, 1 << bit, size)]
        value = keep + got
    take = lambda xor: lax.dynamic_index_in_dim(value, place[3] ^ xor, 0, keepdims=False)
    got = yield [across(take(mask // 4), mask, size) for mask in Z]
    return take(0) + (got[0] + (got[1] + got[2]))


def up_to_parts(expand_shard, size, rows, parts):
    r = expand_shard.shape[0]
    return expand_shard.reshape(r, size, parts, rows).transpose(0, 2, 1, 3).reshape(r, -1)


def up_from_parts(expand_shard, size, rows, parts):
    r = expand_shard.shape[0]
    return expand_shard.reshape(r, parts, size, rows).transpose(0, 2, 1, 3).reshape(r, -1)


def half_of(value, core):
    half = value.shape[1] // 2
    return lax.dynamic_slice_in_dim(value, core * half, half, 1)


def body(
    fsdp,
    codons,
    masked,
    segments,
    inward,
    outward,
    expand,
    shrink,
    codon_table,
    norm_params,
    inward_first,
    inward_second,
    outward_first,
    outward_second,
    expand_first,
    expand_second,
    shrink_first,
    shrink_second,
    table_first,
    table_second,
    norm_first,
    norm_second,
):
    layers = inward.shape[0]
    length = codons.shape[0]
    rows = inward.shape[1]
    width = rows * fsdp
    half = width // 2
    parts = shrink.shape[1] // rows
    fast = fsdp == 16 and rows % 16 == 0
    core, index = lax.axis_index("dp"), lax.axis_index("fsdp")
    bit = lambda b: lax.rem(lax.div(index, b), 2)
    place = jnp.stack([core, bit(1), bit(2), lax.div(index, 4)]).astype(jnp.int32)
    weight = masked.astype(FULL)
    inputs = jnp.where(masked == 1, V - 1, codons)

    def tiles_of(l):
        w_in, w_out = inward[l].astype(LOW), outward[l].astype(LOW)
        pieces = [half_of(w_in[:, p * width : (p + 1) * width], core) for p in range(3)]
        pieces.append(half_of(w_out, core))
        mixer = [jnp.concatenate(pieces[:2], 1), jnp.concatenate(pieces[2:], 1)]
        up = half_of(up_to_parts(expand[l].astype(LOW), fsdp, rows, parts), core)
        down = lax.dynamic_slice_in_dim(shrink[l].astype(LOW), core * 2 * rows, 2 * rows, 0)
        return mixer + [up[:, :width], up[:, width:], down[:rows], down[rows:]]

    norms = norm_params.shape[0] * 2
    small = jnp.concatenate(
        [codon_table.astype(LOW), norm_params.astype(LOW).reshape(norms, rows)], 0
    )
    small = jnp.pad(small.T, ((0, 0), (0, -small.shape[0] % 128)))
    sides = jnp.concatenate([small] + sum([tiles_of(l) for l in range(layers)], []), 1)
    sides = lax.all_gather(sides, "fsdp", axis=0, tiled=True)
    cut = small.shape[1]
    small = sides[:, : V + norms].T
    mixers, hiddens = [], []
    for l in range(layers):
        own = sides[:, cut : cut + 2 * width]
        mixers.append((own, swap_cores(own)))
        own = sides[:, cut + 2 * width : cut + 6 * width]
        hiddens.append((own, swap_cores(own)))
        cut += 6 * width
    table_low = small[:V]
    gains = small[V:].astype(FULL).reshape(-1, 2, width)

    cosine, sine = rotary_tables(length)
    vocab_ids = jnp.arange(V, dtype=jnp.int32)
    chosen = (inputs[:, None] == vocab_ids[None, :]).astype(LOW)
    resid = dot(chosen, table_low)
    kept = []
    for l in range(layers):
        gain = gains[2 * l : 2 * l + 2]
        middle, query, keys, values, lse, pack = attention_forward(
            place, resid, mixers[l], gain[0], cosine, sine, segments
        )
        if l > 0:
            middle, came = tie(middle, kept[-1][-1])
            kept[-1] = kept[-1][:-1] + (came,)
        pack_came = swap_cores(pack)
        output, active, pack_mid, hidden = hidden_forward(place, middle, hiddens[l], gain[1])
        output, pack_came = tie(output, pack_came)
        kept.append(
            (resid, query, keys, values, lse, pack, pack_came, middle, hidden, active, pack_mid)
            + (swap_cores(pack_mid),)
        )
        resid = output
    final_gain = gains[2 * layers]
    normed_out, unit_out, inverse_out = normalize(resid, final_gain[0], final_gain[1])
    head_in = normed_out.astype(LOW)
    logits = jnp.einsum("sd,vd->sv", head_in, table_low, preferred_element_type=FULL)
    top = jnp.max(logits, -1, keepdims=True)
    lse_head = top + jnp.log(jnp.sum(jnp.exp(logits - top), -1, keepdims=True))
    targets = (codons[:, None] == vocab_ids[None, :]).astype(FULL)
    picked = jnp.sum(logits * targets, -1)
    loss_local = jnp.sum((lse_head[:, 0] - picked) * weight)
    grad_logits = ((jnp.exp(logits - lse_head) - targets) * weight[:, None]).astype(LOW)
    grad_table = cross(grad_logits, head_in)
    grad_head = dot(grad_logits, table_low)
    grad, grad_final_gain, grad_final_bias = normalize_back(
        grad_head, unit_out, inverse_out, final_gain[0]
    )
    branch = grad.astype(LOW)
    grad_norms = [grad_final_gain, grad_final_bias]
    grad, branch, came = tie(grad, branch, kept[-1][-1])
    kept[-1] = kept[-1][:-1] + (came,)

    rounds = Rounds(place, rows, width) if fast else PlainRounds()
    whole = lambda array, i=None: (array, i, None, None)
    tile = lambda left, right, other_left, other_right: [
        (0, width, [(left, right), (other_left, other_right)])
    ]
    chunk = []
    for l in reversed(range(layers)):
        (resid, query, keys, values, lse, pack, pack_came, middle, hidden, active, pack_mid, mid_came) = kept[l]
        gain = gains[2 * l : 2 * l + 2]
        branch_came = swap_cores(branch)
        chunk.append(
            [
                tile(
                    whole(active, s), whole(branch), whole(mid_came, 1 + s), whole(branch_came)
                )
                for s in range(2)
            ]
        )
        grad, branch = rounds.step(chunk, grad, branch)
        grad_middle, gains_mid, up_own, up_other = hidden_back(
            place, grad, branch, middle, hidden, hiddens[l], gain[1]
        )
        grad_middle, up_own, up_other = rounds.finish(grad_middle, up_own, up_other)
        up_came = swap_cores(up_other)
        (grad_middle,) = rounds.step(
            [
                [
                    tile(
                        whole(pack_mid, 0), whole(up_own, s), whole(mid_came, 0), whole(up_came, s)
                    )
                    for s in range(2)
                ]
            ],
            grad_middle,
        )
        grad, branch, gains_in, mix_own, mix_other = attention_back(
            place, grad_middle, resid, mixers[l], gain[0], cosine, sine, segments,
            query, keys, values, lse,
        )
        grad_norms = [gains_in, gains_mid] + grad_norms
        grad, branch, mix_own, mix_other = rounds.finish(grad, branch, mix_own, mix_other)
        mix_came = swap_cores(mix_other)
        products = lambda i, a, b: [
            ((pack, i, None, None), (mix_own, 1, a, b)),
            ((pack_came, i, None, None), (mix_came, 1, a, b)),
        ]
        chunk = [
            [
                tile(whole(pack, 0), whole(mix_own, 0), whole(pack_came, 0), whole(mix_came, 0)),
                [(0, half, products(0, 0, half)), (half, width, products(1, half, width))],
            ]
        ]
    grad_table = grad_table + cross(chosen, branch)
    grad_small = jnp.concatenate([grad_table] + grad_norms, 0)
    if fast:
        steps = small_steps(grad_small, place, fsdp, rows)
        messages = steps.send(next(steps))
        rounds.step(chunk)
        share_small = None
        while rounds.left() or share_small is None:
            ((messages,),) = (rounds.finish(messages),)
            try:
                messages = steps.send(messages) if share_small is None else []
            except StopIteration as end:
                share_small, messages = end.value, []
            if rounds.left():
                rounds.step([])
    else:
        rounds.step(chunk)
        share_small = lax.psum_scatter(
            grad_small + swap_cores(grad_small), "fsdp", scatter_dimension=1, tiled=True
        )

    squares = 0.5 * jnp.sum(share_small * share_small)
    for value in rounds.squares:
        squares = squares + jnp.sum(value)
    totals = jnp.stack([loss_local, jnp.sum(weight), squares])
    totals = total_of(jnp.pad(totals, (0, 125))[None], fsdp)
    loss_sum, count, square_total = totals[0, 0], totals[0, 1], totals[0, 2]

    both = []
    for share, other in rounds.shares:
        first = core == 0
        both.append((jnp.where(first, share, other), jnp.where(first, other, share)))
    share_in, share_out, share_up, share_down = ([None] * layers for _ in range(4))
    side = lambda *values: jnp.concatenate(values, 1)
    for l in range(layers):
        at = 2 * (layers - 1 - l)
        down, up, mix = (at, at and 1), (at + 1, 0), (at + 2, 0)
        tiles = lambda where: [both[where[0]][c][where[1], s] for c in range(2) for s in range(2)]
        a_0, b_0, a_1, b_1 = tiles(mix)
        share_in[l] = side(
            a_0[:, :half], a_1[:, :half], a_0[:, half:], a_1[:, half:], b_0[:, :half], b_1[:, :half]
        )
        share_out[l] = side(b_0[:, half:], b_1[:, half:])
        share_up[l] = up_from_parts(side(*tiles(up)), fsdp, rows, parts)
        share_down[l] = jnp.concatenate(tiles(down), 0)
    group = (
        jnp.stack(share_in),
        jnp.stack(share_out),
        jnp.stack(share_up),
        jnp.stack(share_down),
        share_small[:V],
        share_small[V:].reshape(-1, 2, rows),
    )
    grad_norm = jnp.sqrt(square_total) / count
    factor = CLIP / jnp.maximum(grad_norm, CLIP)
    masters = (inward, outward, expand, shrink, codon_table, norm_params)
    firsts = (inward_first, outward_first, expand_first, shrink_first, table_first, norm_first)
    seconds = (
        inward_second,
        outward_second,
        expand_second,
        shrink_second,
        table_second,
        norm_second,
    )
    result = [loss_sum, count, grad_norm]
    for index in range(6):
        rate = RATE_VECTOR if index == 5 else RATE_MATRIX
        decay = 0.0 if index == 5 else DECAY
        clipped = group[index] / count * factor
        result.extend(
            adam_step(masters[index], clipped, firsts[index], seconds[index], rate, decay)
        )
    return tuple(result)


def solution(mesh):
    in_specs = (
        P(("fsdp", "dp")),
        P(("fsdp", "dp")),
        P(("fsdp", "dp")),
        P(None, "fsdp", None),
        P(None, "fsdp", None),
        P(None, "fsdp", None),
        P(None, "fsdp", None),
        P(None, "fsdp"),
        P(None, None, "fsdp"),
        P(None, "fsdp", None),
        P(None, "fsdp", None),
        P(None, "fsdp", None),
        P(None, "fsdp", None),
        P(None, "fsdp", None),
        P(None, "fsdp", None),
        P(None, "fsdp", None),
        P(None, "fsdp", None),
        P(None, "fsdp"),
        P(None, "fsdp"),
        P(None, None, "fsdp"),
        P(None, None, "fsdp"),
    )
    out_specs = (
        P(),
        P(),
        P(),
        P(None, "fsdp", None),
        P(None, "fsdp", None),
        P(None, "fsdp", None),
        P(None, "fsdp", None),
        P(None, "fsdp", None),
        P(None, "fsdp", None),
        P(None, "fsdp", None),
        P(None, "fsdp", None),
        P(None, "fsdp", None),
        P(None, "fsdp", None),
        P(None, "fsdp", None),
        P(None, "fsdp", None),
        P(None, "fsdp"),
        P(None, "fsdp"),
        P(None, "fsdp"),
        P(None, None, "fsdp"),
        P(None, None, "fsdp"),
        P(None, None, "fsdp"),
    )
    step = functools.partial(body, mesh.shape["fsdp"])
    return jax.shard_map(step, mesh=mesh, in_specs=in_specs, out_specs=out_specs, check_vma=False)
```

```python
import functools

import jax
import jax.numpy as jnp
from jax import lax
from jax.experimental import pallas as pl
from jax.experimental.pallas import tpu as pltpu
from jax.sharding import PartitionSpec as P

HD = 64
V = 70
STEP = 10


NORM_EPS = 1e-05
BETA_ONE = 0.9
BETA_TWO = 0.95
ADAM_EPS = 1e-08
DECAY = 0.1
RATE_MATRIX = 0.05
RATE_VECTOR = 0.3
CLIP = 0.05


def rotary_tables(length):
    freq = 10000.0 ** (-jnp.arange(HD // 2, dtype=jnp.float32) * 2.0 / HD)
    angle = jnp.arange(length, dtype=jnp.float32)[:, None] * freq[None, :]
    cosine, sine = jnp.cos(angle), jnp.sin(angle)
    return (
        jnp.concatenate([cosine] * 4, 1),
        jnp.concatenate([-sine, sine] * 2, 1),
    )


def normalize(resid, gain, bias):
    mean = jnp.mean(resid, -1, keepdims=True)
    centred = resid - mean
    inverse = lax.rsqrt(jnp.mean(centred * centred, -1, keepdims=True) + NORM_EPS)
    unit = centred * inverse
    return (unit * gain + bias, unit, inverse)


def normalize_back(grad, unit, inverse, gain):
    scaled = grad * gain
    across = (
        scaled
        - jnp.mean(scaled, -1, keepdims=True)
        - unit * jnp.mean(scaled * unit, -1, keepdims=True)
    )
    return (across * inverse, jnp.sum(grad * unit, 0, keepdims=True), jnp.sum(grad, 0, keepdims=True))


def dot(left, right):
    return jnp.dot(left, right, preferred_element_type=jnp.float32)


def dot_nt(left, right):
    return lax.dot_general(
        left, right, (((1,), (1,)), ((), ())), preferred_element_type=jnp.float32
    )


def cross(left, right):
    return lax.dot_general(
        left, right, (((0,), (0,)), ((), ())), preferred_element_type=jnp.float32
    )


VMEM_LIMIT = 56 * 1024 * 1024
LOW, FULL = jnp.bfloat16, jnp.float32


def call(kernel, scalars, out_shapes, ins, anys, scratch, flops, outs_any=0):
    whole = pl.BlockSpec(memory_space=pltpu.VMEM)
    left = pl.BlockSpec(memory_space=pl.ANY)
    n = len(out_shapes)
    return pl.pallas_call(
        kernel,
        out_shape=[jax.ShapeDtypeStruct(s, t) for s, t in out_shapes],
        in_specs=[pl.BlockSpec(memory_space=pltpu.SMEM)]
        + [whole] * len(ins)
        + [left] * len(anys),
        out_specs=[whole] * (n - outs_any) + [left] * outs_any,
        scratch_shapes=scratch,
        compiler_params=pltpu.CompilerParams(vmem_limit_bytes=VMEM_LIMIT),
        cost_estimate=pl.CostEstimate(
            flops=flops,
            bytes_accessed=sum(x.size * x.dtype.itemsize for x in ins + anys),
            transcendentals=0,
        ),
    )(scalars, *ins, *anys)


def fetch(sources, targets, sems):
    copies = [
        pltpu.make_async_copy(s, t, sems.at[i]) for i, (s, t) in enumerate(zip(sources, targets))
    ]
    for c in copies:
        c.start()
    return copies


def tile_of(ref, core, at):
    return ref.at[:, core, :, at : at + ref.shape[0] * ref.shape[2]]


def matrix(ref, place, low=None, high=None):
    value = ref[place] if low is None else ref[place, :, :, low:high]
    return value.reshape(-1, value.shape[-1])


def tile_scratch(count, weights):
    blocks, _, rows, _ = weights.shape
    return pltpu.VMEM((count, blocks, rows, blocks * rows), LOW)


def swap_halves(value):
    lane = lax.broadcasted_iota(jnp.int32, value.shape, 1)
    return jnp.where(
        lax.rem(lane, HD) < HD // 2,
        pltpu.roll(value, 128 - HD // 2, 1),
        pltpu.roll(value, HD // 2, 1),
    )


def ordered(first, own, other):
    return jnp.concatenate([jnp.where(first, own, other), jnp.where(first, other, own)], 1)


def head_mask(shape, head):
    lane = lax.broadcasted_iota(jnp.int32, shape, 1)
    return (lane < HD) if head == 0 else (lane >= HD)


def attention_forward_kernel(
    base, place_of, resid, seg_col, seg_row, cosine, sine, gains, weights,
    middle, query, keys, values, lse, pack,
    w_a, w_b, mixed, same, sems,
):
    width = resid.shape[1]
    half = width // 2
    copies = fetch(
        [tile_of(weights, c, base + t * width) for t in range(2) for c in (place_of[0], 1 - place_of[0])],
        [w.at[place] for w in (w_a, w_b) for place in range(2)],
        sems,
    )
    first = place_of[0] == 0
    normed, _, _ = normalize(resid[...], gains[0:1], gains[1:2])
    normed_low, attended = pack.at[0], pack.at[1]
    normed_low[...] = normed.astype(LOW)
    same[...] = jnp.where(seg_col[...] == seg_row[...], 0.0, 1.0)
    for place in range(2):
        copies[place].wait()
        mixed[...] = dot(normed_low[...], matrix(w_a, place))
        for p in range(half // 128):
            for part, target in ((0, query), (1, keys)):
                x = mixed[:, part * half + p * 128 : part * half + (p + 1) * 128]
                x = x * cosine[...] + swap_halves(x) * sine[...]
                target[:, place * half + p * 128 : place * half + (p + 1) * 128] = x.astype(LOW)
    for place in range(2):
        copies[2 + place].wait()
        values[:, place * half : (place + 1) * half] = dot(
            normed_low[...], matrix(w_b, place, 0, half)
        ).astype(LOW)

    lse[...] = jnp.zeros_like(lse)

    def pair(p, _):
        columns = pl.ds(pl.multiple_of(p * 128, 128), 128)
        q, k, v = query[:, columns], keys[:, columns], values[:, columns]
        out = []
        for head in range(2):
            masked_q = jnp.where(head_mask(q.shape, head), q, jnp.zeros_like(q))
            scores = dot_nt(masked_q, k) * HD ** (-0.5)
            scores = jnp.where(same[...] > 0.5, -1000000000.0, scores)
            top = jnp.max(scores, -1, keepdims=True)
            expo = jnp.exp(scores - top)
            total = jnp.sum(expo, -1, keepdims=True)
            probs = (expo / total).astype(LOW)
            out.append(dot(probs, v))
            lane = lax.broadcasted_iota(jnp.int32, lse.shape, 1)
            lse[...] = jnp.where(lane == 2 * p + head, top + jnp.log(total), lse[...])
        attended[:, columns] = jnp.where(head_mask(out[0].shape, 0), out[0], out[1]).astype(LOW)
        return 0

    lax.fori_loop(0, width // 128, pair, 0)
    attended[...] = ordered(first, attended[:, :half], attended[:, half:])
    out = ordered(
        first,
        dot(attended[...], matrix(w_b, 0, half, width)),
        dot(attended[...], matrix(w_b, 1, half, width)),
    )
    middle[...] = resid[...] + out


def attention_forward(place, resid, weights, base, gains, cosine, sine, segments):
    length, width = resid.shape
    one = (length, width)
    outs = [(one, FULL)] + [(one, LOW)] * 3 + [((length, 128), FULL), ((2,) + one, LOW)]
    return call(
        functools.partial(attention_forward_kernel, base),
        place,
        outs,
        [resid, segments[:, None], segments[None, :], cosine, sine, gains],
        [weights],
        [
            tile_scratch(2, weights),
            tile_scratch(2, weights),
            pltpu.VMEM(one, FULL),
            pltpu.VMEM((length, length), FULL),
            pltpu.SemaphoreType.DMA((4,)),
        ],
        8 * length * width * width + 4 * length * length * width,
    )


GELU_SCALE = 0.7978845608028654
GELU_CUBE = 0.044715


def hidden_tiles(weights, core, base, width):
    tiles = [
        [tile_of(weights, c, base + t * width) for c in (core, 1 - core) for t in pair]
        for pair in ((2, 3), (4, 5))
    ]
    return tiles[0], tiles[1]


def hidden_forward_kernel(
    base, place_of, middle, gains, weights,
    output, active, pack, hidden, ups, downs, hidden_here, sems, out_sems,
):
    u, d = hidden_tiles(weights, place_of[0], base, middle.shape[1])
    ins = fetch(
        [r for t in range(4) for r in (u[t], d[t])],
        [w.at[t] for t in range(4) for w in (ups, downs)],
        sems,
    )
    normed, _, _ = normalize(middle[...], gains[0:1], gains[1:2])
    pack[0] = normed.astype(LOW)
    outs = []
    for t in range(4):
        ins[2 * t].wait()
        x = dot(pack[0], matrix(ups, t))
        hidden_here[t] = x
        out = pltpu.make_async_copy(hidden_here.at[t], hidden.at[t], out_sems.at[t])
        out.start()
        outs.append(out)
        inner = jnp.tanh(GELU_SCALE * (x + GELU_CUBE * (x * x * x)))
        target = active.at[t] if t < 2 else pack.at[t - 1]
        target[...] = (x * (0.5 * (1.0 + inner))).astype(LOW)
        ins[2 * t + 1].wait()
        product = dot(target[...], matrix(downs, t))
        output[...] = (middle[...] if t == 0 else output[...]) + product
    for out in outs:
        out.wait()


def hidden_forward(place, middle, weights, base, gains):
    length, width = middle.shape
    one = (length, width)
    outs = [(one, FULL), ((2,) + one, LOW), ((3,) + one, LOW), ((4,) + one, FULL)]
    return call(
        functools.partial(hidden_forward_kernel, base),
        place,
        outs,
        [middle, gains],
        [weights],
        [
            tile_scratch(4, weights),
            tile_scratch(4, weights),
            pltpu.VMEM((4,) + one, FULL),
            pltpu.SemaphoreType.DMA((8,)),
            pltpu.SemaphoreType.DMA((4,)),
        ],
        16 * length * width * width,
        outs_any=1,
    )


def hidden_back_kernel(
    base, place_of, grad, branch, middle, gains, hidden, weights,
    grad_middle, grad_gains, grad_own, grad_other, ups, downs, hidden_here, total, sems,
):
    u, d = hidden_tiles(weights, place_of[0], base, middle.shape[1])
    ins = fetch(
        [r for t in range(4) for r in (d[t], hidden.at[t], u[t])],
        [w.at[t] for t in range(4) for w in (downs, hidden_here, ups)],
        sems,
    )
    for t in range(4):
        ins[3 * t].wait()
        grad_active = dot_nt(branch[...], matrix(downs, t))
        ins[3 * t + 1].wait()
        x = hidden_here[t]
        inner = jnp.tanh(GELU_SCALE * (x + GELU_CUBE * (x * x * x)))
        slope = 0.5 * (1.0 + inner) + (0.5 * GELU_SCALE) * x * (1.0 - inner * inner) * (
            1.0 + (3.0 * GELU_CUBE) * (x * x)
        )
        target = grad_own.at[t] if t < 2 else grad_other.at[t - 2]
        target[...] = (grad_active * slope).astype(LOW)
        ins[3 * t + 2].wait()
        product = dot_nt(target[...], matrix(ups, t))
        total[...] = product if t == 0 else total[...] + product
    _, unit, inverse = normalize(middle[...], gains[0:1], gains[1:2])
    back, gain, bias = normalize_back(total[...], unit, inverse, gains[0:1])
    grad_middle[...] = grad[...] + back
    grad_gains[0:1] = gain
    grad_gains[1:2] = bias


def hidden_back(place, grad, branch, middle, hidden, weights, base, gains):
    length, width = middle.shape
    one = (length, width)
    outs = [(one, FULL), ((2, width), FULL), ((2,) + one, LOW), ((2,) + one, LOW)]
    return call(
        functools.partial(hidden_back_kernel, base),
        place,
        outs,
        [grad, branch, middle, gains],
        [hidden, weights],
        [
            tile_scratch(4, weights),
            tile_scratch(4, weights),
            pltpu.VMEM((4,) + one, FULL),
            pltpu.VMEM(one, FULL),
            pltpu.SemaphoreType.DMA((12,)),
        ],
        16 * length * width * width,
    )


def attention_back_kernel(
    base, place_of, grad_middle, resid, seg_col, seg_row, cosine, sine, gains, query, keys, values, lse,
    weights,
    grad, branch, grad_gains, grad_own, grad_other,
    w_a, w_b, same, ga, gq, gk, gv, sems,
):
    width = resid.shape[1]
    half = width // 2
    copies = fetch(
        [tile_of(weights, c, base + t * width) for t in (1, 0) for c in (place_of[0], 1 - place_of[0])],
        [w.at[place] for w in (w_b, w_a) for place in range(2)],
        sems,
    )
    first = place_of[0] == 0
    scale = HD ** (-0.5)
    grads = (grad_own, grad_other)
    same[...] = jnp.where(seg_col[...] == seg_row[...], 0.0, 1.0)
    attn_grad = grad_middle[...].astype(LOW)
    left, right = attn_grad[:, :half], attn_grad[:, half:]
    grad_own[1, :, half:] = jnp.where(first, left, right)
    grad_other[1, :, half:] = jnp.where(first, right, left)
    copies[0].wait()
    copies[1].wait()
    natural = dot_nt(grad_own[1, :, half:], matrix(w_b, 0, half, width)) + dot_nt(
        grad_other[1, :, half:], matrix(w_b, 1, half, width)
    )
    natural = natural.astype(LOW)
    ga[:, :half] = jnp.where(first, natural[:, :half], natural[:, half:])
    ga[:, half:] = jnp.where(first, natural[:, half:], natural[:, :half])

    def pair(p, _):
        columns = pl.ds(pl.multiple_of(p * 128, 128), 128)
        q, k, v, g = query[:, columns], keys[:, columns], values[:, columns], ga[:, columns]
        out_q, out_k, out_v = [], [], []
        for head in range(2):
            mask = head_mask(q.shape, head)
            zero = jnp.zeros_like(q)
            scores = dot_nt(k, jnp.where(mask, q, zero)) * scale
            scores = jnp.where(same[...] > 0.5, -1000000000.0, scores)
            probs = jnp.exp(scores - lse[pl.ds(2 * p + head, 1), :])
            grad_probs = dot_nt(v, jnp.where(mask, g, zero))
            across = jnp.sum(probs * grad_probs, 0, keepdims=True)
            grad_scores = (probs * (grad_probs - across)).astype(LOW)
            out_k.append(dot(grad_scores, q))
            out_q.append(cross(grad_scores, k))
            out_v.append(dot(probs.astype(LOW), g))
        for out, target in ((out_q, gq), (out_k, gk)):
            x = jnp.where(head_mask(out[0].shape, 0), out[0], out[1]) * scale
            x = x * cosine[...] - swap_halves(x) * sine[...]
            target[:, columns] = x.astype(LOW)
        gv[:, columns] = jnp.where(head_mask(out_v[0].shape, 0), out_v[0], out_v[1]).astype(LOW)
        return 0

    lax.fori_loop(0, width // 128, pair, 0)
    for place in range(2):
        columns = slice(place * half, (place + 1) * half)
        grads[place][0, :, :half] = gq[:, columns]
        grads[place][0, :, half:] = gk[:, columns]
        grads[place][1, :, :half] = gv[:, columns]
    copies[2].wait()
    copies[3].wait()
    total = dot_nt(grad_own[0], matrix(w_a, 0)) + dot_nt(grad_other[0], matrix(w_a, 1))
    total = total + dot_nt(grad_own[1, :, :half], matrix(w_b, 0, 0, half))
    total = total + dot_nt(grad_other[1, :, :half], matrix(w_b, 1, 0, half))
    _, unit, inverse = normalize(resid[...], gains[0:1], gains[1:2])
    back, gain, bias = normalize_back(total, unit, inverse, gains[0:1])
    back = grad_middle[...] + back
    grad[...] = back
    branch[...] = back.astype(LOW)
    grad_gains[0:1] = gain
    grad_gains[1:2] = bias


def attention_back(place, grad_middle, resid, weights, base, gains, cosine, sine, segments, query, keys, values, lse):
    length, width = resid.shape
    one = (length, width)
    outs = [(one, FULL), (one, LOW), ((2, width), FULL)] + [((2,) + one, LOW)] * 2
    ins = [grad_middle, resid, segments[:, None], segments[None, :], cosine, sine, gains]
    ins += [query, keys, values, lse.T[: width // HD]]
    return call(
        functools.partial(attention_back_kernel, base),
        place,
        outs,
        ins,
        [weights],
        [
            tile_scratch(2, weights),
            tile_scratch(2, weights),
            pltpu.VMEM((length, length), FULL),
        ]
        + [pltpu.VMEM(one, LOW)] * 4
        + [pltpu.SemaphoreType.DMA((4,))],
        8 * length * width * width + 10 * length * length * width,
    )


def adam_step(master, grad, first, second, rate, decay):
    first = BETA_ONE * first + (1.0 - BETA_ONE) * grad
    second = BETA_TWO * second + (1.0 - BETA_TWO) * grad * grad
    fix_one = 1.0 - BETA_ONE**STEP
    fix_two = 1.0 - BETA_TWO**STEP
    update = first / fix_one / (jnp.sqrt(second / fix_two) + ADAM_EPS) + decay * master
    return (master - rate * update, first, second)


def optimizer_kernel(chunks, layers, place_of, scale, *refs):
    n = (len(refs) - 25) // 2
    own, other, up, masters = refs[:n], refs[n : 2 * n], refs[2 * n], refs[2 * n + 1 : 2 * n + 13]
    outs = refs[2 * n + 13 :]
    first = place_of[0] == 0
    count, factor = scale[0], scale[1]

    def step(which, at, grad):
        master, moment, square = (masters[3 * which + i][at] for i in range(3))
        clipped = grad / count * factor
        values = adam_step(master, clipped, moment, square, RATE_MATRIX, DECAY)
        for i in range(3):
            outs[3 * which + i][at] = values[i]

    def tile(where, s, core):
        a, b = own[where[0]][where[1], s], other[where[0]][where[1], s]
        return jnp.where(first, a, b) if core == 0 else jnp.where(first, b, a)

    rows, width = own[0].shape[-2:]
    half = width // 2
    for l in range(layers):
        mixer, down = chunks[l]
        for core in range(2):
            columns = lambda p: pl.ds(p * width + core * half, half)
            value = tile(mixer, 0, core)
            step(0, (l, slice(None), columns(0)), value[:, :half])
            step(0, (l, slice(None), columns(1)), value[:, half:])
            value = tile(mixer, 1, core)
            step(0, (l, slice(None), columns(2)), value[:, :half])
            step(1, (l, slice(None), columns(0)), value[:, half:])
            for s in range(2):
                at = (l, pl.ds((2 * core + s) * rows, rows), slice(None))
                step(3, at, tile(down, s, core))
        step(2, l, up[l])


def optimizer(place, scale, chunks, own, other, up, masters):
    ins = list(own) + list(other) + [up] + list(masters)
    whole = pl.BlockSpec(memory_space=pltpu.VMEM)
    return pl.pallas_call(
        functools.partial(optimizer_kernel, chunks, up.shape[0]),
        out_shape=[jax.ShapeDtypeStruct(m.shape, m.dtype) for m in masters],
        in_specs=[pl.BlockSpec(memory_space=pltpu.SMEM)] * 2 + [whole] * len(ins),
        out_specs=[whole] * len(masters),
        compiler_params=pltpu.CompilerParams(vmem_limit_bytes=VMEM_LIMIT),
        cost_estimate=pl.CostEstimate(
            flops=20 * sum(m.size for m in masters),
            bytes_accessed=8 * sum(m.size for m in masters),
            transcendentals=0,
        ),
    )(place, scale, *ins)


def swap_cores(value):
    return lax.ppermute(value, "dp", [(0, 1), (1, 0)])


def across(value, mask, size):
    return lax.ppermute(value, "fsdp", [(i, i ^ mask) for i in range(size)])


def tie(*values):
    return lax.optimization_barrier(values)


def total_of(value, size):
    value = value + swap_cores(value)
    bit = 1
    while bit < size:
        if 2 * bit < size:
            a, b, c = (across(value, m * bit, size) for m in (1, 2, 3))
            value = (value + a) + (b + c)
        else:
            value = value + across(value, bit, size)
        bit *= 4
    return value


X, Y = 1, 2
Z = (4, 8, 12)


SMALL = 128


def round_kernel(jobs, small_job, n_ins, counts, smalls, last, *refs):
    new, once, twice, done = counts
    small_new, small_once, small_twice, small_done = smalls
    place_of, ins = refs[0], refs[1 : 1 + n_ins]
    rest = list(refs[1 + n_ins :])
    pop = lambda present, n=1: [rest.pop(0) for _ in range(n)] if present else [None] * n
    (keep_once,), (small_keep_once,) = pop(once), pop(small_once)
    (keep_twice,), (small_keep_twice,) = pop(twice), pop(small_twice)
    from_x, from_y = pop(once or twice, 2)
    (keep_done,), (small_keep_done,) = pop(done), pop(small_done)
    from_z = pop(done, 3)
    (squares_in,), (sums,) = pop(done), pop(last)
    to_x, to_y = pop(new or once, 2)
    (out_once,), (small_out_once,) = pop(new), pop(small_new)
    (out_twice,), (small_out_twice,) = pop(once), pop(small_once)
    (out_done,), (small_out_done,) = pop(twice), pop(small_twice)
    to_z = pop(twice, 3)
    (share,), (small_share,), (squares,) = pop(done), pop(small_done), pop(done)
    (totals,) = pop(last)
    (tile,), (small_tile,) = pop(new), pop(small_new)
    rows = (out_once if new else out_twice if once else out_done if twice else share).shape[-2]
    rows = rows // (8 if new else 4 if once else 1)
    bits, z = (place_of[1], place_of[2]), place_of[3]
    to, came = (to_x, to_y), (from_x, from_y)

    def block(index, size=rows):
        if isinstance(index, int):
            return pl.ds(index * size, size)
        return pl.ds(pl.multiple_of(index * size, 16), size)

    def factor(spec):
        which, index, low, high = spec
        ref = ins[which] if index is None else ins[which].at[index]
        return ref[...] if low is None else ref[:, low:high]

    def put_small(ref, start, group, side, value):
        for q in range(rows // 16):
            lanes = side * (rows // 16) + q
            ref[pl.ds(start + group * 16, 16), lanes * SMALL : (lanes + 1) * SMALL] = value[
                q * 16 : (q + 1) * 16
            ].astype(LOW)

    def take_small(ref, start, group, side):
        parts = []
        for q in range(rows // 16):
            lanes = side * (rows // 16) + q
            at = pl.ds(pl.multiple_of(start + group * 16, 16), 16)
            parts.append(ref[at, lanes * SMALL : (lanes + 1) * SMALL])
        return jnp.concatenate(parts, 0).astype(FULL)

    for p in range(new):
        for s in range(2):
            for low, high, products in jobs[2 * p + s]:
                total = None
                for left, right in products:
                    product = cross(factor(left), factor(right))
                    total = product if total is None else total + product
                tile[:, low:high] = total
            for zz in range(4):
                for other in range(2):
                    at = zz * 2 + other
                    index = lambda bit: zz * 4 + (other * 2 + bit if s == 0 else bit * 2 + other)
                    to[s][block(p * 8 + at), :] = tile[block(index(1 - bits[s])), :].astype(LOW)
                    out_once[p, s, block(at), :] = tile[block(index(bits[s])), :]
    if small_new:
        products, norms, norms_came = small_job
        total = None
        for left, right in products:
            product = cross(factor(left), factor(right))
            total = product if total is None else total + product
        norms = ins[norms][...] + ins[norms_came][...]
        high = norms.astype(LOW)
        shape = (norms.shape[0], SMALL)
        column = lax.broadcasted_iota(jnp.int32, shape, 1) - V
        pick = jnp.where(lax.broadcasted_iota(jnp.int32, shape, 0) == column, 1.0, 0.0).astype(LOW)
        total = total + (cross(high, pick) + cross((norms - high.astype(FULL)).astype(LOW), pick))
        small_tile[...] = total
        for zz in range(4):
            for other in range(2):
                index = lambda bit: zz * 4 + other * 2 + bit
                send = small_tile[block(index(1 - bits[0])), :]
                put_small(to_x, (new * 8 + once * 4) * rows, other * 2 + zz // 2, zz % 2, send)
                small_out_once[block(zz * 2 + other), :] = small_tile[block(index(bits[0])), :]
    for p in range(once):
        for s in range(2):
            for zz in range(4):
                for bit in range(2):
                    at = zz * 2 + (bits[1 - s] if bit else 1 - bits[1 - s])
                    value = keep_once[p, s, block(at), :] + came[s][block(p * 8 + at), :].astype(FULL)
                    if bit:
                        out_twice[p, s, block(zz), :] = value
                    else:
                        to[1 - s][block(new * 8 + p * 4 + zz), :] = value.astype(LOW)
    if small_once:
        start = (once * 8 + twice * 4) * rows
        for zz in range(4):
            for bit in range(2):
                other = bits[1] if bit else 1 - bits[1]
                value = small_keep_once[block(zz * 2 + other), :]
                value = value + take_small(from_x, start, other * 2 + zz // 2, zz % 2)
                if bit:
                    small_out_twice[block(zz), :] = value
                else:
                    put_small(to_y, (new * 8 + once * 4) * rows, zz, 0, value)
    for p in range(twice):
        for s in range(2):
            for xor in range(4):
                at = jnp.bitwise_xor(z, xor)
                value = keep_twice[p, s, block(at), :] + came[1 - s][
                    block(once * 8 + p * 4 + at), :
                ].astype(FULL)
                if xor == 0:
                    out_done[p, s] = value
                else:
                    to_z[xor - 1][block(2 * p + s), :] = value.astype(LOW)
    if small_twice:
        for xor in range(4):
            at = jnp.bitwise_xor(z, xor)
            value = small_keep_twice[block(at), :]
            value = value + take_small(from_y, (once * 8 + twice * 4) * rows, at, 0)
            if xor == 0:
                small_out_done[...] = value
            else:
                put_small(to_z[xor - 1], twice * 2 * rows, 0, 0, value)
    if done:
        squares[...] = squares_in[...]
    for p in range(done):
        for s in range(2):
            value = keep_done[p, s]
            for f in from_z:
                value = value + f[block(2 * p + s), :].astype(FULL)
            share[p, s] = value
            squares[...] += jnp.sum(value * value, 0, keepdims=True)
    if small_done:
        value = small_keep_done[...]
        for f in from_z:
            value = value + take_small(f, done * 2 * rows, 0, 0)
        small_share[...] = value
    if last:
        total = jnp.sum(squares[...], 1, keepdims=True)
        if small_done:
            square = jnp.sum(jnp.sum(value * value, 0, keepdims=True), 1, keepdims=True)
            total = total + jnp.where(place_of[0] == 0, square, jnp.zeros_like(square))
        lane = lax.broadcasted_iota(jnp.int32, sums.shape, 1)
        totals[...] = jnp.where(lane == 2, total, sums[...])


class Rounds:
    def __init__(self, place, rows, width, sums):
        self.place, self.rows, self.width, self.sums = place, rows, width, sums
        self.counts, self.smalls = (0,) * 4, (False,) * 4
        self.kept, self.small_kept = [None] * 3, [None] * 3
        self.came = self.came_z = self.totals = None
        self.shares, self.others, self.small_share = [], [], None
        self.squares = jnp.zeros((1, width), FULL)
        self.flying, self.swapping = [], 0

    def step(self, chunk, *ties, small=None):
        rows, width = self.rows, self.width
        new, once, twice, done = counts = (len(chunk),) + self.counts[:3]
        smalls = (small is not None,) + self.smalls[:3]
        last = not (new or once or twice)
        arrays, jobs = [], []

        def number(spec):
            array, *place = spec
            for i, known in enumerate(arrays):
                if known is array:
                    return (i, *place)
            arrays.append(array)
            return (len(arrays) - 1, *place)

        for pair in chunk:
            for tile in pair:
                jobs.append(
                    [(a, b, [(number(l), number(r)) for l, r in ps]) for a, b, ps in tile]
                )
        small_job = None
        if small is not None:
            products, norms, norms_came = small
            small_job = [(number(l), number(r)) for l, r in products]
            small_job = (small_job, number((norms,))[0], number((norms_came,))[0])
        ins = list(arrays)
        for stage in range(2):
            ins += [self.kept[stage]] * (counts[1 + stage] > 0)
            ins += [self.small_kept[stage]] * smalls[1 + stage]
        if once or twice:
            ins += self.came
        if done:
            ins += [self.kept[2]] + [self.small_kept[2]] * smalls[3] + self.came_z + [self.squares]
        ins += [self.sums] * last
        outs = []
        if new or once:
            for added in (64 * smalls[0], 64 * smalls[1]):
                outs.append((((new * 8 + once * 4) * rows + added, width), LOW))
        for stage, blocks in enumerate((8, 4, 1)):
            if counts[stage]:
                outs.append(((counts[stage], 2, blocks * rows, width), FULL))
            if smalls[stage]:
                outs.append(((blocks * rows, SMALL), FULL))
        if twice:
            outs += [((twice * 2 * rows + 16 * smalls[2], width), LOW)] * 3
        if done:
            outs.append(((done, 2, rows, width), FULL))
            outs += [((rows, SMALL), FULL)] * smalls[3]
            outs.append(((1, width), FULL))
        outs += [((1, SMALL), FULL)] * last
        length = 2 * arrays[0].shape[-2] if new else 0
        scratch = [pltpu.VMEM((16 * rows, width), FULL)] if new else []
        scratch += [pltpu.VMEM((16 * rows, SMALL), FULL)] * smalls[0]
        got = list(
            call(
                functools.partial(
                    round_kernel, jobs, small_job, len(arrays), counts, smalls, last
                ),
                self.place,
                outs,
                ins,
                [],
                scratch,
                4 * new * length * width * width,
            )
        )
        if last:
            self.totals = got.pop()
        if done:
            self.squares = got.pop()
            if smalls[3]:
                self.small_share = got.pop()
            self.shares.append(got.pop())
        self.counts, self.smalls = counts, smalls
        self.kept, self.small_kept = [None] * 3, [None] * 3
        if last:
            return ties
        got, ties = tie(got, ties)
        to = [got.pop(0) for _ in range(2)] if new or once else []
        for stage in range(3):
            if counts[stage]:
                self.kept[stage] = got.pop(0)
            if smalls[stage]:
                self.small_kept[stage] = got.pop(0)
        self.flying = [across(v, mask, 16) for v, mask in zip(to, (X, Y))]
        self.flying += [across(v, mask, 16) for v, mask in zip(got, Z)]
        self.swapping = 0
        while len(self.flying) < 5 and len(self.others) + self.swapping < len(self.shares):
            self.flying.append(swap_cores(self.shares[len(self.others) + self.swapping]))
            self.swapping += 1
        return ties

    def finish(self, *ties):
        flying, ties = tie(self.flying, ties)
        self.came = self.came_z = None
        if self.counts[0] or self.counts[1]:
            self.came, flying = flying[:2], flying[2:]
        if self.counts[2]:
            self.came_z, flying = flying[:3], flying[3:]
        self.others += flying
        return ties

    def left(self):
        return any(self.counts[:3])

    def swap_rest(self):
        self.others += [swap_cores(v) for v in self.shares[len(self.others) :]]


class PlainRounds:
    def __init__(self):
        self.shares, self.squares = [], []

    def step(self, chunk, *ties):
        def factor(spec):
            array, index, low, high = spec
            array = array if index is None else array[index]
            return array if low is None else array[:, low:high]

        def summed(tile):
            parts = [sum(cross(factor(l), factor(r)) for l, r in ps) for _, _, ps in tile]
            return lax.psum_scatter(
                jnp.concatenate(parts, 1), "fsdp", scatter_dimension=0, tiled=True
            )

        share = jnp.stack([jnp.stack([summed(tile) for tile in pair]) for pair in chunk])
        self.shares.append((share, swap_cores(share)))
        self.squares.append(jnp.sum(share * share, (0, 1, 2))[None])
        return ties

    def finish(self, *ties):
        return ties

    def left(self):
        return False


def up_to_parts(expand_shard, size, rows, parts):
    r = expand_shard.shape[0]
    return expand_shard.reshape(r, size, parts, rows).transpose(0, 2, 1, 3).reshape(r, -1)


def up_from_parts(expand_shard, size, rows, parts):
    r = expand_shard.shape[0]
    return expand_shard.reshape(r, parts, size, rows).transpose(0, 2, 1, 3).reshape(r, -1)


def half_of(value, core):
    half = value.shape[1] // 2
    return lax.dynamic_slice_in_dim(value, core * half, half, 1)


def body(
    fsdp,
    codons,
    masked,
    segments,
    inward,
    outward,
    expand,
    shrink,
    codon_table,
    norm_params,
    inward_first,
    inward_second,
    outward_first,
    outward_second,
    expand_first,
    expand_second,
    shrink_first,
    shrink_second,
    table_first,
    table_second,
    norm_first,
    norm_second,
):
    layers = inward.shape[0]
    length = codons.shape[0]
    rows = inward.shape[1]
    width = rows * fsdp
    half = width // 2
    parts = shrink.shape[1] // rows
    fast = fsdp == 16 and rows == 48
    core, index = lax.axis_index("dp"), lax.axis_index("fsdp")
    bit = lambda b: lax.rem(lax.div(index, b), 2)
    place = jnp.stack([core, bit(1), bit(2), lax.div(index, 4)]).astype(jnp.int32)
    weight = masked.astype(FULL)
    inputs = jnp.where(masked == 1, V - 1, codons)

    def tiles_of(l):
        w_in, w_out = inward[l].astype(LOW), outward[l].astype(LOW)
        pieces = [half_of(w_in[:, p * width : (p + 1) * width], core) for p in range(3)]
        pieces.append(half_of(w_out, core))
        mixer = [jnp.concatenate(pieces[:2], 1), jnp.concatenate(pieces[2:], 1)]
        up = half_of(up_to_parts(expand[l].astype(LOW), fsdp, rows, parts), core)
        down = lax.dynamic_slice_in_dim(shrink[l].astype(LOW), core * 2 * rows, 2 * rows, 0)
        return mixer + [up[:, :width], up[:, width:], down[:rows], down[rows:]]

    norms = norm_params.shape[0] * 2
    small = jnp.concatenate(
        [codon_table.astype(LOW), norm_params.astype(LOW).reshape(norms, rows)], 0
    )
    small = jnp.pad(small.T, ((0, 0), (0, -small.shape[0] % 128)))
    weights = jnp.concatenate([small] + sum([tiles_of(l) for l in range(layers)], []), 1)
    weights = lax.all_gather(weights, ("fsdp", "dp"), axis=0, tiled=True)
    weights = weights.reshape(fsdp, 2, rows, -1)
    if not fast:
        weights = weights.transpose(1, 0, 2, 3).reshape(1, 2, width, -1)
    small = weights[:, 0, :, : V + norms].reshape(width, V + norms).T
    base = lambda l: weights.shape[3] - (layers - l) * 6 * width
    table_low = small[:V]
    gains = small[V:].astype(FULL).reshape(-1, 2, width)

    cosine, sine = rotary_tables(length)
    vocab_ids = jnp.arange(V, dtype=jnp.int32)
    chosen = (inputs[:, None] == jnp.arange(SMALL, dtype=jnp.int32)[None, :]).astype(LOW)
    resid = dot(chosen, jnp.pad(table_low, ((0, SMALL - V), (0, 0))))
    kept = []
    for l in range(layers):
        gain = gains[2 * l : 2 * l + 2]
        middle, query, keys, values, lse, pack = attention_forward(
            place, resid, weights, base(l), gain[0], cosine, sine, segments
        )
        if l > 0:
            middle, came = tie(middle, kept[-1][-1])
            kept[-1] = kept[-1][:-1] + (came,)
        pack_came = swap_cores(pack)
        output, active, pack_mid, hidden = hidden_forward(
            place, middle, weights, base(l), gain[1]
        )
        output, pack_came = tie(output, pack_came)
        kept.append(
            (resid, query, keys, values, lse, pack, pack_came, middle, hidden, active, pack_mid)
            + (swap_cores(pack_mid),)
        )
        resid = output
    final_gain = gains[2 * layers]
    normed_out, unit_out, inverse_out = normalize(resid, final_gain[0], final_gain[1])
    head_in = normed_out.astype(LOW)
    logits = jnp.einsum("sd,vd->sv", head_in, table_low, preferred_element_type=FULL)
    top = jnp.max(logits, -1, keepdims=True)
    lse_head = top + jnp.log(jnp.sum(jnp.exp(logits - top), -1, keepdims=True))
    targets = (codons[:, None] == vocab_ids[None, :]).astype(FULL)
    picked = jnp.sum(logits * targets, -1)
    loss_local = jnp.sum((lse_head[:, 0] - picked) * weight)
    grad_logits = ((jnp.exp(logits - lse_head) - targets) * weight[:, None]).astype(LOW)
    grad_head = dot(grad_logits, table_low)
    grad_logits = jnp.pad(grad_logits, ((0, 0), (0, SMALL - V)))
    early = (head_in, grad_logits, chosen)
    early_came = [swap_cores(v) for v in early]
    sums = jnp.pad(jnp.stack([loss_local, jnp.sum(weight)]), (0, SMALL - 2))[None]
    grad, grad_final_gain, grad_final_bias = normalize_back(
        grad_head, unit_out, inverse_out, final_gain[0]
    )
    branch = grad.astype(LOW)
    grad_norms = [grad_final_gain, grad_final_bias]
    grad, branch, came = tie(grad, branch, kept[-1][-1])
    kept[-1] = kept[-1][:-1] + (came,)

    rounds = Rounds(place, rows, width, sums) if fast else PlainRounds()
    whole = lambda array, i=None: (array, i, None, None)
    tile = lambda left, right, other_left, other_right: [
        (0, width, [(left, right), (other_left, other_right)])
    ]
    chunk = []
    for l in reversed(range(layers)):
        (resid, query, keys, values, lse, pack, pack_came, middle, hidden, active, pack_mid, mid_came) = kept[l]
        gain = gains[2 * l : 2 * l + 2]
        branch_came = swap_cores(branch)
        chunk.append(
            [
                tile(
                    whole(active, s), whole(branch), whole(mid_came, 1 + s), whole(branch_came)
                )
                for s in range(2)
            ]
        )
        grad, branch = rounds.step(chunk, grad, branch)
        grad_middle, gains_mid, up_own, up_other = hidden_back(
            place, grad, branch, middle, hidden, weights, base(l), gain[1]
        )
        grad_middle, up_own, up_other, early_came = rounds.finish(
            grad_middle, up_own, up_other, early_came
        )
        up_came = swap_cores(up_other)
        (grad_middle,) = rounds.step(
            [
                [
                    tile(
                        whole(pack_mid, 0), whole(up_own, s), whole(mid_came, 0), whole(up_came, s)
                    )
                    for s in range(2)
                ]
            ],
            grad_middle,
        )
        grad, branch, gains_in, mix_own, mix_other = attention_back(
            place, grad_middle, resid, weights, base(l), gain[0], cosine, sine, segments,
            query, keys, values, lse,
        )
        grad_norms = [gains_in, gains_mid] + grad_norms
        grad, branch, mix_own, mix_other = rounds.finish(grad, branch, mix_own, mix_other)
        mix_came = swap_cores(mix_other)
        products = lambda i, a, b: [
            ((pack, i, None, None), (mix_own, 1, a, b)),
            ((pack_came, i, None, None), (mix_came, 1, a, b)),
        ]
        chunk = [
            [
                tile(whole(pack, 0), whole(mix_own, 0), whole(pack_came, 0), whole(mix_came, 0)),
                [(0, half, products(0, 0, half)), (half, width, products(1, half, width))],
            ]
        ]
    norm_rows = -(-norms // 16) * 16
    grad_norms = jnp.concatenate(grad_norms + [jnp.zeros((norm_rows - norms, width), FULL)], 0)
    branch_came, norms_came = swap_cores(branch), swap_cores(grad_norms)
    products = [(whole(early[0]), whole(early[1])), (whole(early_came[0]), whole(early_came[1]))]
    products += [(whole(branch), whole(early[2])), (whole(branch_came), whole(early_came[2]))]
    if fast:
        rounds.step(chunk, small=(products, grad_norms, norms_came))
        while rounds.left():
            rounds.finish()
            rounds.step([])
        rounds.swap_rest()
        share_small = rounds.small_share
        small_other = swap_cores(share_small)
        totals, rest = tie(rounds.totals, [rounds.others, small_other])
        share_small = jnp.where(core == 0, share_small, small_other)
    else:
        rounds.step(chunk)
        table = sum(cross(l[0], r[0]) for l, r in products)
        table = table + jnp.pad((grad_norms + norms_came).T, ((0, 0), (V, SMALL - V - norm_rows)))
        table = jnp.where(core == 0, table, swap_cores(table))
        share_small = lax.psum_scatter(table, "fsdp", scatter_dimension=0, tiled=True)
        squares = jnp.sum(share_small * share_small) * (core == 0)
        for value in rounds.squares:
            squares = squares + jnp.sum(value)
        totals = sums + jnp.where(jnp.arange(SMALL) == 2, squares, 0.0)[None]
    totals = total_of(totals, fsdp)
    loss_sum, count, square_total = totals[0, 0], totals[0, 1], totals[0, 2]
    share_small = share_small[:, : V + norms].T

    shares = list(zip(rounds.shares, rounds.others)) if fast else rounds.shares
    places = [(2 * (layers - 1 - l), 0 if l == layers - 1 else 1) for l in range(layers)]

    def tiles_at(chunk, pair):
        own, other = (v[pair] for v in shares[chunk])
        ordered = (jnp.where(core == 0, own, other), jnp.where(core == 0, other, own))
        return [v[s] for v in ordered for s in range(2)]

    share_up = jnp.stack(
        [
            up_from_parts(jnp.concatenate(tiles_at(at + 1, 0), 1), fsdp, rows, parts)
            for at, _ in places
        ]
    )
    share_small = (share_small[:V], share_small[V:].reshape(-1, 2, rows))
    if not fast:
        share_in, share_out, share_down = [], [], []
        side = lambda *values: jnp.concatenate(values, 1)
        for at, pair in places:
            a_0, b_0, a_1, b_1 = tiles_at(at + 2, 0)
            share_in.append(
                side(
                    a_0[:, :half], a_1[:, :half], a_0[:, half:],
                    a_1[:, half:], b_0[:, :half], b_1[:, :half],
                )
            )
            share_out.append(side(b_0[:, half:], b_1[:, half:]))
            share_down.append(jnp.concatenate(tiles_at(at, pair), 0))
        share_in, share_out, share_down = (
            jnp.stack(v) for v in (share_in, share_out, share_down)
        )
    grad_norm = jnp.sqrt(square_total) / count
    factor = CLIP / jnp.maximum(grad_norm, CLIP)
    masters = (inward, outward, expand, shrink, codon_table, norm_params)
    firsts = (inward_first, outward_first, expand_first, shrink_first, table_first, norm_first)
    seconds = (
        inward_second,
        outward_second,
        expand_second,
        shrink_second,
        table_second,
        norm_second,
    )
    if fast:
        matrices = [v for group in zip(masters[:4], firsts[:4], seconds[:4]) for v in group]
        chunks = [((at + 2, 0), (at, pair)) for at, pair in places]
        own, other = zip(*shares)
        scale = jnp.stack([count, factor])
        values = list(optimizer(place, scale, chunks, own, other, share_up, matrices))
    else:
        values = []
        for index, grad in enumerate((share_in, share_out, share_up, share_down)):
            clipped = grad / count * factor
            values.extend(
                adam_step(
                    masters[index], clipped, firsts[index], seconds[index], RATE_MATRIX, DECAY
                )
            )
    for index, rate, decay in ((4, RATE_MATRIX, DECAY), (5, RATE_VECTOR, 0.0)):
        clipped = share_small[index - 4] / count * factor
        values.extend(
            adam_step(masters[index], clipped, firsts[index], seconds[index], rate, decay)
        )
    return (loss_sum, count, grad_norm, *values)


def solution(mesh):
    in_specs = (
        P(("fsdp", "dp")),
        P(("fsdp", "dp")),
        P(("fsdp", "dp")),
        P(None, "fsdp", None),
        P(None, "fsdp", None),
        P(None, "fsdp", None),
        P(None, "fsdp", None),
        P(None, "fsdp"),
        P(None, None, "fsdp"),
        P(None, "fsdp", None),
        P(None, "fsdp", None),
        P(None, "fsdp", None),
        P(None, "fsdp", None),
        P(None, "fsdp", None),
        P(None, "fsdp", None),
        P(None, "fsdp", None),
        P(None, "fsdp", None),
        P(None, "fsdp"),
        P(None, "fsdp"),
        P(None, None, "fsdp"),
        P(None, None, "fsdp"),
    )
    out_specs = (
        P(),
        P(),
        P(),
        P(None, "fsdp", None),
        P(None, "fsdp", None),
        P(None, "fsdp", None),
        P(None, "fsdp", None),
        P(None, "fsdp", None),
        P(None, "fsdp", None),
        P(None, "fsdp", None),
        P(None, "fsdp", None),
        P(None, "fsdp", None),
        P(None, "fsdp", None),
        P(None, "fsdp", None),
        P(None, "fsdp", None),
        P(None, "fsdp"),
        P(None, "fsdp"),
        P(None, "fsdp"),
        P(None, None, "fsdp"),
        P(None, None, "fsdp"),
        P(None, None, "fsdp"),
    )
    step = functools.partial(body, mesh.shape["fsdp"])
    return jax.shard_map(step, mesh=mesh, in_specs=in_specs, out_specs=out_specs, check_vma=False)
```

```python
import functools

import jax
import jax.numpy as jnp
from jax import lax
from jax.experimental import pallas as pl
from jax.experimental.pallas import tpu as pltpu
from jax.sharding import PartitionSpec as P

HD = 64
V = 70
STEP = 10


NORM_EPS = 1e-05
BETA_ONE = 0.9
BETA_TWO = 0.95
ADAM_EPS = 1e-08
DECAY = 0.1
RATE_MATRIX = 0.05
RATE_VECTOR = 0.3
CLIP = 0.05


def rotary_tables(length):
    freq = 10000.0 ** (-jnp.arange(HD // 2, dtype=jnp.float32) * 2.0 / HD)
    angle = jnp.arange(length, dtype=jnp.float32)[:, None] * freq[None, :]
    cosine, sine = jnp.cos(angle), jnp.sin(angle)
    return (
        jnp.concatenate([cosine] * 4, 1),
        jnp.concatenate([-sine, sine] * 2, 1),
    )


def normalize(resid, gain, bias):
    mean = jnp.mean(resid, -1, keepdims=True)
    centred = resid - mean
    inverse = lax.rsqrt(jnp.mean(centred * centred, -1, keepdims=True) + NORM_EPS)
    unit = centred * inverse
    return (unit * gain + bias, unit, inverse)


def normalize_back(grad, unit, inverse, gain):
    scaled = grad * gain
    across = (
        scaled
        - jnp.mean(scaled, -1, keepdims=True)
        - unit * jnp.mean(scaled * unit, -1, keepdims=True)
    )
    return (across * inverse, jnp.sum(grad * unit, 0, keepdims=True), jnp.sum(grad, 0, keepdims=True))


def dot(left, right):
    return jnp.dot(left, right, preferred_element_type=jnp.float32)


def dot_nt(left, right):
    return lax.dot_general(
        left, right, (((1,), (1,)), ((), ())), preferred_element_type=jnp.float32
    )


def cross(left, right):
    return lax.dot_general(
        left, right, (((0,), (0,)), ((), ())), preferred_element_type=jnp.float32
    )


VMEM_LIMIT = 56 * 1024 * 1024
LOW, FULL = jnp.bfloat16, jnp.float32


class Lazy:
    def __init__(self, source, target, sem):
        self.copy = pltpu.make_async_copy(source, target, sem)
        self.copy.start()
        self.here, self.shape = target, target.shape

    def ready(self):
        if self.copy is not None:
            self.copy.wait()
            self.copy = None
        return self.here

    def __getitem__(self, at):
        return self.ready()[at]

    @property
    def at(self):
        return self.ready().at


class Sent:
    def __init__(self, here, there, sems):
        self.here, self.there, self.sems = here, there, sems
        self.shape, self.at = here.shape, here.at
        self.copies = []

    def __getitem__(self, at):
        return self.here[at]

    def __setitem__(self, at, value):
        self.here[at] = value

    def send(self, index=None):
        here, there = self.here, self.there
        if index is not None:
            here, there = here.at[index], there.at[index]
        copy = pltpu.make_async_copy(here, there, self.sems.at[len(self.copies)])
        copy.start()
        self.copies.append(copy)


def ready(*inputs):
    for value in inputs:
        if isinstance(value, Lazy):
            value.ready()


def call(kernel, scalars, outs, ins, anys=(), scratch=(), flops=0, sent=()):
    whole = pl.BlockSpec(memory_space=pltpu.VMEM)
    left = pl.BlockSpec(memory_space=pl.ANY)
    large = [x.size >= 1 << 16 for x in ins]
    buffers = [pltpu.VMEM(x.shape, x.dtype) for x, lazy in zip(ins, large) if lazy]
    buffers += [pltpu.VMEM(*outs[i]) for i in sent]

    def body(scalars, *refs):
        refs = list(refs)
        take = lambda n: [refs.pop(0) for _ in range(n)]
        sources, any_refs, out_refs = take(len(ins)), take(len(anys)), take(len(outs))
        here, here_out = take(sum(large)), take(len(sent))
        extra, (sems, out_sems) = refs[:-2], refs[-2:]
        values = []
        for source, lazy in zip(sources, large):
            at = sum(isinstance(v, Lazy) for v in values)
            values.append(Lazy(source, here[at], sems.at[at]) if lazy else source)
        for n, i in enumerate(sent):
            out_refs[i] = Sent(here_out[n], out_refs[i], out_sems.at[n])
        kernel(scalars, values, any_refs, out_refs, *extra)
        ready(*values)
        for i in sent:
            for copy in out_refs[i].copies:
                copy.wait()

    return pl.pallas_call(
        body,
        out_shape=[jax.ShapeDtypeStruct(s, t) for s, t in outs],
        in_specs=[pl.BlockSpec(memory_space=pltpu.SMEM)]
        + [left if lazy else whole for lazy in large]
        + [left] * len(anys),
        out_specs=[left if i in sent else whole for i in range(len(outs))],
        scratch_shapes=buffers
        + list(scratch)
        + [
            pltpu.SemaphoreType.DMA((max(sum(large), 1),)),
            pltpu.SemaphoreType.DMA((max(len(sent), 1), 4)),
        ],
        compiler_params=pltpu.CompilerParams(vmem_limit_bytes=VMEM_LIMIT),
        cost_estimate=pl.CostEstimate(
            flops=flops,
            bytes_accessed=sum(x.size * x.dtype.itemsize for x in list(ins) + list(anys)),
            transcendentals=0,
        ),
    )(scalars, *ins, *anys)


def fetch(sources, targets, sems):
    copies = [
        pltpu.make_async_copy(s, t, sems.at[i]) for i, (s, t) in enumerate(zip(sources, targets))
    ]
    for c in copies:
        c.start()
    return copies


def tile_of(ref, core, at):
    return ref.at[:, core, :, at : at + ref.shape[0] * ref.shape[2]]


def matrix(ref, place, low=None, high=None):
    value = ref[place] if low is None else ref[place, :, :, low:high]
    return value.reshape(-1, value.shape[-1])


def tile_scratch(count, weights):
    blocks, _, rows, _ = weights.shape
    return pltpu.VMEM((count, blocks, rows, blocks * rows), LOW)


def swap_halves(value):
    lane = lax.broadcasted_iota(jnp.int32, value.shape, 1)
    return jnp.where(
        lax.rem(lane, HD) < HD // 2,
        pltpu.roll(value, 128 - HD // 2, 1),
        pltpu.roll(value, HD // 2, 1),
    )


def ordered(first, own, other):
    return jnp.concatenate([jnp.where(first, own, other), jnp.where(first, other, own)], 1)


def head_mask(shape, head):
    lane = lax.broadcasted_iota(jnp.int32, shape, 1)
    return (lane < HD) if head == 0 else (lane >= HD)


def attention_forward_kernel(base, place_of, ins, anys, outs, w_a, w_b, mixed, bias, sems):
    resid, seg_col, seg_row, cosine, sine, gains = ins
    middle, query, keys, values, lse, pack = outs
    (weights,) = anys
    width = resid.shape[1]
    half = width // 2
    cores = (place_of[0], 1 - place_of[0])
    copies = fetch(
        [tile_of(weights, c, base + t * width) for t in range(2) for c in cores],
        [w.at[place] for w in (w_a, w_b) for place in range(2)],
        sems,
    )
    first = place_of[0] == 0
    normed, _, _ = normalize(resid[...], gains[0:1], gains[1:2])
    normed_low, attended = pack.at[0], pack.at[1]
    normed_low[...] = normed.astype(LOW)
    pack.send(0)
    bias[...] = jnp.where(seg_col[...] == seg_row[...], 0.0, -1000000000.0)
    for place in range(2):
        copies[place].wait()
        mixed[...] = dot(normed_low[...], matrix(w_a, place))
        for p in range(half // 128):
            for part, target, scale in ((0, query, HD ** (-0.5)), (1, keys, 1.0)):
                x = mixed[:, part * half + p * 128 : part * half + (p + 1) * 128]
                x = x * cosine[...] + swap_halves(x) * sine[...]
                x = (x * scale if scale != 1.0 else x).astype(LOW)
                target[:, place * half + p * 128 : place * half + (p + 1) * 128] = x
    query.send()
    keys.send()
    for place in range(2):
        copies[2 + place].wait()
        values[:, place * half : (place + 1) * half] = dot(
            normed_low[...], matrix(w_b, place, 0, half)
        ).astype(LOW)
    values.send()

    lse[...] = jnp.zeros_like(lse)

    def pair(p, _):
        columns = pl.ds(pl.multiple_of(p * 128, 128), 128)
        q, k, v = query[:, columns], keys[:, columns], values[:, columns]
        out = []
        for head in range(2):
            masked_q = jnp.where(head_mask(q.shape, head), q, jnp.zeros_like(q))
            scores = dot_nt(masked_q, k) + bias[...]
            top = jnp.max(scores, -1, keepdims=True)
            expo = jnp.exp(scores - top)
            total = jnp.sum(expo, -1, keepdims=True)
            probs = (expo * (1.0 / total)).astype(LOW)
            out.append(dot(probs, v))
            lane = lax.broadcasted_iota(jnp.int32, lse.shape, 1)
            lse[...] = jnp.where(lane == 2 * p + head, top + jnp.log(total), lse[...])
        attended[:, columns] = jnp.where(head_mask(out[0].shape, 0), out[0], out[1]).astype(LOW)
        return 0

    lax.fori_loop(0, width // 128, pair, 0)
    attended[...] = ordered(first, attended[:, :half], attended[:, half:])
    pack.send(1)
    out = ordered(
        first,
        dot(attended[...], matrix(w_b, 0, half, width)),
        dot(attended[...], matrix(w_b, 1, half, width)),
    )
    middle[...] = resid[...] + out


def attention_forward(place, resid, weights, base, gains, cosine, sine, segments):
    length, width = resid.shape
    one = (length, width)
    return call(
        functools.partial(attention_forward_kernel, base),
        place,
        [(one, FULL)] + [(one, LOW)] * 3 + [((length, 128), FULL), ((2,) + one, LOW)],
        [resid, segments[:, None], segments[None, :], cosine, sine, gains],
        [weights],
        [
            tile_scratch(2, weights),
            tile_scratch(2, weights),
            pltpu.VMEM(one, FULL),
            pltpu.VMEM((length, length), FULL),
            pltpu.SemaphoreType.DMA((4,)),
        ],
        8 * length * width * width + 4 * length * length * width,
        sent=(1, 2, 3, 5),
    )


GELU_SCALE = 0.7978845608028654
GELU_CUBE = 0.044715


def hidden_tiles(weights, core, base, width):
    tiles = [
        [tile_of(weights, c, base + t * width) for c in (core, 1 - core) for t in pair]
        for pair in ((2, 3), (4, 5))
    ]
    return tiles[0], tiles[1]


def hidden_forward_kernel(base, place_of, ins, anys, outs, ups, downs, sems):
    middle, gains = ins
    output, active, pack, hidden = outs
    u, d = hidden_tiles(anys[0], place_of[0], base, middle.shape[1])
    copies = fetch(
        [r for t in range(4) for r in (u[t], d[t])],
        [w.at[t] for t in range(4) for w in (ups, downs)],
        sems,
    )
    normed, _, _ = normalize(middle[...], gains[0:1], gains[1:2])
    pack[0] = normed.astype(LOW)
    pack.send(0)
    for t in range(4):
        copies[2 * t].wait()
        x = dot(pack[0], matrix(ups, t))
        hidden[t] = x
        hidden.send(t)
        inner = jnp.tanh(x * (GELU_SCALE + (GELU_SCALE * GELU_CUBE) * (x * x)))
        value = x * 0.5
        value = (value + value * inner).astype(LOW)
        target, at = (active, t) if t < 2 else (pack, t - 1)
        target[at] = value
        target.send(at)
        copies[2 * t + 1].wait()
        product = dot(value, matrix(downs, t))
        output[...] = (middle[...] if t == 0 else output[...]) + product


def hidden_forward(place, middle, weights, base, gains):
    length, width = middle.shape
    one = (length, width)
    return call(
        functools.partial(hidden_forward_kernel, base),
        place,
        [(one, FULL), ((2,) + one, LOW), ((3,) + one, LOW), ((4,) + one, FULL)],
        [middle, gains],
        [weights],
        [
            tile_scratch(4, weights),
            tile_scratch(4, weights),
            pltpu.SemaphoreType.DMA((8,)),
        ],
        16 * length * width * width,
        sent=(1, 2, 3),
    )


def hidden_back_kernel(base, place_of, ins, anys, outs, ups, downs, hidden_here, total, sems):
    branch, grad, middle, gains = ins
    hidden, weights = anys
    grad_middle, grad_gains, grad_own, grad_other = outs
    u, d = hidden_tiles(weights, place_of[0], base, middle.shape[1])
    copies = fetch(
        [r for t in range(4) for r in (d[t], hidden.at[t], u[t])],
        [w.at[t] for t in range(4) for w in (downs, hidden_here, ups)],
        sems,
    )
    for t in range(4):
        copies[3 * t].wait()
        grad_active = dot_nt(branch[...], matrix(downs, t))
        copies[3 * t + 1].wait()
        x = hidden_here[t]
        square = x * x
        inner = jnp.tanh(x * (GELU_SCALE + (GELU_SCALE * GELU_CUBE) * square))
        slope = x * (GELU_SCALE + (3.0 * GELU_SCALE * GELU_CUBE) * square)
        slope = (0.5 + 0.5 * inner) * (1.0 + slope * (1.0 - inner))
        value = (grad_active * slope).astype(LOW)
        target = grad_own if t < 2 else grad_other
        target[t % 2] = value
        target.send(t % 2)
        copies[3 * t + 2].wait()
        product = dot_nt(value, matrix(ups, t))
        total[...] = product if t == 0 else total[...] + product
    _, unit, inverse = normalize(middle[...], gains[0:1], gains[1:2])
    back, gain, bias = normalize_back(total[...], unit, inverse, gains[0:1])
    grad_middle[...] = grad[...] + back
    grad_gains[0:1] = gain
    grad_gains[1:2] = bias


def hidden_back(place, grad, branch, middle, hidden, weights, base, gains):
    length, width = middle.shape
    one = (length, width)
    return call(
        functools.partial(hidden_back_kernel, base),
        place,
        [(one, FULL), ((2, width), FULL), ((2,) + one, LOW), ((2,) + one, LOW)],
        [branch, grad, middle, gains],
        [hidden, weights],
        [
            tile_scratch(4, weights),
            tile_scratch(4, weights),
            pltpu.VMEM((4,) + one, FULL),
            pltpu.VMEM(one, FULL),
            pltpu.SemaphoreType.DMA((12,)),
        ],
        16 * length * width * width,
        sent=(2, 3),
    )


def attention_back_kernel(base, place_of, ins, anys, outs, w_a, w_b, bias, ga, gq, gk, gv, sems):
    grad_middle, query, keys, values, lse, seg_col, seg_row, cosine, sine, gains, resid = ins
    (weights,) = anys
    grad, branch, grad_gains, grad_own, grad_other = outs
    width = resid.shape[1]
    half = width // 2
    cores = (place_of[0], 1 - place_of[0])
    copies = fetch(
        [tile_of(weights, c, base + t * width) for t in (1, 0) for c in cores],
        [w.at[place] for w in (w_b, w_a) for place in range(2)],
        sems,
    )
    first = place_of[0] == 0
    grads = (grad_own, grad_other)
    bias[...] = jnp.where(seg_col[...] == seg_row[...], 0.0, -1000000000.0)
    attn_grad = grad_middle[...].astype(LOW)
    left, right = attn_grad[:, :half], attn_grad[:, half:]
    grad_own[1, :, half:] = jnp.where(first, left, right)
    grad_other[1, :, half:] = jnp.where(first, right, left)
    copies[0].wait()
    copies[1].wait()
    natural = dot_nt(grad_own[1, :, half:], matrix(w_b, 0, half, width)) + dot_nt(
        grad_other[1, :, half:], matrix(w_b, 1, half, width)
    )
    natural = natural.astype(LOW)
    ga[:, :half] = jnp.where(first, natural[:, :half], natural[:, half:])
    ga[:, half:] = jnp.where(first, natural[:, half:], natural[:, :half])
    ready(query, keys, values, lse, cosine, sine)

    def pair(p, _):
        columns = pl.ds(pl.multiple_of(p * 128, 128), 128)
        q, k, v, g = query[:, columns], keys[:, columns], values[:, columns], ga[:, columns]
        out_q, out_k, out_v = [], [], []
        for head in range(2):
            mask = head_mask(q.shape, head)
            zero = jnp.zeros_like(q)
            scores = dot_nt(k, jnp.where(mask, q, zero)) + bias[...]
            probs = jnp.exp(scores - lse[pl.ds(2 * p + head, 1), :])
            grad_probs = dot_nt(v, jnp.where(mask, g, zero))
            across = jnp.sum(probs * grad_probs, 0, keepdims=True)
            grad_scores = (probs * (grad_probs - across)).astype(LOW)
            out_k.append(dot(grad_scores, q))
            out_q.append(cross(grad_scores, k))
            out_v.append(dot(probs.astype(LOW), g))
        for out, target, scale in ((out_q, gq, HD ** (-0.5)), (out_k, gk, 1.0)):
            x = jnp.where(head_mask(out[0].shape, 0), out[0], out[1])
            x = x * scale if scale != 1.0 else x
            x = x * cosine[...] - swap_halves(x) * sine[...]
            target[:, columns] = x.astype(LOW)
        gv[:, columns] = jnp.where(head_mask(out_v[0].shape, 0), out_v[0], out_v[1]).astype(LOW)
        return 0

    lax.fori_loop(0, width // 128, pair, 0)
    for place in (1, 0):
        columns = slice(place * half, (place + 1) * half)
        grads[place][0, :, :half] = gq[:, columns]
        grads[place][0, :, half:] = gk[:, columns]
        grads[place][1, :, :half] = gv[:, columns]
        grads[place].send()
    copies[2].wait()
    copies[3].wait()
    total = dot_nt(grad_own[0], matrix(w_a, 0)) + dot_nt(grad_other[0], matrix(w_a, 1))
    total = total + dot_nt(grad_own[1, :, :half], matrix(w_b, 0, 0, half))
    total = total + dot_nt(grad_other[1, :, :half], matrix(w_b, 1, 0, half))
    _, unit, inverse = normalize(resid[...], gains[0:1], gains[1:2])
    back, gain, bias_grad = normalize_back(total, unit, inverse, gains[0:1])
    back = grad_middle[...] + back
    grad[...] = back
    branch[...] = back.astype(LOW)
    grad_gains[0:1] = gain
    grad_gains[1:2] = bias_grad


def attention_back(place, grad_middle, resid, weights, base, gains, cosine, sine, segments, query, keys, values, lse):
    length, width = resid.shape
    one = (length, width)
    return call(
        functools.partial(attention_back_kernel, base),
        place,
        [(one, FULL), (one, LOW), ((2, width), FULL)] + [((2,) + one, LOW)] * 2,
        [grad_middle, query, keys, values, lse.T[: width // HD]]
        + [segments[:, None], segments[None, :], cosine, sine, gains, resid],
        [weights],
        [
            tile_scratch(2, weights),
            tile_scratch(2, weights),
            pltpu.VMEM((length, length), FULL),
        ]
        + [pltpu.VMEM(one, LOW)] * 4
        + [pltpu.SemaphoreType.DMA((4,))],
        8 * length * width * width + 10 * length * length * width,
        sent=(3, 4),
    )


def adam_step(master, grad, first, second, rate, decay):
    first = BETA_ONE * first + (1.0 - BETA_ONE) * grad
    second = BETA_TWO * second + (1.0 - BETA_TWO) * grad * grad
    fix_one = 1.0 - BETA_ONE**STEP
    fix_two = 1.0 - BETA_TWO**STEP
    update = first / fix_one / (jnp.sqrt(second / fix_two) + ADAM_EPS) + decay * master
    return (master - rate * update, first, second)


def optimizer_kernel(chunks, layers, place_of, scale, *refs):
    n = (len(refs) - 25) // 2
    own, other, up, masters = refs[:n], refs[n : 2 * n], refs[2 * n], refs[2 * n + 1 : 2 * n + 13]
    outs = refs[2 * n + 13 :]
    first = place_of[0] == 0
    count, factor = scale[0], scale[1]

    def step(which, at, grad):
        master, moment, square = (masters[3 * which + i][at] for i in range(3))
        clipped = grad / count * factor
        values = adam_step(master, clipped, moment, square, RATE_MATRIX, DECAY)
        for i in range(3):
            outs[3 * which + i][at] = values[i]

    def tile(where, s, core):
        a, b = own[where[0]][where[1], s], other[where[0]][where[1], s]
        return jnp.where(first, a, b) if core == 0 else jnp.where(first, b, a)

    rows, width = own[0].shape[-2:]
    half = width // 2
    for l in range(layers):
        mixer, down = chunks[l]
        for core in range(2):
            columns = lambda p: pl.ds(p * width + core * half, half)
            value = tile(mixer, 0, core)
            step(0, (l, slice(None), columns(0)), value[:, :half])
            step(0, (l, slice(None), columns(1)), value[:, half:])
            value = tile(mixer, 1, core)
            step(0, (l, slice(None), columns(2)), value[:, :half])
            step(1, (l, slice(None), columns(0)), value[:, half:])
            for s in range(2):
                at = (l, pl.ds((2 * core + s) * rows, rows), slice(None))
                step(3, at, tile(down, s, core))
        step(2, l, up[l])


def optimizer(place, scale, chunks, own, other, up, masters):
    ins = list(own) + list(other) + [up] + list(masters)
    whole = pl.BlockSpec(memory_space=pltpu.VMEM)
    return pl.pallas_call(
        functools.partial(optimizer_kernel, chunks, up.shape[0]),
        out_shape=[jax.ShapeDtypeStruct(m.shape, m.dtype) for m in masters],
        in_specs=[pl.BlockSpec(memory_space=pltpu.SMEM)] * 2 + [whole] * len(ins),
        out_specs=[whole] * len(masters),
        compiler_params=pltpu.CompilerParams(vmem_limit_bytes=VMEM_LIMIT),
        cost_estimate=pl.CostEstimate(
            flops=20 * sum(m.size for m in masters),
            bytes_accessed=8 * sum(m.size for m in masters),
            transcendentals=0,
        ),
    )(place, scale, *ins)


def swap_cores(value):
    return lax.ppermute(value, "dp", [(0, 1), (1, 0)])


def across(value, mask, size):
    return lax.ppermute(value, "fsdp", [(i, i ^ mask) for i in range(size)])


def tie(*values):
    return lax.optimization_barrier(values)


def total_of(value, size):
    value = value + swap_cores(value)
    bit = 1
    while bit < size:
        if 2 * bit < size:
            a, b, c = (across(value, m * bit, size) for m in (1, 2, 3))
            value = (value + a) + (b + c)
        else:
            value = value + across(value, bit, size)
        bit *= 4
    return value


X, Y = 1, 2
Z = (4, 8, 12)


SMALL = 128


def round_kernel(jobs, small_job, n_ins, counts, smalls, last, place_of, ins, anys, outs, *scratch):
    new, once, twice, done = counts
    small_new, small_once, small_twice, small_done = smalls
    rest = list(ins[n_ins:]) + list(outs) + list(scratch)
    pop = lambda present, n=1: [rest.pop(0) for _ in range(n)] if present else [None] * n
    (keep_once,), (small_keep_once,) = pop(once), pop(small_once)
    (keep_twice,), (small_keep_twice,) = pop(twice), pop(small_twice)
    from_x, from_y = pop(once or twice, 2)
    (keep_done,), (small_keep_done,) = pop(done), pop(small_done)
    from_z = pop(done, 3)
    (squares_in,), (sums,) = pop(done), pop(last)
    to_x, to_y = pop(new or once, 2)
    (out_once,), (small_out_once,) = pop(new), pop(small_new)
    (out_twice,), (small_out_twice,) = pop(once), pop(small_once)
    (out_done,), (small_out_done,) = pop(twice), pop(small_twice)
    to_z = pop(twice, 3)
    (share,), (small_share,), (squares,) = pop(done), pop(small_done), pop(done)
    (totals,) = pop(last)
    (tile,), (small_tile,) = pop(new), pop(small_new)
    rows = (out_once if new else out_twice if once else out_done if twice else share).shape[-2]
    rows = rows // (8 if new else 4 if once else 1)
    bits, z = (place_of[1], place_of[2]), place_of[3]
    to, came = (to_x, to_y), (from_x, from_y)

    def block(index, size=rows):
        if isinstance(index, int):
            return pl.ds(index * size, size)
        return pl.ds(pl.multiple_of(index * size, 16), size)

    def factor(spec):
        which, index, low, high = spec
        ref = ins[which] if index is None else ins[which].at[index]
        return ref[...] if low is None else ref[:, low:high]

    def put_small(ref, start, group, side, value):
        for q in range(rows // 16):
            lanes = side * (rows // 16) + q
            ref[pl.ds(start + group * 16, 16), lanes * SMALL : (lanes + 1) * SMALL] = value[
                q * 16 : (q + 1) * 16
            ].astype(LOW)

    def take_small(ref, start, group, side):
        parts = []
        for q in range(rows // 16):
            lanes = side * (rows // 16) + q
            at = pl.ds(pl.multiple_of(start + group * 16, 16), 16)
            parts.append(ref[at, lanes * SMALL : (lanes + 1) * SMALL])
        return jnp.concatenate(parts, 0).astype(FULL)

    for p in range(new):
        for s in range(2):
            for low, high, products in jobs[2 * p + s]:
                total = None
                for left, right in products:
                    product = cross(factor(left), factor(right))
                    total = product if total is None else total + product
                tile[:, low:high] = total
            for zz in range(4):
                for other in range(2):
                    at = zz * 2 + other
                    index = lambda bit: zz * 4 + (other * 2 + bit if s == 0 else bit * 2 + other)
                    to[s][block(p * 8 + at), :] = tile[block(index(1 - bits[s])), :].astype(LOW)
                    out_once[p, s, block(at), :] = tile[block(index(bits[s])), :]
    if small_new:
        products, norms_at = small_job
        total = None
        for left, right in products:
            product = cross(factor(left), factor(right))
            total = product if total is None else total + product
        norms = jnp.concatenate([ins[mine][...] + ins[theirs][...] for mine, theirs in norms_at], 0)
        high = norms.astype(LOW)
        shape = (norms.shape[0], SMALL)
        column = lax.broadcasted_iota(jnp.int32, shape, 1) - V
        pick = jnp.where(lax.broadcasted_iota(jnp.int32, shape, 0) == column, 1.0, 0.0).astype(LOW)
        total = total + (cross(high, pick) + cross((norms - high.astype(FULL)).astype(LOW), pick))
        small_tile[...] = total
        for zz in range(4):
            for other in range(2):
                index = lambda bit: zz * 4 + other * 2 + bit
                send = small_tile[block(index(1 - bits[0])), :]
                put_small(to_x, (new * 8 + once * 4) * rows, other * 2 + zz // 2, zz % 2, send)
                small_out_once[block(zz * 2 + other), :] = small_tile[block(index(bits[0])), :]
    for p in range(once):
        for s in range(2):
            for zz in range(4):
                for bit in range(2):
                    at = zz * 2 + (bits[1 - s] if bit else 1 - bits[1 - s])
                    value = keep_once[p, s, block(at), :] + came[s][block(p * 8 + at), :].astype(FULL)
                    if bit:
                        out_twice[p, s, block(zz), :] = value
                    else:
                        to[1 - s][block(new * 8 + p * 4 + zz), :] = value.astype(LOW)
    if small_once:
        start = (once * 8 + twice * 4) * rows
        for zz in range(4):
            for bit in range(2):
                other = bits[1] if bit else 1 - bits[1]
                value = small_keep_once[block(zz * 2 + other), :]
                value = value + take_small(from_x, start, other * 2 + zz // 2, zz % 2)
                if bit:
                    small_out_twice[block(zz), :] = value
                else:
                    put_small(to_y, (new * 8 + once * 4) * rows, zz, 0, value)
    for p in range(twice):
        for s in range(2):
            for xor in range(4):
                at = jnp.bitwise_xor(z, xor)
                value = keep_twice[p, s, block(at), :] + came[1 - s][
                    block(once * 8 + p * 4 + at), :
                ].astype(FULL)
                if xor == 0:
                    out_done[p, s] = value
                else:
                    to_z[xor - 1][block(2 * p + s), :] = value.astype(LOW)
    if small_twice:
        for xor in range(4):
            at = jnp.bitwise_xor(z, xor)
            value = small_keep_twice[block(at), :]
            value = value + take_small(from_y, (once * 8 + twice * 4) * rows, at, 0)
            if xor == 0:
                small_out_done[...] = value
            else:
                put_small(to_z[xor - 1], twice * 2 * rows, 0, 0, value)
    if done:
        squares[...] = squares_in[...]
    for p in range(done):
        for s in range(2):
            value = keep_done[p, s]
            for f in from_z:
                value = value + f[block(2 * p + s), :].astype(FULL)
            share[p, s] = value
            squares[...] += jnp.sum(value * value, 0, keepdims=True)
    if small_done:
        value = small_keep_done[...]
        for f in from_z:
            value = value + take_small(f, done * 2 * rows, 0, 0)
        small_share[...] = value
    if last:
        total = jnp.sum(squares[...], 1, keepdims=True)
        if small_done:
            square = jnp.sum(jnp.sum(value * value, 0, keepdims=True), 1, keepdims=True)
            total = total + jnp.where(place_of[0] == 0, square, jnp.zeros_like(square))
        lane = lax.broadcasted_iota(jnp.int32, sums.shape, 1)
        totals[...] = jnp.where(lane == 2, total, sums[...])


class Rounds:
    def __init__(self, place, rows, width, sums):
        self.place, self.rows, self.width, self.sums = place, rows, width, sums
        self.counts, self.smalls = (0,) * 4, (False,) * 4
        self.kept, self.small_kept = [None] * 3, [None] * 3
        self.came = self.came_z = self.totals = None
        self.shares, self.others, self.small_share = [], [], None
        self.squares = jnp.zeros((1, width), FULL)
        self.flying, self.swapping = [], 0

    def step(self, chunk, *ties, small=None):
        rows, width = self.rows, self.width
        new, once, twice, done = counts = (len(chunk),) + self.counts[:3]
        smalls = (small is not None,) + self.smalls[:3]
        last = not (new or once or twice)
        arrays, jobs = [], []

        def number(spec):
            array, *place = spec
            for i, known in enumerate(arrays):
                if known is array:
                    return (i, *place)
            arrays.append(array)
            return (len(arrays) - 1, *place)

        for pair in chunk:
            for tile in pair:
                jobs.append(
                    [(a, b, [(number(l), number(r)) for l, r in ps]) for a, b, ps in tile]
                )
        small_job = None
        if small is not None:
            small_job = (
                [(number(l), number(r)) for l, r in small[0]],
                [(number((a,))[0], number((b,))[0]) for a, b in small[1]],
            )
        ins = list(arrays)
        for stage in range(2):
            ins += [self.kept[stage]] * (counts[1 + stage] > 0)
            ins += [self.small_kept[stage]] * smalls[1 + stage]
        if once or twice:
            ins += self.came
        if done:
            ins += [self.kept[2]] + [self.small_kept[2]] * smalls[3] + self.came_z + [self.squares]
        ins += [self.sums] * last
        outs = []
        if new or once:
            for added in (64 * smalls[0], 64 * smalls[1]):
                outs.append((((new * 8 + once * 4) * rows + added, width), LOW))
        for stage, blocks in enumerate((8, 4, 1)):
            if counts[stage]:
                outs.append(((counts[stage], 2, blocks * rows, width), FULL))
            if smalls[stage]:
                outs.append(((blocks * rows, SMALL), FULL))
        if twice:
            outs += [((twice * 2 * rows + 16 * smalls[2], width), LOW)] * 3
        if done:
            outs.append(((done, 2, rows, width), FULL))
            outs += [((rows, SMALL), FULL)] * smalls[3]
            outs.append(((1, width), FULL))
        outs += [((1, SMALL), FULL)] * last
        length = 2 * arrays[0].shape[-2] if new else 0
        scratch = [pltpu.VMEM((16 * rows, width), FULL)] if new else []
        scratch += [pltpu.VMEM((16 * rows, SMALL), FULL)] * smalls[0]
        got = list(
            call(
                functools.partial(
                    round_kernel, jobs, small_job, len(arrays), counts, smalls, last
                ),
                self.place,
                outs,
                ins,
                [],
                scratch,
                4 * new * length * width * width,
            )
        )
        if last:
            self.totals = got.pop()
        if done:
            self.squares = got.pop()
            if smalls[3]:
                self.small_share = got.pop()
            self.shares.append(got.pop())
        self.counts, self.smalls = counts, smalls
        self.kept, self.small_kept = [None] * 3, [None] * 3
        if last:
            return ties
        got, ties = tie(got, ties)
        to = [got.pop(0) for _ in range(2)] if new or once else []
        for stage in range(3):
            if counts[stage]:
                self.kept[stage] = got.pop(0)
            if smalls[stage]:
                self.small_kept[stage] = got.pop(0)
        self.flying = [across(v, mask, 16) for v, mask in zip(to, (X, Y))]
        self.flying += [across(v, mask, 16) for v, mask in zip(got, Z)]
        self.swapping = 0
        while len(self.flying) < 5 and len(self.others) + self.swapping < len(self.shares):
            self.flying.append(swap_cores(self.shares[len(self.others) + self.swapping]))
            self.swapping += 1
        return ties

    def finish(self, *ties):
        flying, ties = tie(self.flying, ties)
        self.came = self.came_z = None
        if self.counts[0] or self.counts[1]:
            self.came, flying = flying[:2], flying[2:]
        if self.counts[2]:
            self.came_z, flying = flying[:3], flying[3:]
        self.others += flying
        return ties

    def left(self):
        return any(self.counts[:3])

    def swap_rest(self):
        self.others += [swap_cores(v) for v in self.shares[len(self.others) :]]


class PlainRounds:
    def __init__(self):
        self.shares, self.squares = [], []

    def step(self, chunk, *ties):
        def factor(spec):
            array, index, low, high = spec
            array = array if index is None else array[index]
            return array if low is None else array[:, low:high]

        def summed(tile):
            parts = [sum(cross(factor(l), factor(r)) for l, r in ps) for _, _, ps in tile]
            return lax.psum_scatter(
                jnp.concatenate(parts, 1), "fsdp", scatter_dimension=0, tiled=True
            )

        share = jnp.stack([jnp.stack([summed(tile) for tile in pair]) for pair in chunk])
        self.shares.append((share, swap_cores(share)))
        self.squares.append(jnp.sum(share * share, (0, 1, 2))[None])
        return ties

    def finish(self, *ties):
        return ties

    def left(self):
        return False


def up_to_parts(expand_shard, size, rows, parts):
    r = expand_shard.shape[0]
    return expand_shard.reshape(r, size, parts, rows).transpose(0, 2, 1, 3).reshape(r, -1)


def up_from_parts(expand_shard, size, rows, parts):
    r = expand_shard.shape[0]
    return expand_shard.reshape(r, parts, size, rows).transpose(0, 2, 1, 3).reshape(r, -1)


def half_of(value, core):
    half = value.shape[1] // 2
    return lax.dynamic_slice_in_dim(value, core * half, half, 1)


def body(
    fsdp,
    codons,
    masked,
    segments,
    inward,
    outward,
    expand,
    shrink,
    codon_table,
    norm_params,
    inward_first,
    inward_second,
    outward_first,
    outward_second,
    expand_first,
    expand_second,
    shrink_first,
    shrink_second,
    table_first,
    table_second,
    norm_first,
    norm_second,
):
    layers = inward.shape[0]
    length = codons.shape[0]
    rows = inward.shape[1]
    width = rows * fsdp
    half = width // 2
    parts = shrink.shape[1] // rows
    fast = fsdp == 16 and rows == 48
    core, index = lax.axis_index("dp"), lax.axis_index("fsdp")
    bit = lambda b: lax.rem(lax.div(index, b), 2)
    place = jnp.stack([core, bit(1), bit(2), lax.div(index, 4)]).astype(jnp.int32)
    weight = masked.astype(FULL)
    inputs = jnp.where(masked == 1, V - 1, codons)

    def tiles_of(l):
        w_in, w_out = inward[l].astype(LOW), outward[l].astype(LOW)
        pieces = [half_of(w_in[:, p * width : (p + 1) * width], core) for p in range(3)]
        pieces.append(half_of(w_out, core))
        mixer = [jnp.concatenate(pieces[:2], 1), jnp.concatenate(pieces[2:], 1)]
        up = half_of(up_to_parts(expand[l].astype(LOW), fsdp, rows, parts), core)
        down = lax.dynamic_slice_in_dim(shrink[l].astype(LOW), core * 2 * rows, 2 * rows, 0)
        return mixer + [up[:, :width], up[:, width:], down[:rows], down[rows:]]

    norms = norm_params.shape[0] * 2
    small = jnp.concatenate(
        [codon_table.astype(LOW), norm_params.astype(LOW).reshape(norms, rows)], 0
    )
    small = jnp.pad(small.T, ((0, 0), (0, -small.shape[0] % 128)))
    weights = jnp.concatenate([small] + sum([tiles_of(l) for l in range(layers)], []), 1)
    weights = lax.all_gather(weights, ("fsdp", "dp"), axis=0, tiled=True)
    weights = weights.reshape(fsdp, 2, rows, -1)
    if not fast:
        weights = weights.transpose(1, 0, 2, 3).reshape(1, 2, width, -1)
    small = weights[:, 0, :, : V + norms].reshape(width, V + norms).T
    base = lambda l: weights.shape[3] - (layers - l) * 6 * width
    table_low = small[:V]
    gains = small[V:].astype(FULL).reshape(-1, 2, width)

    cosine, sine = rotary_tables(length)
    vocab_ids = jnp.arange(V, dtype=jnp.int32)
    chosen = (inputs[:, None] == jnp.arange(SMALL, dtype=jnp.int32)[None, :]).astype(LOW)
    resid = dot(chosen, jnp.pad(table_low, ((0, SMALL - V), (0, 0))))
    kept = []
    for l in range(layers):
        gain = gains[2 * l : 2 * l + 2]
        middle, query, keys, values, lse, pack = attention_forward(
            place, resid, weights, base(l), gain[0], cosine, sine, segments
        )
        if l > 0:
            middle, came = tie(middle, kept[-1][-1])
            kept[-1] = kept[-1][:-1] + (came,)
        pack_came = swap_cores(pack)
        output, active, pack_mid, hidden = hidden_forward(
            place, middle, weights, base(l), gain[1]
        )
        output, pack_came = tie(output, pack_came)
        kept.append(
            (resid, query, keys, values, lse, pack, pack_came, middle, hidden, active, pack_mid)
            + (swap_cores(pack_mid),)
        )
        resid = output
    final_gain = gains[2 * layers]
    normed_out, unit_out, inverse_out = normalize(resid, final_gain[0], final_gain[1])
    head_in = normed_out.astype(LOW)
    logits = jnp.einsum("sd,vd->sv", head_in, table_low, preferred_element_type=FULL)
    top = jnp.max(logits, -1, keepdims=True)
    lse_head = top + jnp.log(jnp.sum(jnp.exp(logits - top), -1, keepdims=True))
    targets = (codons[:, None] == vocab_ids[None, :]).astype(FULL)
    picked = jnp.sum(logits * targets, -1)
    loss_local = jnp.sum((lse_head[:, 0] - picked) * weight)
    grad_logits = ((jnp.exp(logits - lse_head) - targets) * weight[:, None]).astype(LOW)
    grad_head = dot(grad_logits, table_low)
    grad_logits = jnp.pad(grad_logits, ((0, 0), (0, SMALL - V)))
    early = (head_in, grad_logits, chosen)
    early_came = [swap_cores(v) for v in early]
    sums = jnp.pad(jnp.stack([loss_local, jnp.sum(weight)]), (0, SMALL - 2))[None]
    grad, grad_final_gain, grad_final_bias = normalize_back(
        grad_head, unit_out, inverse_out, final_gain[0]
    )
    branch = grad.astype(LOW)
    grad_norms = [grad_final_gain, grad_final_bias]
    grad, branch, came = tie(grad, branch, kept[-1][-1])
    kept[-1] = kept[-1][:-1] + (came,)

    rounds = Rounds(place, rows, width, sums) if fast else PlainRounds()
    whole = lambda array, i=None: (array, i, None, None)
    tile = lambda left, right, other_left, other_right: [
        (0, width, [(left, right), (other_left, other_right)])
    ]
    chunk = []
    for l in reversed(range(layers)):
        (resid, query, keys, values, lse, pack, pack_came, middle, hidden, active, pack_mid, mid_came) = kept[l]
        gain = gains[2 * l : 2 * l + 2]
        branch_came = swap_cores(branch)
        chunk.append(
            [
                tile(
                    whole(active, s), whole(branch), whole(mid_came, 1 + s), whole(branch_came)
                )
                for s in range(2)
            ]
        )
        grad, branch = rounds.step(chunk, grad, branch)
        grad_middle, gains_mid, up_own, up_other = hidden_back(
            place, grad, branch, middle, hidden, weights, base(l), gain[1]
        )
        grad_middle, up_own, up_other, early_came = rounds.finish(
            grad_middle, up_own, up_other, early_came
        )
        up_came = swap_cores(up_other)
        if l == 0:
            norms_early = jnp.concatenate([gains_mid] + grad_norms, 0)
            norms_early = (norms_early, swap_cores(norms_early))
        (grad_middle,) = rounds.step(
            [
                [
                    tile(
                        whole(pack_mid, 0), whole(up_own, s), whole(mid_came, 0), whole(up_came, s)
                    )
                    for s in range(2)
                ]
            ],
            grad_middle,
        )
        grad, branch, gains_in, mix_own, mix_other = attention_back(
            place, grad_middle, resid, weights, base(l), gain[0], cosine, sine, segments,
            query, keys, values, lse,
        )
        grad_norms = [gains_in, gains_mid] + grad_norms
        grad, branch, mix_own, mix_other = rounds.finish(grad, branch, mix_own, mix_other)
        mix_came = swap_cores(mix_other)
        products = lambda i, a, b: [
            ((pack, i, None, None), (mix_own, 1, a, b)),
            ((pack_came, i, None, None), (mix_came, 1, a, b)),
        ]
        chunk = [
            [
                tile(whole(pack, 0), whole(mix_own, 0), whole(pack_came, 0), whole(mix_came, 0)),
                [(0, half, products(0, 0, half)), (half, width, products(1, half, width))],
            ]
        ]
    late = (grad_norms[0], swap_cores(grad_norms[0]))
    branch_came = swap_cores(branch)
    products = [(whole(early[0]), whole(early[1])), (whole(early_came[0]), whole(early_came[1]))]
    products += [(whole(branch), whole(early[2])), (whole(branch_came), whole(early_came[2]))]
    if fast:
        rounds.step(chunk, small=(products, [late, norms_early]))
        while rounds.left():
            rounds.finish()
            rounds.step([])
        rounds.swap_rest()
        share_small = rounds.small_share
        small_other = swap_cores(share_small)
        totals, rest = tie(rounds.totals, [rounds.others, small_other])
        share_small = jnp.where(core == 0, share_small, small_other)
    else:
        rounds.step(chunk)
        table = sum(cross(l[0], r[0]) for l, r in products)
        table = table + jnp.pad(
            jnp.concatenate([a + b for a, b in (late, norms_early)], 0).T,
            ((0, 0), (V, SMALL - V - norms)),
        )
        table = jnp.where(core == 0, table, swap_cores(table))
        share_small = lax.psum_scatter(table, "fsdp", scatter_dimension=0, tiled=True)
        squares = jnp.sum(share_small * share_small) * (core == 0)
        for value in rounds.squares:
            squares = squares + jnp.sum(value)
        totals = sums + jnp.where(jnp.arange(SMALL) == 2, squares, 0.0)[None]
    totals = total_of(totals, fsdp)
    loss_sum, count, square_total = totals[0, 0], totals[0, 1], totals[0, 2]
    share_small = share_small[:, : V + norms].T

    shares = list(zip(rounds.shares, rounds.others)) if fast else rounds.shares
    places = [(2 * (layers - 1 - l), 0 if l == layers - 1 else 1) for l in range(layers)]

    def tiles_at(chunk, pair):
        own, other = (v[pair] for v in shares[chunk])
        ordered = (jnp.where(core == 0, own, other), jnp.where(core == 0, other, own))
        return [v[s] for v in ordered for s in range(2)]

    share_up = jnp.stack(
        [
            up_from_parts(jnp.concatenate(tiles_at(at + 1, 0), 1), fsdp, rows, parts)
            for at, _ in places
        ]
    )
    share_small = (share_small[:V], share_small[V:].reshape(-1, 2, rows))
    if not fast:
        share_in, share_out, share_down = [], [], []
        side = lambda *values: jnp.concatenate(values, 1)
        for at, pair in places:
            a_0, b_0, a_1, b_1 = tiles_at(at + 2, 0)
            share_in.append(
                side(
                    a_0[:, :half], a_1[:, :half], a_0[:, half:],
                    a_1[:, half:], b_0[:, :half], b_1[:, :half],
                )
            )
            share_out.append(side(b_0[:, half:], b_1[:, half:]))
            share_down.append(jnp.concatenate(tiles_at(at, pair), 0))
        share_in, share_out, share_down = (
            jnp.stack(v) for v in (share_in, share_out, share_down)
        )
    grad_norm = jnp.sqrt(square_total) / count
    factor = CLIP / jnp.maximum(grad_norm, CLIP)
    masters = (inward, outward, expand, shrink, codon_table, norm_params)
    firsts = (inward_first, outward_first, expand_first, shrink_first, table_first, norm_first)
    seconds = (
        inward_second,
        outward_second,
        expand_second,
        shrink_second,
        table_second,
        norm_second,
    )
    if fast:
        matrices = [v for group in zip(masters[:4], firsts[:4], seconds[:4]) for v in group]
        chunks = [((at + 2, 0), (at, pair)) for at, pair in places]
        own, other = zip(*shares)
        scale = jnp.stack([count, factor])
        values = list(optimizer(place, scale, chunks, own, other, share_up, matrices))
    else:
        values = []
        for index, grad in enumerate((share_in, share_out, share_up, share_down)):
            clipped = grad / count * factor
            values.extend(
                adam_step(
                    masters[index], clipped, firsts[index], seconds[index], RATE_MATRIX, DECAY
                )
            )
    for index, rate, decay in ((4, RATE_MATRIX, DECAY), (5, RATE_VECTOR, 0.0)):
        clipped = share_small[index - 4] / count * factor
        values.extend(
            adam_step(masters[index], clipped, firsts[index], seconds[index], rate, decay)
        )
    return (loss_sum, count, grad_norm, *values)


def solution(mesh):
    in_specs = (
        P(("fsdp", "dp")),
        P(("fsdp", "dp")),
        P(("fsdp", "dp")),
        P(None, "fsdp", None),
        P(None, "fsdp", None),
        P(None, "fsdp", None),
        P(None, "fsdp", None),
        P(None, "fsdp"),
        P(None, None, "fsdp"),
        P(None, "fsdp", None),
        P(None, "fsdp", None),
        P(None, "fsdp", None),
        P(None, "fsdp", None),
        P(None, "fsdp", None),
        P(None, "fsdp", None),
        P(None, "fsdp", None),
        P(None, "fsdp", None),
        P(None, "fsdp"),
        P(None, "fsdp"),
        P(None, None, "fsdp"),
        P(None, None, "fsdp"),
    )
    out_specs = (
        P(),
        P(),
        P(),
        P(None, "fsdp", None),
        P(None, "fsdp", None),
        P(None, "fsdp", None),
        P(None, "fsdp", None),
        P(None, "fsdp", None),
        P(None, "fsdp", None),
        P(None, "fsdp", None),
        P(None, "fsdp", None),
        P(None, "fsdp", None),
        P(None, "fsdp", None),
        P(None, "fsdp", None),
        P(None, "fsdp", None),
        P(None, "fsdp"),
        P(None, "fsdp"),
        P(None, "fsdp"),
        P(None, None, "fsdp"),
        P(None, None, "fsdp"),
        P(None, None, "fsdp"),
    )
    step = functools.partial(body, mesh.shape["fsdp"])
    return jax.shard_map(step, mesh=mesh, in_specs=in_specs, out_specs=out_specs, check_vma=False)
```

```python
import functools

import jax
import jax.numpy as jnp
from jax import lax
from jax.experimental import pallas as pl
from jax.experimental.pallas import tpu as pltpu
from jax.sharding import PartitionSpec as P

HD = 64
V = 70
STEP = 10


NORM_EPS = 1e-05
BETA_ONE = 0.9
BETA_TWO = 0.95
ADAM_EPS = 1e-08
DECAY = 0.1
RATE_MATRIX = 0.05
RATE_VECTOR = 0.3
CLIP = 0.05


def rotary_tables(length):
    freq = 10000.0 ** (-jnp.arange(HD // 2, dtype=jnp.float32) * 2.0 / HD)
    angle = jnp.arange(length, dtype=jnp.float32)[:, None] * freq[None, :]
    cosine, sine = jnp.cos(angle), jnp.sin(angle)
    return (
        jnp.concatenate([cosine] * 4, 1),
        jnp.concatenate([-sine, sine] * 2, 1),
    )


def normalize(resid, gain, bias):
    mean = jnp.mean(resid, -1, keepdims=True)
    centred = resid - mean
    inverse = lax.rsqrt(jnp.mean(centred * centred, -1, keepdims=True) + NORM_EPS)
    unit = centred * inverse
    return (unit * gain + bias, unit, inverse)


def normalize_back(grad, unit, inverse, gain):
    scaled = grad * gain
    across = (
        scaled
        - jnp.mean(scaled, -1, keepdims=True)
        - unit * jnp.mean(scaled * unit, -1, keepdims=True)
    )
    return (across * inverse, jnp.sum(grad * unit, 0, keepdims=True), jnp.sum(grad, 0, keepdims=True))


def dot(left, right):
    return jnp.dot(left, right, preferred_element_type=jnp.float32)


def dot_nt(left, right):
    return lax.dot_general(
        left, right, (((1,), (1,)), ((), ())), preferred_element_type=jnp.float32
    )


def cross(left, right):
    return lax.dot_general(
        left, right, (((0,), (0,)), ((), ())), preferred_element_type=jnp.float32
    )


VMEM_LIMIT = 56 * 1024 * 1024
LOW, FULL = jnp.bfloat16, jnp.float32


class Sent:
    def __init__(self, here, there, sems):
        self.here, self.there, self.sems = here, there, sems
        self.shape, self.at = here.shape, here.at
        self.copies = []

    def __getitem__(self, at):
        return self.here[at]

    def __setitem__(self, at, value):
        self.here[at] = value

    def send(self, index=None):
        here, there = self.here, self.there
        if index is not None:
            here, there = here.at[index], there.at[index]
        copy = pltpu.make_async_copy(here, there, self.sems.at[len(self.copies)])
        copy.start()
        self.copies.append(copy)


def call(kernel, scalars, outs, ins, anys=(), scratch=(), flops=0, sent=()):
    whole = pl.BlockSpec(memory_space=pltpu.VMEM)
    left = pl.BlockSpec(memory_space=pl.ANY)

    def body(scalars, *refs):
        refs = list(refs)
        take = lambda n: [refs.pop(0) for _ in range(n)]
        in_refs, any_refs, out_refs = take(len(ins)), take(len(anys)), take(len(outs))
        here = take(len(sent))
        for n, i in enumerate(sent):
            out_refs[i] = Sent(here[n], out_refs[i], refs[-1].at[n])
        kernel(scalars, in_refs, any_refs, out_refs, *(refs[:-1] if sent else refs))
        for i in sent:
            for copy in out_refs[i].copies:
                copy.wait()

    return pl.pallas_call(
        body,
        out_shape=[jax.ShapeDtypeStruct(s, t) for s, t in outs],
        in_specs=[pl.BlockSpec(memory_space=pltpu.SMEM)]
        + [whole] * len(ins)
        + [left] * len(anys),
        out_specs=[left if i in sent else whole for i in range(len(outs))],
        scratch_shapes=[pltpu.VMEM(*outs[i]) for i in sent]
        + list(scratch)
        + [pltpu.SemaphoreType.DMA((len(sent), 5))] * (len(sent) > 0),
        compiler_params=pltpu.CompilerParams(vmem_limit_bytes=VMEM_LIMIT),
        cost_estimate=pl.CostEstimate(
            flops=flops,
            bytes_accessed=sum(x.size * x.dtype.itemsize for x in list(ins) + list(anys)),
            transcendentals=0,
        ),
    )(scalars, *ins, *anys)


def fetch(sources, targets, sems, first=0):
    copies = [
        pltpu.make_async_copy(s, t, sems.at[first + i])
        for i, (s, t) in enumerate(zip(sources, targets))
    ]
    for c in copies:
        c.start()
    return copies


def tile_of(ref, core, at):
    return ref.at[:, core, :, at : at + ref.shape[0] * ref.shape[2]]


def matrix(ref, place, low=None, high=None):
    value = ref[place] if low is None else ref[place, :, :, low:high]
    return value.reshape(-1, value.shape[-1])


def tile_scratch(count, weights):
    blocks, _, rows, _ = weights.shape
    return pltpu.VMEM((count, blocks, rows, blocks * rows), LOW)


def swap_halves(value):
    lane = lax.broadcasted_iota(jnp.int32, value.shape, 1)
    return jnp.where(
        lax.rem(lane, HD) < HD // 2,
        pltpu.roll(value, 128 - HD // 2, 1),
        pltpu.roll(value, HD // 2, 1),
    )


def ordered(first, own, other):
    return jnp.concatenate([jnp.where(first, own, other), jnp.where(first, other, own)], 1)


def head_mask(shape, head):
    lane = lax.broadcasted_iota(jnp.int32, shape, 1)
    return (lane < HD) if head == 0 else (lane >= HD)


def attention_forward_kernel(base, place_of, ins, anys, outs, w_a, w_b, mixed, bias, sems):
    resid, seg_col, seg_row, cosine, sine, gains = ins
    middle, query, keys, values, lse, pack = outs
    (weights,) = anys
    width = resid.shape[1]
    half = width // 2
    cores = (place_of[0], 1 - place_of[0])
    copies = fetch(
        [tile_of(weights, c, base + t * width) for t in range(2) for c in cores],
        [w.at[place] for w in (w_a, w_b) for place in range(2)],
        sems,
    )
    first = place_of[0] == 0
    normed, _, _ = normalize(resid[...], gains[0:1], gains[1:2])
    normed_low, attended = pack.at[0], pack.at[1]
    normed_low[...] = normed.astype(LOW)
    bias[...] = jnp.where(seg_col[...] == seg_row[...], 0.0, -1000000000.0)
    for place in range(2):
        copies[place].wait()
        mixed[...] = dot(normed_low[...], matrix(w_a, place))
        for p in range(half // 128):
            for part, target, scale in ((0, query, HD ** (-0.5)), (1, keys, 1.0)):
                x = mixed[:, part * half + p * 128 : part * half + (p + 1) * 128]
                x = x * cosine[...] + swap_halves(x) * sine[...]
                x = (x * scale if scale != 1.0 else x).astype(LOW)
                target[:, place * half + p * 128 : place * half + (p + 1) * 128] = x
    for place in range(2):
        copies[2 + place].wait()
        values[:, place * half : (place + 1) * half] = dot(
            normed_low[...], matrix(w_b, place, 0, half)
        ).astype(LOW)

    lse[...] = jnp.zeros_like(lse)

    for p in range(width // 128):
        columns = slice(p * 128, (p + 1) * 128)
        q, k, v = query[:, columns], keys[:, columns], values[:, columns]
        out = []
        for head in range(2):
            masked_q = jnp.where(head_mask(q.shape, head), q, jnp.zeros_like(q))
            scores = dot_nt(masked_q, k) + bias[...]
            top = jnp.max(scores, -1, keepdims=True)
            expo = jnp.exp(scores - top)
            total = jnp.sum(expo, -1, keepdims=True)
            probs = (expo * (1.0 / total)).astype(LOW)
            out.append(dot(probs, v))
            lane = lax.broadcasted_iota(jnp.int32, lse.shape, 1)
            lse[...] = jnp.where(lane == 2 * p + head, top + jnp.log(total), lse[...])
        attended[:, columns] = jnp.where(head_mask(out[0].shape, 0), out[0], out[1]).astype(LOW)
    attended[...] = ordered(first, attended[:, :half], attended[:, half:])
    out = ordered(
        first,
        dot(attended[...], matrix(w_b, 0, half, width)),
        dot(attended[...], matrix(w_b, 1, half, width)),
    )
    middle[...] = resid[...] + out


def attention_forward(place, resid, weights, base, gains, cosine, sine, segments):
    length, width = resid.shape
    one = (length, width)
    return call(
        functools.partial(attention_forward_kernel, base),
        place,
        [(one, FULL)] + [(one, LOW)] * 3 + [((length, 128), FULL), ((2,) + one, LOW)],
        [resid, segments[:, None], segments[None, :], cosine, sine, gains],
        [weights],
        [
            tile_scratch(2, weights),
            tile_scratch(2, weights),
            pltpu.VMEM(one, FULL),
            pltpu.VMEM((length, length), FULL),
            pltpu.SemaphoreType.DMA((4,)),
        ],
        8 * length * width * width + 4 * length * length * width,
    )


GELU_SCALE = 0.7978845608028654
GELU_CUBE = 0.044715


def fetch_hidden(weights, base, ups, downs, sems):
    blocks, _, rows, _ = weights.shape
    width = blocks * rows
    half, some = width // 2, max(blocks // 4, 1)
    copies = {}
    for t in range(4):
        copies[0, t] = fetch(
            [tile_of(weights, t // 2, base + (2 + t % 2) * width)], [ups.at[t]], sems, t
        )
        if blocks >= 4 or t == 0:
            sources, targets = [], []
            for core in range(2):
                for j in range(4):
                    at = base + 4 * width + j * half
                    sources.append(weights.at[pl.ds(t * some, some), core, :, at : at + half])
                    targets.append(
                        downs.at[pl.ds(t * some, some), j, :, core * half : (core + 1) * half]
                    )
            copies[1, t] = fetch(sources, targets, sems, 4 + 8 * t)

    def wait(which, t):
        for copy in copies.pop((which, t), []):
            copy.wait()

    return wait


def rows_of(downs, t):
    blocks, parts, rows, width = downs.shape
    if blocks >= 4:
        some = blocks // 4
        return downs[t * some : (t + 1) * some].reshape(some * parts * rows, width)
    return downs[0, t]


def hidden_scratch(weights):
    blocks, _, rows, _ = weights.shape
    return [
        tile_scratch(4, weights),
        pltpu.VMEM((blocks, 4, rows, blocks * rows), LOW),
        pltpu.SemaphoreType.DMA((36,)),
    ]


def hidden_forward_kernel(base, place_of, ins, anys, outs, ups, downs, sems):
    middle, gains = ins
    output, pack, hidden = outs
    wait = fetch_hidden(anys[0], base, ups, downs, sems)
    normed, _, _ = normalize(middle[...], gains[0:1], gains[1:2])
    pack[0] = normed.astype(LOW)
    pack.send(0)
    for t in range(4):
        wait(0, t)
        x = dot(pack[0], matrix(ups, t))
        hidden[t] = x
        hidden.send(t)
        inner = jnp.tanh(x * (GELU_SCALE + (GELU_SCALE * GELU_CUBE) * (x * x)))
        value = x * 0.5
        value = (value + value * inner).astype(LOW)
        pack[1 + t] = value
        pack.send(1 + t)
        wait(1, t)
        product = dot(value, rows_of(downs, t))
        output[...] = (middle[...] if t == 0 else output[...]) + product


def hidden_forward(place, middle, weights, base, gains):
    length, width = middle.shape
    one = (length, width)
    return call(
        functools.partial(hidden_forward_kernel, base),
        place,
        [(one, FULL), ((5,) + one, LOW), ((4,) + one, FULL)],
        [middle, gains],
        [weights],
        hidden_scratch(weights),
        16 * length * width * width,
        sent=(1, 2),
    )


def hidden_back_kernel(base, place_of, ins, anys, outs, ups, downs, sems, hidden_here, total, own_sems):
    branch, grad, middle, gains = ins
    hidden, weights = anys
    grad_middle, grad_gains, grad_own, grad_other = outs
    wait = fetch_hidden(weights, base, ups, downs, sems)
    copies = fetch([hidden.at[t] for t in range(4)], [hidden_here.at[t] for t in range(4)], own_sems)
    for t in range(4):
        wait(1, t)
        grad_active = dot_nt(branch[...], rows_of(downs, t))
        copies[t].wait()
        x = hidden_here[t]
        square = x * x
        inner = jnp.tanh(x * (GELU_SCALE + (GELU_SCALE * GELU_CUBE) * square))
        slope = x * (GELU_SCALE + (3.0 * GELU_SCALE * GELU_CUBE) * square)
        slope = (0.5 + 0.5 * inner) * (1.0 + slope * (1.0 - inner))
        value = (grad_active * slope).astype(LOW)
        mine = place_of[0] == t // 2

        @pl.when(mine)
        def _():
            grad_own[t % 2] = value

        @pl.when(jnp.logical_not(mine))
        def _():
            grad_other[t % 2] = value

        wait(0, t)
        product = dot_nt(value, matrix(ups, t))
        total[...] = product if t == 0 else total[...] + product
    _, unit, inverse = normalize(middle[...], gains[0:1], gains[1:2])
    back, gain, bias = normalize_back(total[...], unit, inverse, gains[0:1])
    grad_middle[...] = grad[...] + back
    grad_gains[0:1] = gain
    grad_gains[1:2] = bias


def hidden_back(place, grad, branch, middle, hidden, weights, base, gains):
    length, width = middle.shape
    one = (length, width)
    return call(
        functools.partial(hidden_back_kernel, base),
        place,
        [(one, FULL), ((2, width), FULL), ((2,) + one, LOW), ((2,) + one, LOW)],
        [branch, grad, middle, gains],
        [hidden, weights],
        hidden_scratch(weights)
        + [
            pltpu.VMEM((4,) + one, FULL),
            pltpu.VMEM(one, FULL),
            pltpu.SemaphoreType.DMA((4,)),
        ],
        16 * length * width * width,
    )


def attention_back_kernel(base, place_of, ins, anys, outs, w_a, w_b, bias, ga, gq, gk, gv, sems):
    grad_middle, query, keys, values, lse, seg_col, seg_row, cosine, sine, gains, resid = ins
    (weights,) = anys
    grad, branch, branch_own, branch_other, grad_gains, grad_own, grad_other = outs
    width = resid.shape[1]
    half = width // 2
    cores = (place_of[0], 1 - place_of[0])
    copies = fetch(
        [tile_of(weights, c, base + t * width) for t in (1, 0) for c in cores],
        [w.at[place] for w in (w_b, w_a) for place in range(2)],
        sems,
    )
    first = place_of[0] == 0
    grads = (grad_own, grad_other)
    bias[...] = jnp.where(seg_col[...] == seg_row[...], 0.0, -1000000000.0)
    attn_grad = grad_middle[...].astype(LOW)
    left, right = attn_grad[:, :half], attn_grad[:, half:]
    grad_own[1, :, half:] = jnp.where(first, left, right)
    grad_other[1, :, half:] = jnp.where(first, right, left)
    copies[0].wait()
    copies[1].wait()
    natural = dot_nt(grad_own[1, :, half:], matrix(w_b, 0, half, width)) + dot_nt(
        grad_other[1, :, half:], matrix(w_b, 1, half, width)
    )
    natural = natural.astype(LOW)
    ga[:, :half] = jnp.where(first, natural[:, :half], natural[:, half:])
    ga[:, half:] = jnp.where(first, natural[:, half:], natural[:, :half])

    for p in range(width // 128):
        columns = slice(p * 128, (p + 1) * 128)
        q, k, v, g = query[:, columns], keys[:, columns], values[:, columns], ga[:, columns]
        out_q, out_k, out_v = [], [], []
        for head in range(2):
            mask = head_mask(q.shape, head)
            zero = jnp.zeros_like(q)
            scores = dot_nt(k, jnp.where(mask, q, zero)) + bias[...]
            probs = jnp.exp(scores - lse[2 * p + head : 2 * p + head + 1, :])
            grad_probs = dot_nt(v, jnp.where(mask, g, zero))
            across = jnp.sum(probs * grad_probs, 0, keepdims=True)
            grad_scores = (probs * (grad_probs - across)).astype(LOW)
            out_k.append(dot(grad_scores, q))
            out_q.append(cross(grad_scores, k))
            out_v.append(dot(probs.astype(LOW), g))
        for out, target, scale in ((out_q, gq, HD ** (-0.5)), (out_k, gk, 1.0)):
            x = jnp.where(head_mask(out[0].shape, 0), out[0], out[1])
            x = x * scale if scale != 1.0 else x
            x = x * cosine[...] - swap_halves(x) * sine[...]
            target[:, columns] = x.astype(LOW)
        gv[:, columns] = jnp.where(head_mask(out_v[0].shape, 0), out_v[0], out_v[1]).astype(LOW)
    for place in (1, 0):
        columns = slice(place * half, (place + 1) * half)
        grads[place][0, :, :half] = gq[:, columns]
        grads[place][0, :, half:] = gk[:, columns]
        grads[place][1, :, :half] = gv[:, columns]
    copies[2].wait()
    copies[3].wait()
    total = dot_nt(grad_own[0], matrix(w_a, 0)) + dot_nt(grad_other[0], matrix(w_a, 1))
    total = total + dot_nt(grad_own[1, :, :half], matrix(w_b, 0, 0, half))
    total = total + dot_nt(grad_other[1, :, :half], matrix(w_b, 1, 0, half))
    _, unit, inverse = normalize(resid[...], gains[0:1], gains[1:2])
    back, gain, bias_grad = normalize_back(total, unit, inverse, gains[0:1])
    back = grad_middle[...] + back
    grad[...] = back
    back = back.astype(LOW)
    branch[...] = back
    branch_own[...] = jnp.where(first, back[:, :half], back[:, half:])
    branch_other[...] = jnp.where(first, back[:, half:], back[:, :half])
    grad_gains[0:1] = gain
    grad_gains[1:2] = bias_grad


def attention_back(place, grad_middle, resid, weights, base, gains, cosine, sine, segments, query, keys, values, lse):
    length, width = resid.shape
    one = (length, width)
    return call(
        functools.partial(attention_back_kernel, base),
        place,
        [(one, FULL), (one, LOW)]
        + [((length, width // 2), LOW)] * 2
        + [((2, width), FULL)]
        + [((2,) + one, LOW)] * 2,
        [grad_middle, query, keys, values, lse.T[: width // HD]]
        + [segments[:, None], segments[None, :], cosine, sine, gains, resid],
        [weights],
        [
            tile_scratch(2, weights),
            tile_scratch(2, weights),
            pltpu.VMEM((length, length), FULL),
        ]
        + [pltpu.VMEM(one, LOW)] * 4
        + [pltpu.SemaphoreType.DMA((4,))],
        8 * length * width * width + 10 * length * length * width,
    )


def adam_step(master, grad, first, second, rate, decay):
    first = BETA_ONE * first + (1.0 - BETA_ONE) * grad
    second = BETA_TWO * second + (1.0 - BETA_TWO) * grad * grad
    fix_one = 1.0 - BETA_ONE**STEP
    fix_two = 1.0 - BETA_TWO**STEP
    update = first / fix_one / (jnp.sqrt(second / fix_two) + ADAM_EPS) + decay * master
    return (master - rate * update, first, second)


def optimizer_kernel(chunks, layers, place_of, scale, *refs):
    n = (len(refs) - 24) // 2
    own, other, masters = refs[:n], refs[n : 2 * n], refs[2 * n : 2 * n + 12]
    outs = refs[2 * n + 12 :]
    first = place_of[0] == 0
    count, factor = scale[0], scale[1]

    def step(which, at, grad):
        master, moment, square = (masters[3 * which + i][at] for i in range(3))
        clipped = grad / count * factor
        values = adam_step(master, clipped, moment, square, RATE_MATRIX, DECAY)
        for i in range(3):
            outs[3 * which + i][at] = values[i]

    def tile(where, s, core):
        a, b = own[where[0]][where[1], s], other[where[0]][where[1], s]
        return jnp.where(first, a, b) if core == 0 else jnp.where(first, b, a)

    rows, width = own[0].shape[-2:]
    half = width // 2
    for l in range(layers):
        mixer, up, down = chunks[l]
        for core in range(2):
            columns = lambda p: pl.ds(p * width + core * half, half)
            value = tile(mixer, 0, core)
            step(0, (l, slice(None), columns(0)), value[:, :half])
            step(0, (l, slice(None), columns(1)), value[:, half:])
            value = tile(mixer, 1, core)
            step(0, (l, slice(None), columns(2)), value[:, :half])
            step(1, (l, slice(None), columns(0)), value[:, half:])
            for s in range(2):
                step(2, (l, slice(None), pl.ds((2 * core + s) * width, width)), tile(up, s, core))
                value = tile(down, s, core)
                for j in range(2):
                    at = (l, pl.ds((2 * s + j) * rows, rows), columns(0))
                    step(3, at, value[:, j * half : (j + 1) * half])


def optimizer(place, scale, chunks, own, other, masters):
    ins = list(own) + list(other) + list(masters)
    whole = pl.BlockSpec(memory_space=pltpu.VMEM)
    return pl.pallas_call(
        functools.partial(optimizer_kernel, chunks, len(chunks)),
        out_shape=[jax.ShapeDtypeStruct(m.shape, m.dtype) for m in masters],
        in_specs=[pl.BlockSpec(memory_space=pltpu.SMEM)] * 2 + [whole] * len(ins),
        out_specs=[whole] * len(masters),
        compiler_params=pltpu.CompilerParams(vmem_limit_bytes=VMEM_LIMIT),
        cost_estimate=pl.CostEstimate(
            flops=20 * sum(m.size for m in masters),
            bytes_accessed=8 * sum(m.size for m in masters),
            transcendentals=0,
        ),
    )(place, scale, *ins)


def pack_kernel(layers, place_of, ins, anys, outs):
    inward, outward, expand, shrink, small = ins
    (out,) = outs
    first = place_of[0] == 0
    rows = inward.shape[1]
    width = inward.shape[2] // 3
    half = width // 2
    at = small.shape[1]
    out[:, :at] = small[...]
    for l in range(layers):
        sources = [inward[l, :, p * width : (p + 1) * width] for p in range(3)] + [outward[l]]
        sources.append(expand[l])
        sources += [shrink[l, j * rows : (j + 1) * rows] for j in range(shrink.shape[1] // rows)]
        for value in sources:
            part = value.shape[1] // 2
            value = jnp.where(first, value[:, :part], value[:, part:])
            out[:, at : at + part] = value.astype(LOW)
            at += part


def swap_cores(value):
    return lax.ppermute(value, "dp", [(0, 1), (1, 0)])


def across(value, mask, size):
    return lax.ppermute(value, "fsdp", [(i, i ^ mask) for i in range(size)])


def tie(*values):
    return lax.optimization_barrier(values)


def total_of(value, size):
    value = value + swap_cores(value)
    bit = 1
    while bit < size:
        if 2 * bit < size:
            a, b, c = (across(value, m * bit, size) for m in (1, 2, 3))
            value = (value + a) + (b + c)
        else:
            value = value + across(value, bit, size)
        bit *= 4
    return value


X, Y = 1, 2
Z = (4, 8, 12)


SMALL = 128


def round_kernel(jobs, small_job, n_ins, counts, smalls, last, place_of, ins, anys, outs, *scratch):
    new, once, twice, done = counts
    small_new, small_once, small_twice, small_done = smalls
    rest = list(ins[n_ins:]) + list(outs) + list(scratch)
    pop = lambda present, n=1: [rest.pop(0) for _ in range(n)] if present else [None] * n
    (keep_once,), (small_keep_once,) = pop(once), pop(small_once)
    (keep_twice,), (small_keep_twice,) = pop(twice), pop(small_twice)
    from_x, from_y = pop(once or twice, 2)
    (keep_done,), (small_keep_done,) = pop(done), pop(small_done)
    from_z = pop(done, 3)
    (squares_in,), (sums,) = pop(done), pop(last)
    to_x, to_y = pop(new or once, 2)
    (out_once,), (small_out_once,) = pop(new), pop(small_new)
    (out_twice,), (small_out_twice,) = pop(once), pop(small_once)
    (out_done,), (small_out_done,) = pop(twice), pop(small_twice)
    to_z = pop(twice, 3)
    (share,), (small_share,), (squares,) = pop(done), pop(small_done), pop(done)
    (totals,) = pop(last)
    (tile,), (unit,), (small_tile,) = pop(new), pop(new), pop(small_new)
    rows = (out_once if new else out_twice if once else out_done if twice else share).shape[-2]
    rows = rows // (8 if new else 4 if once else 1)
    bits, z = (place_of[1], place_of[2]), place_of[3]
    to, came = (to_x, to_y), (from_x, from_y)

    def block(index, size=rows):
        if isinstance(index, int):
            return pl.ds(index * size, size)
        return pl.ds(pl.multiple_of(index * size, 16), size)

    def factor(spec):
        which, index, low, high = spec
        ref = ins[which] if index is None else ins[which].at[index]
        return ref[...] if low is None else ref[:, low:high]

    def put_small(ref, start, group, side, value):
        for q in range(rows // 16):
            lanes = side * (rows // 16) + q
            ref[pl.ds(start + group * 16, 16), lanes * SMALL : (lanes + 1) * SMALL] = value[
                q * 16 : (q + 1) * 16
            ].astype(LOW)

    def take_small(ref, start, group, side):
        parts = []
        for q in range(rows // 16):
            lanes = side * (rows // 16) + q
            at = pl.ds(pl.multiple_of(start + group * 16, 16), 16)
            parts.append(ref[at, lanes * SMALL : (lanes + 1) * SMALL])
        return jnp.concatenate(parts, 0).astype(FULL)

    def summed(products):
        total = None
        for left, right in products:
            product = cross(factor(left), factor(right))
            total = product if total is None else total + product
        return total

    for p in range(new):
        if len(jobs[p]) == 4:
            for quarter, products in enumerate(jobs[p]):
                unit[...] = summed(products)
                half = unit.shape[1]
                for index in range(4):
                    for s in range(2):
                        for j in range(2):
                            tile[s, block(quarter * 4 + index), j * half : (j + 1) * half] = unit[
                                block(index * 4 + 2 * s + j), :
                            ]
        else:
            for s in range(2):
                for low, high, products in jobs[p][s]:
                    tile[s, :, low:high] = summed(products)
        for s in range(2):
            for zz in range(4):
                for other in range(2):
                    at = zz * 2 + other
                    index = lambda bit: zz * 4 + (other * 2 + bit if s == 0 else bit * 2 + other)
                    to[s][block(p * 8 + at), :] = tile[s, block(index(1 - bits[s])), :].astype(LOW)
                    out_once[p, s, block(at), :] = tile[s, block(index(bits[s])), :]
    if small_new:
        products, norms_at = small_job
        total = summed(products)
        norms = jnp.concatenate([ins[mine][...] + ins[theirs][...] for mine, theirs in norms_at], 0)
        high = norms.astype(LOW)
        shape = (norms.shape[0], SMALL)
        column = lax.broadcasted_iota(jnp.int32, shape, 1) - V
        pick = jnp.where(lax.broadcasted_iota(jnp.int32, shape, 0) == column, 1.0, 0.0).astype(LOW)
        total = total + (cross(high, pick) + cross((norms - high.astype(FULL)).astype(LOW), pick))
        small_tile[...] = total
        for zz in range(4):
            for other in range(2):
                index = lambda bit: zz * 4 + other * 2 + bit
                send = small_tile[block(index(1 - bits[0])), :]
                put_small(to_x, (new * 8 + once * 4) * rows, other * 2 + zz // 2, zz % 2, send)
                small_out_once[block(zz * 2 + other), :] = small_tile[block(index(bits[0])), :]
    for p in range(once):
        for s in range(2):
            for zz in range(4):
                for bit in range(2):
                    at = zz * 2 + (bits[1 - s] if bit else 1 - bits[1 - s])
                    value = keep_once[p, s, block(at), :] + came[s][block(p * 8 + at), :].astype(FULL)
                    if bit:
                        out_twice[p, s, block(zz), :] = value
                    else:
                        to[1 - s][block(new * 8 + p * 4 + zz), :] = value.astype(LOW)
    if small_once:
        start = (once * 8 + twice * 4) * rows
        for zz in range(4):
            for bit in range(2):
                other = bits[1] if bit else 1 - bits[1]
                value = small_keep_once[block(zz * 2 + other), :]
                value = value + take_small(from_x, start, other * 2 + zz // 2, zz % 2)
                if bit:
                    small_out_twice[block(zz), :] = value
                else:
                    put_small(to_y, (new * 8 + once * 4) * rows, zz, 0, value)
    for p in range(twice):
        for s in range(2):
            for xor in range(4):
                at = jnp.bitwise_xor(z, xor)
                value = keep_twice[p, s, block(at), :] + came[1 - s][
                    block(once * 8 + p * 4 + at), :
                ].astype(FULL)
                if xor == 0:
                    out_done[p, s] = value
                else:
                    to_z[xor - 1][block(2 * p + s), :] = value.astype(LOW)
    if small_twice:
        for xor in range(4):
            at = jnp.bitwise_xor(z, xor)
            value = small_keep_twice[block(at), :]
            value = value + take_small(from_y, (once * 8 + twice * 4) * rows, at, 0)
            if xor == 0:
                small_out_done[...] = value
            else:
                put_small(to_z[xor - 1], twice * 2 * rows, 0, 0, value)
    if done:
        squares[...] = squares_in[...]
    for p in range(done):
        for s in range(2):
            value = keep_done[p, s]
            for f in from_z:
                value = value + f[block(2 * p + s), :].astype(FULL)
            share[p, s] = value
            squares[...] += jnp.sum(value * value, 0, keepdims=True)
    if small_done:
        value = small_keep_done[...]
        for f in from_z:
            value = value + take_small(f, done * 2 * rows, 0, 0)
        small_share[...] = value
    if last:
        total = jnp.sum(squares[...], 1, keepdims=True)
        if small_done:
            square = jnp.sum(jnp.sum(value * value, 0, keepdims=True), 1, keepdims=True)
            total = total + jnp.where(place_of[0] == 0, square, jnp.zeros_like(square))
        lane = lax.broadcasted_iota(jnp.int32, sums.shape, 1)
        totals[...] = jnp.where(lane == 2, total, sums[...])


class Rounds:
    def __init__(self, place, rows, width, sums):
        self.place, self.rows, self.width, self.sums = place, rows, width, sums
        self.counts, self.smalls = (0,) * 4, (False,) * 4
        self.kept, self.small_kept = [None] * 3, [None] * 3
        self.came = self.came_z = self.totals = None
        self.shares, self.others, self.small_share = [], [], None
        self.squares = jnp.zeros((1, width), FULL)
        self.flying, self.swapping = [], 0

    def step(self, chunk, *ties, small=None):
        rows, width = self.rows, self.width
        new, once, twice, done = counts = (len(chunk),) + self.counts[:3]
        smalls = (small is not None,) + self.smalls[:3]
        last = not (new or once or twice)
        arrays, jobs = [], []

        def number(spec):
            array, *place = spec
            for i, known in enumerate(arrays):
                if known is array:
                    return (i, *place)
            arrays.append(array)
            return (len(arrays) - 1, *place)

        numbered = lambda products: [(number(l), number(r)) for l, r in products]
        for pair in chunk:
            if len(pair) == 4:
                jobs.append([numbered(products) for products in pair])
            else:
                jobs.append([[(a, b, numbered(ps)) for a, b, ps in tile] for tile in pair])
        small_job = None
        if small is not None:
            small_job = (
                [(number(l), number(r)) for l, r in small[0]],
                [(number((a,))[0], number((b,))[0]) for a, b in small[1]],
            )
        ins = list(arrays)
        for stage in range(2):
            ins += [self.kept[stage]] * (counts[1 + stage] > 0)
            ins += [self.small_kept[stage]] * smalls[1 + stage]
        if once or twice:
            ins += self.came
        if done:
            ins += [self.kept[2]] + [self.small_kept[2]] * smalls[3] + self.came_z + [self.squares]
        ins += [self.sums] * last
        outs = []
        if new or once:
            for added in (64 * smalls[0], 64 * smalls[1]):
                outs.append((((new * 8 + once * 4) * rows + added, width), LOW))
        for stage, blocks in enumerate((8, 4, 1)):
            if counts[stage]:
                outs.append(((counts[stage], 2, blocks * rows, width), FULL))
            if smalls[stage]:
                outs.append(((blocks * rows, SMALL), FULL))
        if twice:
            outs += [((twice * 2 * rows + 16 * smalls[2], width), LOW)] * 3
        if done:
            outs.append(((done, 2, rows, width), FULL))
            outs += [((rows, SMALL), FULL)] * smalls[3]
            outs.append(((1, width), FULL))
        outs += [((1, SMALL), FULL)] * last
        length = 2 * arrays[0].shape[-2] if new else 0
        scratch = []
        if new:
            scratch.append(pltpu.VMEM((2, 16 * rows, width), FULL))
            scratch.append(pltpu.VMEM((16 * rows, width // 2), FULL))
        scratch += [pltpu.VMEM((16 * rows, SMALL), FULL)] * smalls[0]
        got = list(
            call(
                functools.partial(
                    round_kernel, jobs, small_job, len(arrays), counts, smalls, last
                ),
                self.place,
                outs,
                ins,
                [],
                scratch,
                4 * new * length * width * width,
            )
        )
        if last:
            self.totals = got.pop()
        if done:
            self.squares = got.pop()
            if smalls[3]:
                self.small_share = got.pop()
            self.shares.append(got.pop())
        self.counts, self.smalls = counts, smalls
        self.kept, self.small_kept = [None] * 3, [None] * 3
        if last:
            return ties
        got, ties = tie(got, ties)
        to = [got.pop(0) for _ in range(2)] if new or once else []
        for stage in range(3):
            if counts[stage]:
                self.kept[stage] = got.pop(0)
            if smalls[stage]:
                self.small_kept[stage] = got.pop(0)
        self.flying = [across(v, mask, 16) for v, mask in zip(to, (X, Y))]
        self.flying += [across(v, mask, 16) for v, mask in zip(got, Z)]
        self.swapping = 0
        while len(self.flying) < 5 and len(self.others) + self.swapping < len(self.shares):
            self.flying.append(swap_cores(self.shares[len(self.others) + self.swapping]))
            self.swapping += 1
        return ties

    def finish(self, *ties):
        flying, ties = tie(self.flying, ties)
        self.came = self.came_z = None
        if self.counts[0] or self.counts[1]:
            self.came, flying = flying[:2], flying[2:]
        if self.counts[2]:
            self.came_z, flying = flying[:3], flying[3:]
        self.others += flying
        return ties

    def left(self):
        return any(self.counts[:3])

    def swap_rest(self):
        self.others += [swap_cores(v) for v in self.shares[len(self.others) :]]


class PlainRounds:
    def __init__(self):
        self.shares, self.squares = [], []

    def step(self, chunk, *ties):
        def factor(spec):
            array, index, low, high = spec
            array = array if index is None else array[index]
            return array if low is None else array[:, low:high]

        summed = lambda products: sum(cross(factor(l), factor(r)) for l, r in products)
        scatter = lambda v: lax.psum_scatter(v, "fsdp", scatter_dimension=0, tiled=True)
        shares = []
        for pair in chunk:
            if len(pair) == 4:
                v = scatter(jnp.concatenate([summed(products) for products in pair], 0))
                v = v.reshape(2, 2, -1, v.shape[1])
                shares.append(jnp.concatenate([v[:, 0], v[:, 1]], 2))
            else:
                tiles = [jnp.concatenate([summed(ps) for _, _, ps in t], 1) for t in pair]
                shares.append(jnp.stack([scatter(t) for t in tiles]))
        share = jnp.stack(shares)
        self.shares.append((share, swap_cores(share)))
        self.squares.append(jnp.sum(share * share, (0, 1, 2))[None])
        return ties

    def finish(self, *ties):
        return ties

    def left(self):
        return False


def half_of(value, core):
    half = value.shape[1] // 2
    return lax.dynamic_slice_in_dim(value, core * half, half, 1)


def body(
    fsdp,
    codons,
    masked,
    segments,
    inward,
    outward,
    expand,
    shrink,
    codon_table,
    norm_params,
    inward_first,
    inward_second,
    outward_first,
    outward_second,
    expand_first,
    expand_second,
    shrink_first,
    shrink_second,
    table_first,
    table_second,
    norm_first,
    norm_second,
):
    layers = inward.shape[0]
    length = codons.shape[0]
    rows = inward.shape[1]
    width = rows * fsdp
    half = width // 2
    fast = fsdp == 16 and rows == 48
    core, index = lax.axis_index("dp"), lax.axis_index("fsdp")
    bit = lambda b: lax.rem(lax.div(index, b), 2)
    place = jnp.stack([core, bit(1), bit(2), lax.div(index, 4)]).astype(jnp.int32)
    weight = masked.astype(FULL)
    inputs = jnp.where(masked == 1, V - 1, codons)

    norms = norm_params.shape[0] * 2
    small = jnp.concatenate(
        [codon_table.astype(LOW), norm_params.astype(LOW).reshape(norms, rows)], 0
    )
    small = jnp.pad(small.T, ((0, 0), (0, -small.shape[0] % 128)))
    (weights,) = call(
        functools.partial(pack_kernel, layers),
        place,
        [((rows, small.shape[1] + layers * 6 * width), LOW)],
        [inward, outward, expand, shrink, small],
    )
    weights = lax.all_gather(weights, ("fsdp", "dp"), axis=0, tiled=True)
    weights = weights.reshape(fsdp, 2, rows, -1)
    if not fast:
        columns = [weights[:, :, :, : small.shape[1]]]
        for at in range(small.shape[1], weights.shape[3], 6 * width):
            columns.append(weights[:, :, :, at : at + 4 * width])
            quarter = weights[:, :, :, at + 4 * width : at + 6 * width]
            quarter = quarter.reshape(fsdp, 2, rows, 4, half).transpose(1, 0, 3, 2, 4)
            quarter = quarter.reshape(2, 4, width, half).transpose(0, 2, 1, 3)
            columns.append(quarter.reshape(2, fsdp, rows, 2 * width).transpose(1, 0, 2, 3))
        weights = jnp.concatenate(columns, 3).transpose(1, 0, 2, 3).reshape(1, 2, width, -1)
    small = weights[:, 0, :, : V + norms].reshape(width, V + norms).T
    base = lambda l: weights.shape[3] - (layers - l) * 6 * width
    table_low = small[:V]
    gains = small[V:].astype(FULL).reshape(-1, 2, width)

    cosine, sine = rotary_tables(length)
    vocab_ids = jnp.arange(V, dtype=jnp.int32)
    chosen = (inputs[:, None] == jnp.arange(SMALL, dtype=jnp.int32)[None, :]).astype(LOW)
    resid = dot(chosen, jnp.pad(table_low, ((0, SMALL - V), (0, 0))))
    kept = []
    for l in range(layers):
        gain = gains[2 * l : 2 * l + 2]
        middle, query, keys, values, lse, pack = attention_forward(
            place, resid, weights, base(l), gain[0], cosine, sine, segments
        )
        if l > 0:
            middle, came = tie(middle, kept[-1][-1])
            kept[-1] = kept[-1][:-1] + (came,)
        pack_came = swap_cores(pack)
        output, pack_mid, hidden = hidden_forward(
            place, middle, weights, base(l), gain[1]
        )
        output, pack_came = tie(output, pack_came)
        kept.append(
            (resid, query, keys, values, lse, pack, pack_came, middle, hidden, pack_mid)
            + (swap_cores(pack_mid),)
        )
        resid = output
    final_gain = gains[2 * layers]
    normed_out, unit_out, inverse_out = normalize(resid, final_gain[0], final_gain[1])
    head_in = normed_out.astype(LOW)
    logits = jnp.einsum("sd,vd->sv", head_in, table_low, preferred_element_type=FULL)
    top = jnp.max(logits, -1, keepdims=True)
    lse_head = top + jnp.log(jnp.sum(jnp.exp(logits - top), -1, keepdims=True))
    targets = (codons[:, None] == vocab_ids[None, :]).astype(FULL)
    picked = jnp.sum(logits * targets, -1)
    loss_local = jnp.sum((lse_head[:, 0] - picked) * weight)
    grad_logits = ((jnp.exp(logits - lse_head) - targets) * weight[:, None]).astype(LOW)
    grad_head = dot(grad_logits, table_low)
    grad_logits = jnp.pad(grad_logits, ((0, 0), (0, SMALL - V)))
    early = (head_in, grad_logits, chosen)
    early_came = [swap_cores(v) for v in early]
    sums = jnp.pad(jnp.stack([loss_local, jnp.sum(weight)]), (0, SMALL - 2))[None]
    grad, grad_final_gain, grad_final_bias = normalize_back(
        grad_head, unit_out, inverse_out, final_gain[0]
    )
    branch = grad.astype(LOW)
    branch_own, branch_other = half_of(branch, core), half_of(branch, 1 - core)
    grad_norms = [grad_final_gain, grad_final_bias]
    grad, branch, came = tie(grad, branch, kept[-1][-1])
    kept[-1] = kept[-1][:-1] + (came,)

    rounds = Rounds(place, rows, width, sums) if fast else PlainRounds()
    whole = lambda array, i=None: (array, i, None, None)
    tile = lambda left, right, other_left, other_right: [
        (0, width, [(left, right), (other_left, other_right)])
    ]
    chunk = []
    for l in reversed(range(layers)):
        (resid, query, keys, values, lse, pack, pack_came, middle, hidden, pack_mid, mid_came) = kept[l]
        gain = gains[2 * l : 2 * l + 2]
        branch_came = swap_cores(branch_other)
        chunk.append(
            [
                [
                    (whole(pack_mid, 1 + t), whole(branch_own)),
                    (whole(mid_came, 1 + t), whole(branch_came)),
                ]
                for t in range(4)
            ]
        )
        grad, branch = rounds.step(chunk, grad, branch)
        grad_middle, gains_mid, up_own, up_other = hidden_back(
            place, grad, branch, middle, hidden, weights, base(l), gain[1]
        )
        grad_middle, up_own, up_other, early_came = rounds.finish(
            grad_middle, up_own, up_other, early_came
        )
        up_came = swap_cores(up_other)
        if l == 0:
            norms_early = jnp.concatenate([gains_mid] + grad_norms, 0)
            norms_early = (norms_early, swap_cores(norms_early))
        (grad_middle,) = rounds.step(
            [
                [
                    tile(
                        whole(pack_mid, 0), whole(up_own, s), whole(mid_came, 0), whole(up_came, s)
                    )
                    for s in range(2)
                ]
            ],
            grad_middle,
        )
        grad, branch, branch_own, branch_other, gains_in, mix_own, mix_other = attention_back(
            place, grad_middle, resid, weights, base(l), gain[0], cosine, sine, segments,
            query, keys, values, lse,
        )
        grad_norms = [gains_in, gains_mid] + grad_norms
        grad, branch, branch_own, branch_other, mix_own, mix_other = rounds.finish(
            grad, branch, branch_own, branch_other, mix_own, mix_other
        )
        mix_came = swap_cores(mix_other)
        products = lambda i, a, b: [
            ((pack, i, None, None), (mix_own, 1, a, b)),
            ((pack_came, i, None, None), (mix_came, 1, a, b)),
        ]
        chunk = [
            [
                tile(whole(pack, 0), whole(mix_own, 0), whole(pack_came, 0), whole(mix_came, 0)),
                [(0, half, products(0, 0, half)), (half, width, products(1, half, width))],
            ]
        ]
    late = (grad_norms[0], swap_cores(grad_norms[0]))
    branch_came = swap_cores(branch)
    products = [(whole(early[0]), whole(early[1])), (whole(early_came[0]), whole(early_came[1]))]
    products += [(whole(branch), whole(early[2])), (whole(branch_came), whole(early_came[2]))]
    if fast:
        rounds.step(chunk, small=(products, [late, norms_early]))
        while rounds.left():
            rounds.finish()
            rounds.step([])
        rounds.swap_rest()
        share_small = rounds.small_share
        small_other = swap_cores(share_small)
        totals, rest = tie(rounds.totals, [rounds.others, small_other])
        share_small = jnp.where(core == 0, share_small, small_other)
    else:
        rounds.step(chunk)
        table = sum(cross(l[0], r[0]) for l, r in products)
        table = table + jnp.pad(
            jnp.concatenate([a + b for a, b in (late, norms_early)], 0).T,
            ((0, 0), (V, SMALL - V - norms)),
        )
        table = jnp.where(core == 0, table, swap_cores(table))
        share_small = lax.psum_scatter(table, "fsdp", scatter_dimension=0, tiled=True)
        squares = jnp.sum(share_small * share_small) * (core == 0)
        for value in rounds.squares:
            squares = squares + jnp.sum(value)
        totals = sums + jnp.where(jnp.arange(SMALL) == 2, squares, 0.0)[None]
    totals = total_of(totals, fsdp)
    loss_sum, count, square_total = totals[0, 0], totals[0, 1], totals[0, 2]
    share_small = share_small[:, : V + norms].T

    shares = list(zip(rounds.shares, rounds.others)) if fast else rounds.shares
    places = [(2 * (layers - 1 - l), 0 if l == layers - 1 else 1) for l in range(layers)]

    def tiles_at(chunk, pair):
        own, other = (v[pair] for v in shares[chunk])
        ordered = (jnp.where(core == 0, own, other), jnp.where(core == 0, other, own))
        return [v[s] for v in ordered for s in range(2)]

    share_small = (share_small[:V], share_small[V:].reshape(-1, 2, rows))
    if not fast:
        share_in, share_out, share_up, share_down = [], [], [], []
        side = lambda *values: jnp.concatenate(values, 1)
        for at, pair in places:
            a_0, b_0, a_1, b_1 = tiles_at(at + 2, 0)
            share_in.append(
                side(
                    a_0[:, :half], a_1[:, :half], a_0[:, half:],
                    a_1[:, half:], b_0[:, :half], b_1[:, :half],
                )
            )
            share_out.append(side(b_0[:, half:], b_1[:, half:]))
            share_up.append(side(*tiles_at(at + 1, 0)))
            a_0, b_0, a_1, b_1 = tiles_at(at, pair)
            share_down.append(
                jnp.concatenate(
                    [
                        side(x[:, j * half : (j + 1) * half], y[:, j * half : (j + 1) * half])
                        for x, y in ((a_0, a_1), (b_0, b_1))
                        for j in range(2)
                    ],
                    0,
                )
            )
        share_in, share_out, share_up, share_down = (
            jnp.stack(v) for v in (share_in, share_out, share_up, share_down)
        )
    grad_norm = jnp.sqrt(square_total) / count
    factor = CLIP / jnp.maximum(grad_norm, CLIP)
    masters = (inward, outward, expand, shrink, codon_table, norm_params)
    firsts = (inward_first, outward_first, expand_first, shrink_first, table_first, norm_first)
    seconds = (
        inward_second,
        outward_second,
        expand_second,
        shrink_second,
        table_second,
        norm_second,
    )
    if fast:
        matrices = [v for group in zip(masters[:4], firsts[:4], seconds[:4]) for v in group]
        chunks = [((at + 2, 0), (at + 1, 0), (at, pair)) for at, pair in places]
        own, other = zip(*shares)
        scale = jnp.stack([count, factor])
        values = list(optimizer(place, scale, chunks, own, other, matrices))
    else:
        values = []
        for index, grad in enumerate((share_in, share_out, share_up, share_down)):
            clipped = grad / count * factor
            values.extend(
                adam_step(
                    masters[index], clipped, firsts[index], seconds[index], RATE_MATRIX, DECAY
                )
            )
    for index, rate, decay in ((4, RATE_MATRIX, DECAY), (5, RATE_VECTOR, 0.0)):
        clipped = share_small[index - 4] / count * factor
        values.extend(
            adam_step(masters[index], clipped, firsts[index], seconds[index], rate, decay)
        )
    return (loss_sum, count, grad_norm, *values)


def solution(mesh):
    in_specs = (
        P(("fsdp", "dp")),
        P(("fsdp", "dp")),
        P(("fsdp", "dp")),
        P(None, "fsdp", None),
        P(None, "fsdp", None),
        P(None, "fsdp", None),
        P(None, "fsdp", None),
        P(None, "fsdp"),
        P(None, None, "fsdp"),
        P(None, "fsdp", None),
        P(None, "fsdp", None),
        P(None, "fsdp", None),
        P(None, "fsdp", None),
        P(None, "fsdp", None),
        P(None, "fsdp", None),
        P(None, "fsdp", None),
        P(None, "fsdp", None),
        P(None, "fsdp"),
        P(None, "fsdp"),
        P(None, None, "fsdp"),
        P(None, None, "fsdp"),
    )
    out_specs = (
        P(),
        P(),
        P(),
        P(None, "fsdp", None),
        P(None, "fsdp", None),
        P(None, "fsdp", None),
        P(None, "fsdp", None),
        P(None, "fsdp", None),
        P(None, "fsdp", None),
        P(None, "fsdp", None),
        P(None, "fsdp", None),
        P(None, "fsdp", None),
        P(None, "fsdp", None),
        P(None, "fsdp", None),
        P(None, "fsdp", None),
        P(None, "fsdp"),
        P(None, "fsdp"),
        P(None, "fsdp"),
        P(None, None, "fsdp"),
        P(None, None, "fsdp"),
        P(None, None, "fsdp"),
    )
    step = functools.partial(body, mesh.shape["fsdp"])
    return jax.shard_map(step, mesh=mesh, in_specs=in_specs, out_specs=out_specs, check_vma=False)
```

```python
import functools

import jax
import jax.numpy as jnp
from jax import lax
from jax.experimental import pallas as pl
from jax.experimental.pallas import tpu as pltpu
from jax.sharding import PartitionSpec as P

HD = 64
V = 70
STEP = 10


NORM_EPS = 1e-05
BETA_ONE = 0.9
BETA_TWO = 0.95
ADAM_EPS = 1e-08
DECAY = 0.1
RATE_MATRIX = 0.05
RATE_VECTOR = 0.3
CLIP = 0.05


def rotary_tables(length):
    freq = 10000.0 ** (-jnp.arange(HD // 2, dtype=jnp.float32) * 2.0 / HD)
    angle = jnp.arange(length, dtype=jnp.float32)[:, None] * freq[None, :]
    cosine, sine = jnp.cos(angle), jnp.sin(angle)
    return (
        jnp.concatenate([cosine] * 4, 1),
        jnp.concatenate([-sine, sine] * 2, 1),
    )


def normalize(resid, gain, bias):
    mean = jnp.mean(resid, -1, keepdims=True)
    centred = resid - mean
    inverse = lax.rsqrt(jnp.mean(centred * centred, -1, keepdims=True) + NORM_EPS)
    unit = centred * inverse
    return (unit * gain + bias, unit, inverse)


def normalize_back(grad, unit, inverse, gain):
    scaled = grad * gain
    across = (
        scaled
        - jnp.mean(scaled, -1, keepdims=True)
        - unit * jnp.mean(scaled * unit, -1, keepdims=True)
    )
    return (across * inverse, jnp.sum(grad * unit, 0, keepdims=True), jnp.sum(grad, 0, keepdims=True))


def dot(left, right):
    return jnp.dot(left, right, preferred_element_type=jnp.float32)


def dot_nt(left, right):
    return lax.dot_general(
        left, right, (((1,), (1,)), ((), ())), preferred_element_type=jnp.float32
    )


def cross(left, right):
    return lax.dot_general(
        left, right, (((0,), (0,)), ((), ())), preferred_element_type=jnp.float32
    )


def granted(shapes, margin):
    total = margin << 20
    for shape, kind in shapes:
        size = jnp.dtype(kind).itemsize
        *lead, rows, lanes = (1,) + tuple(shape)
        for n in lead:
            size *= n
        total += size * (-(-rows // 16) * 16) * (-(-lanes // 128) * 128)
    return min(total, 60 << 20)


LOW, FULL = jnp.bfloat16, jnp.float32


class Sent:
    def __init__(self, here, there, sems):
        self.here, self.there, self.sems = here, there, sems
        self.shape, self.at = here.shape, here.at
        self.copies = []

    def __getitem__(self, at):
        return self.here[at]

    def __setitem__(self, at, value):
        self.here[at] = value

    def send(self, index=None):
        here, there = self.here, self.there
        if index is not None:
            here, there = here.at[index], there.at[index]
        copy = pltpu.make_async_copy(here, there, self.sems.at[len(self.copies)])
        copy.start()
        self.copies.append(copy)


def call(kernel, scalars, outs, ins, anys=(), scratch=(), flops=0, sent=(), margin=6):
    whole = pl.BlockSpec(memory_space=pltpu.VMEM)
    left = pl.BlockSpec(memory_space=pl.ANY)

    def body(scalars, *refs):
        refs = list(refs)
        take = lambda n: [refs.pop(0) for _ in range(n)]
        in_refs, any_refs, out_refs = take(len(ins)), take(len(anys)), take(len(outs))
        here = take(len(sent))
        for n, i in enumerate(sent):
            out_refs[i] = Sent(here[n], out_refs[i], refs[-1].at[n])
        kernel(scalars, in_refs, any_refs, out_refs, *(refs[:-1] if sent else refs))
        for i in sent:
            for copy in out_refs[i].copies:
                copy.wait()

    held = [(x.shape, x.dtype) for x in ins] + list(outs)
    held += [(x.shape, x.dtype) for x in scratch if x.memory_space == pltpu.VMEM]
    return pl.pallas_call(
        body,
        out_shape=[jax.ShapeDtypeStruct(s, t) for s, t in outs],
        in_specs=[pl.BlockSpec(memory_space=pltpu.SMEM)]
        + [whole] * len(ins)
        + [left] * len(anys),
        out_specs=[left if i in sent else whole for i in range(len(outs))],
        scratch_shapes=[pltpu.VMEM(*outs[i]) for i in sent]
        + list(scratch)
        + [pltpu.SemaphoreType.DMA((len(sent), 5))] * (len(sent) > 0),
        compiler_params=pltpu.CompilerParams(vmem_limit_bytes=granted(held, margin)),
        cost_estimate=pl.CostEstimate(
            flops=flops,
            bytes_accessed=sum(x.size * x.dtype.itemsize for x in list(ins) + list(anys)),
            transcendentals=0,
        ),
    )(scalars, *ins, *anys)


def fetch(sources, targets, sems, first=0):
    copies = [
        pltpu.make_async_copy(s, t, sems.at[first + i])
        for i, (s, t) in enumerate(zip(sources, targets))
    ]
    for c in copies:
        c.start()
    return copies


def tile_of(ref, core, at):
    return ref.at[:, core, :, at : at + ref.shape[0] * ref.shape[2]]


def matrix(ref, place, low=None, high=None):
    value = ref[place] if low is None else ref[place, :, :, low:high]
    return value.reshape(-1, value.shape[-1])


def tile_scratch(count, weights):
    blocks, _, rows, _ = weights.shape
    return pltpu.VMEM((count, blocks, rows, blocks * rows), LOW)


def swap_halves(value):
    lane = lax.broadcasted_iota(jnp.int32, value.shape, 1)
    return jnp.where(
        lax.rem(lane, HD) < HD // 2,
        pltpu.roll(value, 128 - HD // 2, 1),
        pltpu.roll(value, HD // 2, 1),
    )


def ordered(first, own, other):
    return jnp.concatenate([jnp.where(first, own, other), jnp.where(first, other, own)], 1)


def head_mask(shape, head):
    lane = lax.broadcasted_iota(jnp.int32, shape, 1)
    return (lane < HD) if head == 0 else (lane >= HD)


def attention_forward_kernel(base, place_of, ins, anys, outs, w_a, w_b, mixed, bias, sems):
    resid, seg_col, seg_row, cosine, sine, gains = ins
    middle, query, keys, values, lse, pack = outs
    (weights,) = anys
    width = resid.shape[1]
    half = width // 2
    cores = (place_of[0], 1 - place_of[0])
    copies = fetch(
        [tile_of(weights, c, base + t * width) for t in range(2) for c in cores],
        [w.at[place] for w in (w_a, w_b) for place in range(2)],
        sems,
    )
    first = place_of[0] == 0
    normed, _, _ = normalize(resid[...], gains[0:1], gains[1:2])
    normed_low, attended = pack.at[0], pack.at[1]
    normed_low[...] = normed.astype(LOW)
    bias[...] = jnp.where(seg_col[...] == seg_row[...], 0.0, -1000000000.0)
    for place in range(2):
        copies[place].wait()
        mixed[...] = dot(normed_low[...], matrix(w_a, place))
        for p in range(half // 128):
            for part, target, scale in ((0, query, HD ** (-0.5)), (1, keys, 1.0)):
                x = mixed[:, part * half + p * 128 : part * half + (p + 1) * 128]
                x = x * cosine[...] + swap_halves(x) * sine[...]
                x = (x * scale if scale != 1.0 else x).astype(LOW)
                target[:, place * half + p * 128 : place * half + (p + 1) * 128] = x
    for place in range(2):
        copies[2 + place].wait()
        values[:, place * half : (place + 1) * half] = dot(
            normed_low[...], matrix(w_b, place, 0, half)
        ).astype(LOW)

    lse[...] = jnp.zeros_like(lse)

    for p in range(width // 128):
        columns = slice(p * 128, (p + 1) * 128)
        q, k, v = query[:, columns], keys[:, columns], values[:, columns]
        out = []
        for head in range(2):
            masked_q = jnp.where(head_mask(q.shape, head), q, jnp.zeros_like(q))
            scores = dot_nt(masked_q, k) + bias[...]
            top = jnp.max(scores, -1, keepdims=True)
            expo = jnp.exp(scores - top)
            total = jnp.sum(expo, -1, keepdims=True)
            probs = (expo * (1.0 / total)).astype(LOW)
            out.append(dot(probs, v))
            lane = lax.broadcasted_iota(jnp.int32, lse.shape, 1)
            lse[...] = jnp.where(lane == 2 * p + head, top + jnp.log(total), lse[...])
        attended[:, columns] = jnp.where(head_mask(out[0].shape, 0), out[0], out[1]).astype(LOW)
    attended[...] = ordered(first, attended[:, :half], attended[:, half:])
    out = ordered(
        first,
        dot(attended[...], matrix(w_b, 0, half, width)),
        dot(attended[...], matrix(w_b, 1, half, width)),
    )
    middle[...] = resid[...] + out


def attention_forward(place, resid, weights, base, gains, cosine, sine, segments):
    length, width = resid.shape
    one = (length, width)
    return call(
        functools.partial(attention_forward_kernel, base),
        place,
        [(one, FULL)] + [(one, LOW)] * 3 + [((length, 128), FULL), ((2,) + one, LOW)],
        [resid, segments[:, None], segments[None, :], cosine, sine, gains],
        [weights],
        [
            tile_scratch(2, weights),
            tile_scratch(2, weights),
            pltpu.VMEM(one, FULL),
            pltpu.VMEM((length, length), FULL),
            pltpu.SemaphoreType.DMA((4,)),
        ],
        8 * length * width * width + 4 * length * length * width,
    )


GELU_SCALE = 0.7978845608028654
GELU_CUBE = 0.044715


def fetch_hidden(weights, base, order, ups, downs, sems):
    blocks, _, rows, _ = weights.shape
    width = blocks * rows
    half, some = width // 2, max(blocks // 4, 1)
    copies = {}
    for t, (core_of, within) in enumerate(order):
        copies[0, t] = fetch(
            [tile_of(weights, core_of, base + (2 + within) * width)], [ups.at[t]], sems, t
        )
        if blocks >= 4 or t == 0:
            sources, targets = [], []
            first = (2 * core_of + within) * some if blocks >= 4 else 0
            for core in range(2):
                for j in range(4):
                    at = base + 4 * width + j * half
                    sources.append(weights.at[pl.ds(first, some), core, :, at : at + half])
                    targets.append(
                        downs.at[pl.ds(t * some, some), j, :, core * half : (core + 1) * half]
                    )
            copies[1, t] = fetch(sources, targets, sems, 4 + 8 * t)

    def wait(which, t):
        for copy in copies.pop((which, t), []):
            copy.wait()

    return wait


def rows_of(downs, t, order):
    blocks, parts, rows, width = downs.shape
    if blocks >= 4:
        some = blocks // 4
        return downs[t * some : (t + 1) * some].reshape(some * parts * rows, width)
    return downs[0, 2 * order[t][0] + order[t][1]]


def hidden_scratch(weights):
    blocks, _, rows, _ = weights.shape
    return [
        tile_scratch(4, weights),
        pltpu.VMEM((blocks, 4, rows, blocks * rows), LOW),
        pltpu.SemaphoreType.DMA((36,)),
    ]


def hidden_forward_kernel(base, place_of, ins, anys, outs, ups, downs, sems):
    middle, gains = ins
    output, pack, hidden = outs
    order = [(t // 2, t % 2) for t in range(4)]
    wait = fetch_hidden(anys[0], base, order, ups, downs, sems)
    normed, _, _ = normalize(middle[...], gains[0:1], gains[1:2])
    pack[0] = normed.astype(LOW)
    pack.send(0)
    for t in range(4):
        wait(0, t)
        x = dot(pack[0], matrix(ups, t))
        hidden[t] = x
        hidden.send(t)
        inner = jnp.tanh(x * (GELU_SCALE + (GELU_SCALE * GELU_CUBE) * (x * x)))
        value = x * 0.5
        value = (value + value * inner).astype(LOW)
        pack[1 + t] = value
        pack.send(1 + t)
        wait(1, t)
        product = dot(value, rows_of(downs, t, order))
        output[...] = (middle[...] if t == 0 else output[...]) + product


def hidden_forward(place, middle, weights, base, gains):
    length, width = middle.shape
    one = (length, width)
    return call(
        functools.partial(hidden_forward_kernel, base),
        place,
        [(one, FULL), ((5,) + one, LOW), ((4,) + one, FULL)],
        [middle, gains],
        [weights],
        hidden_scratch(weights),
        16 * length * width * width,
        sent=(1, 2),
    )


def hidden_back_kernel(base, place_of, ins, anys, outs, ups, downs, sems, hidden_here, total, own_sems):
    branch, grad, middle, gains = ins
    hidden, weights = anys
    grad_middle, grad_gains, grad_own, grad_other = outs
    order = [(core, t) for core in (place_of[0], 1 - place_of[0]) for t in range(2)]
    wait = fetch_hidden(weights, base, order, ups, downs, sems)
    copies = fetch(
        [hidden.at[2 * core + t] for core, t in order], [hidden_here.at[t] for t in range(4)], own_sems
    )
    for t in range(4):
        wait(1, t)
        grad_active = dot_nt(branch[...], rows_of(downs, t, order))
        copies[t].wait()
        x = hidden_here[t]
        square = x * x
        inner = jnp.tanh(x * (GELU_SCALE + (GELU_SCALE * GELU_CUBE) * square))
        slope = x * (GELU_SCALE + (3.0 * GELU_SCALE * GELU_CUBE) * square)
        slope = (0.5 + 0.5 * inner) * (1.0 + slope * (1.0 - inner))
        value = (grad_active * slope).astype(LOW)
        (grad_own if t < 2 else grad_other)[t % 2] = value
        wait(0, t)
        product = dot_nt(value, matrix(ups, t))
        total[...] = product if t == 0 else total[...] + product
    _, unit, inverse = normalize(middle[...], gains[0:1], gains[1:2])
    back, gain, bias = normalize_back(total[...], unit, inverse, gains[0:1])
    grad_middle[...] = grad[...] + back
    grad_gains[0:1] = gain
    grad_gains[1:2] = bias


def hidden_back(place, grad, branch, middle, hidden, weights, base, gains):
    length, width = middle.shape
    one = (length, width)
    return call(
        functools.partial(hidden_back_kernel, base),
        place,
        [(one, FULL), ((2, width), FULL), ((2,) + one, LOW), ((2,) + one, LOW)],
        [branch, grad, middle, gains],
        [hidden, weights],
        hidden_scratch(weights)
        + [
            pltpu.VMEM((4,) + one, FULL),
            pltpu.VMEM(one, FULL),
            pltpu.SemaphoreType.DMA((4,)),
        ],
        16 * length * width * width,
    )


def attention_back_kernel(base, place_of, ins, anys, outs, w_a, w_b, bias, ga, gq, gk, gv, sems):
    grad_middle, query, keys, values, lse, seg_col, seg_row, cosine, sine, gains, resid = ins
    (weights,) = anys
    grad, branch, branch_own, branch_other, grad_gains, grad_own, grad_other = outs
    width = resid.shape[1]
    half = width // 2
    cores = (place_of[0], 1 - place_of[0])
    copies = fetch(
        [tile_of(weights, c, base + t * width) for t in (1, 0) for c in cores],
        [w.at[place] for w in (w_b, w_a) for place in range(2)],
        sems,
    )
    first = place_of[0] == 0
    grads = (grad_own, grad_other)
    bias[...] = jnp.where(seg_col[...] == seg_row[...], 0.0, -1000000000.0)
    attn_grad = grad_middle[...].astype(LOW)
    left, right = attn_grad[:, :half], attn_grad[:, half:]
    grad_own[1, :, half:] = jnp.where(first, left, right)
    grad_other[1, :, half:] = jnp.where(first, right, left)
    copies[0].wait()
    copies[1].wait()
    natural = dot_nt(grad_own[1, :, half:], matrix(w_b, 0, half, width)) + dot_nt(
        grad_other[1, :, half:], matrix(w_b, 1, half, width)
    )
    natural = natural.astype(LOW)
    ga[:, :half] = jnp.where(first, natural[:, :half], natural[:, half:])
    ga[:, half:] = jnp.where(first, natural[:, half:], natural[:, :half])

    for p in range(width // 128):
        columns = slice(p * 128, (p + 1) * 128)
        q, k, v, g = query[:, columns], keys[:, columns], values[:, columns], ga[:, columns]
        flipped = k.T
        out_q, out_k, out_v = [], [], []
        for head in range(2):
            mask = head_mask(q.shape, head)
            zero = jnp.zeros_like(q)
            scores = dot_nt(k, jnp.where(mask, q, zero)) + bias[...]
            probs = jnp.exp(scores - lse[2 * p + head : 2 * p + head + 1, :])
            grad_probs = dot_nt(v, jnp.where(mask, g, zero))
            across = jnp.sum(probs * grad_probs, 0, keepdims=True)
            grad_scores = (probs * (grad_probs - across)).astype(LOW)
            out_k.append(dot(grad_scores, q))
            out_q.append(dot(flipped[head * HD : (head + 1) * HD], grad_scores))
            out_v.append(dot(probs.astype(LOW), g))
        out_q = jnp.concatenate(out_q, 0).T * HD ** (-0.5)
        out_k = jnp.where(head_mask(out_k[0].shape, 0), out_k[0], out_k[1])
        for x, target in ((out_q, gq), (out_k, gk)):
            x = x * cosine[...] - swap_halves(x) * sine[...]
            target[:, columns] = x.astype(LOW)
        gv[:, columns] = jnp.where(head_mask(out_v[0].shape, 0), out_v[0], out_v[1]).astype(LOW)
    for place in (1, 0):
        columns = slice(place * half, (place + 1) * half)
        grads[place][0, :, :half] = gq[:, columns]
        grads[place][0, :, half:] = gk[:, columns]
        grads[place][1, :, :half] = gv[:, columns]
    copies[2].wait()
    copies[3].wait()
    total = dot_nt(grad_own[0], matrix(w_a, 0)) + dot_nt(grad_other[0], matrix(w_a, 1))
    total = total + dot_nt(grad_own[1, :, :half], matrix(w_b, 0, 0, half))
    total = total + dot_nt(grad_other[1, :, :half], matrix(w_b, 1, 0, half))
    _, unit, inverse = normalize(resid[...], gains[0:1], gains[1:2])
    back, gain, bias_grad = normalize_back(total, unit, inverse, gains[0:1])
    back = grad_middle[...] + back
    grad[...] = back
    back = back.astype(LOW)
    branch[...] = back
    branch_own[...] = jnp.where(first, back[:, :half], back[:, half:])
    branch_other[...] = jnp.where(first, back[:, half:], back[:, :half])
    grad_gains[0:1] = gain
    grad_gains[1:2] = bias_grad


def attention_back(place, grad_middle, resid, weights, base, gains, cosine, sine, segments, query, keys, values, lse):
    length, width = resid.shape
    one = (length, width)
    return call(
        functools.partial(attention_back_kernel, base),
        place,
        [(one, FULL), (one, LOW)]
        + [((length, width // 2), LOW)] * 2
        + [((2, width), FULL)]
        + [((2,) + one, LOW)] * 2,
        [grad_middle, query, keys, values, lse.T[: width // HD]]
        + [segments[:, None], segments[None, :], cosine, sine, gains, resid],
        [weights],
        [
            tile_scratch(2, weights),
            tile_scratch(2, weights),
            pltpu.VMEM((length, length), FULL),
        ]
        + [pltpu.VMEM(one, LOW)] * 4
        + [pltpu.SemaphoreType.DMA((4,))],
        8 * length * width * width + 10 * length * length * width,
    )


def adam_step(master, grad, first, second, rate, decay):
    first = BETA_ONE * first + (1.0 - BETA_ONE) * grad
    second = BETA_TWO * second + (1.0 - BETA_TWO) * grad * grad
    fix_one = 1.0 / (1.0 - BETA_ONE**STEP)
    fix_two = 1.0 / (1.0 - BETA_TWO**STEP)
    update = first * fix_one / (jnp.sqrt(second * fix_two) + ADAM_EPS) + decay * master
    return (master - rate * update, first, second)


def scale_of(totals):
    count = totals[0:1, 1:2]
    grad_norm = jnp.sqrt(totals[0:1, 2:3]) / count
    return grad_norm, CLIP / jnp.maximum(grad_norm, CLIP) / count


def optimizer_kernel(chunks, place_of, ins, anys, outs):
    totals, small_own, small_other, *rest = ins
    n = (len(rest) - 18) // 2
    own, other, masters = rest[:n], rest[n : 2 * n], rest[2 * n :]
    layers = len(chunks)
    first = place_of[0] == 0
    grad_norm, scale = scale_of(totals[...])
    outs[0][...] = grad_norm

    def step(which, at, grad, rate=RATE_MATRIX, decay=DECAY):
        master, moment, square = (masters[3 * which + i][at] for i in range(3))
        values = adam_step(master, grad * scale, moment, square, rate, decay)
        for i in range(3):
            outs[1 + 3 * which + i][at] = values[i]

    def tile(where, s, core):
        a, b = own[where[0]][where[1], s], other[where[0]][where[1], s]
        return jnp.where(first, a, b) if core == 0 else jnp.where(first, b, a)

    rows, width = own[0].shape[-2:]
    half = width // 2
    for l in range(layers):
        mixer, up, down = chunks[l]
        for core in range(2):
            columns = lambda p: pl.ds(p * width + core * half, half)
            value = tile(mixer, 0, core)
            step(0, (l, slice(None), columns(0)), value[:, :half])
            step(0, (l, slice(None), columns(1)), value[:, half:])
            value = tile(mixer, 1, core)
            step(0, (l, slice(None), columns(2)), value[:, :half])
            step(1, (l, slice(None), columns(0)), value[:, half:])
            for s in range(2):
                step(2, (l, slice(None), pl.ds((2 * core + s) * width, width)), tile(up, s, core))
                value = tile(down, s, core)
                for j in range(2):
                    at = (l, pl.ds((2 * s + j) * rows, rows), columns(0))
                    step(3, at, value[:, j * half : (j + 1) * half])
    small = jnp.where(first, small_own[...], small_other[...]).T
    step(4, (slice(None), slice(None)), small[:V])
    for n in range(masters[15].shape[0]):
        step(5, n, small[V + 2 * n : V + 2 * n + 2], RATE_VECTOR, 0.0)


def optimizer(place, totals, small, chunks, own, other, masters):
    return call(
        functools.partial(optimizer_kernel, chunks),
        place,
        [((1, 1), FULL)] + [(m.shape, m.dtype) for m in masters],
        [totals, *small, *own, *other, *masters],
        flops=20 * sum(m.size for m in masters),
    )


def pack_kernel(layers, place_of, ins, anys, outs):
    inward, outward, expand, shrink, small = ins
    (out,) = outs
    first = place_of[0] == 0
    rows = inward.shape[1]
    width = inward.shape[2] // 3
    half = width // 2
    at = small.shape[1]
    out[:, :at] = small[...]
    for l in range(layers):
        sources = [inward[l, :, p * width : (p + 1) * width] for p in range(3)] + [outward[l]]
        sources.append(expand[l])
        sources += [shrink[l, j * rows : (j + 1) * rows] for j in range(shrink.shape[1] // rows)]
        for value in sources:
            part = value.shape[1] // 2
            value = jnp.where(first, value[:, :part], value[:, part:])
            out[:, at : at + part] = value.astype(LOW)
            at += part


def swap_cores(value):
    return lax.ppermute(value, "dp", [(0, 1), (1, 0)])


def across(value, mask, size):
    return lax.ppermute(value, "fsdp", [(i, i ^ mask) for i in range(size)])


def tie(*values):
    return lax.optimization_barrier(values)


def total_of(value, size):
    value = value + swap_cores(value)
    bit = 1
    while bit < size:
        if 2 * bit < size:
            a, b, c = (across(value, m * bit, size) for m in (1, 2, 3))
            value = (value + a) + (b + c)
        else:
            value = value + across(value, bit, size)
        bit *= 4
    return value


X, Y = 1, 2
Z = (4, 8, 12)


SMALL = 128


def round_kernel(jobs, small_job, n_ins, counts, smalls, last, place_of, ins, anys, outs, *scratch):
    new, once, twice, done = counts
    small_new, small_once, small_twice, small_done = smalls
    rest = list(ins[n_ins:]) + list(outs) + list(scratch)
    pop = lambda present, n=1: [rest.pop(0) for _ in range(n)] if present else [None] * n
    (keep_once,), (small_keep_once,) = pop(once), pop(small_once)
    (keep_twice,), (small_keep_twice,) = pop(twice), pop(small_twice)
    from_x, from_y = pop(once or twice, 2)
    (keep_done,), (small_keep_done,) = pop(done), pop(small_done)
    from_z = pop(done, 3)
    (squares_in,), (sums,) = pop(done), pop(last)
    to_x, to_y = pop(new or once, 2)
    (out_once,), (small_out_once,) = pop(new), pop(small_new)
    (out_twice,), (small_out_twice,) = pop(once), pop(small_once)
    (out_done,), (small_out_done,) = pop(twice), pop(small_twice)
    to_z = pop(twice, 3)
    (share,), (small_share,), (squares,) = pop(done), pop(small_done), pop(done)
    (totals,) = pop(last)
    (tile,), (unit,), (small_tile,) = pop(new), pop(new), pop(small_new)
    rows = (out_once if new else out_twice if once else out_done if twice else share).shape[-2]
    rows = rows // (8 if new else 4 if once else 1)
    bits, z = (place_of[1], place_of[2]), place_of[3]
    to, came = (to_x, to_y), (from_x, from_y)

    def block(index, size=rows):
        if isinstance(index, int):
            return pl.ds(index * size, size)
        return pl.ds(pl.multiple_of(index * size, 16), size)

    def factor(spec):
        which, index, low, high = spec
        ref = ins[which] if index is None else ins[which].at[index]
        return ref[...] if low is None else ref[:, low:high]

    def put_small(ref, start, group, side, value):
        for q in range(rows // 16):
            lanes = side * (rows // 16) + q
            ref[pl.ds(start + group * 16, 16), lanes * SMALL : (lanes + 1) * SMALL] = value[
                q * 16 : (q + 1) * 16
            ].astype(LOW)

    def take_small(ref, start, group, side):
        parts = []
        for q in range(rows // 16):
            lanes = side * (rows // 16) + q
            at = pl.ds(pl.multiple_of(start + group * 16, 16), 16)
            parts.append(ref[at, lanes * SMALL : (lanes + 1) * SMALL])
        return jnp.concatenate(parts, 0).astype(FULL)

    def summed(products):
        total = None
        for left, right in products:
            product = cross(factor(left), factor(right))
            total = product if total is None else total + product
        return total

    for p in range(new):
        if len(jobs[p]) == 4:
            for quarter, products in enumerate(jobs[p]):
                unit[...] = summed(products)
                half = unit.shape[1]
                for index in range(4):
                    for s in range(2):
                        for j in range(2):
                            tile[s, block(quarter * 4 + index), j * half : (j + 1) * half] = unit[
                                block(index * 4 + 2 * s + j), :
                            ]
        else:
            for s in range(2):
                for low, high, products in jobs[p][s]:
                    tile[s, :, low:high] = summed(products)
        for s in range(2):
            for zz in range(4):
                for other in range(2):
                    at = zz * 2 + other
                    index = lambda bit: zz * 4 + (other * 2 + bit if s == 0 else bit * 2 + other)
                    to[s][block(p * 8 + at), :] = tile[s, block(index(1 - bits[s])), :].astype(LOW)
                    out_once[p, s, block(at), :] = tile[s, block(index(bits[s])), :]
    if small_new:
        products, norms_at = small_job
        total = summed(products)
        norms = jnp.concatenate([ins[mine][...] + ins[theirs][...] for mine, theirs in norms_at], 0)
        high = norms.astype(LOW)
        shape = (norms.shape[0], SMALL)
        column = lax.broadcasted_iota(jnp.int32, shape, 1) - V
        pick = jnp.where(lax.broadcasted_iota(jnp.int32, shape, 0) == column, 1.0, 0.0).astype(LOW)
        total = total + (cross(high, pick) + cross((norms - high.astype(FULL)).astype(LOW), pick))
        small_tile[...] = total
        for zz in range(4):
            for other in range(2):
                index = lambda bit: zz * 4 + other * 2 + bit
                send = small_tile[block(index(1 - bits[0])), :]
                put_small(to_x, (new * 8 + once * 4) * rows, other * 2 + zz // 2, zz % 2, send)
                small_out_once[block(zz * 2 + other), :] = small_tile[block(index(bits[0])), :]
    for p in range(once):
        for s in range(2):
            for zz in range(4):
                for bit in range(2):
                    at = zz * 2 + (bits[1 - s] if bit else 1 - bits[1 - s])
                    value = keep_once[p, s, block(at), :] + came[s][block(p * 8 + at), :].astype(FULL)
                    if bit:
                        out_twice[p, s, block(zz), :] = value
                    else:
                        to[1 - s][block(new * 8 + p * 4 + zz), :] = value.astype(LOW)
    if small_once:
        start = (once * 8 + twice * 4) * rows
        for zz in range(4):
            for bit in range(2):
                other = bits[1] if bit else 1 - bits[1]
                value = small_keep_once[block(zz * 2 + other), :]
                value = value + take_small(from_x, start, other * 2 + zz // 2, zz % 2)
                if bit:
                    small_out_twice[block(zz), :] = value
                else:
                    put_small(to_y, (new * 8 + once * 4) * rows, zz, 0, value)
    for p in range(twice):
        for s in range(2):
            for xor in range(4):
                at = jnp.bitwise_xor(z, xor)
                value = keep_twice[p, s, block(at), :] + came[1 - s][
                    block(once * 8 + p * 4 + at), :
                ].astype(FULL)
                if xor == 0:
                    out_done[p, s] = value
                else:
                    to_z[xor - 1][block(2 * p + s), :] = value.astype(LOW)
    if small_twice:
        for xor in range(4):
            at = jnp.bitwise_xor(z, xor)
            value = small_keep_twice[block(at), :]
            value = value + take_small(from_y, (once * 8 + twice * 4) * rows, at, 0)
            if xor == 0:
                small_out_done[...] = value
            else:
                put_small(to_z[xor - 1], twice * 2 * rows, 0, 0, value)
    if done:
        squares[...] = squares_in[...]
    for p in range(done):
        for s in range(2):
            value = keep_done[p, s]
            for f in from_z:
                value = value + f[block(2 * p + s), :].astype(FULL)
            share[p, s] = value
            squares[...] += jnp.sum(value * value, 0, keepdims=True)
    if small_done:
        value = small_keep_done[...]
        for f in from_z:
            value = value + take_small(f, done * 2 * rows, 0, 0)
        small_share[...] = value
    if last:
        total = jnp.sum(squares[...], 1, keepdims=True)
        if small_done:
            square = jnp.sum(jnp.sum(value * value, 0, keepdims=True), 1, keepdims=True)
            total = total + jnp.where(place_of[0] == 0, square, jnp.zeros_like(square))
        lane = lax.broadcasted_iota(jnp.int32, sums.shape, 1)
        totals[...] = jnp.where(lane == 2, total, sums[...])


class Rounds:
    def __init__(self, place, rows, width, sums):
        self.place, self.rows, self.width, self.sums = place, rows, width, sums
        self.counts, self.smalls = (0,) * 4, (False,) * 4
        self.kept, self.small_kept = [None] * 3, [None] * 3
        self.came = self.came_z = self.totals = None
        self.shares, self.others, self.small_share = [], [], None
        self.squares = jnp.zeros((1, width), FULL)
        self.flying, self.swapping = [], 0

    def step(self, chunk, *ties, small=None):
        rows, width = self.rows, self.width
        new, once, twice, done = counts = (len(chunk),) + self.counts[:3]
        smalls = (small is not None,) + self.smalls[:3]
        last = not (new or once or twice)
        arrays, jobs = [], []

        def number(spec):
            array, *place = spec
            for i, known in enumerate(arrays):
                if known is array:
                    return (i, *place)
            arrays.append(array)
            return (len(arrays) - 1, *place)

        numbered = lambda products: [(number(l), number(r)) for l, r in products]
        for pair in chunk:
            if len(pair) == 4:
                jobs.append([numbered(products) for products in pair])
            else:
                jobs.append([[(a, b, numbered(ps)) for a, b, ps in tile] for tile in pair])
        small_job = None
        if small is not None:
            small_job = (
                [(number(l), number(r)) for l, r in small[0]],
                [(number((a,))[0], number((b,))[0]) for a, b in small[1]],
            )
        ins = list(arrays)
        for stage in range(2):
            ins += [self.kept[stage]] * (counts[1 + stage] > 0)
            ins += [self.small_kept[stage]] * smalls[1 + stage]
        if once or twice:
            ins += self.came
        if done:
            ins += [self.kept[2]] + [self.small_kept[2]] * smalls[3] + self.came_z + [self.squares]
        ins += [self.sums] * last
        outs = []
        if new or once:
            for added in (64 * smalls[0], 64 * smalls[1]):
                outs.append((((new * 8 + once * 4) * rows + added, width), LOW))
        for stage, blocks in enumerate((8, 4, 1)):
            if counts[stage]:
                outs.append(((counts[stage], 2, blocks * rows, width), FULL))
            if smalls[stage]:
                outs.append(((blocks * rows, SMALL), FULL))
        if twice:
            outs += [((twice * 2 * rows + 16 * smalls[2], width), LOW)] * 3
        if done:
            outs.append(((done, 2, rows, width), FULL))
            outs += [((rows, SMALL), FULL)] * smalls[3]
            outs.append(((1, width), FULL))
        outs += [((1, SMALL), FULL)] * last
        length = 2 * arrays[0].shape[-2] if new else 0
        scratch = []
        if new:
            scratch.append(pltpu.VMEM((2, 16 * rows, width), FULL))
            scratch.append(pltpu.VMEM((16 * rows, width // 2), FULL))
        scratch += [pltpu.VMEM((16 * rows, SMALL), FULL)] * smalls[0]
        got = list(
            call(
                functools.partial(
                    round_kernel, jobs, small_job, len(arrays), counts, smalls, last
                ),
                self.place,
                outs,
                ins,
                [],
                scratch,
                4 * new * length * width * width,
            )
        )
        if last:
            self.totals = got.pop()
        if done:
            self.squares = got.pop()
            if smalls[3]:
                self.small_share = got.pop()
            self.shares.append(got.pop())
        self.counts, self.smalls = counts, smalls
        self.kept, self.small_kept = [None] * 3, [None] * 3
        if last:
            return ties
        got, ties = tie(got, ties)
        to = [got.pop(0) for _ in range(2)] if new or once else []
        for stage in range(3):
            if counts[stage]:
                self.kept[stage] = got.pop(0)
            if smalls[stage]:
                self.small_kept[stage] = got.pop(0)
        self.flying = [across(v, mask, 16) for v, mask in zip(to, (X, Y))]
        self.flying += [across(v, mask, 16) for v, mask in zip(got, Z)]
        self.swapping = 0
        while len(self.flying) < 5 and len(self.others) + self.swapping < len(self.shares):
            self.flying.append(swap_cores(self.shares[len(self.others) + self.swapping]))
            self.swapping += 1
        return ties

    def finish(self, *ties):
        flying, ties = tie(self.flying, ties)
        self.came = self.came_z = None
        if self.counts[0] or self.counts[1]:
            self.came, flying = flying[:2], flying[2:]
        if self.counts[2]:
            self.came_z, flying = flying[:3], flying[3:]
        self.others += flying
        return ties

    def left(self):
        return any(self.counts[:3])

    def swap_rest(self):
        self.others += [swap_cores(v) for v in self.shares[len(self.others) :]]


class PlainRounds:
    def __init__(self):
        self.shares, self.squares = [], []

    def step(self, chunk, *ties):
        def factor(spec):
            array, index, low, high = spec
            array = array if index is None else array[index]
            return array if low is None else array[:, low:high]

        summed = lambda products: sum(cross(factor(l), factor(r)) for l, r in products)
        scatter = lambda v: lax.psum_scatter(v, "fsdp", scatter_dimension=0, tiled=True)
        shares = []
        for pair in chunk:
            if len(pair) == 4:
                v = scatter(jnp.concatenate([summed(products) for products in pair], 0))
                v = v.reshape(2, 2, -1, v.shape[1])
                shares.append(jnp.concatenate([v[:, 0], v[:, 1]], 2))
            else:
                tiles = [jnp.concatenate([summed(ps) for _, _, ps in t], 1) for t in pair]
                shares.append(jnp.stack([scatter(t) for t in tiles]))
        share = jnp.stack(shares)
        self.shares.append((share, swap_cores(share)))
        self.squares.append(jnp.sum(share * share, (0, 1, 2))[None])
        return ties

    def finish(self, *ties):
        return ties

    def left(self):
        return False


def half_of(value, core):
    half = value.shape[1] // 2
    return lax.dynamic_slice_in_dim(value, core * half, half, 1)


def body(
    fsdp,
    codons,
    masked,
    segments,
    inward,
    outward,
    expand,
    shrink,
    codon_table,
    norm_params,
    inward_first,
    inward_second,
    outward_first,
    outward_second,
    expand_first,
    expand_second,
    shrink_first,
    shrink_second,
    table_first,
    table_second,
    norm_first,
    norm_second,
):
    layers = inward.shape[0]
    length = codons.shape[0]
    rows = inward.shape[1]
    width = rows * fsdp
    half = width // 2
    fast = fsdp == 16 and rows == 48
    core, index = lax.axis_index("dp"), lax.axis_index("fsdp")
    bit = lambda b: lax.rem(lax.div(index, b), 2)
    place = jnp.stack([core, bit(1), bit(2), lax.div(index, 4)]).astype(jnp.int32)
    weight = masked.astype(FULL)
    inputs = jnp.where(masked == 1, V - 1, codons)

    norms = norm_params.shape[0] * 2
    small = jnp.concatenate(
        [codon_table.astype(LOW), norm_params.astype(LOW).reshape(norms, rows)], 0
    )
    small = jnp.pad(small.T, ((0, 0), (0, -small.shape[0] % 128)))
    (weights,) = call(
        functools.partial(pack_kernel, layers),
        place,
        [((rows, small.shape[1] + layers * 6 * width), LOW)],
        [inward, outward, expand, shrink, small],
    )
    weights = lax.all_gather(weights, ("fsdp", "dp"), axis=0, tiled=True)
    weights = weights.reshape(fsdp, 2, rows, -1)
    if not fast:
        columns = [weights[:, :, :, : small.shape[1]]]
        for at in range(small.shape[1], weights.shape[3], 6 * width):
            columns.append(weights[:, :, :, at : at + 4 * width])
            quarter = weights[:, :, :, at + 4 * width : at + 6 * width]
            quarter = quarter.reshape(fsdp, 2, rows, 4, half).transpose(1, 0, 3, 2, 4)
            quarter = quarter.reshape(2, 4, width, half).transpose(0, 2, 1, 3)
            columns.append(quarter.reshape(2, fsdp, rows, 2 * width).transpose(1, 0, 2, 3))
        weights = jnp.concatenate(columns, 3).transpose(1, 0, 2, 3).reshape(1, 2, width, -1)
    small = weights[:, 0, :, : V + norms].reshape(width, V + norms).T
    base = lambda l: weights.shape[3] - (layers - l) * 6 * width
    table_low = small[:V]
    gains = small[V:].astype(FULL).reshape(-1, 2, width)

    cosine, sine = rotary_tables(length)
    vocab_ids = jnp.arange(V, dtype=jnp.int32)
    chosen = (inputs[:, None] == jnp.arange(SMALL, dtype=jnp.int32)[None, :]).astype(LOW)
    resid = dot(chosen, jnp.pad(table_low, ((0, SMALL - V), (0, 0))))
    kept = []
    for l in range(layers):
        gain = gains[2 * l : 2 * l + 2]
        middle, query, keys, values, lse, pack = attention_forward(
            place, resid, weights, base(l), gain[0], cosine, sine, segments
        )
        output, pack_mid, hidden = hidden_forward(place, middle, weights, base(l), gain[1])
        kept.append((resid, query, keys, values, lse, pack, middle, hidden, pack_mid))
        resid = output
    final_gain = gains[2 * layers]
    normed_out, unit_out, inverse_out = normalize(resid, final_gain[0], final_gain[1])
    head_in = normed_out.astype(LOW)
    logits = jnp.einsum("sd,vd->sv", head_in, table_low, preferred_element_type=FULL)
    top = jnp.max(logits, -1, keepdims=True)
    lse_head = top + jnp.log(jnp.sum(jnp.exp(logits - top), -1, keepdims=True))
    targets = (codons[:, None] == vocab_ids[None, :]).astype(FULL)
    picked = jnp.sum(logits * targets, -1)
    loss_local = jnp.sum((lse_head[:, 0] - picked) * weight)
    grad_logits = ((jnp.exp(logits - lse_head) - targets) * weight[:, None]).astype(LOW)
    grad_head = dot(grad_logits, table_low)
    grad_logits = jnp.pad(grad_logits, ((0, 0), (0, SMALL - V)))
    early = (head_in, grad_logits, chosen)
    early_came = [swap_cores(v) for v in early]
    sums = jnp.pad(jnp.stack([loss_local, jnp.sum(weight)]), (0, SMALL - 2))[None]
    grad, grad_final_gain, grad_final_bias = normalize_back(
        grad_head, unit_out, inverse_out, final_gain[0]
    )
    branch = grad.astype(LOW)
    branch_own, branch_other = half_of(branch, core), half_of(branch, 1 - core)
    grad_norms = [grad_final_gain, grad_final_bias]
    mid_came = [swap_cores(saved[-1]) for saved in kept]
    pack_came = [swap_cores(saved[5]) for saved in kept]
    grad, branch, mid_came[-1] = tie(grad, branch, mid_came[-1])

    rounds = Rounds(place, rows, width, sums) if fast else PlainRounds()
    whole = lambda array, i=None: (array, i, None, None)
    tile = lambda left, right, other_left, other_right: [
        (0, width, [(left, right), (other_left, other_right)])
    ]
    chunk = []
    for l in reversed(range(layers)):
        resid, query, keys, values, lse, pack, middle, hidden, pack_mid = kept[l]
        gain = gains[2 * l : 2 * l + 2]
        branch_came = swap_cores(branch_other)
        chunk.append(
            [
                [
                    (whole(pack_mid, 1 + t), whole(branch_own)),
                    (whole(mid_came[l], 1 + t), whole(branch_came)),
                ]
                for t in range(4)
            ]
        )
        grad, branch = rounds.step(chunk, grad, branch)
        grad_middle, gains_mid, up_own, up_other = hidden_back(
            place, grad, branch, middle, hidden, weights, base(l), gain[1]
        )
        grad_middle, up_own, up_other, early_came = rounds.finish(
            grad_middle, up_own, up_other, early_came
        )
        up_came = swap_cores(up_other)
        if l == 0:
            norms_early = jnp.concatenate([gains_mid] + grad_norms, 0)
            norms_early = (norms_early, swap_cores(norms_early))
        (grad_middle,) = rounds.step(
            [
                [
                    tile(
                        whole(pack_mid, 0), whole(up_own, s), whole(mid_came[l], 0), whole(up_came, s)
                    )
                    for s in range(2)
                ]
            ],
            grad_middle,
        )
        grad, branch, branch_own, branch_other, gains_in, mix_own, mix_other = attention_back(
            place, grad_middle, resid, weights, base(l), gain[0], cosine, sine, segments,
            query, keys, values, lse,
        )
        grad_norms = [gains_in, gains_mid] + grad_norms
        grad, branch, branch_own, branch_other, mix_own, mix_other, mid_came, pack_came = (
            rounds.finish(
                grad, branch, branch_own, branch_other, mix_own, mix_other, mid_came, pack_came
            )
        )
        mix_came = swap_cores(mix_other)
        products = lambda i, a, b: [
            ((pack, i, None, None), (mix_own, 1, a, b)),
            ((pack_came[l], i, None, None), (mix_came, 1, a, b)),
        ]
        chunk = [
            [
                tile(whole(pack, 0), whole(mix_own, 0), whole(pack_came[l], 0), whole(mix_came, 0)),
                [(0, half, products(0, 0, half)), (half, width, products(1, half, width))],
            ]
        ]
    late = (grad_norms[0], swap_cores(grad_norms[0]))
    branch_came = swap_cores(branch)
    products = [(whole(early[0]), whole(early[1])), (whole(early_came[0]), whole(early_came[1]))]
    products += [(whole(branch), whole(early[2])), (whole(branch_came), whole(early_came[2]))]
    if fast:
        rounds.step(chunk, small=(products, [late, norms_early]))
        while rounds.left():
            rounds.finish()
            rounds.step([])
        rounds.swap_rest()
        share_small = rounds.small_share
        small_other = swap_cores(share_small)
        totals = rounds.totals
    else:
        rounds.step(chunk)
        table = sum(cross(l[0], r[0]) for l, r in products)
        table = table + jnp.pad(
            jnp.concatenate([a + b for a, b in (late, norms_early)], 0).T,
            ((0, 0), (V, SMALL - V - norms)),
        )
        table = jnp.where(core == 0, table, swap_cores(table))
        share_small = lax.psum_scatter(table, "fsdp", scatter_dimension=0, tiled=True)
        squares = jnp.sum(share_small * share_small) * (core == 0)
        for value in rounds.squares:
            squares = squares + jnp.sum(value)
        totals = sums + jnp.where(jnp.arange(SMALL) == 2, squares, 0.0)[None]
    totals = total_of(totals, fsdp)
    shares = list(zip(rounds.shares, rounds.others)) if fast else rounds.shares
    places = [(2 * (layers - 1 - l), 0 if l == layers - 1 else 1) for l in range(layers)]

    def tiles_at(chunk, pair):
        own, other = (v[pair] for v in shares[chunk])
        ordered = (jnp.where(core == 0, own, other), jnp.where(core == 0, other, own))
        return [v[s] for v in ordered for s in range(2)]

    if not fast:
        share_in, share_out, share_up, share_down = [], [], [], []
        side = lambda *values: jnp.concatenate(values, 1)
        for at, pair in places:
            a_0, b_0, a_1, b_1 = tiles_at(at + 2, 0)
            share_in.append(
                side(
                    a_0[:, :half], a_1[:, :half], a_0[:, half:],
                    a_1[:, half:], b_0[:, :half], b_1[:, :half],
                )
            )
            share_out.append(side(b_0[:, half:], b_1[:, half:]))
            share_up.append(side(*tiles_at(at + 1, 0)))
            a_0, b_0, a_1, b_1 = tiles_at(at, pair)
            share_down.append(
                jnp.concatenate(
                    [
                        side(x[:, j * half : (j + 1) * half], y[:, j * half : (j + 1) * half])
                        for x, y in ((a_0, a_1), (b_0, b_1))
                        for j in range(2)
                    ],
                    0,
                )
            )
        share_in, share_out, share_up, share_down = (
            jnp.stack(v) for v in (share_in, share_out, share_up, share_down)
        )
    masters = (inward, outward, expand, shrink, codon_table, norm_params)
    firsts = (inward_first, outward_first, expand_first, shrink_first, table_first, norm_first)
    seconds = (
        inward_second,
        outward_second,
        expand_second,
        shrink_second,
        table_second,
        norm_second,
    )
    if fast:
        chunks = [((at + 2, 0), (at + 1, 0), (at, pair)) for at, pair in places]
        own, other = zip(*shares)
        states = [v for group in zip(masters, firsts, seconds) for v in group]
        grad_norm, *values = optimizer(
            place, totals, (share_small, small_other), chunks, own, other, states
        )
    else:
        grad_norm, scale = scale_of(totals)
        share_small = share_small[:, : V + norms].T
        grads = (share_in, share_out, share_up, share_down)
        grads += (share_small[:V], share_small[V:].reshape(-1, 2, rows))
        values = []
        for index, grad in enumerate(grads):
            rate, decay = (RATE_VECTOR, 0.0) if index == 5 else (RATE_MATRIX, DECAY)
            values.extend(
                adam_step(masters[index], grad * scale.reshape(()), firsts[index], seconds[index], rate, decay)
            )
    return (totals[0, 0], totals[0, 1], grad_norm.reshape(()), *values)


def solution(mesh):
    in_specs = (
        P(("fsdp", "dp")),
        P(("fsdp", "dp")),
        P(("fsdp", "dp")),
        P(None, "fsdp", None),
        P(None, "fsdp", None),
        P(None, "fsdp", None),
        P(None, "fsdp", None),
        P(None, "fsdp"),
        P(None, None, "fsdp"),
        P(None, "fsdp", None),
        P(None, "fsdp", None),
        P(None, "fsdp", None),
        P(None, "fsdp", None),
        P(None, "fsdp", None),
        P(None, "fsdp", None),
        P(None, "fsdp", None),
        P(None, "fsdp", None),
        P(None, "fsdp"),
        P(None, "fsdp"),
        P(None, None, "fsdp"),
        P(None, None, "fsdp"),
    )
    out_specs = (
        P(),
        P(),
        P(),
        P(None, "fsdp", None),
        P(None, "fsdp", None),
        P(None, "fsdp", None),
        P(None, "fsdp", None),
        P(None, "fsdp", None),
        P(None, "fsdp", None),
        P(None, "fsdp", None),
        P(None, "fsdp", None),
        P(None, "fsdp", None),
        P(None, "fsdp", None),
        P(None, "fsdp", None),
        P(None, "fsdp", None),
        P(None, "fsdp"),
        P(None, "fsdp"),
        P(None, "fsdp"),
        P(None, None, "fsdp"),
        P(None, None, "fsdp"),
        P(None, None, "fsdp"),
    )
    step = functools.partial(body, mesh.shape["fsdp"])
    return jax.shard_map(step, mesh=mesh, in_specs=in_specs, out_specs=out_specs, check_vma=False)
```

```python
import functools

import jax
import jax.numpy as jnp
from jax import lax
from jax.experimental import pallas as pl
from jax.experimental.pallas import tpu as pltpu
from jax.sharding import PartitionSpec as P

HD = 64
V = 70
STEP = 10


NORM_EPS = 1e-05
BETA_ONE = 0.9
BETA_TWO = 0.95
ADAM_EPS = 1e-08
DECAY = 0.1
RATE_MATRIX = 0.05
RATE_VECTOR = 0.3
CLIP = 0.05


def rotary_tables(length):
    freq = 10000.0 ** (-jnp.arange(HD // 2, dtype=jnp.float32) * 2.0 / HD)
    angle = jnp.arange(length, dtype=jnp.float32)[:, None] * freq[None, :]
    cosine, sine = jnp.cos(angle), jnp.sin(angle)
    return (
        jnp.concatenate([cosine] * 4, 1),
        jnp.concatenate([-sine, sine] * 2, 1),
    )


def normalize(resid, gain, bias):
    mean = jnp.mean(resid, -1, keepdims=True)
    centred = resid - mean
    inverse = lax.rsqrt(jnp.mean(centred * centred, -1, keepdims=True) + NORM_EPS)
    unit = centred * inverse
    return (unit * gain + bias, unit, inverse)


def normalize_back(grad, unit, inverse, gain):
    scaled = grad * gain
    across = (
        scaled
        - jnp.mean(scaled, -1, keepdims=True)
        - unit * jnp.mean(scaled * unit, -1, keepdims=True)
    )
    return (across * inverse, jnp.sum(grad * unit, 0, keepdims=True), jnp.sum(grad, 0, keepdims=True))


def dot(left, right):
    return jnp.dot(left, right, preferred_element_type=jnp.float32)


def dot_nt(left, right):
    return lax.dot_general(
        left, right, (((1,), (1,)), ((), ())), preferred_element_type=jnp.float32
    )


def cross(left, right):
    return lax.dot_general(
        left, right, (((0,), (0,)), ((), ())), preferred_element_type=jnp.float32
    )


def granted(shapes, margin):
    total = margin << 20
    for shape, kind in shapes:
        size = jnp.dtype(kind).itemsize
        *lead, rows, lanes = (1,) + tuple(shape)
        for n in lead:
            size *= n
        total += size * (-(-rows // 16) * 16) * (-(-lanes // 128) * 128)
    return min(max(total, 50 << 20), 60 << 20)


LOW, FULL = jnp.bfloat16, jnp.float32


class Sent:
    def __init__(self, here, there, sems):
        self.here, self.there, self.sems = here, there, sems
        self.shape, self.at = here.shape, here.at
        self.copies = []

    def __getitem__(self, at):
        return self.here[at]

    def __setitem__(self, at, value):
        self.here[at] = value

    def send(self, index=None):
        here, there = self.here, self.there
        if index is not None:
            here, there = here.at[index], there.at[index]
        copy = pltpu.make_async_copy(here, there, self.sems.at[len(self.copies)])
        copy.start()
        self.copies.append(copy)


def call(kernel, scalars, outs, ins, anys=(), scratch=(), flops=0, sent=(), margin=6):
    whole = pl.BlockSpec(memory_space=pltpu.VMEM)
    left = pl.BlockSpec(memory_space=pl.ANY)

    def body(scalars, *refs):
        refs = list(refs)
        take = lambda n: [refs.pop(0) for _ in range(n)]
        in_refs, any_refs, out_refs = take(len(ins)), take(len(anys)), take(len(outs))
        here = take(len(sent))
        for n, i in enumerate(sent):
            out_refs[i] = Sent(here[n], out_refs[i], refs[-1].at[n])
        kernel(scalars, in_refs, any_refs, out_refs, *(refs[:-1] if sent else refs))
        for i in sent:
            for copy in out_refs[i].copies:
                copy.wait()

    held = [(x.shape, x.dtype) for x in ins] + list(outs)
    held += [(x.shape, x.dtype) for x in scratch if x.memory_space == pltpu.VMEM]
    return pl.pallas_call(
        body,
        out_shape=[jax.ShapeDtypeStruct(s, t) for s, t in outs],
        in_specs=[pl.BlockSpec(memory_space=pltpu.SMEM)]
        + [whole] * len(ins)
        + [left] * len(anys),
        out_specs=[left if i in sent else whole for i in range(len(outs))],
        scratch_shapes=[pltpu.VMEM(*outs[i]) for i in sent]
        + list(scratch)
        + [pltpu.SemaphoreType.DMA((len(sent), 5))] * (len(sent) > 0),
        compiler_params=pltpu.CompilerParams(vmem_limit_bytes=granted(held, margin)),
        cost_estimate=pl.CostEstimate(
            flops=flops,
            bytes_accessed=sum(x.size * x.dtype.itemsize for x in list(ins) + list(anys)),
            transcendentals=0,
        ),
    )(scalars, *ins, *anys)


def fetch(sources, targets, sems, first=0):
    copies = [
        pltpu.make_async_copy(s, t, sems.at[first + i])
        for i, (s, t) in enumerate(zip(sources, targets))
    ]
    for c in copies:
        c.start()
    return copies


def tile_of(ref, core, at):
    return ref.at[:, core, :, at : at + ref.shape[0] * ref.shape[2]]


def matrix(ref, place, low=None, high=None):
    value = ref[place] if low is None else ref[place, :, :, low:high]
    return value.reshape(-1, value.shape[-1])


def tile_scratch(count, weights):
    blocks, _, rows, _ = weights.shape
    return pltpu.VMEM((count, blocks, rows, blocks * rows), LOW)


def swap_halves(value):
    lane = lax.broadcasted_iota(jnp.int32, value.shape, 1)
    return jnp.where(
        lax.rem(lane, HD) < HD // 2,
        pltpu.roll(value, 128 - HD // 2, 1),
        pltpu.roll(value, HD // 2, 1),
    )


def ordered(first, own, other):
    return jnp.concatenate([jnp.where(first, own, other), jnp.where(first, other, own)], 1)


def head_mask(shape, head):
    lane = lax.broadcasted_iota(jnp.int32, shape, 1)
    return (lane < HD) if head == 0 else (lane >= HD)


def attention_forward_kernel(base, place_of, ins, anys, outs, w_a, w_b, mixed, bias, sems):
    resid, seg_col, seg_row, cosine, sine, gains = ins
    middle, query, keys, values, lse, pack = outs
    (weights,) = anys
    width = resid.shape[1]
    half = width // 2
    cores = (place_of[0], 1 - place_of[0])
    copies = fetch(
        [tile_of(weights, c, base + t * width) for t in range(2) for c in cores],
        [w.at[place] for w in (w_a, w_b) for place in range(2)],
        sems,
    )
    first = place_of[0] == 0
    normed, _, _ = normalize(resid[...], gains[0:1], gains[1:2])
    normed_low, attended = pack.at[0], pack.at[1]
    normed_low[...] = normed.astype(LOW)
    bias[...] = jnp.where(seg_col[...] == seg_row[...], 0.0, -1000000000.0)
    for place in range(2):
        copies[place].wait()
        mixed[...] = dot(normed_low[...], matrix(w_a, place))
        for p in range(half // 128):
            for part, target, scale in ((0, query, HD ** (-0.5)), (1, keys, 1.0)):
                x = mixed[:, part * half + p * 128 : part * half + (p + 1) * 128]
                x = x * cosine[...] + swap_halves(x) * sine[...]
                x = (x * scale if scale != 1.0 else x).astype(LOW)
                target[:, place * half + p * 128 : place * half + (p + 1) * 128] = x
    for place in range(2):
        copies[2 + place].wait()
        values[:, place * half : (place + 1) * half] = dot(
            normed_low[...], matrix(w_b, place, 0, half)
        ).astype(LOW)

    lse[...] = jnp.zeros_like(lse)

    for p in range(width // 128):
        columns = slice(p * 128, (p + 1) * 128)
        q, k, v = query[:, columns], keys[:, columns], values[:, columns]
        out = []
        for head in range(2):
            masked_q = jnp.where(head_mask(q.shape, head), q, jnp.zeros_like(q))
            scores = dot_nt(masked_q, k) + bias[...]
            top = jnp.max(scores, -1, keepdims=True)
            expo = jnp.exp(scores - top)
            total = jnp.sum(expo, -1, keepdims=True)
            probs = (expo * (1.0 / total)).astype(LOW)
            out.append(dot(probs, v))
            lane = lax.broadcasted_iota(jnp.int32, lse.shape, 1)
            lse[...] = jnp.where(lane == 2 * p + head, top + jnp.log(total), lse[...])
        attended[:, columns] = jnp.where(head_mask(out[0].shape, 0), out[0], out[1]).astype(LOW)
    attended[...] = ordered(first, attended[:, :half], attended[:, half:])
    out = ordered(
        first,
        dot(attended[...], matrix(w_b, 0, half, width)),
        dot(attended[...], matrix(w_b, 1, half, width)),
    )
    middle[...] = resid[...] + out


def attention_forward(place, resid, weights, base, gains, cosine, sine, segments):
    length, width = resid.shape
    one = (length, width)
    return call(
        functools.partial(attention_forward_kernel, base),
        place,
        [(one, FULL)] + [(one, LOW)] * 3 + [((length, 128), FULL), ((2,) + one, LOW)],
        [resid, segments[:, None], segments[None, :], cosine, sine, gains],
        [weights],
        [
            tile_scratch(2, weights),
            tile_scratch(2, weights),
            pltpu.VMEM(one, FULL),
            pltpu.VMEM((length, length), FULL),
            pltpu.SemaphoreType.DMA((4,)),
        ],
        8 * length * width * width + 4 * length * length * width,
    )


GELU_SCALE = 0.7978845608028654
GELU_CUBE = 0.044715


def fetch_hidden(weights, base, order, ups, downs, sems):
    blocks, _, rows, _ = weights.shape
    width = blocks * rows
    half, some = width // 2, max(blocks // 4, 1)
    copies = {}
    for t, (core_of, within) in enumerate(order):
        copies[0, t] = fetch(
            [tile_of(weights, core_of, base + (2 + within) * width)], [ups.at[t]], sems, t
        )
        if blocks >= 4 or t == 0:
            sources, targets = [], []
            first = (2 * core_of + within) * some if blocks >= 4 else 0
            for core in range(2):
                for j in range(4):
                    at = base + 4 * width + j * half
                    sources.append(weights.at[pl.ds(first, some), core, :, at : at + half])
                    targets.append(
                        downs.at[pl.ds(t * some, some), j, :, core * half : (core + 1) * half]
                    )
            copies[1, t] = fetch(sources, targets, sems, 4 + 8 * t)

    def wait(which, t):
        for copy in copies.pop((which, t), []):
            copy.wait()

    return wait


def rows_of(downs, t, order):
    blocks, parts, rows, width = downs.shape
    if blocks >= 4:
        some = blocks // 4
        return downs[t * some : (t + 1) * some].reshape(some * parts * rows, width)
    return downs[0, 2 * order[t][0] + order[t][1]]


def hidden_scratch(weights):
    blocks, _, rows, _ = weights.shape
    return [
        tile_scratch(4, weights),
        pltpu.VMEM((blocks, 4, rows, blocks * rows), LOW),
        pltpu.SemaphoreType.DMA((36,)),
    ]


def hidden_forward_kernel(base, place_of, ins, anys, outs, ups, downs, sems):
    middle, gains = ins
    output, pack, hidden = outs
    order = [(t // 2, t % 2) for t in range(4)]
    wait = fetch_hidden(anys[0], base, order, ups, downs, sems)
    normed, _, _ = normalize(middle[...], gains[0:1], gains[1:2])
    pack[0] = normed.astype(LOW)
    pack.send(0)
    for t in range(4):
        wait(0, t)
        x = dot(pack[0], matrix(ups, t))
        hidden[t] = x
        hidden.send(t)
        inner = jnp.tanh(x * (GELU_SCALE + (GELU_SCALE * GELU_CUBE) * (x * x)))
        value = x * 0.5
        value = (value + value * inner).astype(LOW)
        pack[1 + t] = value
        pack.send(1 + t)
        wait(1, t)
        product = dot(value, rows_of(downs, t, order))
        output[...] = (middle[...] if t == 0 else output[...]) + product


def hidden_forward(place, middle, weights, base, gains):
    length, width = middle.shape
    one = (length, width)
    return call(
        functools.partial(hidden_forward_kernel, base),
        place,
        [(one, FULL), ((5,) + one, LOW), ((4,) + one, FULL)],
        [middle, gains],
        [weights],
        hidden_scratch(weights),
        16 * length * width * width,
        sent=(1, 2),
    )


def hidden_back_kernel(base, place_of, ins, anys, outs, ups, downs, sems, hidden_here, total, own_sems):
    branch, grad, middle, gains = ins
    hidden, weights = anys
    grad_middle, grad_gains, grad_own, grad_other = outs
    order = [(core, t) for core in (place_of[0], 1 - place_of[0]) for t in range(2)]
    wait = fetch_hidden(weights, base, order, ups, downs, sems)
    copies = fetch(
        [hidden.at[2 * core + t] for core, t in order], [hidden_here.at[t] for t in range(4)], own_sems
    )
    for t in range(4):
        wait(1, t)
        grad_active = dot_nt(branch[...], rows_of(downs, t, order))
        copies[t].wait()
        x = hidden_here[t]
        square = x * x
        inner = jnp.tanh(x * (GELU_SCALE + (GELU_SCALE * GELU_CUBE) * square))
        slope = x * (GELU_SCALE + (3.0 * GELU_SCALE * GELU_CUBE) * square)
        slope = (0.5 + 0.5 * inner) * (1.0 + slope * (1.0 - inner))
        value = (grad_active * slope).astype(LOW)
        (grad_own if t < 2 else grad_other)[t % 2] = value
        wait(0, t)
        product = dot_nt(value, matrix(ups, t))
        total[...] = product if t == 0 else total[...] + product
    _, unit, inverse = normalize(middle[...], gains[0:1], gains[1:2])
    back, gain, bias = normalize_back(total[...], unit, inverse, gains[0:1])
    grad_middle[...] = grad[...] + back
    grad_gains[0:1] = gain
    grad_gains[1:2] = bias


def hidden_back(place, grad, branch, middle, hidden, weights, base, gains):
    length, width = middle.shape
    one = (length, width)
    return call(
        functools.partial(hidden_back_kernel, base),
        place,
        [(one, FULL), ((2, width), FULL), ((2,) + one, LOW), ((2,) + one, LOW)],
        [branch, grad, middle, gains],
        [hidden, weights],
        hidden_scratch(weights)
        + [
            pltpu.VMEM((4,) + one, FULL),
            pltpu.VMEM(one, FULL),
            pltpu.SemaphoreType.DMA((4,)),
        ],
        16 * length * width * width,
    )


def attention_back_kernel(base, place_of, ins, anys, outs, w_a, w_b, bias, ga, gq, gk, gv, sems):
    grad_middle, query, keys, values, lse, seg_col, seg_row, cosine, sine, gains, resid = ins
    (weights,) = anys
    grad, branch, branch_own, branch_other, grad_gains, grad_own, grad_other = outs
    width = resid.shape[1]
    half = width // 2
    cores = (place_of[0], 1 - place_of[0])
    copies = fetch(
        [tile_of(weights, c, base + t * width) for t in (1, 0) for c in cores],
        [w.at[place] for w in (w_b, w_a) for place in range(2)],
        sems,
    )
    first = place_of[0] == 0
    grads = (grad_own, grad_other)
    bias[...] = jnp.where(seg_col[...] == seg_row[...], 0.0, -1000000000.0)
    attn_grad = grad_middle[...].astype(LOW)
    left, right = attn_grad[:, :half], attn_grad[:, half:]
    grad_own[1, :, half:] = jnp.where(first, left, right)
    grad_other[1, :, half:] = jnp.where(first, right, left)
    copies[0].wait()
    copies[1].wait()
    natural = dot_nt(grad_own[1, :, half:], matrix(w_b, 0, half, width)) + dot_nt(
        grad_other[1, :, half:], matrix(w_b, 1, half, width)
    )
    natural = natural.astype(LOW)
    ga[:, :half] = jnp.where(first, natural[:, :half], natural[:, half:])
    ga[:, half:] = jnp.where(first, natural[:, half:], natural[:, :half])

    for p in range(width // 128):
        columns = slice(p * 128, (p + 1) * 128)
        q, k, v, g = query[:, columns], keys[:, columns], values[:, columns], ga[:, columns]
        flipped = k.T
        out_q, out_k, out_v = [], [], []
        for head in range(2):
            mask = head_mask(q.shape, head)
            zero = jnp.zeros_like(q)
            scores = dot_nt(k, jnp.where(mask, q, zero)) + bias[...]
            probs = jnp.exp(scores - lse[2 * p + head : 2 * p + head + 1, :])
            grad_probs = dot_nt(v, jnp.where(mask, g, zero))
            across = jnp.sum(probs * grad_probs, 0, keepdims=True)
            grad_scores = (probs * (grad_probs - across)).astype(LOW)
            out_k.append(dot(grad_scores, q))
            out_q.append(dot(flipped[head * HD : (head + 1) * HD], grad_scores))
            out_v.append(dot(probs.astype(LOW), g))
        out_q = jnp.concatenate(out_q, 0).T * HD ** (-0.5)
        out_k = jnp.where(head_mask(out_k[0].shape, 0), out_k[0], out_k[1])
        for x, target in ((out_q, gq), (out_k, gk)):
            x = x * cosine[...] - swap_halves(x) * sine[...]
            target[:, columns] = x.astype(LOW)
        gv[:, columns] = jnp.where(head_mask(out_v[0].shape, 0), out_v[0], out_v[1]).astype(LOW)
    for place in (1, 0):
        columns = slice(place * half, (place + 1) * half)
        grads[place][0, :, :half] = gq[:, columns]
        grads[place][0, :, half:] = gk[:, columns]
        grads[place][1, :, :half] = gv[:, columns]
    copies[2].wait()
    copies[3].wait()
    total = dot_nt(grad_own[0], matrix(w_a, 0)) + dot_nt(grad_other[0], matrix(w_a, 1))
    total = total + dot_nt(grad_own[1, :, :half], matrix(w_b, 0, 0, half))
    total = total + dot_nt(grad_other[1, :, :half], matrix(w_b, 1, 0, half))
    _, unit, inverse = normalize(resid[...], gains[0:1], gains[1:2])
    back, gain, bias_grad = normalize_back(total, unit, inverse, gains[0:1])
    back = grad_middle[...] + back
    grad[...] = back
    back = back.astype(LOW)
    branch[...] = back
    branch_own[...] = jnp.where(first, back[:, :half], back[:, half:])
    branch_other[...] = jnp.where(first, back[:, half:], back[:, :half])
    grad_gains[0:1] = gain
    grad_gains[1:2] = bias_grad


def attention_back(place, grad_middle, resid, weights, base, gains, cosine, sine, segments, query, keys, values, lse):
    length, width = resid.shape
    one = (length, width)
    return call(
        functools.partial(attention_back_kernel, base),
        place,
        [(one, FULL), (one, LOW)]
        + [((length, width // 2), LOW)] * 2
        + [((2, width), FULL)]
        + [((2,) + one, LOW)] * 2,
        [grad_middle, query, keys, values, lse.T[: width // HD]]
        + [segments[:, None], segments[None, :], cosine, sine, gains, resid],
        [weights],
        [
            tile_scratch(2, weights),
            tile_scratch(2, weights),
            pltpu.VMEM((length, length), FULL),
        ]
        + [pltpu.VMEM(one, LOW)] * 4
        + [pltpu.SemaphoreType.DMA((4,))],
        8 * length * width * width + 10 * length * length * width,
    )


def adam_step(master, grad, first, second, rate, decay):
    first = BETA_ONE * first + (1.0 - BETA_ONE) * grad
    second = BETA_TWO * second + (1.0 - BETA_TWO) * grad * grad
    fix_one = 1.0 / (1.0 - BETA_ONE**STEP)
    fix_two = 1.0 / (1.0 - BETA_TWO**STEP)
    update = first * fix_one / (jnp.sqrt(second * fix_two) + ADAM_EPS) + decay * master
    return (master - rate * update, first, second)


def scale_of(totals):
    count = totals[0:1, 1:2]
    grad_norm = jnp.sqrt(totals[0:1, 2:3]) / count
    return grad_norm, CLIP / jnp.maximum(grad_norm, CLIP) / count


def optimizer_kernel(chunks, place_of, ins, anys, outs):
    totals, small_own, small_other, *rest = ins
    n = (len(rest) - 18) // 2
    own, other, masters = rest[:n], rest[n : 2 * n], rest[2 * n :]
    layers = len(chunks)
    first = place_of[0] == 0
    grad_norm, scale = scale_of(totals[...])
    outs[0][...] = grad_norm

    def step(which, at, grad, rate=RATE_MATRIX, decay=DECAY):
        master, moment, square = (masters[3 * which + i][at] for i in range(3))
        values = adam_step(master, grad * scale, moment, square, rate, decay)
        for i in range(3):
            outs[1 + 3 * which + i][at] = values[i]

    def tile(where, s, core):
        a, b = own[where[0]][where[1], s], other[where[0]][where[1], s]
        return jnp.where(first, a, b) if core == 0 else jnp.where(first, b, a)

    rows, width = own[0].shape[-2:]
    half = width // 2
    for l in range(layers):
        mixer, up, down = chunks[l]
        for core in range(2):
            columns = lambda p: pl.ds(p * width + core * half, half)
            value = tile(mixer, 0, core)
            step(0, (l, slice(None), columns(0)), value[:, :half])
            step(0, (l, slice(None), columns(1)), value[:, half:])
            value = tile(mixer, 1, core)
            step(0, (l, slice(None), columns(2)), value[:, :half])
            step(1, (l, slice(None), columns(0)), value[:, half:])
            for s in range(2):
                step(2, (l, slice(None), pl.ds((2 * core + s) * width, width)), tile(up, s, core))
                value = tile(down, s, core)
                for j in range(2):
                    at = (l, pl.ds((2 * s + j) * rows, rows), columns(0))
                    step(3, at, value[:, j * half : (j + 1) * half])
    small = jnp.where(first, small_own[...], small_other[...]).T
    step(4, (slice(None), slice(None)), small[:V])
    for n in range(masters[15].shape[0]):
        step(5, n, small[V + 2 * n : V + 2 * n + 2], RATE_VECTOR, 0.0)


def optimizer(place, totals, small, chunks, own, other, masters):
    return call(
        functools.partial(optimizer_kernel, chunks),
        place,
        [((1, 1), FULL)] + [(m.shape, m.dtype) for m in masters],
        [totals, *small, *own, *other, *masters],
        flops=20 * sum(m.size for m in masters),
    )


def pack_kernel(layers, place_of, ins, anys, outs):
    inward, outward, expand, shrink, small = ins
    (out,) = outs
    first = place_of[0] == 0
    rows = inward.shape[1]
    width = inward.shape[2] // 3
    half = width // 2
    at = small.shape[1]
    out[:, :at] = small[...]
    for l in range(layers):
        sources = [inward[l, :, p * width : (p + 1) * width] for p in range(3)] + [outward[l]]
        sources.append(expand[l])
        sources += [shrink[l, j * rows : (j + 1) * rows] for j in range(shrink.shape[1] // rows)]
        for value in sources:
            part = value.shape[1] // 2
            value = jnp.where(first, value[:, :part], value[:, part:])
            out[:, at : at + part] = value.astype(LOW)
            at += part


def swap_cores(value):
    return lax.ppermute(value, "dp", [(0, 1), (1, 0)])


def across(value, mask, size):
    return lax.ppermute(value, "fsdp", [(i, i ^ mask) for i in range(size)])


def tie(*values):
    return lax.optimization_barrier(values)


def total_of(value, size):
    value = value + swap_cores(value)
    bit = 1
    while bit < size:
        if 2 * bit < size:
            a, b, c = (across(value, m * bit, size) for m in (1, 2, 3))
            value = (value + a) + (b + c)
        else:
            value = value + across(value, bit, size)
        bit *= 4
    return value


X, Y = 1, 2
Z = (4, 8, 12)


SMALL = 128


def round_kernel(jobs, small_job, n_ins, counts, smalls, last, place_of, ins, anys, outs, *scratch):
    new, once, twice, done = counts
    small_new, small_once, small_twice, small_done = smalls
    rest = list(ins[n_ins:]) + list(outs) + list(scratch)
    pop = lambda present, n=1: [rest.pop(0) for _ in range(n)] if present else [None] * n
    (keep_once,), (small_keep_once,) = pop(once), pop(small_once)
    (keep_twice,), (small_keep_twice,) = pop(twice), pop(small_twice)
    from_x, from_y = pop(once or twice, 2)
    (keep_done,), (small_keep_done,) = pop(done), pop(small_done)
    from_z = pop(done, 3)
    (squares_in,), (sums,) = pop(done), pop(last)
    to_x, to_y = pop(new or once, 2)
    (out_once,), (small_out_once,) = pop(new), pop(small_new)
    (out_twice,), (small_out_twice,) = pop(once), pop(small_once)
    (out_done,), (small_out_done,) = pop(twice), pop(small_twice)
    to_z = pop(twice, 3)
    (share,), (small_share,), (squares,) = pop(done), pop(small_done), pop(done)
    (totals,) = pop(last)
    (tile,), (unit,), (small_tile,) = pop(new), pop(new), pop(small_new)
    rows = (out_once if new else out_twice if once else out_done if twice else share).shape[-2]
    rows = rows // (8 if new else 4 if once else 1)
    bits, z = (place_of[1], place_of[2]), place_of[3]
    to, came = (to_x, to_y), (from_x, from_y)

    def block(index, size=rows):
        if isinstance(index, int):
            return pl.ds(index * size, size)
        return pl.ds(pl.multiple_of(index * size, 16), size)

    def factor(spec):
        which, index, low, high = spec
        ref = ins[which] if index is None else ins[which].at[index]
        return ref[...] if low is None else ref[:, low:high]

    def put_small(ref, start, group, side, value):
        for q in range(rows // 16):
            lanes = side * (rows // 16) + q
            ref[pl.ds(start + group * 16, 16), lanes * SMALL : (lanes + 1) * SMALL] = value[
                q * 16 : (q + 1) * 16
            ].astype(LOW)

    def take_small(ref, start, group, side):
        parts = []
        for q in range(rows // 16):
            lanes = side * (rows // 16) + q
            at = pl.ds(pl.multiple_of(start + group * 16, 16), 16)
            parts.append(ref[at, lanes * SMALL : (lanes + 1) * SMALL])
        return jnp.concatenate(parts, 0).astype(FULL)

    def summed(products):
        total = None
        for left, right in products:
            product = cross(factor(left), factor(right))
            total = product if total is None else total + product
        return total

    for p in range(new):
        if len(jobs[p]) == 4:
            for quarter, products in enumerate(jobs[p]):
                unit[...] = summed(products)
                half = unit.shape[1]
                for index in range(4):
                    for s in range(2):
                        for j in range(2):
                            tile[s, block(quarter * 4 + index), j * half : (j + 1) * half] = unit[
                                block(index * 4 + 2 * s + j), :
                            ]
        else:
            for s in range(2):
                for low, high, products in jobs[p][s]:
                    tile[s, :, low:high] = summed(products)
        for s in range(2):
            for zz in range(4):
                for other in range(2):
                    at = zz * 2 + other
                    index = lambda bit: zz * 4 + (other * 2 + bit if s == 0 else bit * 2 + other)
                    to[s][block(p * 8 + at), :] = tile[s, block(index(1 - bits[s])), :].astype(LOW)
                    out_once[p, s, block(at), :] = tile[s, block(index(bits[s])), :]
    if small_new:
        products, norms_at = small_job
        total = summed(products)
        norms = jnp.concatenate([ins[mine][...] + ins[theirs][...] for mine, theirs in norms_at], 0)
        high = norms.astype(LOW)
        shape = (norms.shape[0], SMALL)
        column = lax.broadcasted_iota(jnp.int32, shape, 1) - V
        pick = jnp.where(lax.broadcasted_iota(jnp.int32, shape, 0) == column, 1.0, 0.0).astype(LOW)
        total = total + (cross(high, pick) + cross((norms - high.astype(FULL)).astype(LOW), pick))
        small_tile[...] = total
        for zz in range(4):
            for other in range(2):
                index = lambda bit: zz * 4 + other * 2 + bit
                send = small_tile[block(index(1 - bits[0])), :]
                put_small(to_x, (new * 8 + once * 4) * rows, other * 2 + zz // 2, zz % 2, send)
                small_out_once[block(zz * 2 + other), :] = small_tile[block(index(bits[0])), :]
    for p in range(once):
        for s in range(2):
            for zz in range(4):
                for bit in range(2):
                    at = zz * 2 + (bits[1 - s] if bit else 1 - bits[1 - s])
                    value = keep_once[p, s, block(at), :] + came[s][block(p * 8 + at), :].astype(FULL)
                    if bit:
                        out_twice[p, s, block(zz), :] = value
                    else:
                        to[1 - s][block(new * 8 + p * 4 + zz), :] = value.astype(LOW)
    if small_once:
        start = (once * 8 + twice * 4) * rows
        for zz in range(4):
            for bit in range(2):
                other = bits[1] if bit else 1 - bits[1]
                value = small_keep_once[block(zz * 2 + other), :]
                value = value + take_small(from_x, start, other * 2 + zz // 2, zz % 2)
                if bit:
                    small_out_twice[block(zz), :] = value
                else:
                    put_small(to_y, (new * 8 + once * 4) * rows, zz, 0, value)
    for p in range(twice):
        for s in range(2):
            for xor in range(4):
                at = jnp.bitwise_xor(z, xor)
                value = keep_twice[p, s, block(at), :] + came[1 - s][
                    block(once * 8 + p * 4 + at), :
                ].astype(FULL)
                if xor == 0:
                    out_done[p, s] = value
                else:
                    to_z[xor - 1][block(2 * p + s), :] = value.astype(LOW)
    if small_twice:
        for xor in range(4):
            at = jnp.bitwise_xor(z, xor)
            value = small_keep_twice[block(at), :]
            value = value + take_small(from_y, (once * 8 + twice * 4) * rows, at, 0)
            if xor == 0:
                small_out_done[...] = value
            else:
                put_small(to_z[xor - 1], twice * 2 * rows, 0, 0, value)
    if done:
        squares[...] = squares_in[...]
    for p in range(done):
        for s in range(2):
            value = keep_done[p, s]
            for f in from_z:
                value = value + f[block(2 * p + s), :].astype(FULL)
            share[p, s] = value
            squares[...] += jnp.sum(value * value, 0, keepdims=True)
    if small_done:
        value = small_keep_done[...]
        for f in from_z:
            value = value + take_small(f, done * 2 * rows, 0, 0)
        small_share[...] = value
    if last:
        total = jnp.sum(squares[...], 1, keepdims=True)
        if small_done:
            square = jnp.sum(jnp.sum(value * value, 0, keepdims=True), 1, keepdims=True)
            total = total + jnp.where(place_of[0] == 0, square, jnp.zeros_like(square))
        lane = lax.broadcasted_iota(jnp.int32, sums.shape, 1)
        totals[...] = jnp.where(lane == 2, total, sums[...])


class Rounds:
    def __init__(self, place, rows, width, sums):
        self.place, self.rows, self.width, self.sums = place, rows, width, sums
        self.counts, self.smalls = (0,) * 4, (False,) * 4
        self.kept, self.small_kept = [None] * 3, [None] * 3
        self.came = self.came_z = self.totals = None
        self.shares, self.others, self.small_share = [], [], None
        self.squares = jnp.zeros((1, width), FULL)
        self.flying, self.swapping = [], 0

    def step(self, chunk, *ties, small=None):
        rows, width = self.rows, self.width
        new, once, twice, done = counts = (len(chunk),) + self.counts[:3]
        smalls = (small is not None,) + self.smalls[:3]
        last = not (new or once or twice)
        arrays, jobs = [], []

        def number(spec):
            array, *place = spec
            for i, known in enumerate(arrays):
                if known is array:
                    return (i, *place)
            arrays.append(array)
            return (len(arrays) - 1, *place)

        numbered = lambda products: [(number(l), number(r)) for l, r in products]
        for pair in chunk:
            if len(pair) == 4:
                jobs.append([numbered(products) for products in pair])
            else:
                jobs.append([[(a, b, numbered(ps)) for a, b, ps in tile] for tile in pair])
        small_job = None
        if small is not None:
            small_job = (
                [(number(l), number(r)) for l, r in small[0]],
                [(number((a,))[0], number((b,))[0]) for a, b in small[1]],
            )
        ins = list(arrays)
        for stage in range(2):
            ins += [self.kept[stage]] * (counts[1 + stage] > 0)
            ins += [self.small_kept[stage]] * smalls[1 + stage]
        if once or twice:
            ins += self.came
        if done:
            ins += [self.kept[2]] + [self.small_kept[2]] * smalls[3] + self.came_z + [self.squares]
        ins += [self.sums] * last
        outs = []
        if new or once:
            for added in (64 * smalls[0], 64 * smalls[1]):
                outs.append((((new * 8 + once * 4) * rows + added, width), LOW))
        for stage, blocks in enumerate((8, 4, 1)):
            if counts[stage]:
                outs.append(((counts[stage], 2, blocks * rows, width), FULL))
            if smalls[stage]:
                outs.append(((blocks * rows, SMALL), FULL))
        if twice:
            outs += [((twice * 2 * rows + 16 * smalls[2], width), LOW)] * 3
        if done:
            outs.append(((done, 2, rows, width), FULL))
            outs += [((rows, SMALL), FULL)] * smalls[3]
            outs.append(((1, width), FULL))
        outs += [((1, SMALL), FULL)] * last
        length = 2 * arrays[0].shape[-2] if new else 0
        scratch = []
        if new:
            scratch.append(pltpu.VMEM((2, 16 * rows, width), FULL))
            scratch.append(pltpu.VMEM((16 * rows, width // 2), FULL))
        scratch += [pltpu.VMEM((16 * rows, SMALL), FULL)] * smalls[0]
        got = list(
            call(
                functools.partial(
                    round_kernel, jobs, small_job, len(arrays), counts, smalls, last
                ),
                self.place,
                outs,
                ins,
                [],
                scratch,
                4 * new * length * width * width,
            )
        )
        if last:
            self.totals = got.pop()
        if done:
            self.squares = got.pop()
            if smalls[3]:
                self.small_share = got.pop()
            self.shares.append(got.pop())
        self.counts, self.smalls = counts, smalls
        self.kept, self.small_kept = [None] * 3, [None] * 3
        if last:
            return ties
        got, ties = tie(got, ties)
        to = [got.pop(0) for _ in range(2)] if new or once else []
        for stage in range(3):
            if counts[stage]:
                self.kept[stage] = got.pop(0)
            if smalls[stage]:
                self.small_kept[stage] = got.pop(0)
        self.flying = [across(v, mask, 16) for v, mask in zip(to, (X, Y))]
        self.flying += [across(v, mask, 16) for v, mask in zip(got, Z)]
        self.swapping = 0
        while len(self.flying) < 5 and len(self.others) + self.swapping < len(self.shares):
            self.flying.append(swap_cores(self.shares[len(self.others) + self.swapping]))
            self.swapping += 1
        return ties

    def finish(self, *ties):
        flying, ties = tie(self.flying, ties)
        self.came = self.came_z = None
        if self.counts[0] or self.counts[1]:
            self.came, flying = flying[:2], flying[2:]
        if self.counts[2]:
            self.came_z, flying = flying[:3], flying[3:]
        self.others += flying
        return ties

    def left(self):
        return any(self.counts[:3])

    def swap_rest(self):
        self.others += [swap_cores(v) for v in self.shares[len(self.others) :]]


class PlainRounds:
    def __init__(self):
        self.shares, self.squares = [], []

    def step(self, chunk, *ties):
        def factor(spec):
            array, index, low, high = spec
            array = array if index is None else array[index]
            return array if low is None else array[:, low:high]

        summed = lambda products: sum(cross(factor(l), factor(r)) for l, r in products)
        scatter = lambda v: lax.psum_scatter(v, "fsdp", scatter_dimension=0, tiled=True)
        shares = []
        for pair in chunk:
            if len(pair) == 4:
                v = scatter(jnp.concatenate([summed(products) for products in pair], 0))
                v = v.reshape(2, 2, -1, v.shape[1])
                shares.append(jnp.concatenate([v[:, 0], v[:, 1]], 2))
            else:
                tiles = [jnp.concatenate([summed(ps) for _, _, ps in t], 1) for t in pair]
                shares.append(jnp.stack([scatter(t) for t in tiles]))
        share = jnp.stack(shares)
        self.shares.append((share, swap_cores(share)))
        self.squares.append(jnp.sum(share * share, (0, 1, 2))[None])
        return ties

    def finish(self, *ties):
        return ties

    def left(self):
        return False


def half_of(value, core):
    half = value.shape[1] // 2
    return lax.dynamic_slice_in_dim(value, core * half, half, 1)


def body(
    fsdp,
    codons,
    masked,
    segments,
    inward,
    outward,
    expand,
    shrink,
    codon_table,
    norm_params,
    inward_first,
    inward_second,
    outward_first,
    outward_second,
    expand_first,
    expand_second,
    shrink_first,
    shrink_second,
    table_first,
    table_second,
    norm_first,
    norm_second,
):
    layers = inward.shape[0]
    length = codons.shape[0]
    rows = inward.shape[1]
    width = rows * fsdp
    half = width // 2
    fast = fsdp == 16 and rows == 48
    core, index = lax.axis_index("dp"), lax.axis_index("fsdp")
    bit = lambda b: lax.rem(lax.div(index, b), 2)
    place = jnp.stack([core, bit(1), bit(2), lax.div(index, 4)]).astype(jnp.int32)
    weight = masked.astype(FULL)
    inputs = jnp.where(masked == 1, V - 1, codons)

    norms = norm_params.shape[0] * 2
    small = jnp.concatenate(
        [codon_table.astype(LOW), norm_params.astype(LOW).reshape(norms, rows)], 0
    )
    small = jnp.pad(small.T, ((0, 0), (0, -small.shape[0] % 128)))
    (weights,) = call(
        functools.partial(pack_kernel, layers),
        place,
        [((rows, small.shape[1] + layers * 6 * width), LOW)],
        [inward, outward, expand, shrink, small],
    )
    weights = lax.all_gather(weights, ("fsdp", "dp"), axis=0, tiled=True)
    weights = weights.reshape(fsdp, 2, rows, -1)
    if not fast:
        columns = [weights[:, :, :, : small.shape[1]]]
        for at in range(small.shape[1], weights.shape[3], 6 * width):
            columns.append(weights[:, :, :, at : at + 4 * width])
            quarter = weights[:, :, :, at + 4 * width : at + 6 * width]
            quarter = quarter.reshape(fsdp, 2, rows, 4, half).transpose(1, 0, 3, 2, 4)
            quarter = quarter.reshape(2, 4, width, half).transpose(0, 2, 1, 3)
            columns.append(quarter.reshape(2, fsdp, rows, 2 * width).transpose(1, 0, 2, 3))
        weights = jnp.concatenate(columns, 3).transpose(1, 0, 2, 3).reshape(1, 2, width, -1)
    small = weights[:, 0, :, : V + norms].reshape(width, V + norms).T
    base = lambda l: weights.shape[3] - (layers - l) * 6 * width
    table_low = small[:V]
    gains = small[V:].astype(FULL).reshape(-1, 2, width)

    cosine, sine = rotary_tables(length)
    vocab_ids = jnp.arange(V, dtype=jnp.int32)
    chosen = (inputs[:, None] == jnp.arange(SMALL, dtype=jnp.int32)[None, :]).astype(LOW)
    resid = dot(chosen, jnp.pad(table_low, ((0, SMALL - V), (0, 0))))
    kept = []
    for l in range(layers):
        gain = gains[2 * l : 2 * l + 2]
        middle, query, keys, values, lse, pack = attention_forward(
            place, resid, weights, base(l), gain[0], cosine, sine, segments
        )
        output, pack_mid, hidden = hidden_forward(place, middle, weights, base(l), gain[1])
        kept.append((resid, query, keys, values, lse, pack, middle, hidden, pack_mid))
        resid = output
    final_gain = gains[2 * layers]
    normed_out, unit_out, inverse_out = normalize(resid, final_gain[0], final_gain[1])
    head_in = normed_out.astype(LOW)
    logits = jnp.einsum("sd,vd->sv", head_in, table_low, preferred_element_type=FULL)
    top = jnp.max(logits, -1, keepdims=True)
    lse_head = top + jnp.log(jnp.sum(jnp.exp(logits - top), -1, keepdims=True))
    targets = (codons[:, None] == vocab_ids[None, :]).astype(FULL)
    picked = jnp.sum(logits * targets, -1)
    loss_local = jnp.sum((lse_head[:, 0] - picked) * weight)
    grad_logits = ((jnp.exp(logits - lse_head) - targets) * weight[:, None]).astype(LOW)
    grad_head = dot(grad_logits, table_low)
    grad_logits = jnp.pad(grad_logits, ((0, 0), (0, SMALL - V)))
    early = (head_in, grad_logits, chosen)
    early_came = [swap_cores(v) for v in early]
    sums = jnp.pad(jnp.stack([loss_local, jnp.sum(weight)]), (0, SMALL - 2))[None]
    grad, grad_final_gain, grad_final_bias = normalize_back(
        grad_head, unit_out, inverse_out, final_gain[0]
    )
    branch = grad.astype(LOW)
    branch_own, branch_other = half_of(branch, core), half_of(branch, 1 - core)
    grad_norms = [grad_final_gain, grad_final_bias]
    mid_came = [swap_cores(saved[-1]) for saved in kept]
    pack_came = [swap_cores(saved[5]) for saved in kept]
    grad, branch, mid_came[-1] = tie(grad, branch, mid_came[-1])

    rounds = Rounds(place, rows, width, sums) if fast else PlainRounds()
    whole = lambda array, i=None: (array, i, None, None)
    tile = lambda left, right, other_left, other_right: [
        (0, width, [(left, right), (other_left, other_right)])
    ]
    chunk = []
    for l in reversed(range(layers)):
        resid, query, keys, values, lse, pack, middle, hidden, pack_mid = kept[l]
        gain = gains[2 * l : 2 * l + 2]
        branch_came = swap_cores(branch_other)
        chunk.append(
            [
                [
                    (whole(pack_mid, 1 + t), whole(branch_own)),
                    (whole(mid_came[l], 1 + t), whole(branch_came)),
                ]
                for t in range(4)
            ]
        )
        grad, branch = rounds.step(chunk, grad, branch)
        grad_middle, gains_mid, up_own, up_other = hidden_back(
            place, grad, branch, middle, hidden, weights, base(l), gain[1]
        )
        grad_middle, up_own, up_other, early_came = rounds.finish(
            grad_middle, up_own, up_other, early_came
        )
        up_came = swap_cores(up_other)
        if l == 0:
            norms_early = jnp.concatenate([gains_mid] + grad_norms, 0)
            norms_early = (norms_early, swap_cores(norms_early))
        (grad_middle,) = rounds.step(
            [
                [
                    tile(
                        whole(pack_mid, 0), whole(up_own, s), whole(mid_came[l], 0), whole(up_came, s)
                    )
                    for s in range(2)
                ]
            ],
            grad_middle,
        )
        grad, branch, branch_own, branch_other, gains_in, mix_own, mix_other = attention_back(
            place, grad_middle, resid, weights, base(l), gain[0], cosine, sine, segments,
            query, keys, values, lse,
        )
        grad_norms = [gains_in, gains_mid] + grad_norms
        grad, branch, branch_own, branch_other, mix_own, mix_other, mid_came, pack_came = (
            rounds.finish(
                grad, branch, branch_own, branch_other, mix_own, mix_other, mid_came, pack_came
            )
        )
        mix_came = swap_cores(mix_other)
        products = lambda i, a, b: [
            ((pack, i, None, None), (mix_own, 1, a, b)),
            ((pack_came[l], i, None, None), (mix_came, 1, a, b)),
        ]
        chunk = [
            [
                tile(whole(pack, 0), whole(mix_own, 0), whole(pack_came[l], 0), whole(mix_came, 0)),
                [(0, half, products(0, 0, half)), (half, width, products(1, half, width))],
            ]
        ]
    late = (grad_norms[0], swap_cores(grad_norms[0]))
    branch_came = swap_cores(branch)
    products = [(whole(early[0]), whole(early[1])), (whole(early_came[0]), whole(early_came[1]))]
    products += [(whole(branch), whole(early[2])), (whole(branch_came), whole(early_came[2]))]
    if fast:
        rounds.step(chunk, small=(products, [late, norms_early]))
        while rounds.left():
            rounds.finish()
            rounds.step([])
        rounds.swap_rest()
        share_small = rounds.small_share
        small_other = swap_cores(share_small)
        totals = rounds.totals
    else:
        rounds.step(chunk)
        table = sum(cross(l[0], r[0]) for l, r in products)
        table = table + jnp.pad(
            jnp.concatenate([a + b for a, b in (late, norms_early)], 0).T,
            ((0, 0), (V, SMALL - V - norms)),
        )
        table = jnp.where(core == 0, table, swap_cores(table))
        share_small = lax.psum_scatter(table, "fsdp", scatter_dimension=0, tiled=True)
        squares = jnp.sum(share_small * share_small) * (core == 0)
        for value in rounds.squares:
            squares = squares + jnp.sum(value)
        totals = sums + jnp.where(jnp.arange(SMALL) == 2, squares, 0.0)[None]
    totals = total_of(totals, fsdp)
    shares = list(zip(rounds.shares, rounds.others)) if fast else rounds.shares
    places = [(2 * (layers - 1 - l), 0 if l == layers - 1 else 1) for l in range(layers)]

    def tiles_at(chunk, pair):
        own, other = (v[pair] for v in shares[chunk])
        ordered = (jnp.where(core == 0, own, other), jnp.where(core == 0, other, own))
        return [v[s] for v in ordered for s in range(2)]

    if not fast:
        share_in, share_out, share_up, share_down = [], [], [], []
        side = lambda *values: jnp.concatenate(values, 1)
        for at, pair in places:
            a_0, b_0, a_1, b_1 = tiles_at(at + 2, 0)
            share_in.append(
                side(
                    a_0[:, :half], a_1[:, :half], a_0[:, half:],
                    a_1[:, half:], b_0[:, :half], b_1[:, :half],
                )
            )
            share_out.append(side(b_0[:, half:], b_1[:, half:]))
            share_up.append(side(*tiles_at(at + 1, 0)))
            a_0, b_0, a_1, b_1 = tiles_at(at, pair)
            share_down.append(
                jnp.concatenate(
                    [
                        side(x[:, j * half : (j + 1) * half], y[:, j * half : (j + 1) * half])
                        for x, y in ((a_0, a_1), (b_0, b_1))
                        for j in range(2)
                    ],
                    0,
                )
            )
        share_in, share_out, share_up, share_down = (
            jnp.stack(v) for v in (share_in, share_out, share_up, share_down)
        )
    masters = (inward, outward, expand, shrink, codon_table, norm_params)
    firsts = (inward_first, outward_first, expand_first, shrink_first, table_first, norm_first)
    seconds = (
        inward_second,
        outward_second,
        expand_second,
        shrink_second,
        table_second,
        norm_second,
    )
    if fast:
        chunks = [((at + 2, 0), (at + 1, 0), (at, pair)) for at, pair in places]
        own, other = zip(*shares)
        states = [v for group in zip(masters, firsts, seconds) for v in group]
        grad_norm, *values = optimizer(
            place, totals, (share_small, small_other), chunks, own, other, states
        )
    else:
        grad_norm, scale = scale_of(totals)
        share_small = share_small[:, : V + norms].T
        grads = (share_in, share_out, share_up, share_down)
        grads += (share_small[:V], share_small[V:].reshape(-1, 2, rows))
        values = []
        for index, grad in enumerate(grads):
            rate, decay = (RATE_VECTOR, 0.0) if index == 5 else (RATE_MATRIX, DECAY)
            values.extend(
                adam_step(masters[index], grad * scale.reshape(()), firsts[index], seconds[index], rate, decay)
            )
    return (totals[0, 0], totals[0, 1], grad_norm.reshape(()), *values)


def solution(mesh):
    in_specs = (
        P(("fsdp", "dp")),
        P(("fsdp", "dp")),
        P(("fsdp", "dp")),
        P(None, "fsdp", None),
        P(None, "fsdp", None),
        P(None, "fsdp", None),
        P(None, "fsdp", None),
        P(None, "fsdp"),
        P(None, None, "fsdp"),
        P(None, "fsdp", None),
        P(None, "fsdp", None),
        P(None, "fsdp", None),
        P(None, "fsdp", None),
        P(None, "fsdp", None),
        P(None, "fsdp", None),
        P(None, "fsdp", None),
        P(None, "fsdp", None),
        P(None, "fsdp"),
        P(None, "fsdp"),
        P(None, None, "fsdp"),
        P(None, None, "fsdp"),
    )
    out_specs = (
        P(),
        P(),
        P(),
        P(None, "fsdp", None),
        P(None, "fsdp", None),
        P(None, "fsdp", None),
        P(None, "fsdp", None),
        P(None, "fsdp", None),
        P(None, "fsdp", None),
        P(None, "fsdp", None),
        P(None, "fsdp", None),
        P(None, "fsdp", None),
        P(None, "fsdp", None),
        P(None, "fsdp", None),
        P(None, "fsdp", None),
        P(None, "fsdp"),
        P(None, "fsdp"),
        P(None, "fsdp"),
        P(None, None, "fsdp"),
        P(None, None, "fsdp"),
        P(None, None, "fsdp"),
    )
    step = functools.partial(body, mesh.shape["fsdp"])
    return jax.shard_map(step, mesh=mesh, in_specs=in_specs, out_specs=out_specs, check_vma=False)
```

```python
import functools

import jax
import jax.numpy as jnp
from jax import lax
from jax.experimental import pallas as pl
from jax.experimental.pallas import tpu as pltpu
from jax.sharding import PartitionSpec as P

HD = 64
V = 70
STEP = 10


NORM_EPS = 1e-05
BETA_ONE = 0.9
BETA_TWO = 0.95
ADAM_EPS = 1e-08
DECAY = 0.1
RATE_MATRIX = 0.05
RATE_VECTOR = 0.3
CLIP = 0.05


def rotary_tables(length):
    freq = 10000.0 ** (-jnp.arange(HD // 2, dtype=jnp.float32) * 2.0 / HD)
    angle = jnp.arange(length, dtype=jnp.float32)[:, None] * freq[None, :]
    cosine, sine = jnp.cos(angle), jnp.sin(angle)
    return (
        jnp.concatenate([cosine] * 4, 1),
        jnp.concatenate([-sine, sine] * 2, 1),
    )


def normalize(resid, gain, bias):
    mean = jnp.mean(resid, -1, keepdims=True)
    centred = resid - mean
    inverse = lax.rsqrt(jnp.mean(centred * centred, -1, keepdims=True) + NORM_EPS)
    unit = centred * inverse
    return (unit * gain + bias, unit, inverse)


def normalize_back(grad, unit, inverse, gain):
    scaled = grad * gain
    across = (
        scaled
        - jnp.mean(scaled, -1, keepdims=True)
        - unit * jnp.mean(scaled * unit, -1, keepdims=True)
    )
    return (across * inverse, jnp.sum(grad * unit, 0, keepdims=True), jnp.sum(grad, 0, keepdims=True))


def dot(left, right):
    return jnp.dot(left, right, preferred_element_type=jnp.float32)


def dot_nt(left, right):
    return lax.dot_general(
        left, right, (((1,), (1,)), ((), ())), preferred_element_type=jnp.float32
    )


def cross(left, right):
    return lax.dot_general(
        left, right, (((0,), (0,)), ((), ())), preferred_element_type=jnp.float32
    )


VMEM_LIMIT = 56 * 1024 * 1024
LOW, FULL = jnp.bfloat16, jnp.float32
SMALL = 128


class Sent:
    def __init__(self, here, there, sems):
        self.here, self.there, self.sems = here, there, sems
        self.shape, self.at = here.shape, here.at
        self.copies = []

    def __getitem__(self, at):
        return self.here[at]

    def __setitem__(self, at, value):
        self.here[at] = value

    def send(self, index=None):
        here, there = self.here, self.there
        if index is not None:
            here, there = here.at[index], there.at[index]
        copy = pltpu.make_async_copy(here, there, self.sems.at[len(self.copies)])
        copy.start()
        self.copies.append(copy)


def call(kernel, scalars, outs, ins, anys=(), scratch=(), flops=0, sent=()):
    whole = pl.BlockSpec(memory_space=pltpu.VMEM)
    left = pl.BlockSpec(memory_space=pl.ANY)

    def body(scalars, *refs):
        refs = list(refs)
        take = lambda n: [refs.pop(0) for _ in range(n)]
        in_refs, any_refs, out_refs = take(len(ins)), take(len(anys)), take(len(outs))
        here = take(len(sent))
        for n, i in enumerate(sent):
            out_refs[i] = Sent(here[n], out_refs[i], refs[-1].at[n])
        kernel(scalars, in_refs, any_refs, out_refs, *(refs[:-1] if sent else refs))
        for i in sent:
            for copy in out_refs[i].copies:
                copy.wait()

    return pl.pallas_call(
        body,
        out_shape=[jax.ShapeDtypeStruct(s, t) for s, t in outs],
        in_specs=[pl.BlockSpec(memory_space=pltpu.SMEM)]
        + [whole] * len(ins)
        + [left] * len(anys),
        out_specs=[left if i in sent else whole for i in range(len(outs))],
        scratch_shapes=[pltpu.VMEM(*outs[i]) for i in sent]
        + list(scratch)
        + [pltpu.SemaphoreType.DMA((len(sent), 5))] * (len(sent) > 0),
        compiler_params=pltpu.CompilerParams(vmem_limit_bytes=VMEM_LIMIT),
        cost_estimate=pl.CostEstimate(
            flops=flops,
            bytes_accessed=sum(x.size * x.dtype.itemsize for x in list(ins) + list(anys)),
            transcendentals=0,
        ),
    )(scalars, *ins, *anys)


def fetch(sources, targets, sems, first=0):
    copies = [
        pltpu.make_async_copy(s, t, sems.at[first + i])
        for i, (s, t) in enumerate(zip(sources, targets))
    ]
    for c in copies:
        c.start()
    return copies


def tile_of(ref, core, at):
    return ref.at[:, core, :, at : at + ref.shape[0] * ref.shape[2]]


def matrix(ref, place, low=None, high=None):
    value = ref[place] if low is None else ref[place, :, :, low:high]
    return value.reshape(-1, value.shape[-1])


def tile_scratch(count, weights):
    blocks, _, rows, _ = weights.shape
    return pltpu.VMEM((count, blocks, rows, blocks * rows), LOW)


def swap_halves(value):
    lane = lax.broadcasted_iota(jnp.int32, value.shape, 1)
    return jnp.where(
        lax.rem(lane, HD) < HD // 2,
        pltpu.roll(value, 128 - HD // 2, 1),
        pltpu.roll(value, HD // 2, 1),
    )


def ordered(first, own, other):
    return jnp.concatenate([jnp.where(first, own, other), jnp.where(first, other, own)], 1)


def head_mask(shape, head):
    lane = lax.broadcasted_iota(jnp.int32, shape, 1)
    return (lane < HD) if head == 0 else (lane >= HD)


def attention_forward_kernel(base, place_of, ins, anys, outs, w_a, w_b, mixed, bias, sems):
    resid, seg_col, seg_row, cosine, sine, gains = ins
    middle, query, keys, values, lse, pack = outs
    (weights,) = anys
    width = resid.shape[1]
    half = width // 2
    cores = (place_of[0], 1 - place_of[0])
    copies = fetch(
        [tile_of(weights, c, base + t * width) for t in range(2) for c in cores],
        [w.at[place] for w in (w_a, w_b) for place in range(2)],
        sems,
    )
    first = place_of[0] == 0
    normed, _, _ = normalize(resid[...], gains[0:1], gains[1:2])
    normed_low, attended = pack.at[0], pack.at[1]
    normed_low[...] = normed.astype(LOW)
    bias[...] = jnp.where(seg_col[...] == seg_row[...], 0.0, -1000000000.0)
    for place in range(2):
        copies[place].wait()
        mixed[...] = dot(normed_low[...], matrix(w_a, place))
        for p in range(half // 128):
            for part, target, scale in ((0, query, HD ** (-0.5)), (1, keys, 1.0)):
                x = mixed[:, part * half + p * 128 : part * half + (p + 1) * 128]
                x = x * cosine[...] + swap_halves(x) * sine[...]
                x = (x * scale if scale != 1.0 else x).astype(LOW)
                target[:, place * half + p * 128 : place * half + (p + 1) * 128] = x
    for place in range(2):
        copies[2 + place].wait()
        values[:, place * half : (place + 1) * half] = dot(
            normed_low[...], matrix(w_b, place, 0, half)
        ).astype(LOW)

    lse[...] = jnp.zeros_like(lse)

    for p in range(width // 128):
        columns = slice(p * 128, (p + 1) * 128)
        q, k, v = query[:, columns], keys[:, columns], values[:, columns]
        out = []
        for head in range(2):
            masked_q = jnp.where(head_mask(q.shape, head), q, jnp.zeros_like(q))
            scores = dot_nt(masked_q, k) + bias[...]
            top = jnp.max(scores, -1, keepdims=True)
            expo = jnp.exp(scores - top)
            total = jnp.sum(expo, -1, keepdims=True)
            probs = (expo * (1.0 / total)).astype(LOW)
            out.append(dot(probs, v))
            lane = lax.broadcasted_iota(jnp.int32, lse.shape, 1)
            lse[...] = jnp.where(lane == 2 * p + head, top + jnp.log(total), lse[...])
        attended[:, columns] = jnp.where(head_mask(out[0].shape, 0), out[0], out[1]).astype(LOW)
    attended[...] = ordered(first, attended[:, :half], attended[:, half:])
    out = ordered(
        first,
        dot(attended[...], matrix(w_b, 0, half, width)),
        dot(attended[...], matrix(w_b, 1, half, width)),
    )
    middle[...] = resid[...] + out


def attention_forward(place, resid, weights, base, gains, cosine, sine, segments):
    length, width = resid.shape
    one = (length, width)
    return call(
        functools.partial(attention_forward_kernel, base),
        place,
        [(one, FULL)] + [(one, LOW)] * 3 + [((length, 128), FULL), ((2,) + one, LOW)],
        [resid, segments[:, None], segments[None, :], cosine, sine, gains],
        [weights],
        [
            tile_scratch(2, weights),
            tile_scratch(2, weights),
            pltpu.VMEM(one, FULL),
            pltpu.VMEM((length, length), FULL),
            pltpu.SemaphoreType.DMA((4,)),
        ],
        8 * length * width * width + 4 * length * length * width,
    )


GELU_SCALE = 0.7978845608028654
GELU_CUBE = 0.044715


def fetch_hidden(weights, base, order, ups, downs, sems):
    blocks, _, rows, _ = weights.shape
    width = blocks * rows
    half, some = width // 2, max(blocks // 4, 1)
    copies = {}
    for t, (core_of, within) in enumerate(order):
        copies[0, t] = fetch(
            [tile_of(weights, core_of, base + (2 + within) * width)], [ups.at[t]], sems, t
        )
        if blocks >= 4 or t == 0:
            sources, targets = [], []
            first = (2 * core_of + within) * some if blocks >= 4 else 0
            for core in range(2):
                for j in range(4):
                    at = base + 4 * width + j * half
                    sources.append(weights.at[pl.ds(first, some), core, :, at : at + half])
                    targets.append(
                        downs.at[pl.ds(t * some, some), j, :, core * half : (core + 1) * half]
                    )
            copies[1, t] = fetch(sources, targets, sems, 4 + 8 * t)

    def wait(which, t):
        for copy in copies.pop((which, t), []):
            copy.wait()

    return wait


def rows_of(downs, t, order):
    blocks, parts, rows, width = downs.shape
    if blocks >= 4:
        some = blocks // 4
        return downs[t * some : (t + 1) * some].reshape(some * parts * rows, width)
    return downs[0, 2 * order[t][0] + order[t][1]]


def hidden_scratch(weights):
    blocks, _, rows, _ = weights.shape
    return [
        tile_scratch(4, weights),
        pltpu.VMEM((blocks, 4, rows, blocks * rows), LOW),
        pltpu.SemaphoreType.DMA((36,)),
    ]


def hidden_forward_kernel(base, place_of, ins, anys, outs, ups, downs, sems):
    middle, gains = ins
    output, pack, hidden = outs
    order = [(t // 2, t % 2) for t in range(4)]
    wait = fetch_hidden(anys[0], base, order, ups, downs, sems)
    normed, _, _ = normalize(middle[...], gains[0:1], gains[1:2])
    pack[0] = normed.astype(LOW)
    pack.send(0)
    for t in range(4):
        wait(0, t)
        x = dot(pack[0], matrix(ups, t))
        hidden[t] = x
        hidden.send(t)
        inner = jnp.tanh(x * (GELU_SCALE + (GELU_SCALE * GELU_CUBE) * (x * x)))
        value = x * 0.5
        value = (value + value * inner).astype(LOW)
        pack[1 + t] = value
        pack.send(1 + t)
        wait(1, t)
        product = dot(value, rows_of(downs, t, order))
        output[...] = (middle[...] if t == 0 else output[...]) + product


def hidden_forward(place, middle, weights, base, gains):
    length, width = middle.shape
    one = (length, width)
    return call(
        functools.partial(hidden_forward_kernel, base),
        place,
        [(one, FULL), ((5,) + one, LOW), ((4,) + one, FULL)],
        [middle, gains],
        [weights],
        hidden_scratch(weights),
        16 * length * width * width,
        sent=(1, 2),
    )


def hidden_back_kernel(base, place_of, ins, anys, outs, ups, downs, sems, hidden_here, total, own_sems):
    branch, grad, middle, gains = ins
    hidden, weights = anys
    grad_middle, grad_gains, grad_own, grad_other = outs
    order = [(core, t) for core in (place_of[0], 1 - place_of[0]) for t in range(2)]
    wait = fetch_hidden(weights, base, order, ups, downs, sems)
    copies = fetch(
        [hidden.at[2 * core + t] for core, t in order], [hidden_here.at[t] for t in range(4)], own_sems
    )
    for t in range(4):
        wait(1, t)
        grad_active = dot_nt(branch[...], rows_of(downs, t, order))
        copies[t].wait()
        x = hidden_here[t]
        square = x * x
        inner = jnp.tanh(x * (GELU_SCALE + (GELU_SCALE * GELU_CUBE) * square))
        slope = x * (GELU_SCALE + (3.0 * GELU_SCALE * GELU_CUBE) * square)
        slope = (0.5 + 0.5 * inner) * (1.0 + slope * (1.0 - inner))
        value = (grad_active * slope).astype(LOW)
        (grad_own if t < 2 else grad_other)[t % 2] = value
        wait(0, t)
        product = dot_nt(value, matrix(ups, t))
        total[...] = product if t == 0 else total[...] + product
    _, unit, inverse = normalize(middle[...], gains[0:1], gains[1:2])
    back, gain, bias = normalize_back(total[...], unit, inverse, gains[0:1])
    grad_middle[...] = grad[...] + back
    grad_gains[0:1] = gain
    grad_gains[1:2] = bias


def hidden_back(place, grad, branch, middle, hidden, weights, base, gains):
    length, width = middle.shape
    one = (length, width)
    return call(
        functools.partial(hidden_back_kernel, base),
        place,
        [(one, FULL), ((2, width), FULL), ((2,) + one, LOW), ((2,) + one, LOW)],
        [branch, grad, middle, gains],
        [hidden, weights],
        hidden_scratch(weights)
        + [
            pltpu.VMEM((4,) + one, FULL),
            pltpu.VMEM(one, FULL),
            pltpu.SemaphoreType.DMA((4,)),
        ],
        16 * length * width * width,
    )


def attention_back_kernel(base, place_of, ins, anys, outs, w_a, w_b, bias, ga, gq, gk, gv, sems):
    grad_middle, query, keys, values, lse, seg_col, seg_row, cosine, sine, gains, resid = ins
    (weights,) = anys
    grad, branch, branch_own, branch_other, grad_gains, grad_own, grad_other = outs
    width = resid.shape[1]
    half = width // 2
    cores = (place_of[0], 1 - place_of[0])
    copies = fetch(
        [tile_of(weights, c, base + t * width) for t in (1, 0) for c in cores],
        [w.at[place] for w in (w_b, w_a) for place in range(2)],
        sems,
    )
    first = place_of[0] == 0
    grads = (grad_own, grad_other)
    bias[...] = jnp.where(seg_col[...] == seg_row[...], 0.0, -1000000000.0)
    attn_grad = grad_middle[...].astype(LOW)
    left, right = attn_grad[:, :half], attn_grad[:, half:]
    grad_own[1, :, half:] = jnp.where(first, left, right)
    grad_other[1, :, half:] = jnp.where(first, right, left)
    copies[0].wait()
    copies[1].wait()
    natural = dot_nt(grad_own[1, :, half:], matrix(w_b, 0, half, width)) + dot_nt(
        grad_other[1, :, half:], matrix(w_b, 1, half, width)
    )
    natural = natural.astype(LOW)
    ga[:, :half] = jnp.where(first, natural[:, :half], natural[:, half:])
    ga[:, half:] = jnp.where(first, natural[:, half:], natural[:, :half])

    for p in range(width // 128):
        columns = slice(p * 128, (p + 1) * 128)
        q, k, v, g = query[:, columns], keys[:, columns], values[:, columns], ga[:, columns]
        flipped = k.T
        out_q, out_k, out_v = [], [], []
        for head in range(2):
            mask = head_mask(q.shape, head)
            zero = jnp.zeros_like(q)
            scores = dot_nt(k, jnp.where(mask, q, zero)) + bias[...]
            probs = jnp.exp(scores - lse[2 * p + head : 2 * p + head + 1, :])
            grad_probs = dot_nt(v, jnp.where(mask, g, zero))
            across = jnp.sum(probs * grad_probs, 0, keepdims=True)
            grad_scores = (probs * (grad_probs - across)).astype(LOW)
            out_k.append(dot(grad_scores, q))
            out_q.append(dot(flipped[head * HD : (head + 1) * HD], grad_scores))
            out_v.append(dot(probs.astype(LOW), g))
        out_q = jnp.concatenate(out_q, 0).T * HD ** (-0.5)
        out_k = jnp.where(head_mask(out_k[0].shape, 0), out_k[0], out_k[1])
        for x, target in ((out_q, gq), (out_k, gk)):
            x = x * cosine[...] - swap_halves(x) * sine[...]
            target[:, columns] = x.astype(LOW)
        gv[:, columns] = jnp.where(head_mask(out_v[0].shape, 0), out_v[0], out_v[1]).astype(LOW)
    for place in (1, 0):
        columns = slice(place * half, (place + 1) * half)
        grads[place][0, :, :half] = gq[:, columns]
        grads[place][0, :, half:] = gk[:, columns]
        grads[place][1, :, :half] = gv[:, columns]
    copies[2].wait()
    copies[3].wait()
    total = dot_nt(grad_own[0], matrix(w_a, 0)) + dot_nt(grad_other[0], matrix(w_a, 1))
    total = total + dot_nt(grad_own[1, :, :half], matrix(w_b, 0, 0, half))
    total = total + dot_nt(grad_other[1, :, :half], matrix(w_b, 1, 0, half))
    _, unit, inverse = normalize(resid[...], gains[0:1], gains[1:2])
    back, gain, bias_grad = normalize_back(total, unit, inverse, gains[0:1])
    back = grad_middle[...] + back
    grad[...] = back
    back = back.astype(LOW)
    branch[...] = back
    branch_own[...] = jnp.where(first, back[:, :half], back[:, half:])
    branch_other[...] = jnp.where(first, back[:, half:], back[:, :half])
    grad_gains[0:1] = gain
    grad_gains[1:2] = bias_grad


def attention_back(place, grad_middle, resid, weights, base, gains, cosine, sine, segments, query, keys, values, lse):
    length, width = resid.shape
    one = (length, width)
    return call(
        functools.partial(attention_back_kernel, base),
        place,
        [(one, FULL), (one, LOW)]
        + [((length, width // 2), LOW)] * 2
        + [((2, width), FULL)]
        + [((2,) + one, LOW)] * 2,
        [grad_middle, query, keys, values, lse.T[: width // HD]]
        + [segments[:, None], segments[None, :], cosine, sine, gains, resid],
        [weights],
        [
            tile_scratch(2, weights),
            tile_scratch(2, weights),
            pltpu.VMEM((length, length), FULL),
        ]
        + [pltpu.VMEM(one, LOW)] * 4
        + [pltpu.SemaphoreType.DMA((4,))],
        8 * length * width * width + 10 * length * length * width,
    )


def head_kernel(place_of, ins, anys, outs):
    resid, table, gains, codons, weight = ins
    grad, branch, branch_own, branch_other, head_in, grad_logits, grad_gains, sums = outs
    half = resid.shape[1] // 2
    normed, unit, inverse = normalize(resid[...], gains[0:1], gains[1:2])
    head_in[...] = normed.astype(LOW)
    logits = dot_nt(head_in[...], table[...])
    lane = lax.broadcasted_iota(jnp.int32, logits.shape, 1)
    logits = jnp.where(lane < V, logits, -1e30)
    top = jnp.max(logits, 1, keepdims=True)
    lse = top + jnp.log(jnp.sum(jnp.exp(logits - top), 1, keepdims=True))
    hot = jnp.where(lane == codons[...], 1.0, 0.0)
    picked = jnp.sum(logits * hot, 1, keepdims=True)
    loss = jnp.sum((lse - picked) * weight[...], 0, keepdims=True)
    count = jnp.sum(weight[...], 0, keepdims=True)
    lane = lax.broadcasted_iota(jnp.int32, sums.shape, 1)
    sums[...] = jnp.where(lane == 0, loss, jnp.where(lane == 1, count, 0.0))
    grad_logits[...] = ((jnp.exp(logits - lse) - hot) * weight[...]).astype(LOW)
    back, gain, bias = normalize_back(
        dot(grad_logits[...], table[...]), unit, inverse, gains[0:1]
    )
    grad[...] = back
    back = back.astype(LOW)
    branch[...] = back
    first = place_of[0] == 0
    branch_own[...] = jnp.where(first, back[:, :half], back[:, half:])
    branch_other[...] = jnp.where(first, back[:, half:], back[:, :half])
    grad_gains[0:1] = gain
    grad_gains[1:2] = bias


def head(place, resid, table, gains, codons, weight):
    length, width = resid.shape
    one, part = (length, width), (length, width // 2)
    return call(
        head_kernel,
        place,
        [(one, FULL), (one, LOW), (part, LOW), (part, LOW), (one, LOW)]
        + [((length, SMALL), LOW), ((2, width), FULL), ((1, SMALL), FULL)],
        [resid, table, gains, codons[:, None], weight[:, None]],
        flops=4 * length * width * SMALL,
    )


def adam_step(master, grad, first, second, rate, decay):
    first = BETA_ONE * first + (1.0 - BETA_ONE) * grad
    second = BETA_TWO * second + (1.0 - BETA_TWO) * grad * grad
    fix_one = 1.0 / (1.0 - BETA_ONE**STEP)
    fix_two = 1.0 / (1.0 - BETA_TWO**STEP)
    update = first * fix_one / (jnp.sqrt(second * fix_two) + ADAM_EPS) + decay * master
    return (master - rate * update, first, second)


def scale_of(totals):
    count = totals[0:1, 1:2]
    grad_norm = jnp.sqrt(totals[0:1, 2:3]) / count
    return grad_norm, CLIP / jnp.maximum(grad_norm, CLIP) / count


def optimizer_kernel(chunks, place_of, ins, anys, outs, *scratch):
    *masters, sems = scratch
    copies = fetch(anys, masters, sems)
    totals, small_own, small_other, *rest = ins
    n = (len(rest) - 6) // 2
    own, other = rest[:n], rest[n : 2 * n]
    masters += rest[2 * n :]
    layers = len(chunks)
    first = place_of[0] == 0
    grad_norm, scale = scale_of(totals[...])
    outs[0][...] = grad_norm

    def step(which, at, grad, rate=RATE_MATRIX, decay=DECAY):
        master, moment, square = (masters[3 * which + i][at] for i in range(3))
        values = adam_step(master, grad * scale, moment, square, rate, decay)
        for i in range(3):
            outs[1 + 3 * which + i][at] = values[i]

    def tile(where, s, core):
        a, b = own[where[0]][where[1], s], other[where[0]][where[1], s]
        return jnp.where(first, a, b) if core == 0 else jnp.where(first, b, a)

    def arrive(*which):
        for copy in copies[3 * which[0] : 3 * which[-1] + 3]:
            copy.wait()

    def leave(which):
        for i in range(3):
            outs[1 + 3 * which + i].send()

    rows, width = own[0].shape[-2:]
    half = width // 2
    arrive(0, 1)
    for l in range(layers):
        for core in range(2):
            columns = lambda p: pl.ds(p * width + core * half, half)
            value = tile(chunks[l][0], 0, core)
            step(0, (l, slice(None), columns(0)), value[:, :half])
            step(0, (l, slice(None), columns(1)), value[:, half:])
            value = tile(chunks[l][0], 1, core)
            step(0, (l, slice(None), columns(2)), value[:, :half])
            step(1, (l, slice(None), columns(0)), value[:, half:])
    leave(0)
    leave(1)
    arrive(2)
    for l in range(layers):
        for core in range(2):
            for s in range(2):
                at = (l, slice(None), pl.ds((2 * core + s) * width, width))
                step(2, at, tile(chunks[l][1], s, core))
    leave(2)
    arrive(3)
    for l in range(layers):
        for core in range(2):
            for s in range(2):
                value = tile(chunks[l][2], s, core)
                for j in range(2):
                    at = (l, pl.ds((2 * s + j) * rows, rows), pl.ds(core * half, half))
                    step(3, at, value[:, j * half : (j + 1) * half])
    leave(3)
    small = jnp.where(first, small_own[...], small_other[...])
    step(4, (slice(None), slice(None)), small[:, :V])
    small = small.T
    for n in range(masters[15].shape[0]):
        step(5, n, small[V + 2 * n : V + 2 * n + 2], RATE_VECTOR, 0.0)


def optimizer(place, totals, small, chunks, own, other, masters):
    return call(
        functools.partial(optimizer_kernel, chunks),
        place,
        [((1, 1), FULL)] + [(m.shape, m.dtype) for m in masters],
        [totals, *small, *own, *other, *masters[12:]],
        masters[:12],
        [pltpu.VMEM(m.shape, m.dtype) for m in masters[:12]] + [pltpu.SemaphoreType.DMA((12,))],
        flops=20 * sum(m.size for m in masters),
        sent=range(1, 13),
    )


def pack_kernel(layers, place_of, ins, anys, outs):
    inward, outward, expand, shrink, small = ins
    (out,) = outs
    first = place_of[0] == 0
    rows = inward.shape[1]
    width = inward.shape[2] // 3
    half = width // 2
    at = small.shape[1]
    out[:, :at] = small[...]
    for l in range(layers):
        sources = [inward[l, :, p * width : (p + 1) * width] for p in range(3)] + [outward[l]]
        sources.append(expand[l])
        sources += [shrink[l, j * rows : (j + 1) * rows] for j in range(shrink.shape[1] // rows)]
        for value in sources:
            part = value.shape[1] // 2
            value = jnp.where(first, value[:, :part], value[:, part:])
            out[:, at : at + part] = value.astype(LOW)
            at += part


def swap_cores(value):
    return lax.ppermute(value, "dp", [(0, 1), (1, 0)])


def across(value, mask, size):
    return lax.ppermute(value, "fsdp", [(i, i ^ mask) for i in range(size)])


def tie(*values):
    return lax.optimization_barrier(values)


def total_of(value, size):
    value = value + swap_cores(value)
    bit = 1
    while bit < size:
        if 2 * bit < size:
            a, b, c = (across(value, m * bit, size) for m in (1, 2, 3))
            value = (value + a) + (b + c)
        else:
            value = value + across(value, bit, size)
        bit *= 4
    return value


X, Y = 1, 2
Z = (4, 8, 12)


def round_kernel(jobs, small_job, n_ins, counts, smalls, last, place_of, ins, anys, outs, *scratch):
    new, once, twice, done = counts
    small_new, small_once, small_twice, small_done = smalls
    rest = list(ins[n_ins:]) + list(outs) + list(scratch)
    pop = lambda present, n=1: [rest.pop(0) for _ in range(n)] if present else [None] * n
    (keep_once,), (small_keep_once,) = pop(once), pop(small_once)
    (keep_twice,), (small_keep_twice,) = pop(twice), pop(small_twice)
    from_x, from_y = pop(once or twice, 2)
    (keep_done,), (small_keep_done,) = pop(done), pop(small_done)
    from_z = pop(done, 3)
    (squares_in,), (sums,) = pop(done), pop(last)
    to_x, to_y = pop(new or once, 2)
    (out_once,), (small_out_once,) = pop(new), pop(small_new)
    (out_twice,), (small_out_twice,) = pop(once), pop(small_once)
    (out_done,), (small_out_done,) = pop(twice), pop(small_twice)
    to_z = pop(twice, 3)
    (share,), (small_share,), (squares,) = pop(done), pop(small_done), pop(done)
    (totals,) = pop(last)
    (tile,), (unit,), (small_tile,) = pop(new), pop(new), pop(small_new)
    rows = (out_once if new else out_twice if once else out_done if twice else share).shape[-2]
    rows = rows // (8 if new else 4 if once else 1)
    bits, z = (place_of[1], place_of[2]), place_of[3]
    to, came = (to_x, to_y), (from_x, from_y)

    def block(index, size=rows):
        if isinstance(index, int):
            return pl.ds(index * size, size)
        return pl.ds(pl.multiple_of(index * size, 16), size)

    def factor(spec):
        which, index, low, high = spec
        ref = ins[which] if index is None else ins[which].at[index]
        return ref[...] if low is None else ref[:, low:high]

    def put_small(ref, start, group, side, value):
        for q in range(rows // 16):
            lanes = side * (rows // 16) + q
            ref[pl.ds(start + group * 16, 16), lanes * SMALL : (lanes + 1) * SMALL] = value[
                q * 16 : (q + 1) * 16
            ].astype(LOW)

    def take_small(ref, start, group, side):
        parts = []
        for q in range(rows // 16):
            lanes = side * (rows // 16) + q
            at = pl.ds(pl.multiple_of(start + group * 16, 16), 16)
            parts.append(ref[at, lanes * SMALL : (lanes + 1) * SMALL])
        return jnp.concatenate(parts, 0).astype(FULL)

    def summed(products):
        total = None
        for left, right in products:
            product = cross(factor(left), factor(right))
            total = product if total is None else total + product
        return total

    for p in range(new):
        if len(jobs[p]) == 4:
            for quarter, products in enumerate(jobs[p]):
                unit[...] = summed(products)
                half = unit.shape[1]
                for index in range(4):
                    for s in range(2):
                        for j in range(2):
                            tile[s, block(quarter * 4 + index), j * half : (j + 1) * half] = unit[
                                block(index * 4 + 2 * s + j), :
                            ]
        else:
            for s in range(2):
                for low, high, products in jobs[p][s]:
                    tile[s, :, low:high] = summed(products)
        for s in range(2):
            for zz in range(4):
                for other in range(2):
                    at = zz * 2 + other
                    index = lambda bit: zz * 4 + (other * 2 + bit if s == 0 else bit * 2 + other)
                    to[s][block(p * 8 + at), :] = tile[s, block(index(1 - bits[s])), :].astype(LOW)
                    out_once[p, s, block(at), :] = tile[s, block(index(bits[s])), :]
    if small_new:
        products, norms_at = small_job
        total = summed(products)
        norms = jnp.concatenate([ins[mine][...] + ins[theirs][...] for mine, theirs in norms_at], 0)
        high = norms.astype(LOW)
        shape = (norms.shape[0], SMALL)
        column = lax.broadcasted_iota(jnp.int32, shape, 1) - V
        pick = jnp.where(lax.broadcasted_iota(jnp.int32, shape, 0) == column, 1.0, 0.0).astype(LOW)
        total = total + (cross(high, pick) + cross((norms - high.astype(FULL)).astype(LOW), pick))
        small_tile[...] = total
        for zz in range(4):
            for other in range(2):
                index = lambda bit: zz * 4 + other * 2 + bit
                send = small_tile[block(index(1 - bits[0])), :]
                put_small(to_x, (new * 8 + once * 4) * rows, other * 2 + zz // 2, zz % 2, send)
                small_out_once[block(zz * 2 + other), :] = small_tile[block(index(bits[0])), :]
    for p in range(once):
        for s in range(2):
            for zz in range(4):
                for bit in range(2):
                    at = zz * 2 + (bits[1 - s] if bit else 1 - bits[1 - s])
                    value = keep_once[p, s, block(at), :] + came[s][block(p * 8 + at), :].astype(FULL)
                    if bit:
                        out_twice[p, s, block(zz), :] = value
                    else:
                        to[1 - s][block(new * 8 + p * 4 + zz), :] = value.astype(LOW)
    if small_once:
        start = (once * 8 + twice * 4) * rows
        for zz in range(4):
            for bit in range(2):
                other = bits[1] if bit else 1 - bits[1]
                value = small_keep_once[block(zz * 2 + other), :]
                value = value + take_small(from_x, start, other * 2 + zz // 2, zz % 2)
                if bit:
                    small_out_twice[block(zz), :] = value
                else:
                    put_small(to_y, (new * 8 + once * 4) * rows, zz, 0, value)
    for p in range(twice):
        for s in range(2):
            for xor in range(4):
                at = jnp.bitwise_xor(z, xor)
                value = keep_twice[p, s, block(at), :] + came[1 - s][
                    block(once * 8 + p * 4 + at), :
                ].astype(FULL)
                if xor == 0:
                    out_done[p, s] = value
                else:
                    to_z[xor - 1][block(2 * p + s), :] = value.astype(LOW)
    if small_twice:
        for xor in range(4):
            at = jnp.bitwise_xor(z, xor)
            value = small_keep_twice[block(at), :]
            value = value + take_small(from_y, (once * 8 + twice * 4) * rows, at, 0)
            if xor == 0:
                small_out_done[...] = value
            else:
                put_small(to_z[xor - 1], twice * 2 * rows, 0, 0, value)
    if done:
        squares[...] = squares_in[...]
    for p in range(done):
        for s in range(2):
            value = keep_done[p, s]
            for f in from_z:
                value = value + f[block(2 * p + s), :].astype(FULL)
            share[p, s] = value
            squares[...] += jnp.sum(value * value, 0, keepdims=True)
    if small_done:
        value = small_keep_done[...]
        for f in from_z:
            value = value + take_small(f, done * 2 * rows, 0, 0)
        small_share[...] = value
    if last:
        total = jnp.sum(squares[...], 1, keepdims=True)
        if small_done:
            square = jnp.sum(jnp.sum(value * value, 0, keepdims=True), 1, keepdims=True)
            total = total + jnp.where(place_of[0] == 0, square, jnp.zeros_like(square))
        lane = lax.broadcasted_iota(jnp.int32, sums.shape, 1)
        totals[...] = jnp.where(lane == 2, total, sums[...])


class Rounds:
    def __init__(self, place, rows, width, sums):
        self.place, self.rows, self.width, self.sums = place, rows, width, sums
        self.counts, self.smalls = (0,) * 4, (False,) * 4
        self.kept, self.small_kept = [None] * 3, [None] * 3
        self.came = self.came_z = self.totals = None
        self.shares, self.others, self.small_share = [], [], None
        self.squares = jnp.zeros((1, width), FULL)
        self.flying, self.swapping = [], 0

    def step(self, chunk, *ties, small=None):
        rows, width = self.rows, self.width
        new, once, twice, done = counts = (len(chunk),) + self.counts[:3]
        smalls = (small is not None,) + self.smalls[:3]
        last = not (new or once or twice)
        arrays, jobs = [], []

        def number(spec):
            array, *place = spec
            for i, known in enumerate(arrays):
                if known is array:
                    return (i, *place)
            arrays.append(array)
            return (len(arrays) - 1, *place)

        numbered = lambda products: [(number(l), number(r)) for l, r in products]
        for pair in chunk:
            if len(pair) == 4:
                jobs.append([numbered(products) for products in pair])
            else:
                jobs.append([[(a, b, numbered(ps)) for a, b, ps in tile] for tile in pair])
        small_job = None
        if small is not None:
            small_job = (
                [(number(l), number(r)) for l, r in small[0]],
                [(number((a,))[0], number((b,))[0]) for a, b in small[1]],
            )
        ins = list(arrays)
        for stage in range(2):
            ins += [self.kept[stage]] * (counts[1 + stage] > 0)
            ins += [self.small_kept[stage]] * smalls[1 + stage]
        if once or twice:
            ins += self.came
        if done:
            ins += [self.kept[2]] + [self.small_kept[2]] * smalls[3] + self.came_z + [self.squares]
        ins += [self.sums] * last
        outs = []
        if new or once:
            for added in (64 * smalls[0], 64 * smalls[1]):
                outs.append((((new * 8 + once * 4) * rows + added, width), LOW))
        for stage, blocks in enumerate((8, 4, 1)):
            if counts[stage]:
                outs.append(((counts[stage], 2, blocks * rows, width), FULL))
            if smalls[stage]:
                outs.append(((blocks * rows, SMALL), FULL))
        if twice:
            outs += [((twice * 2 * rows + 16 * smalls[2], width), LOW)] * 3
        if done:
            outs.append(((done, 2, rows, width), FULL))
            outs += [((rows, SMALL), FULL)] * smalls[3]
            outs.append(((1, width), FULL))
        outs += [((1, SMALL), FULL)] * last
        length = 2 * arrays[0].shape[-2] if new else 0
        scratch = []
        if new:
            scratch.append(pltpu.VMEM((2, 16 * rows, width), FULL))
            scratch.append(pltpu.VMEM((16 * rows, width // 2), FULL))
        scratch += [pltpu.VMEM((16 * rows, SMALL), FULL)] * smalls[0]
        got = list(
            call(
                functools.partial(
                    round_kernel, jobs, small_job, len(arrays), counts, smalls, last
                ),
                self.place,
                outs,
                ins,
                [],
                scratch,
                4 * new * length * width * width,
            )
        )
        if last:
            self.totals = got.pop()
        if done:
            self.squares = got.pop()
            if smalls[3]:
                self.small_share = got.pop()
            self.shares.append(got.pop())
        self.counts, self.smalls = counts, smalls
        self.kept, self.small_kept = [None] * 3, [None] * 3
        if last:
            return ties
        got, ties = tie(got, ties)
        to = [got.pop(0) for _ in range(2)] if new or once else []
        for stage in range(3):
            if counts[stage]:
                self.kept[stage] = got.pop(0)
            if smalls[stage]:
                self.small_kept[stage] = got.pop(0)
        self.flying = [across(v, mask, 16) for v, mask in zip(to, (X, Y))]
        self.flying += [across(v, mask, 16) for v, mask in zip(got, Z)]
        self.swapping = 0
        while len(self.flying) < 5 and len(self.others) + self.swapping < len(self.shares):
            self.flying.append(swap_cores(self.shares[len(self.others) + self.swapping]))
            self.swapping += 1
        return ties

    def finish(self, *ties):
        flying, ties = tie(self.flying, ties)
        self.came = self.came_z = None
        if self.counts[0] or self.counts[1]:
            self.came, flying = flying[:2], flying[2:]
        if self.counts[2]:
            self.came_z, flying = flying[:3], flying[3:]
        self.others += flying
        return ties

    def left(self):
        return any(self.counts[:3])

    def swap_rest(self):
        self.others += [swap_cores(v) for v in self.shares[len(self.others) :]]


class PlainRounds:
    def __init__(self):
        self.shares, self.squares = [], []

    def step(self, chunk, *ties):
        def factor(spec):
            array, index, low, high = spec
            array = array if index is None else array[index]
            return array if low is None else array[:, low:high]

        summed = lambda products: sum(cross(factor(l), factor(r)) for l, r in products)
        scatter = lambda v: lax.psum_scatter(v, "fsdp", scatter_dimension=0, tiled=True)
        shares = []
        for pair in chunk:
            if len(pair) == 4:
                v = scatter(jnp.concatenate([summed(products) for products in pair], 0))
                v = v.reshape(2, 2, -1, v.shape[1])
                shares.append(jnp.concatenate([v[:, 0], v[:, 1]], 2))
            else:
                tiles = [jnp.concatenate([summed(ps) for _, _, ps in t], 1) for t in pair]
                shares.append(jnp.stack([scatter(t) for t in tiles]))
        share = jnp.stack(shares)
        self.shares.append((share, swap_cores(share)))
        self.squares.append(jnp.sum(share * share, (0, 1, 2))[None])
        return ties

    def finish(self, *ties):
        return ties

    def left(self):
        return False


def half_of(value, core):
    half = value.shape[1] // 2
    return lax.dynamic_slice_in_dim(value, core * half, half, 1)


def body(
    fsdp,
    codons,
    masked,
    segments,
    inward,
    outward,
    expand,
    shrink,
    codon_table,
    norm_params,
    inward_first,
    inward_second,
    outward_first,
    outward_second,
    expand_first,
    expand_second,
    shrink_first,
    shrink_second,
    table_first,
    table_second,
    norm_first,
    norm_second,
):
    layers = inward.shape[0]
    length = codons.shape[0]
    rows = inward.shape[1]
    width = rows * fsdp
    half = width // 2
    fast = fsdp == 16 and rows == 48
    core, index = lax.axis_index("dp"), lax.axis_index("fsdp")
    bit = lambda b: lax.rem(lax.div(index, b), 2)
    place = jnp.stack([core, bit(1), bit(2), lax.div(index, 4)]).astype(jnp.int32)
    weight = masked.astype(FULL)
    inputs = jnp.where(masked == 1, V - 1, codons)

    norms = norm_params.shape[0] * 2
    small = jnp.concatenate(
        [codon_table.astype(LOW), norm_params.astype(LOW).reshape(norms, rows)], 0
    )
    small = jnp.pad(small.T, ((0, 0), (0, -small.shape[0] % 128)))
    (weights,) = call(
        functools.partial(pack_kernel, layers),
        place,
        [((rows, small.shape[1] + layers * 6 * width), LOW)],
        [inward, outward, expand, shrink, small],
    )
    weights = lax.all_gather(weights, ("fsdp", "dp"), axis=0, tiled=True)
    weights = weights.reshape(fsdp, 2, rows, -1)
    if not fast:
        columns = [weights[:, :, :, : small.shape[1]]]
        for at in range(small.shape[1], weights.shape[3], 6 * width):
            columns.append(weights[:, :, :, at : at + 4 * width])
            quarter = weights[:, :, :, at + 4 * width : at + 6 * width]
            quarter = quarter.reshape(fsdp, 2, rows, 4, half).transpose(1, 0, 3, 2, 4)
            quarter = quarter.reshape(2, 4, width, half).transpose(0, 2, 1, 3)
            columns.append(quarter.reshape(2, fsdp, rows, 2 * width).transpose(1, 0, 2, 3))
        weights = jnp.concatenate(columns, 3).transpose(1, 0, 2, 3).reshape(1, 2, width, -1)
    small = weights[:, 0, :, :SMALL].reshape(width, SMALL).T
    base = lambda l: weights.shape[3] - (layers - l) * 6 * width
    gains = small[V : V + norms].astype(FULL).reshape(-1, 2, width)

    cosine, sine = rotary_tables(length)
    chosen = (inputs[:, None] == jnp.arange(SMALL, dtype=jnp.int32)[None, :]).astype(LOW)
    resid = dot(chosen, small)
    kept = []
    for l in range(layers):
        gain = gains[2 * l : 2 * l + 2]
        middle, query, keys, values, lse, pack = attention_forward(
            place, resid, weights, base(l), gain[0], cosine, sine, segments
        )
        output, pack_mid, hidden = hidden_forward(place, middle, weights, base(l), gain[1])
        kept.append((resid, query, keys, values, lse, pack, middle, hidden, pack_mid))
        resid = output
    grad, branch, branch_own, branch_other, head_in, grad_logits, grad_norms, sums = head(
        place, resid, small, gains[2 * layers], codons, weight
    )
    grad_norms = [grad_norms]
    early = (head_in, grad_logits, chosen)
    early_came = [swap_cores(v) for v in early]
    mid_came = [swap_cores(saved[-1]) for saved in kept]
    pack_came = [swap_cores(saved[5]) for saved in kept]
    grad, branch, mid_came[-1] = tie(grad, branch, mid_came[-1])

    rounds = Rounds(place, rows, width, sums) if fast else PlainRounds()
    whole = lambda array, i=None: (array, i, None, None)
    tile = lambda left, right, other_left, other_right: [
        (0, width, [(left, right), (other_left, other_right)])
    ]
    chunk = []
    for l in reversed(range(layers)):
        resid, query, keys, values, lse, pack, middle, hidden, pack_mid = kept[l]
        gain = gains[2 * l : 2 * l + 2]
        branch_came = swap_cores(branch_other)
        chunk.append(
            [
                [
                    (whole(pack_mid, 1 + t), whole(branch_own)),
                    (whole(mid_came[l], 1 + t), whole(branch_came)),
                ]
                for t in range(4)
            ]
        )
        grad, branch = rounds.step(chunk, grad, branch)
        grad_middle, gains_mid, up_own, up_other = hidden_back(
            place, grad, branch, middle, hidden, weights, base(l), gain[1]
        )
        grad_middle, up_own, up_other, early_came = rounds.finish(
            grad_middle, up_own, up_other, early_came
        )
        up_came = swap_cores(up_other)
        if l == 0:
            norms_early = jnp.concatenate([gains_mid] + grad_norms, 0)
            norms_early = (norms_early, swap_cores(norms_early))
        (grad_middle,) = rounds.step(
            [
                [
                    tile(
                        whole(pack_mid, 0), whole(up_own, s), whole(mid_came[l], 0), whole(up_came, s)
                    )
                    for s in range(2)
                ]
            ],
            grad_middle,
        )
        grad, branch, branch_own, branch_other, gains_in, mix_own, mix_other = attention_back(
            place, grad_middle, resid, weights, base(l), gain[0], cosine, sine, segments,
            query, keys, values, lse,
        )
        grad_norms = [gains_in, gains_mid] + grad_norms
        grad, branch, branch_own, branch_other, mix_own, mix_other, mid_came, pack_came = (
            rounds.finish(
                grad, branch, branch_own, branch_other, mix_own, mix_other, mid_came, pack_came
            )
        )
        mix_came = swap_cores(mix_other)
        products = lambda i, a, b: [
            ((pack, i, None, None), (mix_own, 1, a, b)),
            ((pack_came[l], i, None, None), (mix_came, 1, a, b)),
        ]
        chunk = [
            [
                tile(whole(pack, 0), whole(mix_own, 0), whole(pack_came[l], 0), whole(mix_came, 0)),
                [(0, half, products(0, 0, half)), (half, width, products(1, half, width))],
            ]
        ]
    late = (grad_norms[0], swap_cores(grad_norms[0]))
    branch_came = swap_cores(branch)
    products = [(whole(early[0]), whole(early[1])), (whole(early_came[0]), whole(early_came[1]))]
    products += [(whole(branch), whole(early[2])), (whole(branch_came), whole(early_came[2]))]
    if fast:
        rounds.step(chunk, small=(products, [late, norms_early]))
        while rounds.left():
            rounds.finish()
            rounds.step([])
        rounds.swap_rest()
        share_small = rounds.small_share
        small_other = swap_cores(share_small)
        totals = rounds.totals
    else:
        rounds.step(chunk)
        table = sum(cross(l[0], r[0]) for l, r in products)
        table = table + jnp.pad(
            jnp.concatenate([a + b for a, b in (late, norms_early)], 0).T,
            ((0, 0), (V, SMALL - V - norms)),
        )
        table = jnp.where(core == 0, table, swap_cores(table))
        share_small = lax.psum_scatter(table, "fsdp", scatter_dimension=0, tiled=True)
        squares = jnp.sum(share_small * share_small) * (core == 0)
        for value in rounds.squares:
            squares = squares + jnp.sum(value)
        totals = sums + jnp.where(jnp.arange(SMALL) == 2, squares, 0.0)[None]
    totals = total_of(totals, fsdp)
    shares = list(zip(rounds.shares, rounds.others)) if fast else rounds.shares
    places = [(2 * (layers - 1 - l), 0 if l == layers - 1 else 1) for l in range(layers)]

    def tiles_at(chunk, pair):
        own, other = (v[pair] for v in shares[chunk])
        ordered = (jnp.where(core == 0, own, other), jnp.where(core == 0, other, own))
        return [v[s] for v in ordered for s in range(2)]

    if not fast:
        share_in, share_out, share_up, share_down = [], [], [], []
        side = lambda *values: jnp.concatenate(values, 1)
        for at, pair in places:
            a_0, b_0, a_1, b_1 = tiles_at(at + 2, 0)
            share_in.append(
                side(
                    a_0[:, :half], a_1[:, :half], a_0[:, half:],
                    a_1[:, half:], b_0[:, :half], b_1[:, :half],
                )
            )
            share_out.append(side(b_0[:, half:], b_1[:, half:]))
            share_up.append(side(*tiles_at(at + 1, 0)))
            a_0, b_0, a_1, b_1 = tiles_at(at, pair)
            share_down.append(
                jnp.concatenate(
                    [
                        side(x[:, j * half : (j + 1) * half], y[:, j * half : (j + 1) * half])
                        for x, y in ((a_0, a_1), (b_0, b_1))
                        for j in range(2)
                    ],
                    0,
                )
            )
        share_in, share_out, share_up, share_down = (
            jnp.stack(v) for v in (share_in, share_out, share_up, share_down)
        )
    masters = (inward, outward, expand, shrink, codon_table, norm_params)
    firsts = (inward_first, outward_first, expand_first, shrink_first, table_first, norm_first)
    seconds = (
        inward_second,
        outward_second,
        expand_second,
        shrink_second,
        table_second,
        norm_second,
    )
    if fast:
        chunks = [((at + 2, 0), (at + 1, 0), (at, pair)) for at, pair in places]
        own, other = zip(*shares)
        states = [v for group in zip(masters, firsts, seconds) for v in group]
        states[12:15] = [v.T for v in states[12:15]]
        grad_norm, *values = optimizer(
            place, totals, (share_small, small_other), chunks, own, other, states
        )
        values[12:15] = [v.T for v in values[12:15]]
    else:
        grad_norm, scale = scale_of(totals)
        share_small = share_small[:, : V + norms].T
        grads = (share_in, share_out, share_up, share_down)
        grads += (share_small[:V], share_small[V:].reshape(-1, 2, rows))
        values = []
        for index, grad in enumerate(grads):
            rate, decay = (RATE_VECTOR, 0.0) if index == 5 else (RATE_MATRIX, DECAY)
            values.extend(
                adam_step(masters[index], grad * scale.reshape(()), firsts[index], seconds[index], rate, decay)
            )
    return (totals[0, 0], totals[0, 1], grad_norm.reshape(()), *values)


def solution(mesh):
    in_specs = (
        P(("fsdp", "dp")),
        P(("fsdp", "dp")),
        P(("fsdp", "dp")),
        P(None, "fsdp", None),
        P(None, "fsdp", None),
        P(None, "fsdp", None),
        P(None, "fsdp", None),
        P(None, "fsdp"),
        P(None, None, "fsdp"),
        P(None, "fsdp", None),
        P(None, "fsdp", None),
        P(None, "fsdp", None),
        P(None, "fsdp", None),
        P(None, "fsdp", None),
        P(None, "fsdp", None),
        P(None, "fsdp", None),
        P(None, "fsdp", None),
        P(None, "fsdp"),
        P(None, "fsdp"),
        P(None, None, "fsdp"),
        P(None, None, "fsdp"),
    )
    out_specs = (
        P(),
        P(),
        P(),
        P(None, "fsdp", None),
        P(None, "fsdp", None),
        P(None, "fsdp", None),
        P(None, "fsdp", None),
        P(None, "fsdp", None),
        P(None, "fsdp", None),
        P(None, "fsdp", None),
        P(None, "fsdp", None),
        P(None, "fsdp", None),
        P(None, "fsdp", None),
        P(None, "fsdp", None),
        P(None, "fsdp", None),
        P(None, "fsdp"),
        P(None, "fsdp"),
        P(None, "fsdp"),
        P(None, None, "fsdp"),
        P(None, None, "fsdp"),
        P(None, None, "fsdp"),
    )
    step = functools.partial(body, mesh.shape["fsdp"])
    return jax.shard_map(step, mesh=mesh, in_specs=in_specs, out_specs=out_specs, check_vma=False)
```

```python
import functools

import jax
import jax.numpy as jnp
from jax import lax
from jax.experimental import pallas as pl
from jax.experimental.pallas import tpu as pltpu
from jax.sharding import PartitionSpec as P

HD = 64
V = 70
STEP = 10


NORM_EPS = 1e-05
BETA_ONE = 0.9
BETA_TWO = 0.95
ADAM_EPS = 1e-08
DECAY = 0.1
RATE_MATRIX = 0.05
RATE_VECTOR = 0.3
CLIP = 0.05


def rotary_tables(length):
    freq = 10000.0 ** (-jnp.arange(HD // 2, dtype=jnp.float32) * 2.0 / HD)
    angle = jnp.arange(length, dtype=jnp.float32)[:, None] * freq[None, :]
    cosine, sine = jnp.cos(angle), jnp.sin(angle)
    return (
        jnp.concatenate([cosine] * 4, 1),
        jnp.concatenate([-sine, sine] * 2, 1),
    )


def normalize(resid, gain, bias):
    mean = jnp.mean(resid, -1, keepdims=True)
    centred = resid - mean
    inverse = lax.rsqrt(jnp.mean(centred * centred, -1, keepdims=True) + NORM_EPS)
    unit = centred * inverse
    return (unit * gain + bias, unit, inverse)


def normalize_back(grad, unit, inverse, gain):
    scaled = grad * gain
    across = (
        scaled
        - jnp.mean(scaled, -1, keepdims=True)
        - unit * jnp.mean(scaled * unit, -1, keepdims=True)
    )
    return (across * inverse, jnp.sum(grad * unit, 0, keepdims=True), jnp.sum(grad, 0, keepdims=True))


def dot(left, right):
    return jnp.dot(left, right, preferred_element_type=jnp.float32)


def dot_nt(left, right):
    return lax.dot_general(
        left, right, (((1,), (1,)), ((), ())), preferred_element_type=jnp.float32
    )


def cross(left, right):
    return lax.dot_general(
        left, right, (((0,), (0,)), ((), ())), preferred_element_type=jnp.float32
    )


VMEM_LIMIT = 56 * 1024 * 1024
LOW, FULL = jnp.bfloat16, jnp.float32
SMALL = 128


class Sent:
    def __init__(self, here, there, sems):
        self.here, self.there, self.sems = here, there, sems
        self.shape, self.at = here.shape, here.at
        self.copies = []

    def __getitem__(self, at):
        return self.here[at]

    def __setitem__(self, at, value):
        self.here[at] = value

    def send(self, index=None):
        here, there = self.here, self.there
        if index is not None:
            here, there = here.at[index], there.at[index]
        copy = pltpu.make_async_copy(here, there, self.sems.at[len(self.copies)])
        copy.start()
        self.copies.append(copy)


def call(kernel, scalars, outs, ins, anys=(), scratch=(), flops=0, sent=()):
    whole = pl.BlockSpec(memory_space=pltpu.VMEM)
    left = pl.BlockSpec(memory_space=pl.ANY)

    def body(scalars, *refs):
        refs = list(refs)
        take = lambda n: [refs.pop(0) for _ in range(n)]
        in_refs, any_refs, out_refs = take(len(ins)), take(len(anys)), take(len(outs))
        here = take(len(sent))
        for n, i in enumerate(sent):
            out_refs[i] = Sent(here[n], out_refs[i], refs[-1].at[n])
        kernel(scalars, in_refs, any_refs, out_refs, *(refs[:-1] if sent else refs))
        for i in sent:
            for copy in out_refs[i].copies:
                copy.wait()

    return pl.pallas_call(
        body,
        out_shape=[jax.ShapeDtypeStruct(s, t) for s, t in outs],
        in_specs=[pl.BlockSpec(memory_space=pltpu.SMEM)]
        + [whole] * len(ins)
        + [left] * len(anys),
        out_specs=[left if i in sent else whole for i in range(len(outs))],
        scratch_shapes=[pltpu.VMEM(*outs[i]) for i in sent]
        + list(scratch)
        + [pltpu.SemaphoreType.DMA((len(sent), 5))] * (len(sent) > 0),
        compiler_params=pltpu.CompilerParams(vmem_limit_bytes=VMEM_LIMIT),
        cost_estimate=pl.CostEstimate(
            flops=flops,
            bytes_accessed=sum(x.size * x.dtype.itemsize for x in list(ins) + list(anys)),
            transcendentals=0,
        ),
    )(scalars, *ins, *anys)


def fetch(sources, targets, sems, first=0):
    copies = [
        pltpu.make_async_copy(s, t, sems.at[first + i])
        for i, (s, t) in enumerate(zip(sources, targets))
    ]
    for c in copies:
        c.start()
    return copies


def tile_of(ref, core, at):
    return ref.at[:, core, :, at : at + ref.shape[0] * ref.shape[2]]


def matrix(ref, place, low=None, high=None):
    value = ref[place] if low is None else ref[place, :, :, low:high]
    return value.reshape(-1, value.shape[-1])


def tile_scratch(count, weights):
    blocks, rows = (weights.shape[0], weights.shape[2])
    return pltpu.VMEM((count, blocks, rows, blocks * rows), LOW)


def mixer_tile(anys, cores, place, t, base, width):
    if len(anys) == 2:
        return anys[place].at[t]
    return tile_of(anys[0], cores[place], base + t * width)


def mixer_scratch(weights):
    w = weights[0]
    blocks, rows = (w.shape[1], w.shape[2]) if len(weights) == 2 else (w.shape[0], w.shape[2])
    return [pltpu.VMEM((2, blocks, rows, blocks * rows), LOW)] * 2


def swap_halves(value):
    lane = lax.broadcasted_iota(jnp.int32, value.shape, 1)
    return jnp.where(
        lax.rem(lane, HD) < HD // 2,
        pltpu.roll(value, 128 - HD // 2, 1),
        pltpu.roll(value, HD // 2, 1),
    )


def ordered(first, own, other):
    return jnp.concatenate([jnp.where(first, own, other), jnp.where(first, other, own)], 1)


def head_mask(shape, head):
    lane = lax.broadcasted_iota(jnp.int32, shape, 1)
    return (lane < HD) if head == 0 else (lane >= HD)


def attention_forward_kernel(base, place_of, ins, anys, outs, w_a, w_b, mixed, bias, sems):
    resid, seg_col, seg_row, cosine, sine, gains = ins
    middle, query, keys, values, lse, pack = outs
    width = resid.shape[1]
    half = width // 2
    cores = (place_of[0], 1 - place_of[0])
    copies = fetch(
        [mixer_tile(anys, cores, p, t, base, width) for t in range(2) for p in range(2)],
        [w.at[place] for w in (w_a, w_b) for place in range(2)],
        sems,
    )
    first = place_of[0] == 0
    normed, _, _ = normalize(resid[...], gains[0:1], gains[1:2])
    normed_low, attended = pack.at[0], pack.at[1]
    normed_low[...] = normed.astype(LOW)
    bias[...] = jnp.where(seg_col[...] == seg_row[...], 0.0, -1000000000.0)
    for place in range(2):
        copies[place].wait()
        mixed[...] = dot(normed_low[...], matrix(w_a, place))
        for p in range(half // 128):
            for part, target, scale in ((0, query, HD ** (-0.5)), (1, keys, 1.0)):
                x = mixed[:, part * half + p * 128 : part * half + (p + 1) * 128]
                x = x * cosine[...] + swap_halves(x) * sine[...]
                x = (x * scale if scale != 1.0 else x).astype(LOW)
                target[:, place * half + p * 128 : place * half + (p + 1) * 128] = x
    for place in range(2):
        copies[2 + place].wait()
        values[:, place * half : (place + 1) * half] = dot(
            normed_low[...], matrix(w_b, place, 0, half)
        ).astype(LOW)

    lse[...] = jnp.zeros_like(lse)

    for p in range(width // 128):
        columns = slice(p * 128, (p + 1) * 128)
        q, k, v = query[:, columns], keys[:, columns], values[:, columns]
        out = []
        for head in range(2):
            masked_q = jnp.where(head_mask(q.shape, head), q, jnp.zeros_like(q))
            scores = dot_nt(masked_q, k) + bias[...]
            top = jnp.max(scores, -1, keepdims=True)
            expo = jnp.exp(scores - top)
            total = jnp.sum(expo, -1, keepdims=True)
            probs = (expo * (1.0 / total)).astype(LOW)
            out.append(dot(probs, v))
            lane = lax.broadcasted_iota(jnp.int32, lse.shape, 1)
            lse[...] = jnp.where(lane == 2 * p + head, top + jnp.log(total), lse[...])
        attended[:, columns] = jnp.where(head_mask(out[0].shape, 0), out[0], out[1]).astype(LOW)
    attended[...] = ordered(first, attended[:, :half], attended[:, half:])
    out = ordered(
        first,
        dot(attended[...], matrix(w_b, 0, half, width)),
        dot(attended[...], matrix(w_b, 1, half, width)),
    )
    middle[...] = resid[...] + out


def attention_forward(place, resid, weights, base, gains, cosine, sine, segments):
    length, width = resid.shape
    one = (length, width)
    return call(
        functools.partial(attention_forward_kernel, base),
        place,
        [(one, FULL)] + [(one, LOW)] * 3 + [((length, 128), FULL), ((2,) + one, LOW)],
        [resid, segments[:, None], segments[None, :], cosine, sine, gains],
        weights,
        mixer_scratch(weights)
        + [
            pltpu.VMEM(one, FULL),
            pltpu.VMEM((length, length), FULL),
            pltpu.SemaphoreType.DMA((4,)),
        ],
        8 * length * width * width + 4 * length * length * width,
    )


GELU_SCALE = 0.7978845608028654
GELU_CUBE = 0.044715


def fetch_hidden(weights, base, order, ups, downs, sems, between=lambda t: None, down_first=False):
    blocks, _, rows, _ = weights.shape
    width = blocks * rows
    half, some = width // 2, max(blocks // 4, 1)
    copies = {}
    for t, (core_of, within) in enumerate(order):
        up = lambda: fetch(
            [tile_of(weights, core_of, base + (2 + within) * width)], [ups.at[t]], sems, t
        )
        if not down_first:
            copies[0, t] = up()
        if blocks >= 4 or t == 0:
            sources, targets = [], []
            first = (2 * core_of + within) * some if blocks >= 4 else 0
            for core in range(2):
                for j in range(4):
                    at = base + 4 * width + j * half
                    sources.append(weights.at[pl.ds(first, some), core, :, at : at + half])
                    targets.append(
                        downs.at[pl.ds(t * some, some), j, :, core * half : (core + 1) * half]
                    )
            copies[1, t] = fetch(sources, targets, sems, 4 + 8 * t)
        between(t)
        if down_first:
            copies[0, t] = up()

    def wait(which, t):
        for copy in copies.pop((which, t), []):
            copy.wait()

    return wait


def rows_of(downs, t, order):
    blocks, parts, rows, width = downs.shape
    if blocks >= 4:
        some = blocks // 4
        return downs[t * some : (t + 1) * some].reshape(some * parts * rows, width)
    return downs[0, 2 * order[t][0] + order[t][1]]


def hidden_scratch(weights):
    blocks, _, rows, _ = weights.shape
    return [
        tile_scratch(4, weights),
        pltpu.VMEM((blocks, 4, rows, blocks * rows), LOW),
        pltpu.SemaphoreType.DMA((36,)),
    ]


def hidden_forward_kernel(base, place_of, ins, anys, outs, ups, downs, sems):
    middle, gains = ins
    output, pack, hidden = outs
    order = [(t // 2, t % 2) for t in range(4)]
    wait = fetch_hidden(anys[0], base, order, ups, downs, sems)
    normed, _, _ = normalize(middle[...], gains[0:1], gains[1:2])
    pack[0] = normed.astype(LOW)
    pack.send(0)
    for t in range(4):
        wait(0, t)
        x = dot(pack[0], matrix(ups, t))
        hidden[t] = x
        hidden.send(t)
        inner = jnp.tanh(x * (GELU_SCALE + (GELU_SCALE * GELU_CUBE) * (x * x)))
        value = x * 0.5
        value = (value + value * inner).astype(LOW)
        pack[1 + t] = value
        pack.send(1 + t)
        wait(1, t)
        product = dot(value, rows_of(downs, t, order))
        output[...] = (middle[...] if t == 0 else output[...]) + product


def hidden_forward(place, middle, weights, base, gains):
    length, width = middle.shape
    one = (length, width)
    return call(
        functools.partial(hidden_forward_kernel, base),
        place,
        [(one, FULL), ((5,) + one, LOW), ((4,) + one, FULL)],
        [middle, gains],
        [weights],
        hidden_scratch(weights),
        16 * length * width * width,
        sent=(1, 2),
    )


def hidden_back_kernel(base, place_of, ins, anys, outs, ups, downs, sems, hidden_here, total, own_sems):
    branch, grad, middle, gains = ins
    hidden, weights = anys
    grad_middle, grad_gains, grad_own, grad_other = outs
    order = [(core, t) for core in (place_of[0], 1 - place_of[0]) for t in range(2)]
    copies = []

    def fetch_values(t):
        source = hidden.at[2 * order[t][0] + order[t][1]]
        copies.extend(fetch([source], [hidden_here.at[t]], own_sems, t))

    wait = fetch_hidden(weights, base, order, ups, downs, sems, fetch_values, down_first=True)
    for t in range(4):
        wait(1, t)
        grad_active = dot_nt(branch[...], rows_of(downs, t, order))
        copies[t].wait()
        x = hidden_here[t]
        square = x * x
        inner = jnp.tanh(x * (GELU_SCALE + (GELU_SCALE * GELU_CUBE) * square))
        slope = x * (GELU_SCALE + (3.0 * GELU_SCALE * GELU_CUBE) * square)
        slope = (0.5 + 0.5 * inner) * (1.0 + slope * (1.0 - inner))
        value = (grad_active * slope).astype(LOW)
        (grad_own if t < 2 else grad_other)[t % 2] = value
        wait(0, t)
        product = dot_nt(value, matrix(ups, t))
        total[...] = product if t == 0 else total[...] + product
    _, unit, inverse = normalize(middle[...], gains[0:1], gains[1:2])
    back, gain, bias = normalize_back(total[...], unit, inverse, gains[0:1])
    grad_middle[...] = grad[...] + back
    grad_gains[0:1] = gain
    grad_gains[1:2] = bias


def hidden_back(place, grad, branch, middle, hidden, weights, base, gains):
    length, width = middle.shape
    one = (length, width)
    return call(
        functools.partial(hidden_back_kernel, base),
        place,
        [(one, FULL), ((2, width), FULL), ((2,) + one, LOW), ((2,) + one, LOW)],
        [branch, grad, middle, gains],
        [hidden, weights],
        hidden_scratch(weights)
        + [
            pltpu.VMEM((4,) + one, FULL),
            pltpu.VMEM(one, FULL),
            pltpu.SemaphoreType.DMA((4,)),
        ],
        16 * length * width * width,
    )


def attention_back_kernel(base, place_of, ins, anys, outs, w_a, w_b, bias, ga, gq, gk, gv, sems):
    grad_middle, query, keys, values, lse, seg_col, seg_row, cosine, sine, gains, resid = ins
    grad, branch, branch_own, branch_other, grad_gains, grad_own, grad_other = outs
    width = resid.shape[1]
    half = width // 2
    cores = (place_of[0], 1 - place_of[0])
    copies = fetch(
        [mixer_tile(anys, cores, p, t, base, width) for t in (1, 0) for p in range(2)],
        [w.at[place] for w in (w_b, w_a) for place in range(2)],
        sems,
    )
    first = place_of[0] == 0
    grads = (grad_own, grad_other)
    bias[...] = jnp.where(seg_col[...] == seg_row[...], 0.0, -1000000000.0)
    attn_grad = grad_middle[...].astype(LOW)
    left, right = attn_grad[:, :half], attn_grad[:, half:]
    grad_own[1, :, half:] = jnp.where(first, left, right)
    grad_other[1, :, half:] = jnp.where(first, right, left)
    copies[0].wait()
    copies[1].wait()
    natural = dot_nt(grad_own[1, :, half:], matrix(w_b, 0, half, width)) + dot_nt(
        grad_other[1, :, half:], matrix(w_b, 1, half, width)
    )
    natural = natural.astype(LOW)
    ga[:, :half] = jnp.where(first, natural[:, :half], natural[:, half:])
    ga[:, half:] = jnp.where(first, natural[:, half:], natural[:, :half])

    for p in range(width // 128):
        columns = slice(p * 128, (p + 1) * 128)
        q, k, v, g = query[:, columns], keys[:, columns], values[:, columns], ga[:, columns]
        flipped = k.T
        out_q, out_k, out_v = [], [], []
        for head in range(2):
            mask = head_mask(q.shape, head)
            zero = jnp.zeros_like(q)
            scores = dot_nt(k, jnp.where(mask, q, zero)) + bias[...]
            probs = jnp.exp(scores - lse[2 * p + head : 2 * p + head + 1, :])
            grad_probs = dot_nt(v, jnp.where(mask, g, zero))
            across = jnp.sum(probs * grad_probs, 0, keepdims=True)
            grad_scores = (probs * (grad_probs - across)).astype(LOW)
            out_k.append(dot(grad_scores, q))
            out_q.append(dot(flipped[head * HD : (head + 1) * HD], grad_scores))
            out_v.append(dot(probs.astype(LOW), g))
        out_q = jnp.concatenate(out_q, 0).T * HD ** (-0.5)
        out_k = jnp.where(head_mask(out_k[0].shape, 0), out_k[0], out_k[1])
        for x, target in ((out_q, gq), (out_k, gk)):
            x = x * cosine[...] - swap_halves(x) * sine[...]
            target[:, columns] = x.astype(LOW)
        gv[:, columns] = jnp.where(head_mask(out_v[0].shape, 0), out_v[0], out_v[1]).astype(LOW)
    for place in (1, 0):
        columns = slice(place * half, (place + 1) * half)
        grads[place][0, :, :half] = gq[:, columns]
        grads[place][0, :, half:] = gk[:, columns]
        grads[place][1, :, :half] = gv[:, columns]
    copies[2].wait()
    copies[3].wait()
    total = dot_nt(grad_own[0], matrix(w_a, 0)) + dot_nt(grad_other[0], matrix(w_a, 1))
    total = total + dot_nt(grad_own[1, :, :half], matrix(w_b, 0, 0, half))
    total = total + dot_nt(grad_other[1, :, :half], matrix(w_b, 1, 0, half))
    _, unit, inverse = normalize(resid[...], gains[0:1], gains[1:2])
    back, gain, bias_grad = normalize_back(total, unit, inverse, gains[0:1])
    back = grad_middle[...] + back
    grad[...] = back
    back = back.astype(LOW)
    branch[...] = back
    branch_own[...] = jnp.where(first, back[:, :half], back[:, half:])
    branch_other[...] = jnp.where(first, back[:, half:], back[:, :half])
    grad_gains[0:1] = gain
    grad_gains[1:2] = bias_grad


def attention_back(place, grad_middle, resid, weights, base, gains, cosine, sine, segments, query, keys, values, lse):
    length, width = resid.shape
    one = (length, width)
    return call(
        functools.partial(attention_back_kernel, base),
        place,
        [(one, FULL), (one, LOW)]
        + [((length, width // 2), LOW)] * 2
        + [((2, width), FULL)]
        + [((2,) + one, LOW)] * 2,
        [grad_middle, query, keys, values, lse.T[: width // HD]]
        + [segments[:, None], segments[None, :], cosine, sine, gains, resid],
        weights,
        mixer_scratch(weights)
        + [
            pltpu.VMEM((length, length), FULL),
        ]
        + [pltpu.VMEM(one, LOW)] * 4
        + [pltpu.SemaphoreType.DMA((4,))],
        8 * length * width * width + 10 * length * length * width,
    )


def head_kernel(place_of, ins, anys, outs):
    resid, table, gains, codons, weight = ins
    grad, branch, branch_own, branch_other, head_in, grad_logits, grad_gains, sums = outs
    half = resid.shape[1] // 2
    normed, unit, inverse = normalize(resid[...], gains[0:1], gains[1:2])
    head_in[...] = normed.astype(LOW)
    logits = dot_nt(head_in[...], table[...])
    lane = lax.broadcasted_iota(jnp.int32, logits.shape, 1)
    logits = jnp.where(lane < V, logits, -1e30)
    top = jnp.max(logits, 1, keepdims=True)
    lse = top + jnp.log(jnp.sum(jnp.exp(logits - top), 1, keepdims=True))
    hot = jnp.where(lane == codons[...], 1.0, 0.0)
    picked = jnp.sum(logits * hot, 1, keepdims=True)
    loss = jnp.sum((lse - picked) * weight[...], 0, keepdims=True)
    count = jnp.sum(weight[...], 0, keepdims=True)
    lane = lax.broadcasted_iota(jnp.int32, sums.shape, 1)
    sums[...] = jnp.where(lane == 0, loss, jnp.where(lane == 1, count, 0.0))
    grad_logits[...] = ((jnp.exp(logits - lse) - hot) * weight[...]).astype(LOW)
    back, gain, bias = normalize_back(
        dot(grad_logits[...], table[...]), unit, inverse, gains[0:1]
    )
    grad[...] = back
    back = back.astype(LOW)
    branch[...] = back
    first = place_of[0] == 0
    branch_own[...] = jnp.where(first, back[:, :half], back[:, half:])
    branch_other[...] = jnp.where(first, back[:, half:], back[:, :half])
    grad_gains[0:1] = gain
    grad_gains[1:2] = bias


def head(place, resid, table, gains, codons, weight):
    length, width = resid.shape
    one, part = (length, width), (length, width // 2)
    return call(
        head_kernel,
        place,
        [(one, FULL), (one, LOW), (part, LOW), (part, LOW), (one, LOW)]
        + [((length, SMALL), LOW), ((2, width), FULL), ((1, SMALL), FULL)],
        [resid, table, gains, codons[:, None], weight[:, None]],
        flops=4 * length * width * SMALL,
    )


def adam_step(master, grad, first, second, rate, decay):
    first = BETA_ONE * first + (1.0 - BETA_ONE) * grad
    second = BETA_TWO * second + (1.0 - BETA_TWO) * grad * grad
    fix_one = 1.0 / (1.0 - BETA_ONE**STEP)
    fix_two = 1.0 / (1.0 - BETA_TWO**STEP)
    update = first * fix_one / (jnp.sqrt(second * fix_two) + ADAM_EPS) + decay * master
    return (master - rate * update, first, second)


def scale_of(totals):
    count = totals[0:1, 1:2]
    grad_norm = jnp.sqrt(totals[0:1, 2:3]) / count
    return grad_norm, CLIP / jnp.maximum(grad_norm, CLIP) / count


def optimizer_kernel(chunks, place_of, ins, anys, outs, *scratch):
    *masters, sems = scratch
    copies = fetch(anys, masters, sems)
    totals, small_own, small_other, *rest = ins
    n = (len(rest) - 6) // 2
    own, other = rest[:n], rest[n : 2 * n]
    masters += rest[2 * n :]
    layers = len(chunks)
    first = place_of[0] == 0
    grad_norm, scale = scale_of(totals[...])
    outs[0][...] = grad_norm

    def step(which, at, grad, rate=RATE_MATRIX, decay=DECAY):
        master, moment, square = (masters[3 * which + i][at] for i in range(3))
        values = adam_step(master, grad * scale, moment, square, rate, decay)
        for i in range(3):
            outs[1 + 3 * which + i][at] = values[i]

    def tile(where, s, core):
        a, b = own[where[0]][where[1], s], other[where[0]][where[1], s]
        return jnp.where(first, a, b) if core == 0 else jnp.where(first, b, a)

    def arrive(*which):
        for copy in copies[3 * which[0] : 3 * which[-1] + 3]:
            copy.wait()

    def leave(which):
        for i in range(3):
            outs[1 + 3 * which + i].send()

    rows, width = own[0].shape[-2:]
    half = width // 2
    arrive(0, 1)
    for l in range(layers):
        for core in range(2):
            columns = lambda p: pl.ds(p * width + core * half, half)
            value = tile(chunks[l][0], 0, core)
            step(0, (l, slice(None), columns(0)), value[:, :half])
            step(0, (l, slice(None), columns(1)), value[:, half:])
            value = tile(chunks[l][0], 1, core)
            step(0, (l, slice(None), columns(2)), value[:, :half])
            step(1, (l, slice(None), columns(0)), value[:, half:])
    leave(0)
    leave(1)
    arrive(2)
    for l in range(layers):
        for core in range(2):
            for s in range(2):
                at = (l, slice(None), pl.ds((2 * core + s) * width, width))
                step(2, at, tile(chunks[l][1], s, core))
    leave(2)
    arrive(3)
    for l in range(layers):
        for core in range(2):
            for s in range(2):
                value = tile(chunks[l][2], s, core)
                for j in range(2):
                    at = (l, pl.ds((2 * s + j) * rows, rows), pl.ds(core * half, half))
                    step(3, at, value[:, j * half : (j + 1) * half])
    leave(3)
    small = jnp.where(first, small_own[...], small_other[...])
    step(4, (slice(None), slice(None)), small[:, :V])
    small = small.T
    for n in range(masters[15].shape[0]):
        step(5, n, small[V + 2 * n : V + 2 * n + 2], RATE_VECTOR, 0.0)


def optimizer(place, totals, small, chunks, own, other, masters):
    return call(
        functools.partial(optimizer_kernel, chunks),
        place,
        [((1, 1), FULL)] + [(m.shape, m.dtype) for m in masters],
        [totals, *small, *own, *other, *masters[12:]],
        masters[:12],
        [pltpu.VMEM(m.shape, m.dtype) for m in masters[:12]] + [pltpu.SemaphoreType.DMA((12,))],
        flops=20 * sum(m.size for m in masters),
        sent=range(1, 13),
    )


def pack_kernel(layers, place_of, ins, anys, outs):
    inward, outward, expand, shrink, small = ins
    out, *early = outs
    first = place_of[0] == 0
    rows = inward.shape[1]
    width = inward.shape[2] // 3
    half = width // 2
    at = 0
    if early:
        early[0][rows : rows + 16] = jnp.zeros((16, width), LOW)
        for q in range(rows // 16):
            early[0][rows : rows + 16, q * SMALL : (q + 1) * SMALL] = small[q * 16 : (q + 1) * 16]
    else:
        at = small.shape[1]
        out[:, :at] = small[...]
    for l in range(layers):
        sources = [inward[l, :, p * width : (p + 1) * width] for p in range(3)] + [outward[l]]
        sources.append(expand[l])
        sources += [shrink[l, j * rows : (j + 1) * rows] for j in range(shrink.shape[1] // rows)]
        for n, value in enumerate(sources):
            part = value.shape[1] // 2
            value = jnp.where(first, value[:, :part], value[:, part:]).astype(LOW)
            if early and l == 0 and n < 4:
                start = 0 if n < 2 else rows + 16
                early[0][start : start + rows, (n % 2) * half : (n % 2 + 1) * half] = value
                continue
            out[:, at : at + part] = value
            at += part


def swap_cores(value):
    return lax.ppermute(value, "dp", [(0, 1), (1, 0)])


def across(value, mask, size):
    return lax.ppermute(value, "fsdp", [(i, i ^ mask) for i in range(size)])


def tie(*values):
    return lax.optimization_barrier(values)


def total_of(value, size):
    value = value + swap_cores(value)
    bit = 1
    while bit < size:
        if 2 * bit < size:
            a, b, c = (across(value, m * bit, size) for m in (1, 2, 3))
            value = (value + a) + (b + c)
        else:
            value = value + across(value, bit, size)
        bit *= 4
    return value


def arrange_kernel(parts, place_of, ins, anys, outs, sems):
    copies, at = [], 0
    for h in range(2):
        for piece in anys:
            copies += fetch(
                [piece.at[h * parts[0] : h * parts[0] + parts[h]]],
                [outs[0].at[at : at + parts[h]]],
                sems,
                len(copies),
            )
            at += parts[h]
    for copy in copies:
        copy.wait()


def place_kernel(parts, rows, place_of, ins, anys, outs, sems):
    quarter, from_x, from_y, far_a, far_b = anys
    tiles, small = outs
    x, y, z = place_of[1], place_of[2], place_of[3]
    for n in range(16):
        xor_z, xor_y, xor_x = n // 4, n // 2 % 2, n % 2
        index = jnp.bitwise_xor(z, xor_z) * 4 + jnp.bitwise_xor(y, xor_y) * 2 + jnp.bitwise_xor(x, xor_x)
        for h in range(2):
            at = xor_z * parts[h]
            if xor_x and xor_y:
                source = (far_a, far_b)[h]
            else:
                source = from_x if xor_x else from_y if xor_y else quarter
                at += h * 4 * parts[0]
            fetch([source.at[at : at + rows]], [tiles.at[h, index]], sems, h)
            if h == 0:
                fetch([source.at[at + rows : at + parts[0]]], [small.at[index]], sems, 2)
    for n, target in enumerate((tiles.at[0], tiles.at[1], small)):
        pltpu.make_async_copy(target, target, sems.at[n]).wait()


def gather_first(place, shard, rows, width):
    parts = (rows + 16, rows)
    got = [across(shard, mask, 16) for mask in Z]
    (quarter,) = call(
        functools.partial(arrange_kernel, parts),
        place,
        [((4 * sum(parts), width), LOW)],
        [],
        [shard] + got,
        [pltpu.SemaphoreType.DMA((8,))],
    )
    from_x, from_y = across(quarter, X, 16), across(quarter, Y, 16)
    cut = 4 * parts[0]
    far_a, far_b = across(from_y[:cut], X, 16), across(from_x[cut:], Y, 16)
    own, small = call(
        functools.partial(place_kernel, parts, rows),
        place,
        [((2, 16, rows, width), LOW), ((16, 16, width), LOW)],
        [],
        [quarter, from_x, from_y, far_a, far_b],
        [pltpu.SemaphoreType.DMA((3,))],
    )
    small = small[:, :, : rows // 16 * SMALL].reshape(16, 16, rows // 16, SMALL)
    small = small.transpose(0, 2, 1, 3).reshape(width, SMALL)
    return [own, swap_cores(own)], small


X, Y = 1, 2
Z = (4, 8, 12)


def round_kernel(jobs, small_job, n_ins, counts, smalls, last, place_of, ins, anys, outs, *scratch):
    new, once, twice, done = counts
    small_new, small_once, small_twice, small_done = smalls
    rest = list(ins[n_ins:]) + list(outs) + list(scratch)
    pop = lambda present, n=1: [rest.pop(0) for _ in range(n)] if present else [None] * n
    (keep_once,), (small_keep_once,) = pop(once), pop(small_once)
    (keep_twice,), (small_keep_twice,) = pop(twice), pop(small_twice)
    from_x, from_y = pop(once or twice, 2)
    (keep_done,), (small_keep_done,) = pop(done), pop(small_done)
    from_z = pop(done, 3)
    (squares_in,), (sums,) = pop(done), pop(last)
    to_x, to_y = pop(new or once, 2)
    (out_once,), (small_out_once,) = pop(new), pop(small_new)
    (out_twice,), (small_out_twice,) = pop(once), pop(small_once)
    (out_done,), (small_out_done,) = pop(twice), pop(small_twice)
    to_z = pop(twice, 3)
    (share,), (small_share,), (squares,) = pop(done), pop(small_done), pop(done)
    (totals,) = pop(last)
    (tile,), (unit,), (small_tile,) = pop(new), pop(new), pop(small_new)
    rows = (out_once if new else out_twice if once else out_done if twice else share).shape[-2]
    rows = rows // (8 if new else 4 if once else 1)
    bits, z = (place_of[1], place_of[2]), place_of[3]
    to, came = (to_x, to_y), (from_x, from_y)

    def block(index, size=rows):
        if isinstance(index, int):
            return pl.ds(index * size, size)
        return pl.ds(pl.multiple_of(index * size, 16), size)

    def factor(spec):
        which, index, low, high = spec
        ref = ins[which] if index is None else ins[which].at[index]
        return ref[...] if low is None else ref[:, low:high]

    def put_small(ref, start, group, side, value):
        for q in range(rows // 16):
            lanes = side * (rows // 16) + q
            ref[pl.ds(start + group * 16, 16), lanes * SMALL : (lanes + 1) * SMALL] = value[
                q * 16 : (q + 1) * 16
            ].astype(LOW)

    def take_small(ref, start, group, side):
        parts = []
        for q in range(rows // 16):
            lanes = side * (rows // 16) + q
            at = pl.ds(pl.multiple_of(start + group * 16, 16), 16)
            parts.append(ref[at, lanes * SMALL : (lanes + 1) * SMALL])
        return jnp.concatenate(parts, 0).astype(FULL)

    def summed(products):
        total = None
        for left, right in products:
            product = cross(factor(left), factor(right))
            total = product if total is None else total + product
        return total

    for p in range(new):
        if len(jobs[p]) == 4:
            for quarter, products in enumerate(jobs[p]):
                unit[...] = summed(products)
                half = unit.shape[1]
                for index in range(4):
                    for s in range(2):
                        for j in range(2):
                            tile[s, block(quarter * 4 + index), j * half : (j + 1) * half] = unit[
                                block(index * 4 + 2 * s + j), :
                            ]
        else:
            for s in range(2):
                for low, high, products in jobs[p][s]:
                    tile[s, :, low:high] = summed(products)
        for s in range(2):
            for zz in range(4):
                for other in range(2):
                    at = zz * 2 + other
                    index = lambda bit: zz * 4 + (other * 2 + bit if s == 0 else bit * 2 + other)
                    to[s][block(p * 8 + at), :] = tile[s, block(index(1 - bits[s])), :].astype(LOW)
                    out_once[p, s, block(at), :] = tile[s, block(index(bits[s])), :]
    if small_new:
        products, norms_at = small_job
        total = summed(products)
        norms = jnp.concatenate([ins[mine][...] + ins[theirs][...] for mine, theirs in norms_at], 0)
        high = norms.astype(LOW)
        shape = (norms.shape[0], SMALL)
        column = lax.broadcasted_iota(jnp.int32, shape, 1) - V
        pick = jnp.where(lax.broadcasted_iota(jnp.int32, shape, 0) == column, 1.0, 0.0).astype(LOW)
        total = total + (cross(high, pick) + cross((norms - high.astype(FULL)).astype(LOW), pick))
        small_tile[...] = total
        for zz in range(4):
            for other in range(2):
                index = lambda bit: zz * 4 + other * 2 + bit
                send = small_tile[block(index(1 - bits[0])), :]
                put_small(to_x, (new * 8 + once * 4) * rows, other * 2 + zz // 2, zz % 2, send)
                small_out_once[block(zz * 2 + other), :] = small_tile[block(index(bits[0])), :]
    for p in range(once):
        for s in range(2):
            for zz in range(4):
                for bit in range(2):
                    at = zz * 2 + (bits[1 - s] if bit else 1 - bits[1 - s])
                    value = keep_once[p, s, block(at), :] + came[s][block(p * 8 + at), :].astype(FULL)
                    if bit:
                        out_twice[p, s, block(zz), :] = value
                    else:
                        to[1 - s][block(new * 8 + p * 4 + zz), :] = value.astype(LOW)
    if small_once:
        start = (once * 8 + twice * 4) * rows
        for zz in range(4):
            for bit in range(2):
                other = bits[1] if bit else 1 - bits[1]
                value = small_keep_once[block(zz * 2 + other), :]
                value = value + take_small(from_x, start, other * 2 + zz // 2, zz % 2)
                if bit:
                    small_out_twice[block(zz), :] = value
                else:
                    put_small(to_y, (new * 8 + once * 4) * rows, zz, 0, value)
    for p in range(twice):
        for s in range(2):
            for xor in range(4):
                at = jnp.bitwise_xor(z, xor)
                value = keep_twice[p, s, block(at), :] + came[1 - s][
                    block(once * 8 + p * 4 + at), :
                ].astype(FULL)
                if xor == 0:
                    out_done[p, s] = value
                else:
                    to_z[xor - 1][block(2 * p + s), :] = value.astype(LOW)
    if small_twice:
        for xor in range(4):
            at = jnp.bitwise_xor(z, xor)
            value = small_keep_twice[block(at), :]
            value = value + take_small(from_y, (once * 8 + twice * 4) * rows, at, 0)
            if xor == 0:
                small_out_done[...] = value
            else:
                put_small(to_z[xor - 1], twice * 2 * rows, 0, 0, value)
    if done:
        squares[...] = squares_in[...]
    for p in range(done):
        for s in range(2):
            value = keep_done[p, s]
            for f in from_z:
                value = value + f[block(2 * p + s), :].astype(FULL)
            share[p, s] = value
            squares[...] += jnp.sum(value * value, 0, keepdims=True)
    if small_done:
        value = small_keep_done[...]
        for f in from_z:
            value = value + take_small(f, done * 2 * rows, 0, 0)
        small_share[...] = value
    if last:
        total = jnp.sum(squares[...], 1, keepdims=True)
        if small_done:
            square = jnp.sum(jnp.sum(value * value, 0, keepdims=True), 1, keepdims=True)
            total = total + jnp.where(place_of[0] == 0, square, jnp.zeros_like(square))
        lane = lax.broadcasted_iota(jnp.int32, sums.shape, 1)
        totals[...] = jnp.where(lane == 2, total, sums[...])


class Rounds:
    def __init__(self, place, rows, width, sums):
        self.place, self.rows, self.width, self.sums = place, rows, width, sums
        self.counts, self.smalls = (0,) * 4, (False,) * 4
        self.kept, self.small_kept = [None] * 3, [None] * 3
        self.came = self.came_z = self.totals = None
        self.shares, self.others, self.small_share = [], [], None
        self.squares = jnp.zeros((1, width), FULL)
        self.flying, self.swapping = [], 0

    def step(self, chunk, *ties, small=None):
        rows, width = self.rows, self.width
        new, once, twice, done = counts = (len(chunk),) + self.counts[:3]
        smalls = (small is not None,) + self.smalls[:3]
        last = not (new or once or twice)
        arrays, jobs = [], []

        def number(spec):
            array, *place = spec
            for i, known in enumerate(arrays):
                if known is array:
                    return (i, *place)
            arrays.append(array)
            return (len(arrays) - 1, *place)

        numbered = lambda products: [(number(l), number(r)) for l, r in products]
        for pair in chunk:
            if len(pair) == 4:
                jobs.append([numbered(products) for products in pair])
            else:
                jobs.append([[(a, b, numbered(ps)) for a, b, ps in tile] for tile in pair])
        small_job = None
        if small is not None:
            small_job = (
                [(number(l), number(r)) for l, r in small[0]],
                [(number((a,))[0], number((b,))[0]) for a, b in small[1]],
            )
        ins = list(arrays)
        for stage in range(2):
            ins += [self.kept[stage]] * (counts[1 + stage] > 0)
            ins += [self.small_kept[stage]] * smalls[1 + stage]
        if once or twice:
            ins += self.came
        if done:
            ins += [self.kept[2]] + [self.small_kept[2]] * smalls[3] + self.came_z + [self.squares]
        ins += [self.sums] * last
        outs = []
        if new or once:
            for added in (64 * smalls[0], 64 * smalls[1]):
                outs.append((((new * 8 + once * 4) * rows + added, width), LOW))
        for stage, blocks in enumerate((8, 4, 1)):
            if counts[stage]:
                outs.append(((counts[stage], 2, blocks * rows, width), FULL))
            if smalls[stage]:
                outs.append(((blocks * rows, SMALL), FULL))
        if twice:
            outs += [((twice * 2 * rows + 16 * smalls[2], width), LOW)] * 3
        if done:
            outs.append(((done, 2, rows, width), FULL))
            outs += [((rows, SMALL), FULL)] * smalls[3]
            outs.append(((1, width), FULL))
        outs += [((1, SMALL), FULL)] * last
        length = 2 * arrays[0].shape[-2] if new else 0
        scratch = []
        if new:
            scratch.append(pltpu.VMEM((2, 16 * rows, width), FULL))
            scratch.append(pltpu.VMEM((16 * rows, width // 2), FULL))
        scratch += [pltpu.VMEM((16 * rows, SMALL), FULL)] * smalls[0]
        got = list(
            call(
                functools.partial(
                    round_kernel, jobs, small_job, len(arrays), counts, smalls, last
                ),
                self.place,
                outs,
                ins,
                [],
                scratch,
                4 * new * length * width * width,
            )
        )
        if last:
            self.totals = got.pop()
        if done:
            self.squares = got.pop()
            if smalls[3]:
                self.small_share = got.pop()
            self.shares.append(got.pop())
        self.counts, self.smalls = counts, smalls
        self.kept, self.small_kept = [None] * 3, [None] * 3
        if last:
            return ties
        got, ties = tie(got, ties)
        to = [got.pop(0) for _ in range(2)] if new or once else []
        for stage in range(3):
            if counts[stage]:
                self.kept[stage] = got.pop(0)
            if smalls[stage]:
                self.small_kept[stage] = got.pop(0)
        self.flying = [across(v, mask, 16) for v, mask in zip(to, (X, Y))]
        self.flying += [across(v, mask, 16) for v, mask in zip(got, Z)]
        self.swapping = 0
        while len(self.flying) < 5 and len(self.others) + self.swapping < len(self.shares):
            self.flying.append(swap_cores(self.shares[len(self.others) + self.swapping]))
            self.swapping += 1
        return ties

    def finish(self, *ties):
        flying, ties = tie(self.flying, ties)
        self.came = self.came_z = None
        if self.counts[0] or self.counts[1]:
            self.came, flying = flying[:2], flying[2:]
        if self.counts[2]:
            self.came_z, flying = flying[:3], flying[3:]
        self.others += flying
        return ties

    def left(self):
        return any(self.counts[:3])

    def swap_rest(self):
        self.others += [swap_cores(v) for v in self.shares[len(self.others) :]]


class PlainRounds:
    def __init__(self):
        self.shares, self.squares = [], []

    def step(self, chunk, *ties):
        def factor(spec):
            array, index, low, high = spec
            array = array if index is None else array[index]
            return array if low is None else array[:, low:high]

        summed = lambda products: sum(cross(factor(l), factor(r)) for l, r in products)
        scatter = lambda v: lax.psum_scatter(v, "fsdp", scatter_dimension=0, tiled=True)
        shares = []
        for pair in chunk:
            if len(pair) == 4:
                v = scatter(jnp.concatenate([summed(products) for products in pair], 0))
                v = v.reshape(2, 2, -1, v.shape[1])
                shares.append(jnp.concatenate([v[:, 0], v[:, 1]], 2))
            else:
                tiles = [jnp.concatenate([summed(ps) for _, _, ps in t], 1) for t in pair]
                shares.append(jnp.stack([scatter(t) for t in tiles]))
        share = jnp.stack(shares)
        self.shares.append((share, swap_cores(share)))
        self.squares.append(jnp.sum(share * share, (0, 1, 2))[None])
        return ties

    def finish(self, *ties):
        return ties

    def left(self):
        return False


def half_of(value, core):
    half = value.shape[1] // 2
    return lax.dynamic_slice_in_dim(value, core * half, half, 1)


def body(
    fsdp,
    codons,
    masked,
    segments,
    inward,
    outward,
    expand,
    shrink,
    codon_table,
    norm_params,
    inward_first,
    inward_second,
    outward_first,
    outward_second,
    expand_first,
    expand_second,
    shrink_first,
    shrink_second,
    table_first,
    table_second,
    norm_first,
    norm_second,
):
    layers = inward.shape[0]
    length = codons.shape[0]
    rows = inward.shape[1]
    width = rows * fsdp
    half = width // 2
    fast = fsdp == 16 and rows == 48
    core, index = lax.axis_index("dp"), lax.axis_index("fsdp")
    bit = lambda b: lax.rem(lax.div(index, b), 2)
    place = jnp.stack([core, bit(1), bit(2), lax.div(index, 4)]).astype(jnp.int32)
    weight = masked.astype(FULL)
    inputs = jnp.where(masked == 1, V - 1, codons)

    norms = norm_params.shape[0] * 2
    small = jnp.concatenate(
        [codon_table.astype(LOW), norm_params.astype(LOW).reshape(norms, rows)], 0
    )
    small = jnp.pad(small.T, ((0, 0), (0, -small.shape[0] % 128)))
    columns = small.shape[1] + layers * 6 * width
    shapes = [(rows, columns)]
    if fast:
        shapes = [(rows, layers * 6 * width - 2 * width), (2 * rows + 16, width)]
    weights, *early = call(
        functools.partial(pack_kernel, layers),
        place,
        [(shape, LOW) for shape in shapes],
        [inward, outward, expand, shrink, small],
    )
    weights = lax.all_gather(weights, ("fsdp", "dp"), axis=0, tiled=True)
    weights = weights.reshape(fsdp, 2, rows, -1)
    if not fast:
        columns = [weights[:, :, :, : small.shape[1]]]
        for at in range(small.shape[1], weights.shape[3], 6 * width):
            columns.append(weights[:, :, :, at : at + 4 * width])
            quarter = weights[:, :, :, at + 4 * width : at + 6 * width]
            quarter = quarter.reshape(fsdp, 2, rows, 4, half).transpose(1, 0, 3, 2, 4)
            quarter = quarter.reshape(2, 4, width, half).transpose(0, 2, 1, 3)
            columns.append(quarter.reshape(2, fsdp, rows, 2 * width).transpose(1, 0, 2, 3))
        weights = jnp.concatenate(columns, 3).transpose(1, 0, 2, 3).reshape(1, 2, width, -1)
    mixers = [[weights]] * layers
    if fast:
        mixers[0], small = gather_first(place, early[0], rows, width)
        small = small.T
    else:
        small = weights[:, 0, :, :SMALL].reshape(width, SMALL).T
    base = lambda l: weights.shape[3] - (layers - l) * 6 * width
    gains = small[V : V + norms].astype(FULL).reshape(-1, 2, width)

    cosine, sine = rotary_tables(length)
    chosen = (inputs[:, None] == jnp.arange(SMALL, dtype=jnp.int32)[None, :]).astype(LOW)
    resid = dot(chosen, small)
    kept = []
    for l in range(layers):
        gain = gains[2 * l : 2 * l + 2]
        middle, query, keys, values, lse, pack = attention_forward(
            place, resid, mixers[l], base(l), gain[0], cosine, sine, segments
        )
        output, pack_mid, hidden = hidden_forward(place, middle, weights, base(l), gain[1])
        kept.append((resid, query, keys, values, lse, pack, middle, hidden, pack_mid))
        resid = output
    grad, branch, branch_own, branch_other, head_in, grad_logits, grad_norms, sums = head(
        place, resid, small, gains[2 * layers], codons, weight
    )
    grad_norms = [grad_norms]
    early = (head_in, grad_logits, chosen)
    early_came = [swap_cores(v) for v in early]
    mid_came = [swap_cores(saved[-1]) for saved in kept]
    pack_came = [swap_cores(saved[5]) for saved in kept]
    grad, branch, mid_came[-1] = tie(grad, branch, mid_came[-1])

    rounds = Rounds(place, rows, width, sums) if fast else PlainRounds()
    whole = lambda array, i=None: (array, i, None, None)
    tile = lambda left, right, other_left, other_right: [
        (0, width, [(left, right), (other_left, other_right)])
    ]
    chunk = []
    for l in reversed(range(layers)):
        resid, query, keys, values, lse, pack, middle, hidden, pack_mid = kept[l]
        gain = gains[2 * l : 2 * l + 2]
        branch_came = swap_cores(branch_other)
        chunk.append(
            [
                [
                    (whole(pack_mid, 1 + t), whole(branch_own)),
                    (whole(mid_came[l], 1 + t), whole(branch_came)),
                ]
                for t in range(4)
            ]
        )
        grad, branch = rounds.step(chunk, grad, branch)
        grad_middle, gains_mid, up_own, up_other = hidden_back(
            place, grad, branch, middle, hidden, weights, base(l), gain[1]
        )
        grad_middle, up_own, up_other, early_came = rounds.finish(
            grad_middle, up_own, up_other, early_came
        )
        up_came = swap_cores(up_other)
        if l == 0:
            norms_early = jnp.concatenate([gains_mid] + grad_norms, 0)
            norms_early = (norms_early, swap_cores(norms_early))
        (grad_middle,) = rounds.step(
            [
                [
                    tile(
                        whole(pack_mid, 0), whole(up_own, s), whole(mid_came[l], 0), whole(up_came, s)
                    )
                    for s in range(2)
                ]
            ],
            grad_middle,
        )
        grad, branch, branch_own, branch_other, gains_in, mix_own, mix_other = attention_back(
            place, grad_middle, resid, mixers[l], base(l), gain[0], cosine, sine, segments,
            query, keys, values, lse,
        )
        grad_norms = [gains_in, gains_mid] + grad_norms
        grad, branch, branch_own, branch_other, mix_own, mix_other, mid_came, pack_came = (
            rounds.finish(
                grad, branch, branch_own, branch_other, mix_own, mix_other, mid_came, pack_came
            )
        )
        mix_came = swap_cores(mix_other)
        products = lambda i, a, b: [
            ((pack, i, None, None), (mix_own, 1, a, b)),
            ((pack_came[l], i, None, None), (mix_came, 1, a, b)),
        ]
        chunk = [
            [
                tile(whole(pack, 0), whole(mix_own, 0), whole(pack_came[l], 0), whole(mix_came, 0)),
                [(0, half, products(0, 0, half)), (half, width, products(1, half, width))],
            ]
        ]
    late = (grad_norms[0], swap_cores(grad_norms[0]))
    branch_came = swap_cores(branch)
    products = [(whole(early[0]), whole(early[1])), (whole(early_came[0]), whole(early_came[1]))]
    products += [(whole(branch), whole(early[2])), (whole(branch_came), whole(early_came[2]))]
    if fast:
        rounds.step(chunk, small=(products, [late, norms_early]))
        while rounds.left():
            rounds.finish()
            rounds.step([])
        rounds.swap_rest()
        share_small = rounds.small_share
        small_other = swap_cores(share_small)
        totals = rounds.totals
    else:
        rounds.step(chunk)
        table = sum(cross(l[0], r[0]) for l, r in products)
        table = table + jnp.pad(
            jnp.concatenate([a + b for a, b in (late, norms_early)], 0).T,
            ((0, 0), (V, SMALL - V - norms)),
        )
        table = jnp.where(core == 0, table, swap_cores(table))
        share_small = lax.psum_scatter(table, "fsdp", scatter_dimension=0, tiled=True)
        squares = jnp.sum(share_small * share_small) * (core == 0)
        for value in rounds.squares:
            squares = squares + jnp.sum(value)
        totals = sums + jnp.where(jnp.arange(SMALL) == 2, squares, 0.0)[None]
    totals = total_of(totals, fsdp)
    shares = list(zip(rounds.shares, rounds.others)) if fast else rounds.shares
    places = [(2 * (layers - 1 - l), 0 if l == layers - 1 else 1) for l in range(layers)]

    def tiles_at(chunk, pair):
        own, other = (v[pair] for v in shares[chunk])
        ordered = (jnp.where(core == 0, own, other), jnp.where(core == 0, other, own))
        return [v[s] for v in ordered for s in range(2)]

    if not fast:
        share_in, share_out, share_up, share_down = [], [], [], []
        side = lambda *values: jnp.concatenate(values, 1)
        for at, pair in places:
            a_0, b_0, a_1, b_1 = tiles_at(at + 2, 0)
            share_in.append(
                side(
                    a_0[:, :half], a_1[:, :half], a_0[:, half:],
                    a_1[:, half:], b_0[:, :half], b_1[:, :half],
                )
            )
            share_out.append(side(b_0[:, half:], b_1[:, half:]))
            share_up.append(side(*tiles_at(at + 1, 0)))
            a_0, b_0, a_1, b_1 = tiles_at(at, pair)
            share_down.append(
                jnp.concatenate(
                    [
                        side(x[:, j * half : (j + 1) * half], y[:, j * half : (j + 1) * half])
                        for x, y in ((a_0, a_1), (b_0, b_1))
                        for j in range(2)
                    ],
                    0,
                )
            )
        share_in, share_out, share_up, share_down = (
            jnp.stack(v) for v in (share_in, share_out, share_up, share_down)
        )
    masters = (inward, outward, expand, shrink, codon_table, norm_params)
    firsts = (inward_first, outward_first, expand_first, shrink_first, table_first, norm_first)
    seconds = (
        inward_second,
        outward_second,
        expand_second,
        shrink_second,
        table_second,
        norm_second,
    )
    if fast:
        chunks = [((at + 2, 0), (at + 1, 0), (at, pair)) for at, pair in places]
        own, other = zip(*shares)
        states = [v for group in zip(masters, firsts, seconds) for v in group]
        states[12:15] = [v.T for v in states[12:15]]
        grad_norm, *values = optimizer(
            place, totals, (share_small, small_other), chunks, own, other, states
        )
        values[12:15] = [v.T for v in values[12:15]]
    else:
        grad_norm, scale = scale_of(totals)
        share_small = share_small[:, : V + norms].T
        grads = (share_in, share_out, share_up, share_down)
        grads += (share_small[:V], share_small[V:].reshape(-1, 2, rows))
        values = []
        for index, grad in enumerate(grads):
            rate, decay = (RATE_VECTOR, 0.0) if index == 5 else (RATE_MATRIX, DECAY)
            values.extend(
                adam_step(masters[index], grad * scale.reshape(()), firsts[index], seconds[index], rate, decay)
            )
    return (totals[0, 0], totals[0, 1], grad_norm.reshape(()), *values)


def solution(mesh):
    in_specs = (
        P(("fsdp", "dp")),
        P(("fsdp", "dp")),
        P(("fsdp", "dp")),
        P(None, "fsdp", None),
        P(None, "fsdp", None),
        P(None, "fsdp", None),
        P(None, "fsdp", None),
        P(None, "fsdp"),
        P(None, None, "fsdp"),
        P(None, "fsdp", None),
        P(None, "fsdp", None),
        P(None, "fsdp", None),
        P(None, "fsdp", None),
        P(None, "fsdp", None),
        P(None, "fsdp", None),
        P(None, "fsdp", None),
        P(None, "fsdp", None),
        P(None, "fsdp"),
        P(None, "fsdp"),
        P(None, None, "fsdp"),
        P(None, None, "fsdp"),
    )
    out_specs = (
        P(),
        P(),
        P(),
        P(None, "fsdp", None),
        P(None, "fsdp", None),
        P(None, "fsdp", None),
        P(None, "fsdp", None),
        P(None, "fsdp", None),
        P(None, "fsdp", None),
        P(None, "fsdp", None),
        P(None, "fsdp", None),
        P(None, "fsdp", None),
        P(None, "fsdp", None),
        P(None, "fsdp", None),
        P(None, "fsdp", None),
        P(None, "fsdp"),
        P(None, "fsdp"),
        P(None, "fsdp"),
        P(None, None, "fsdp"),
        P(None, None, "fsdp"),
        P(None, None, "fsdp"),
    )
    step = functools.partial(body, mesh.shape["fsdp"])
    return jax.shard_map(step, mesh=mesh, in_specs=in_specs, out_specs=out_specs, check_vma=False)
```

```python
import functools

import jax
import jax.numpy as jnp
from jax import lax
from jax.experimental import pallas as pl
from jax.experimental.pallas import tpu as pltpu
from jax.sharding import PartitionSpec as P

HD = 64
V = 70
STEP = 10


NORM_EPS = 1e-05
BETA_ONE = 0.9
BETA_TWO = 0.95
ADAM_EPS = 1e-08
DECAY = 0.1
RATE_MATRIX = 0.05
RATE_VECTOR = 0.3
CLIP = 0.05


def rotary_tables(length):
    freq = 10000.0 ** (-jnp.arange(HD // 2, dtype=jnp.float32) * 2.0 / HD)
    angle = jnp.arange(length, dtype=jnp.float32)[:, None] * freq[None, :]
    cosine, sine = jnp.cos(angle), jnp.sin(angle)
    return (
        jnp.concatenate([cosine] * 4, 1),
        jnp.concatenate([-sine, sine] * 2, 1),
    )


def normalize(resid, gain, bias):
    mean = jnp.mean(resid, -1, keepdims=True)
    centred = resid - mean
    inverse = lax.rsqrt(jnp.mean(centred * centred, -1, keepdims=True) + NORM_EPS)
    unit = centred * inverse
    return (unit * gain + bias, unit, inverse)


def normalize_back(grad, unit, inverse, gain):
    scaled = grad * gain
    across = (
        scaled
        - jnp.mean(scaled, -1, keepdims=True)
        - unit * jnp.mean(scaled * unit, -1, keepdims=True)
    )
    return (across * inverse, jnp.sum(grad * unit, 0, keepdims=True), jnp.sum(grad, 0, keepdims=True))


def dot(left, right):
    return jnp.dot(left, right, preferred_element_type=jnp.float32)


def dot_nt(left, right):
    return lax.dot_general(
        left, right, (((1,), (1,)), ((), ())), preferred_element_type=jnp.float32
    )


def cross(left, right):
    return lax.dot_general(
        left, right, (((0,), (0,)), ((), ())), preferred_element_type=jnp.float32
    )


VMEM_LIMIT = 56 * 1024 * 1024
LOW, FULL = jnp.bfloat16, jnp.float32
SMALL = 128


class Sent:
    def __init__(self, here, there, sems):
        self.here, self.there, self.sems = here, there, sems
        self.shape, self.at = here.shape, here.at
        self.copies = []

    def __getitem__(self, at):
        return self.here[at]

    def __setitem__(self, at, value):
        self.here[at] = value

    def send(self, index=None):
        here, there = self.here, self.there
        if index is not None:
            here, there = here.at[index], there.at[index]
        copy = pltpu.make_async_copy(here, there, self.sems.at[len(self.copies)])
        copy.start()
        self.copies.append(copy)


def call(kernel, scalars, outs, ins, anys=(), scratch=(), flops=0, sent=()):
    whole = pl.BlockSpec(memory_space=pltpu.VMEM)
    left = pl.BlockSpec(memory_space=pl.ANY)

    def body(scalars, *refs):
        refs = list(refs)
        take = lambda n: [refs.pop(0) for _ in range(n)]
        in_refs, any_refs, out_refs = take(len(ins)), take(len(anys)), take(len(outs))
        here = take(len(sent))
        for n, i in enumerate(sent):
            out_refs[i] = Sent(here[n], out_refs[i], refs[-1].at[n])
        kernel(scalars, in_refs, any_refs, out_refs, *(refs[:-1] if sent else refs))
        for i in sent:
            for copy in out_refs[i].copies:
                copy.wait()

    return pl.pallas_call(
        body,
        out_shape=[jax.ShapeDtypeStruct(s, t) for s, t in outs],
        in_specs=[pl.BlockSpec(memory_space=pltpu.SMEM)]
        + [whole] * len(ins)
        + [left] * len(anys),
        out_specs=[left if i in sent else whole for i in range(len(outs))],
        scratch_shapes=[pltpu.VMEM(*outs[i]) for i in sent]
        + list(scratch)
        + [pltpu.SemaphoreType.DMA((len(sent), 5))] * (len(sent) > 0),
        compiler_params=pltpu.CompilerParams(vmem_limit_bytes=VMEM_LIMIT),
        cost_estimate=pl.CostEstimate(
            flops=flops,
            bytes_accessed=sum(x.size * x.dtype.itemsize for x in list(ins) + list(anys)),
            transcendentals=0,
        ),
    )(scalars, *ins, *anys)


def fetch(sources, targets, sems, first=0):
    copies = [
        pltpu.make_async_copy(s, t, sems.at[first + i])
        for i, (s, t) in enumerate(zip(sources, targets))
    ]
    for c in copies:
        c.start()
    return copies


def tile_of(ref, core, at):
    return ref.at[:, core, :, at : at + ref.shape[0] * ref.shape[2]]


def matrix(ref, place, low=None, high=None):
    value = ref[place] if low is None else ref[place, :, :, low:high]
    return value.reshape(-1, value.shape[-1])


def mixer_tile(anys, cores, place, t, base, width):
    if len(anys) == 2:
        return anys[place].at[t]
    return tile_of(anys[0], cores[place], base + t * width)


def mixer_scratch(weights):
    w = weights[0]
    blocks, rows = (w.shape[1], w.shape[2]) if len(weights) == 2 else (w.shape[0], w.shape[2])
    return [pltpu.VMEM((2, blocks, rows, blocks * rows), LOW)] * 2


def swap_halves(value):
    lane = lax.broadcasted_iota(jnp.int32, value.shape, 1)
    return jnp.where(
        lax.rem(lane, HD) < HD // 2,
        pltpu.roll(value, 128 - HD // 2, 1),
        pltpu.roll(value, HD // 2, 1),
    )


def ordered(first, own, other):
    return jnp.concatenate([jnp.where(first, own, other), jnp.where(first, other, own)], 1)


def head_mask(shape, head):
    lane = lax.broadcasted_iota(jnp.int32, shape, 1)
    return (lane < HD) if head == 0 else (lane >= HD)


def attention_forward_kernel(base, place_of, ins, anys, outs, w_a, w_b, mixed, bias, sems):
    resid, seg_col, seg_row, cosine, sine, gains = ins
    middle, query, keys, values, lse, pack = outs
    width = resid.shape[1]
    half = width // 2
    cores = (place_of[0], 1 - place_of[0])
    copies = fetch(
        [mixer_tile(anys, cores, p, t, base, width) for t in range(2) for p in range(2)],
        [w.at[place] for w in (w_a, w_b) for place in range(2)],
        sems,
    )
    first = place_of[0] == 0
    normed, _, _ = normalize(resid[...], gains[0:1], gains[1:2])
    normed_low, attended = pack.at[0], pack.at[1]
    normed_low[...] = normed.astype(LOW)
    bias[...] = jnp.where(seg_col[...] == seg_row[...], 0.0, -1000000000.0)
    for place in range(2):
        copies[place].wait()
        mixed[...] = dot(normed_low[...], matrix(w_a, place))
        for p in range(half // 128):
            for part, target, scale in ((0, query, HD ** (-0.5)), (1, keys, 1.0)):
                x = mixed[:, part * half + p * 128 : part * half + (p + 1) * 128]
                x = x * cosine[...] + swap_halves(x) * sine[...]
                x = (x * scale if scale != 1.0 else x).astype(LOW)
                target[:, place * half + p * 128 : place * half + (p + 1) * 128] = x
    for place in range(2):
        copies[2 + place].wait()
        values[:, place * half : (place + 1) * half] = dot(
            normed_low[...], matrix(w_b, place, 0, half)
        ).astype(LOW)

    lse[...] = jnp.zeros_like(lse)

    for p in range(width // 128):
        columns = slice(p * 128, (p + 1) * 128)
        q, k, v = query[:, columns], keys[:, columns], values[:, columns]
        out = []
        for head in range(2):
            masked_q = jnp.where(head_mask(q.shape, head), q, jnp.zeros_like(q))
            scores = dot_nt(masked_q, k) + bias[...]
            top = jnp.max(scores, -1, keepdims=True)
            expo = jnp.exp(scores - top)
            total = jnp.sum(expo, -1, keepdims=True)
            probs = (expo * (1.0 / total)).astype(LOW)
            out.append(dot(probs, v))
            lane = lax.broadcasted_iota(jnp.int32, lse.shape, 1)
            lse[...] = jnp.where(lane == 2 * p + head, top + jnp.log(total), lse[...])
        attended[:, columns] = jnp.where(head_mask(out[0].shape, 0), out[0], out[1]).astype(LOW)
    attended[...] = ordered(first, attended[:, :half], attended[:, half:])
    out = ordered(
        first,
        dot(attended[...], matrix(w_b, 0, half, width)),
        dot(attended[...], matrix(w_b, 1, half, width)),
    )
    middle[...] = resid[...] + out


def attention_forward(place, resid, weights, base, gains, cosine, sine, segments):
    length, width = resid.shape
    one = (length, width)
    return call(
        functools.partial(attention_forward_kernel, base),
        place,
        [(one, FULL)] + [(one, LOW)] * 3 + [((length, 128), FULL), ((2,) + one, LOW)],
        [resid, segments[:, None], segments[None, :], cosine, sine, gains],
        weights,
        mixer_scratch(weights)
        + [
            pltpu.VMEM(one, FULL),
            pltpu.VMEM((length, length), FULL),
            pltpu.SemaphoreType.DMA((4,)),
        ],
        8 * length * width * width + 4 * length * length * width,
    )


GELU_SCALE = 0.7978845608028654
GELU_CUBE = 0.044715


def fetch_hidden(anys, base, cores, ups, downs, sems, between=lambda t: None, down_first=False):
    blocks, parts, rows, width = downs.shape
    half, some = width // 2, max(blocks // 4, 1)
    copies = {}

    def up_source(place, within):
        if len(anys) == 2:
            return anys[place].at[2 * within]
        return tile_of(anys[0], cores[place], base + (2 + within) * width)

    def down_source(place, first, j):
        if len(anys) == 2:
            return anys[place].at[1 + j // 2 * 2, pl.ds(first, some), :, j % 2 * half : (j % 2 + 1) * half]
        at = base + 4 * width + j * half
        return anys[0].at[pl.ds(first, some), cores[place], :, at : at + half]

    for t in range(4):
        up = lambda: fetch([up_source(t // 2, t % 2)], [ups.at[t]], sems, t)
        if not down_first:
            copies[0, t] = up()
        if blocks >= 4 or t == 0:
            sources, targets = [], []
            first = (2 * cores[t // 2] + t % 2) * some if blocks >= 4 else 0
            for place in range(2):
                columns = pl.ds(pl.multiple_of(cores[place] * half, 128), half)
                for j in range(4):
                    sources.append(down_source(place, first, j))
                    targets.append(downs.at[pl.ds(t * some, some), j, :, columns])
            copies[1, t] = fetch(sources, targets, sems, 4 + 8 * t)
        between(t)
        if down_first:
            copies[0, t] = up()

    def wait(which, t):
        for copy in copies.pop((which, t), []):
            copy.wait()

    return wait


def rows_of(downs, t, cores):
    blocks, parts, rows, width = downs.shape
    if blocks >= 4:
        some = blocks // 4
        return downs[t * some : (t + 1) * some].reshape(some * parts * rows, width)
    return downs[0, 2 * cores[t // 2] + t % 2]


def hidden_scratch(weights):
    w = weights[0]
    blocks, rows = (w.shape[1], w.shape[2]) if len(weights) == 2 else (w.shape[0], w.shape[2])
    return [
        pltpu.VMEM((4, blocks, rows, blocks * rows), LOW),
        pltpu.VMEM((blocks, 4, rows, blocks * rows), LOW),
        pltpu.SemaphoreType.DMA((36,)),
    ]


def hidden_forward_kernel(base, place_of, ins, anys, outs, ups, downs, sems):
    middle, gains = ins
    output, pack, hidden = outs
    cores = (place_of[0], 1 - place_of[0])
    wait = fetch_hidden(anys, base, cores, ups, downs, sems)
    normed, _, _ = normalize(middle[...], gains[0:1], gains[1:2])
    pack[0] = normed.astype(LOW)
    pack.send(0)
    for t in range(4):
        wait(0, t)
        index = 2 * cores[t // 2] + t % 2
        x = dot(pack[0], matrix(ups, t))
        hidden[index] = x
        hidden.send(index)
        inner = jnp.tanh(x * (GELU_SCALE + (GELU_SCALE * GELU_CUBE) * (x * x)))
        value = x * 0.5
        value = (value + value * inner).astype(LOW)
        pack[1 + index] = value
        pack.send(1 + index)
        wait(1, t)
        product = dot(value, rows_of(downs, t, cores))
        output[...] = (middle[...] if t == 0 else output[...]) + product


def hidden_forward(place, middle, weights, base, gains):
    length, width = middle.shape
    one = (length, width)
    return call(
        functools.partial(hidden_forward_kernel, base),
        place,
        [(one, FULL), ((5,) + one, LOW), ((4,) + one, FULL)],
        [middle, gains],
        weights,
        hidden_scratch(weights),
        16 * length * width * width,
        sent=(1, 2),
    )


def hidden_back_kernel(base, place_of, ins, anys, outs, ups, downs, sems, hidden_here, total, own_sems):
    branch, grad, middle, gains = ins
    hidden, *weights = anys
    grad_middle, grad_gains, grad_own, grad_other = outs
    cores = (place_of[0], 1 - place_of[0])
    copies = []

    def fetch_values(t):
        source = hidden.at[2 * cores[t // 2] + t % 2]
        copies.extend(fetch([source], [hidden_here.at[t]], own_sems, t))

    wait = fetch_hidden(weights, base, cores, ups, downs, sems, fetch_values, down_first=True)
    for t in range(4):
        wait(1, t)
        grad_active = dot_nt(branch[...], rows_of(downs, t, cores))
        copies[t].wait()
        x = hidden_here[t]
        square = x * x
        inner = jnp.tanh(x * (GELU_SCALE + (GELU_SCALE * GELU_CUBE) * square))
        slope = x * (GELU_SCALE + (3.0 * GELU_SCALE * GELU_CUBE) * square)
        slope = (0.5 + 0.5 * inner) * (1.0 + slope * (1.0 - inner))
        value = (grad_active * slope).astype(LOW)
        (grad_own if t < 2 else grad_other)[t % 2] = value
        wait(0, t)
        product = dot_nt(value, matrix(ups, t))
        total[...] = product if t == 0 else total[...] + product
    _, unit, inverse = normalize(middle[...], gains[0:1], gains[1:2])
    back, gain, bias = normalize_back(total[...], unit, inverse, gains[0:1])
    grad_middle[...] = grad[...] + back
    grad_gains[0:1] = gain
    grad_gains[1:2] = bias


def hidden_back(place, grad, branch, middle, hidden, weights, base, gains):
    length, width = middle.shape
    one = (length, width)
    return call(
        functools.partial(hidden_back_kernel, base),
        place,
        [(one, FULL), ((2, width), FULL), ((2,) + one, LOW), ((2,) + one, LOW)],
        [branch, grad, middle, gains],
        [hidden] + weights,
        hidden_scratch(weights)
        + [
            pltpu.VMEM((4,) + one, FULL),
            pltpu.VMEM(one, FULL),
            pltpu.SemaphoreType.DMA((4,)),
        ],
        16 * length * width * width,
    )


def attention_back_kernel(base, place_of, ins, anys, outs, w_a, w_b, bias, ga, gq, gk, gv, sems):
    grad_middle, query, keys, values, lse, seg_col, seg_row, cosine, sine, gains, resid = ins
    grad, branch, branch_own, branch_other, grad_gains, grad_own, grad_other = outs
    width = resid.shape[1]
    half = width // 2
    cores = (place_of[0], 1 - place_of[0])
    copies = fetch(
        [mixer_tile(anys, cores, p, t, base, width) for t in (1, 0) for p in range(2)],
        [w.at[place] for w in (w_b, w_a) for place in range(2)],
        sems,
    )
    first = place_of[0] == 0
    grads = (grad_own, grad_other)
    bias[...] = jnp.where(seg_col[...] == seg_row[...], 0.0, -1000000000.0)
    attn_grad = grad_middle[...].astype(LOW)
    left, right = attn_grad[:, :half], attn_grad[:, half:]
    grad_own[1, :, half:] = jnp.where(first, left, right)
    grad_other[1, :, half:] = jnp.where(first, right, left)
    copies[0].wait()
    copies[1].wait()
    natural = dot_nt(grad_own[1, :, half:], matrix(w_b, 0, half, width)) + dot_nt(
        grad_other[1, :, half:], matrix(w_b, 1, half, width)
    )
    natural = natural.astype(LOW)
    ga[:, :half] = jnp.where(first, natural[:, :half], natural[:, half:])
    ga[:, half:] = jnp.where(first, natural[:, half:], natural[:, :half])

    for p in range(width // 128):
        columns = slice(p * 128, (p + 1) * 128)
        q, k, v, g = query[:, columns], keys[:, columns], values[:, columns], ga[:, columns]
        flipped = k.T
        out_q, out_k, out_v = [], [], []
        for head in range(2):
            mask = head_mask(q.shape, head)
            zero = jnp.zeros_like(q)
            scores = dot_nt(k, jnp.where(mask, q, zero)) + bias[...]
            probs = jnp.exp(scores - lse[2 * p + head : 2 * p + head + 1, :])
            grad_probs = dot_nt(v, jnp.where(mask, g, zero))
            across = jnp.sum(probs * grad_probs, 0, keepdims=True)
            grad_scores = (probs * (grad_probs - across)).astype(LOW)
            out_k.append(dot(grad_scores, q))
            out_q.append(dot(flipped[head * HD : (head + 1) * HD], grad_scores))
            out_v.append(dot(probs.astype(LOW), g))
        out_q = jnp.concatenate(out_q, 0).T * HD ** (-0.5)
        out_k = jnp.where(head_mask(out_k[0].shape, 0), out_k[0], out_k[1])
        for x, target in ((out_q, gq), (out_k, gk)):
            x = x * cosine[...] - swap_halves(x) * sine[...]
            target[:, columns] = x.astype(LOW)
        gv[:, columns] = jnp.where(head_mask(out_v[0].shape, 0), out_v[0], out_v[1]).astype(LOW)
    for place in (1, 0):
        columns = slice(place * half, (place + 1) * half)
        grads[place][0, :, :half] = gq[:, columns]
        grads[place][0, :, half:] = gk[:, columns]
        grads[place][1, :, :half] = gv[:, columns]
    copies[2].wait()
    copies[3].wait()
    total = dot_nt(grad_own[0], matrix(w_a, 0)) + dot_nt(grad_other[0], matrix(w_a, 1))
    total = total + dot_nt(grad_own[1, :, :half], matrix(w_b, 0, 0, half))
    total = total + dot_nt(grad_other[1, :, :half], matrix(w_b, 1, 0, half))
    _, unit, inverse = normalize(resid[...], gains[0:1], gains[1:2])
    back, gain, bias_grad = normalize_back(total, unit, inverse, gains[0:1])
    back = grad_middle[...] + back
    grad[...] = back
    back = back.astype(LOW)
    branch[...] = back
    branch_own[...] = jnp.where(first, back[:, :half], back[:, half:])
    branch_other[...] = jnp.where(first, back[:, half:], back[:, :half])
    grad_gains[0:1] = gain
    grad_gains[1:2] = bias_grad


def attention_back(place, grad_middle, resid, weights, base, gains, cosine, sine, segments, query, keys, values, lse):
    length, width = resid.shape
    one = (length, width)
    return call(
        functools.partial(attention_back_kernel, base),
        place,
        [(one, FULL), (one, LOW)]
        + [((length, width // 2), LOW)] * 2
        + [((2, width), FULL)]
        + [((2,) + one, LOW)] * 2,
        [grad_middle, query, keys, values, lse.T[: width // HD]]
        + [segments[:, None], segments[None, :], cosine, sine, gains, resid],
        weights,
        mixer_scratch(weights)
        + [
            pltpu.VMEM((length, length), FULL),
        ]
        + [pltpu.VMEM(one, LOW)] * 4
        + [pltpu.SemaphoreType.DMA((4,))],
        8 * length * width * width + 10 * length * length * width,
    )


def head_kernel(place_of, ins, anys, outs):
    resid, table, gains, codons, weight = ins
    grad, branch, branch_own, branch_other, head_in, grad_logits, grad_gains, sums = outs
    half = resid.shape[1] // 2
    normed, unit, inverse = normalize(resid[...], gains[0:1], gains[1:2])
    head_in[...] = normed.astype(LOW)
    logits = dot_nt(head_in[...], table[...])
    lane = lax.broadcasted_iota(jnp.int32, logits.shape, 1)
    logits = jnp.where(lane < V, logits, -1e30)
    top = jnp.max(logits, 1, keepdims=True)
    lse = top + jnp.log(jnp.sum(jnp.exp(logits - top), 1, keepdims=True))
    hot = jnp.where(lane == codons[...], 1.0, 0.0)
    picked = jnp.sum(logits * hot, 1, keepdims=True)
    loss = jnp.sum((lse - picked) * weight[...], 0, keepdims=True)
    count = jnp.sum(weight[...], 0, keepdims=True)
    lane = lax.broadcasted_iota(jnp.int32, sums.shape, 1)
    sums[...] = jnp.where(lane == 0, loss, jnp.where(lane == 1, count, 0.0))
    grad_logits[...] = ((jnp.exp(logits - lse) - hot) * weight[...]).astype(LOW)
    back, gain, bias = normalize_back(
        dot(grad_logits[...], table[...]), unit, inverse, gains[0:1]
    )
    grad[...] = back
    back = back.astype(LOW)
    branch[...] = back
    first = place_of[0] == 0
    branch_own[...] = jnp.where(first, back[:, :half], back[:, half:])
    branch_other[...] = jnp.where(first, back[:, half:], back[:, :half])
    grad_gains[0:1] = gain
    grad_gains[1:2] = bias


def head(place, resid, table, gains, codons, weight):
    length, width = resid.shape
    one, part = (length, width), (length, width // 2)
    return call(
        head_kernel,
        place,
        [(one, FULL), (one, LOW), (part, LOW), (part, LOW), (one, LOW)]
        + [((length, SMALL), LOW), ((2, width), FULL), ((1, SMALL), FULL)],
        [resid, table, gains, codons[:, None], weight[:, None]],
        flops=4 * length * width * SMALL,
    )


def adam_step(master, grad, first, second, rate, decay):
    first = BETA_ONE * first + (1.0 - BETA_ONE) * grad
    second = BETA_TWO * second + (1.0 - BETA_TWO) * grad * grad
    fix_one = 1.0 / (1.0 - BETA_ONE**STEP)
    fix_two = 1.0 / (1.0 - BETA_TWO**STEP)
    update = first * fix_one / (jnp.sqrt(second * fix_two) + ADAM_EPS) + decay * master
    return (master - rate * update, first, second)


def scale_of(totals):
    count = totals[0:1, 1:2]
    grad_norm = jnp.sqrt(totals[0:1, 2:3]) / count
    return grad_norm, CLIP / jnp.maximum(grad_norm, CLIP) / count


def optimizer_kernel(chunks, place_of, ins, anys, outs, *scratch):
    *masters, sems = scratch
    copies = fetch(anys, masters, sems)
    totals, small_own, small_other, *rest = ins
    n = (len(rest) - 6) // 2
    own, other = rest[:n], rest[n : 2 * n]
    masters += rest[2 * n :]
    layers = len(chunks)
    first = place_of[0] == 0
    grad_norm, scale = scale_of(totals[...])
    outs[0][...] = grad_norm

    def step(which, at, grad, rate=RATE_MATRIX, decay=DECAY):
        master, moment, square = (masters[3 * which + i][at] for i in range(3))
        values = adam_step(master, grad * scale, moment, square, rate, decay)
        for i in range(3):
            outs[1 + 3 * which + i][at] = values[i]

    def tile(where, s, core):
        a, b = own[where[0]][where[1], s], other[where[0]][where[1], s]
        return jnp.where(first, a, b) if core == 0 else jnp.where(first, b, a)

    def arrive(*which):
        for copy in copies[3 * which[0] : 3 * which[-1] + 3]:
            copy.wait()

    def leave(which):
        for i in range(3):
            outs[1 + 3 * which + i].send()

    rows, width = own[0].shape[-2:]
    half = width // 2
    arrive(0, 1)
    for l in range(layers):
        for core in range(2):
            columns = lambda p: pl.ds(p * width + core * half, half)
            value = tile(chunks[l][0], 0, core)
            step(0, (l, slice(None), columns(0)), value[:, :half])
            step(0, (l, slice(None), columns(1)), value[:, half:])
            value = tile(chunks[l][0], 1, core)
            step(0, (l, slice(None), columns(2)), value[:, :half])
            step(1, (l, slice(None), columns(0)), value[:, half:])
    leave(0)
    leave(1)
    arrive(2)
    for l in range(layers):
        for core in range(2):
            for s in range(2):
                at = (l, slice(None), pl.ds((2 * core + s) * width, width))
                step(2, at, tile(chunks[l][1], s, core))
    leave(2)
    arrive(3)
    for l in range(layers):
        for core in range(2):
            for s in range(2):
                value = tile(chunks[l][2], s, core)
                for j in range(2):
                    at = (l, pl.ds((2 * s + j) * rows, rows), pl.ds(core * half, half))
                    step(3, at, value[:, j * half : (j + 1) * half])
    leave(3)
    small = jnp.where(first, small_own[...], small_other[...])
    step(4, (slice(None), slice(None)), small[:, :V])
    small = small.T
    for n in range(masters[15].shape[0]):
        step(5, n, small[V + 2 * n : V + 2 * n + 2], RATE_VECTOR, 0.0)


def optimizer(place, totals, small, chunks, own, other, masters):
    return call(
        functools.partial(optimizer_kernel, chunks),
        place,
        [((1, 1), FULL)] + [(m.shape, m.dtype) for m in masters],
        [totals, *small, *own, *other, *masters[12:]],
        masters[:12],
        [pltpu.VMEM(m.shape, m.dtype) for m in masters[:12]] + [pltpu.SemaphoreType.DMA((12,))],
        flops=20 * sum(m.size for m in masters),
        sent=range(1, 13),
    )


def pack_kernel(layers, place_of, ins, anys, outs):
    inward, outward, expand, shrink, small = ins
    out, *early = outs
    first = place_of[0] == 0
    rows = inward.shape[1]
    width = inward.shape[2] // 3
    half = width // 2
    at = 0
    if early:
        early[0][rows : rows + 16] = jnp.zeros((16, width), LOW)
        for q in range(rows // 16):
            early[0][rows : rows + 16, q * SMALL : (q + 1) * SMALL] = small[q * 16 : (q + 1) * 16]
    else:
        at = small.shape[1]
        out[:, :at] = small[...]
    for l in range(layers):
        sources = [inward[l, :, p * width : (p + 1) * width] for p in range(3)] + [outward[l]]
        sources.append(expand[l])
        sources += [shrink[l, j * rows : (j + 1) * rows] for j in range(shrink.shape[1] // rows)]
        for n, value in enumerate(sources):
            part = value.shape[1] // 2
            value = jnp.where(first, value[:, :part], value[:, part:]).astype(LOW)
            if early and l == 0 and n < 4:
                start = 0 if n < 2 else rows + 16
                early[0][start : start + rows, (n % 2) * half : (n % 2 + 1) * half] = value
            elif early and l == layers - 1 and n == 4:
                for t in range(2):
                    early[1][2 * t * rows : (2 * t + 1) * rows] = value[:, t * width : (t + 1) * width]
            elif early and l == layers - 1 and n > 4:
                start = (2 * ((n - 5) // 2) + 1) * rows
                lanes = (n - 5) % 2 * half
                early[1][start : start + rows, lanes : lanes + half] = value
            else:
                out[:, at : at + part] = value
                at += part


def swap_cores(value):
    return lax.ppermute(value, "dp", [(0, 1), (1, 0)])


def across(value, mask, size):
    return lax.ppermute(value, "fsdp", [(i, i ^ mask) for i in range(size)])


def tie(*values):
    return lax.optimization_barrier(values)


def total_of(value, size):
    value = value + swap_cores(value)
    bit = 1
    while bit < size:
        if 2 * bit < size:
            a, b, c = (across(value, m * bit, size) for m in (1, 2, 3))
            value = (value + a) + (b + c)
        else:
            value = value + across(value, bit, size)
        bit *= 4
    return value


def arrange_kernel(parts, place_of, ins, anys, outs, sems):
    copies, at = [], 0
    for h in range(2):
        for piece in anys:
            copies += fetch(
                [piece.at[h * parts[0] : h * parts[0] + parts[h]]],
                [outs[0].at[at : at + parts[h]]],
                sems,
                len(copies),
            )
            at += parts[h]
    for copy in copies:
        copy.wait()


def place_kernel(parts, rows, place_of, ins, anys, outs, sems):
    quarter, from_x, from_y, far_a, far_b = anys
    tiles, *small = outs
    count = tiles.shape[0] // 2
    x, y, z = place_of[1], place_of[2], place_of[3]
    for n in range(16):
        xor_z, xor_y, xor_x = n // 4, n // 2 % 2, n % 2
        index = jnp.bitwise_xor(z, xor_z) * 4 + jnp.bitwise_xor(y, xor_y) * 2 + jnp.bitwise_xor(x, xor_x)
        for h in range(2):
            at = xor_z * parts[h]
            if xor_x and xor_y:
                source = (far_a, far_b)[h]
            else:
                source = from_x if xor_x else from_y if xor_y else quarter
                at += h * 4 * parts[0]
            for t in range(count):
                here = source.at[at + t * rows : at + (t + 1) * rows]
                fetch([here], [tiles.at[h * count + t, index]], sems, h * count + t)
            if h == 0 and small:
                here = source.at[at + count * rows : at + parts[0]]
                fetch([here], [small[0].at[index]], sems, 2 * count)
    targets = [tiles.at[t] for t in range(2 * count)] + small
    for n, target in enumerate(targets):
        pltpu.make_async_copy(target, target, sems.at[n]).wait()


class Gather:
    def __init__(self, place, shard, parts, rows):
        self.place, self.shard, self.parts, self.rows = place, shard, parts, rows

    def along_z(self):
        self.got = [across(self.shard, mask, 16) for mask in Z]

    def in_plane(self):
        width = self.shard.shape[1]
        (quarter,) = call(
            functools.partial(arrange_kernel, self.parts),
            self.place,
            [((4 * sum(self.parts), width), LOW)],
            [],
            [self.shard] + self.got,
            [pltpu.SemaphoreType.DMA((8,))],
        )
        self.quarter, self.near = quarter, [across(quarter, X, 16), across(quarter, Y, 16)]

    def forward(self):
        cut = 4 * self.parts[0]
        from_x, from_y = self.near
        self.far = [across(from_y[:cut], X, 16), across(from_x[cut:], Y, 16)]

    def result(self):
        width = self.shard.shape[1]
        count, more = divmod(self.parts[0], self.rows)
        outs = [((2 * count, 16, self.rows, width), LOW)]
        if more:
            outs.append(((16, more, width), LOW))
        return call(
            functools.partial(place_kernel, self.parts, self.rows),
            self.place,
            outs,
            [],
            [self.quarter] + self.near + self.far,
            [pltpu.SemaphoreType.DMA((2 * count + 1,))],
        )


X, Y = 1, 2
Z = (4, 8, 12)


def round_kernel(jobs, small_job, n_ins, counts, smalls, last, place_of, ins, anys, outs, *scratch):
    new, once, twice, done = counts
    small_new, small_once, small_twice, small_done = smalls
    rest = list(ins[n_ins:]) + list(outs) + list(scratch)
    pop = lambda present, n=1: [rest.pop(0) for _ in range(n)] if present else [None] * n
    (keep_once,), (small_keep_once,) = pop(once), pop(small_once)
    (keep_twice,), (small_keep_twice,) = pop(twice), pop(small_twice)
    from_x, from_y = pop(once or twice, 2)
    (keep_done,), (small_keep_done,) = pop(done), pop(small_done)
    from_z = pop(done, 3)
    (squares_in,), (sums,) = pop(done), pop(last)
    to_x, to_y = pop(new or once, 2)
    (out_once,), (small_out_once,) = pop(new), pop(small_new)
    (out_twice,), (small_out_twice,) = pop(once), pop(small_once)
    (out_done,), (small_out_done,) = pop(twice), pop(small_twice)
    to_z = pop(twice, 3)
    (share,), (small_share,), (squares,) = pop(done), pop(small_done), pop(done)
    (totals,) = pop(last)
    (tile,), (unit,), (small_tile,) = pop(new), pop(new), pop(small_new)
    rows = (out_once if new else out_twice if once else out_done if twice else share).shape[-2]
    rows = rows // (8 if new else 4 if once else 1)
    bits, z = (place_of[1], place_of[2]), place_of[3]
    to, came = (to_x, to_y), (from_x, from_y)

    def block(index, size=rows):
        if isinstance(index, int):
            return pl.ds(index * size, size)
        return pl.ds(pl.multiple_of(index * size, 16), size)

    def factor(spec):
        which, index, low, high = spec
        ref = ins[which] if index is None else ins[which].at[index]
        return ref[...] if low is None else ref[:, low:high]

    def put_small(ref, start, group, side, value):
        for q in range(rows // 16):
            lanes = side * (rows // 16) + q
            ref[pl.ds(start + group * 16, 16), lanes * SMALL : (lanes + 1) * SMALL] = value[
                q * 16 : (q + 1) * 16
            ].astype(LOW)

    def take_small(ref, start, group, side):
        parts = []
        for q in range(rows // 16):
            lanes = side * (rows // 16) + q
            at = pl.ds(pl.multiple_of(start + group * 16, 16), 16)
            parts.append(ref[at, lanes * SMALL : (lanes + 1) * SMALL])
        return jnp.concatenate(parts, 0).astype(FULL)

    def summed(products):
        total = None
        for left, right in products:
            product = cross(factor(left), factor(right))
            total = product if total is None else total + product
        return total

    for p in range(new):
        if len(jobs[p]) == 4:
            for quarter, products in enumerate(jobs[p]):
                unit[...] = summed(products)
                half = unit.shape[1]
                for index in range(4):
                    for s in range(2):
                        for j in range(2):
                            tile[s, block(quarter * 4 + index), j * half : (j + 1) * half] = unit[
                                block(index * 4 + 2 * s + j), :
                            ]
        else:
            for s in range(2):
                for low, high, products in jobs[p][s]:
                    tile[s, :, low:high] = summed(products)
        for s in range(2):
            for zz in range(4):
                for other in range(2):
                    at = zz * 2 + other
                    index = lambda bit: zz * 4 + (other * 2 + bit if s == 0 else bit * 2 + other)
                    to[s][block(p * 8 + at), :] = tile[s, block(index(1 - bits[s])), :].astype(LOW)
                    out_once[p, s, block(at), :] = tile[s, block(index(bits[s])), :]
    if small_new:
        products, norms_at = small_job
        total = summed(products)
        norms = jnp.concatenate([ins[mine][...] + ins[theirs][...] for mine, theirs in norms_at], 0)
        high = norms.astype(LOW)
        shape = (norms.shape[0], SMALL)
        column = lax.broadcasted_iota(jnp.int32, shape, 1) - V
        pick = jnp.where(lax.broadcasted_iota(jnp.int32, shape, 0) == column, 1.0, 0.0).astype(LOW)
        total = total + (cross(high, pick) + cross((norms - high.astype(FULL)).astype(LOW), pick))
        small_tile[...] = total
        for zz in range(4):
            for other in range(2):
                index = lambda bit: zz * 4 + other * 2 + bit
                send = small_tile[block(index(1 - bits[0])), :]
                put_small(to_x, (new * 8 + once * 4) * rows, other * 2 + zz // 2, zz % 2, send)
                small_out_once[block(zz * 2 + other), :] = small_tile[block(index(bits[0])), :]
    for p in range(once):
        for s in range(2):
            for zz in range(4):
                for bit in range(2):
                    at = zz * 2 + (bits[1 - s] if bit else 1 - bits[1 - s])
                    value = keep_once[p, s, block(at), :] + came[s][block(p * 8 + at), :].astype(FULL)
                    if bit:
                        out_twice[p, s, block(zz), :] = value
                    else:
                        to[1 - s][block(new * 8 + p * 4 + zz), :] = value.astype(LOW)
    if small_once:
        start = (once * 8 + twice * 4) * rows
        for zz in range(4):
            for bit in range(2):
                other = bits[1] if bit else 1 - bits[1]
                value = small_keep_once[block(zz * 2 + other), :]
                value = value + take_small(from_x, start, other * 2 + zz // 2, zz % 2)
                if bit:
                    small_out_twice[block(zz), :] = value
                else:
                    put_small(to_y, (new * 8 + once * 4) * rows, zz, 0, value)
    for p in range(twice):
        for s in range(2):
            for xor in range(4):
                at = jnp.bitwise_xor(z, xor)
                value = keep_twice[p, s, block(at), :] + came[1 - s][
                    block(once * 8 + p * 4 + at), :
                ].astype(FULL)
                if xor == 0:
                    out_done[p, s] = value
                else:
                    to_z[xor - 1][block(2 * p + s), :] = value.astype(LOW)
    if small_twice:
        for xor in range(4):
            at = jnp.bitwise_xor(z, xor)
            value = small_keep_twice[block(at), :]
            value = value + take_small(from_y, (once * 8 + twice * 4) * rows, at, 0)
            if xor == 0:
                small_out_done[...] = value
            else:
                put_small(to_z[xor - 1], twice * 2 * rows, 0, 0, value)
    if done:
        squares[...] = squares_in[...]
    for p in range(done):
        for s in range(2):
            value = keep_done[p, s]
            for f in from_z:
                value = value + f[block(2 * p + s), :].astype(FULL)
            share[p, s] = value
            squares[...] += jnp.sum(value * value, 0, keepdims=True)
    if small_done:
        value = small_keep_done[...]
        for f in from_z:
            value = value + take_small(f, done * 2 * rows, 0, 0)
        small_share[...] = value
    if last:
        total = jnp.sum(squares[...], 1, keepdims=True)
        if small_done:
            square = jnp.sum(jnp.sum(value * value, 0, keepdims=True), 1, keepdims=True)
            total = total + jnp.where(place_of[0] == 0, square, jnp.zeros_like(square))
        lane = lax.broadcasted_iota(jnp.int32, sums.shape, 1)
        totals[...] = jnp.where(lane == 2, total, sums[...])


class Rounds:
    def __init__(self, place, rows, width, sums):
        self.place, self.rows, self.width, self.sums = place, rows, width, sums
        self.counts, self.smalls = (0,) * 4, (False,) * 4
        self.kept, self.small_kept = [None] * 3, [None] * 3
        self.came = self.came_z = self.totals = None
        self.shares, self.others, self.small_share = [], [], None
        self.squares = jnp.zeros((1, width), FULL)
        self.flying, self.swapping = [], 0

    def step(self, chunk, *ties, small=None):
        rows, width = self.rows, self.width
        new, once, twice, done = counts = (len(chunk),) + self.counts[:3]
        smalls = (small is not None,) + self.smalls[:3]
        last = not (new or once or twice)
        arrays, jobs = [], []

        def number(spec):
            array, *place = spec
            for i, known in enumerate(arrays):
                if known is array:
                    return (i, *place)
            arrays.append(array)
            return (len(arrays) - 1, *place)

        numbered = lambda products: [(number(l), number(r)) for l, r in products]
        for pair in chunk:
            if len(pair) == 4:
                jobs.append([numbered(products) for products in pair])
            else:
                jobs.append([[(a, b, numbered(ps)) for a, b, ps in tile] for tile in pair])
        small_job = None
        if small is not None:
            small_job = (
                [(number(l), number(r)) for l, r in small[0]],
                [(number((a,))[0], number((b,))[0]) for a, b in small[1]],
            )
        ins = list(arrays)
        for stage in range(2):
            ins += [self.kept[stage]] * (counts[1 + stage] > 0)
            ins += [self.small_kept[stage]] * smalls[1 + stage]
        if once or twice:
            ins += self.came
        if done:
            ins += [self.kept[2]] + [self.small_kept[2]] * smalls[3] + self.came_z + [self.squares]
        ins += [self.sums] * last
        outs = []
        if new or once:
            for added in (64 * smalls[0], 64 * smalls[1]):
                outs.append((((new * 8 + once * 4) * rows + added, width), LOW))
        for stage, blocks in enumerate((8, 4, 1)):
            if counts[stage]:
                outs.append(((counts[stage], 2, blocks * rows, width), FULL))
            if smalls[stage]:
                outs.append(((blocks * rows, SMALL), FULL))
        if twice:
            outs += [((twice * 2 * rows + 16 * smalls[2], width), LOW)] * 3
        if done:
            outs.append(((done, 2, rows, width), FULL))
            outs += [((rows, SMALL), FULL)] * smalls[3]
            outs.append(((1, width), FULL))
        outs += [((1, SMALL), FULL)] * last
        length = 2 * arrays[0].shape[-2] if new else 0
        scratch = []
        if new:
            scratch.append(pltpu.VMEM((2, 16 * rows, width), FULL))
            scratch.append(pltpu.VMEM((16 * rows, width // 2), FULL))
        scratch += [pltpu.VMEM((16 * rows, SMALL), FULL)] * smalls[0]
        got = list(
            call(
                functools.partial(
                    round_kernel, jobs, small_job, len(arrays), counts, smalls, last
                ),
                self.place,
                outs,
                ins,
                [],
                scratch,
                4 * new * length * width * width,
            )
        )
        if last:
            self.totals = got.pop()
        if done:
            self.squares = got.pop()
            if smalls[3]:
                self.small_share = got.pop()
            self.shares.append(got.pop())
        self.counts, self.smalls = counts, smalls
        self.kept, self.small_kept = [None] * 3, [None] * 3
        if last:
            return ties
        got, ties = tie(got, ties)
        to = [got.pop(0) for _ in range(2)] if new or once else []
        for stage in range(3):
            if counts[stage]:
                self.kept[stage] = got.pop(0)
            if smalls[stage]:
                self.small_kept[stage] = got.pop(0)
        self.flying = [across(v, mask, 16) for v, mask in zip(to, (X, Y))]
        self.flying += [across(v, mask, 16) for v, mask in zip(got, Z)]
        self.swapping = 0
        while len(self.flying) < 5 and len(self.others) + self.swapping < len(self.shares):
            self.flying.append(swap_cores(self.shares[len(self.others) + self.swapping]))
            self.swapping += 1
        return ties

    def finish(self, *ties):
        flying, ties = tie(self.flying, ties)
        self.came = self.came_z = None
        if self.counts[0] or self.counts[1]:
            self.came, flying = flying[:2], flying[2:]
        if self.counts[2]:
            self.came_z, flying = flying[:3], flying[3:]
        self.others += flying
        return ties

    def left(self):
        return any(self.counts[:3])

    def swap_rest(self):
        self.others += [swap_cores(v) for v in self.shares[len(self.others) :]]


class PlainRounds:
    def __init__(self):
        self.shares, self.squares = [], []

    def step(self, chunk, *ties):
        def factor(spec):
            array, index, low, high = spec
            array = array if index is None else array[index]
            return array if low is None else array[:, low:high]

        summed = lambda products: sum(cross(factor(l), factor(r)) for l, r in products)
        scatter = lambda v: lax.psum_scatter(v, "fsdp", scatter_dimension=0, tiled=True)
        shares = []
        for pair in chunk:
            if len(pair) == 4:
                v = scatter(jnp.concatenate([summed(products) for products in pair], 0))
                v = v.reshape(2, 2, -1, v.shape[1])
                shares.append(jnp.concatenate([v[:, 0], v[:, 1]], 2))
            else:
                tiles = [jnp.concatenate([summed(ps) for _, _, ps in t], 1) for t in pair]
                shares.append(jnp.stack([scatter(t) for t in tiles]))
        share = jnp.stack(shares)
        self.shares.append((share, swap_cores(share)))
        self.squares.append(jnp.sum(share * share, (0, 1, 2))[None])
        return ties

    def finish(self, *ties):
        return ties

    def left(self):
        return False


def half_of(value, core):
    half = value.shape[1] // 2
    return lax.dynamic_slice_in_dim(value, core * half, half, 1)


def body(
    fsdp,
    codons,
    masked,
    segments,
    inward,
    outward,
    expand,
    shrink,
    codon_table,
    norm_params,
    inward_first,
    inward_second,
    outward_first,
    outward_second,
    expand_first,
    expand_second,
    shrink_first,
    shrink_second,
    table_first,
    table_second,
    norm_first,
    norm_second,
):
    layers = inward.shape[0]
    length = codons.shape[0]
    rows = inward.shape[1]
    width = rows * fsdp
    half = width // 2
    fast = fsdp == 16 and rows == 48 and layers > 1
    core, index = lax.axis_index("dp"), lax.axis_index("fsdp")
    bit = lambda b: lax.rem(lax.div(index, b), 2)
    place = jnp.stack([core, bit(1), bit(2), lax.div(index, 4)]).astype(jnp.int32)
    weight = masked.astype(FULL)
    inputs = jnp.where(masked == 1, V - 1, codons)

    norms = norm_params.shape[0] * 2
    small = jnp.concatenate(
        [codon_table.astype(LOW), norm_params.astype(LOW).reshape(norms, rows)], 0
    )
    small = jnp.pad(small.T, ((0, 0), (0, -small.shape[0] % 128)))
    columns = small.shape[1] + layers * 6 * width
    shapes = [(rows, columns)]
    if fast:
        shapes = [(rows, (layers - 1) * 6 * width), (2 * rows + 16, width), (4 * rows, width)]
    weights, *early = call(
        functools.partial(pack_kernel, layers),
        place,
        [(shape, LOW) for shape in shapes],
        [inward, outward, expand, shrink, small],
    )
    weights = lax.all_gather(weights, ("fsdp", "dp"), axis=0, tiled=True)
    weights = weights.reshape(fsdp, 2, rows, -1)
    if not fast:
        columns = [weights[:, :, :, : small.shape[1]]]
        for at in range(small.shape[1], weights.shape[3], 6 * width):
            columns.append(weights[:, :, :, at : at + 4 * width])
            quarter = weights[:, :, :, at + 4 * width : at + 6 * width]
            quarter = quarter.reshape(fsdp, 2, rows, 4, half).transpose(1, 0, 3, 2, 4)
            quarter = quarter.reshape(2, 4, width, half).transpose(0, 2, 1, 3)
            columns.append(quarter.reshape(2, fsdp, rows, 2 * width).transpose(1, 0, 2, 3))
        weights = jnp.concatenate(columns, 3).transpose(1, 0, 2, 3).reshape(1, 2, width, -1)
    mixers, hiddens = [[weights]] * layers, [[weights]] * layers
    if fast:
        first = Gather(place, early[0], (rows + 16, rows), rows)
        last = Gather(place, early[1], (2 * rows, 2 * rows), rows)
        first.along_z()
        first.got, last.shard = tie(first.got, last.shard)
        first.in_plane()
        last.along_z()
        first.near, last.got = tie(first.near, last.got)
        first.forward()
        (first.far,) = tie(first.far)
        own, small = first.result()
        mixers[0] = [own, swap_cores(own)]
        own, last.got = tie(own, last.got)
        last.in_plane()
        small = small[:, :, : rows // 16 * SMALL].reshape(16, 16, rows // 16, SMALL)
        small = small.transpose(0, 2, 1, 3).reshape(width, SMALL).T
    else:
        small = weights[:, 0, :, :SMALL].reshape(width, SMALL).T
    start = -2 * width if fast else weights.shape[3] - layers * 6 * width
    base = lambda l: start + l * 6 * width
    gains = small[V : V + norms].astype(FULL).reshape(-1, 2, width)

    cosine, sine = rotary_tables(length)
    chosen = (inputs[:, None] == jnp.arange(SMALL, dtype=jnp.int32)[None, :]).astype(LOW)
    resid = dot(chosen, small)
    kept = []
    for l in range(layers):
        gain = gains[2 * l : 2 * l + 2]
        middle, query, keys, values, lse, pack = attention_forward(
            place, resid, mixers[l], base(l), gain[0], cosine, sine, segments
        )
        if fast and l == 0:
            middle, last.near = tie(middle, last.near)
            last.forward()
            (own,) = last.result()
            hiddens[-1] = [own, swap_cores(own)]
            middle, hiddens[-1][0] = tie(middle, own)
        output, pack_mid, hidden = hidden_forward(place, middle, hiddens[l], base(l), gain[1])
        kept.append((resid, query, keys, values, lse, pack, middle, hidden, pack_mid))
        resid = output
    grad, branch, branch_own, branch_other, head_in, grad_logits, grad_norms, sums = head(
        place, resid, small, gains[2 * layers], codons, weight
    )
    grad_norms = [grad_norms]
    early = (head_in, grad_logits, chosen)
    early_came = [swap_cores(v) for v in early]
    mid_came = [swap_cores(saved[-1]) for saved in kept]
    pack_came = [swap_cores(saved[5]) for saved in kept]
    grad, branch, mid_came[-1] = tie(grad, branch, mid_came[-1])

    rounds = Rounds(place, rows, width, sums) if fast else PlainRounds()
    whole = lambda array, i=None: (array, i, None, None)
    tile = lambda left, right, other_left, other_right: [
        (0, width, [(left, right), (other_left, other_right)])
    ]
    chunk = []
    for l in reversed(range(layers)):
        resid, query, keys, values, lse, pack, middle, hidden, pack_mid = kept[l]
        gain = gains[2 * l : 2 * l + 2]
        branch_came = swap_cores(branch_other)
        chunk.append(
            [
                [
                    (whole(pack_mid, 1 + t), whole(branch_own)),
                    (whole(mid_came[l], 1 + t), whole(branch_came)),
                ]
                for t in range(4)
            ]
        )
        grad, branch = rounds.step(chunk, grad, branch)
        grad_middle, gains_mid, up_own, up_other = hidden_back(
            place, grad, branch, middle, hidden, hiddens[l], base(l), gain[1]
        )
        grad_middle, up_own, up_other, early_came = rounds.finish(
            grad_middle, up_own, up_other, early_came
        )
        up_came = swap_cores(up_other)
        if l == 0:
            norms_early = jnp.concatenate([gains_mid] + grad_norms, 0)
            norms_early = (norms_early, swap_cores(norms_early))
        (grad_middle,) = rounds.step(
            [
                [
                    tile(
                        whole(pack_mid, 0), whole(up_own, s), whole(mid_came[l], 0), whole(up_came, s)
                    )
                    for s in range(2)
                ]
            ],
            grad_middle,
        )
        grad, branch, branch_own, branch_other, gains_in, mix_own, mix_other = attention_back(
            place, grad_middle, resid, mixers[l], base(l), gain[0], cosine, sine, segments,
            query, keys, values, lse,
        )
        grad_norms = [gains_in, gains_mid] + grad_norms
        grad, branch, branch_own, branch_other, mix_own, mix_other, mid_came, pack_came = (
            rounds.finish(
                grad, branch, branch_own, branch_other, mix_own, mix_other, mid_came, pack_came
            )
        )
        mix_came = swap_cores(mix_other)
        products = lambda i, a, b: [
            ((pack, i, None, None), (mix_own, 1, a, b)),
            ((pack_came[l], i, None, None), (mix_came, 1, a, b)),
        ]
        chunk = [
            [
                tile(whole(pack, 0), whole(mix_own, 0), whole(pack_came[l], 0), whole(mix_came, 0)),
                [(0, half, products(0, 0, half)), (half, width, products(1, half, width))],
            ]
        ]
    late = (grad_norms[0], swap_cores(grad_norms[0]))
    branch_came = swap_cores(branch)
    products = [(whole(early[0]), whole(early[1])), (whole(early_came[0]), whole(early_came[1]))]
    products += [(whole(branch), whole(early[2])), (whole(branch_came), whole(early_came[2]))]
    if fast:
        rounds.step(chunk, small=(products, [late, norms_early]))
        while rounds.left():
            rounds.finish()
            rounds.step([])
        rounds.swap_rest()
        share_small = rounds.small_share
        small_other = swap_cores(share_small)
        totals = rounds.totals
    else:
        rounds.step(chunk)
        table = sum(cross(l[0], r[0]) for l, r in products)
        table = table + jnp.pad(
            jnp.concatenate([a + b for a, b in (late, norms_early)], 0).T,
            ((0, 0), (V, SMALL - V - norms)),
        )
        table = jnp.where(core == 0, table, swap_cores(table))
        share_small = lax.psum_scatter(table, "fsdp", scatter_dimension=0, tiled=True)
        squares = jnp.sum(share_small * share_small) * (core == 0)
        for value in rounds.squares:
            squares = squares + jnp.sum(value)
        totals = sums + jnp.where(jnp.arange(SMALL) == 2, squares, 0.0)[None]
    totals = total_of(totals, fsdp)
    shares = list(zip(rounds.shares, rounds.others)) if fast else rounds.shares
    places = [(2 * (layers - 1 - l), 0 if l == layers - 1 else 1) for l in range(layers)]

    def tiles_at(chunk, pair):
        own, other = (v[pair] for v in shares[chunk])
        ordered = (jnp.where(core == 0, own, other), jnp.where(core == 0, other, own))
        return [v[s] for v in ordered for s in range(2)]

    if not fast:
        share_in, share_out, share_up, share_down = [], [], [], []
        side = lambda *values: jnp.concatenate(values, 1)
        for at, pair in places:
            a_0, b_0, a_1, b_1 = tiles_at(at + 2, 0)
            share_in.append(
                side(
                    a_0[:, :half], a_1[:, :half], a_0[:, half:],
                    a_1[:, half:], b_0[:, :half], b_1[:, :half],
                )
            )
            share_out.append(side(b_0[:, half:], b_1[:, half:]))
            share_up.append(side(*tiles_at(at + 1, 0)))
            a_0, b_0, a_1, b_1 = tiles_at(at, pair)
            share_down.append(
                jnp.concatenate(
                    [
                        side(x[:, j * half : (j + 1) * half], y[:, j * half : (j + 1) * half])
                        for x, y in ((a_0, a_1), (b_0, b_1))
                        for j in range(2)
                    ],
                    0,
                )
            )
        share_in, share_out, share_up, share_down = (
            jnp.stack(v) for v in (share_in, share_out, share_up, share_down)
        )
    masters = (inward, outward, expand, shrink, codon_table, norm_params)
    firsts = (inward_first, outward_first, expand_first, shrink_first, table_first, norm_first)
    seconds = (
        inward_second,
        outward_second,
        expand_second,
        shrink_second,
        table_second,
        norm_second,
    )
    if fast:
        chunks = [((at + 2, 0), (at + 1, 0), (at, pair)) for at, pair in places]
        own, other = zip(*shares)
        states = [v for group in zip(masters, firsts, seconds) for v in group]
        states[12:15] = [v.T for v in states[12:15]]
        grad_norm, *values = optimizer(
            place, totals, (share_small, small_other), chunks, own, other, states
        )
        values[12:15] = [v.T for v in values[12:15]]
    else:
        grad_norm, scale = scale_of(totals)
        share_small = share_small[:, : V + norms].T
        grads = (share_in, share_out, share_up, share_down)
        grads += (share_small[:V], share_small[V:].reshape(-1, 2, rows))
        values = []
        for index, grad in enumerate(grads):
            rate, decay = (RATE_VECTOR, 0.0) if index == 5 else (RATE_MATRIX, DECAY)
            values.extend(
                adam_step(masters[index], grad * scale.reshape(()), firsts[index], seconds[index], rate, decay)
            )
    return (totals[0, 0], totals[0, 1], grad_norm.reshape(()), *values)


def solution(mesh):
    in_specs = (
        P(("fsdp", "dp")),
        P(("fsdp", "dp")),
        P(("fsdp", "dp")),
        P(None, "fsdp", None),
        P(None, "fsdp", None),
        P(None, "fsdp", None),
        P(None, "fsdp", None),
        P(None, "fsdp"),
        P(None, None, "fsdp"),
        P(None, "fsdp", None),
        P(None, "fsdp", None),
        P(None, "fsdp", None),
        P(None, "fsdp", None),
        P(None, "fsdp", None),
        P(None, "fsdp", None),
        P(None, "fsdp", None),
        P(None, "fsdp", None),
        P(None, "fsdp"),
        P(None, "fsdp"),
        P(None, None, "fsdp"),
        P(None, None, "fsdp"),
    )
    out_specs = (
        P(),
        P(),
        P(),
        P(None, "fsdp", None),
        P(None, "fsdp", None),
        P(None, "fsdp", None),
        P(None, "fsdp", None),
        P(None, "fsdp", None),
        P(None, "fsdp", None),
        P(None, "fsdp", None),
        P(None, "fsdp", None),
        P(None, "fsdp", None),
        P(None, "fsdp", None),
        P(None, "fsdp", None),
        P(None, "fsdp", None),
        P(None, "fsdp"),
        P(None, "fsdp"),
        P(None, "fsdp"),
        P(None, None, "fsdp"),
        P(None, None, "fsdp"),
        P(None, None, "fsdp"),
    )
    step = functools.partial(body, mesh.shape["fsdp"])
    return jax.shard_map(step, mesh=mesh, in_specs=in_specs, out_specs=out_specs, check_vma=False)
```

```python
import functools

import jax
import jax.numpy as jnp
from jax import lax
from jax.experimental import pallas as pl
from jax.experimental.pallas import tpu as pltpu
from jax.sharding import PartitionSpec as P

HD = 64
V = 70
STEP = 10


NORM_EPS = 1e-05
BETA_ONE = 0.9
BETA_TWO = 0.95
ADAM_EPS = 1e-08
DECAY = 0.1
RATE_MATRIX = 0.05
RATE_VECTOR = 0.3
CLIP = 0.05


def rotary_tables(length):
    freq = 10000.0 ** (-jnp.arange(HD // 2, dtype=jnp.float32) * 2.0 / HD)
    angle = jnp.arange(length, dtype=jnp.float32)[:, None] * freq[None, :]
    cosine, sine = jnp.cos(angle), jnp.sin(angle)
    return (
        jnp.concatenate([cosine] * 4, 1),
        jnp.concatenate([-sine, sine] * 2, 1),
    )


def normalize(resid, gain, bias):
    mean = jnp.mean(resid, -1, keepdims=True)
    centred = resid - mean
    inverse = lax.rsqrt(jnp.mean(centred * centred, -1, keepdims=True) + NORM_EPS)
    unit = centred * inverse
    return (unit * gain + bias, unit, inverse)


def normalize_back(grad, unit, inverse, gain):
    scaled = grad * gain
    across = (
        scaled
        - jnp.mean(scaled, -1, keepdims=True)
        - unit * jnp.mean(scaled * unit, -1, keepdims=True)
    )
    return (across * inverse, jnp.sum(grad * unit, 0, keepdims=True), jnp.sum(grad, 0, keepdims=True))


def dot(left, right):
    return jnp.dot(left, right, preferred_element_type=jnp.float32)


def dot_nt(left, right):
    return lax.dot_general(
        left, right, (((1,), (1,)), ((), ())), preferred_element_type=jnp.float32
    )


def cross(left, right):
    return lax.dot_general(
        left, right, (((0,), (0,)), ((), ())), preferred_element_type=jnp.float32
    )


VMEM_LIMIT = 56 * 1024 * 1024
LOW, FULL = jnp.bfloat16, jnp.float32
SMALL = 128


class Sent:
    def __init__(self, here, there, sems):
        self.here, self.there, self.sems = here, there, sems
        self.shape, self.at = here.shape, here.at
        self.copies = []

    def __getitem__(self, at):
        return self.here[at]

    def __setitem__(self, at, value):
        self.here[at] = value

    def send(self, index=None):
        here, there = self.here, self.there
        if index is not None:
            here, there = here.at[index], there.at[index]
        copy = pltpu.make_async_copy(here, there, self.sems.at[len(self.copies)])
        copy.start()
        self.copies.append(copy)


def call(kernel, scalars, outs, ins, anys=(), scratch=(), flops=0, sent=(), limit=VMEM_LIMIT):
    whole = pl.BlockSpec(memory_space=pltpu.VMEM)
    left = pl.BlockSpec(memory_space=pl.ANY)

    def body(scalars, *refs):
        refs = list(refs)
        take = lambda n: [refs.pop(0) for _ in range(n)]
        in_refs, any_refs, out_refs = take(len(ins)), take(len(anys)), take(len(outs))
        here = take(len(sent))
        for n, i in enumerate(sent):
            out_refs[i] = Sent(here[n], out_refs[i], refs[-1].at[n])
        kernel(scalars, in_refs, any_refs, out_refs, *(refs[:-1] if sent else refs))
        for i in sent:
            for copy in out_refs[i].copies:
                copy.wait()

    return pl.pallas_call(
        body,
        out_shape=[jax.ShapeDtypeStruct(s, t) for s, t in outs],
        in_specs=[pl.BlockSpec(memory_space=pltpu.SMEM)]
        + [whole] * len(ins)
        + [left] * len(anys),
        out_specs=[left if i in sent else whole for i in range(len(outs))],
        scratch_shapes=[pltpu.VMEM(*outs[i]) for i in sent]
        + list(scratch)
        + [pltpu.SemaphoreType.DMA((len(sent), 5))] * (len(sent) > 0),
        compiler_params=pltpu.CompilerParams(vmem_limit_bytes=limit),
        cost_estimate=pl.CostEstimate(
            flops=flops,
            bytes_accessed=sum(x.size * x.dtype.itemsize for x in list(ins) + list(anys)),
            transcendentals=0,
        ),
    )(scalars, *ins, *anys)


def fetch(sources, targets, sems, first=0):
    copies = [
        pltpu.make_async_copy(s, t, sems.at[first + i])
        for i, (s, t) in enumerate(zip(sources, targets))
    ]
    for c in copies:
        c.start()
    return copies


def tile_of(ref, core, at):
    return ref.at[:, core, :, at : at + ref.shape[0] * ref.shape[2]]


def matrix(ref, place, low=None, high=None):
    value = ref[place] if low is None else ref[place, :, :, low:high]
    return value.reshape(-1, value.shape[-1])


def mixer_tile(anys, cores, place, t, base, width):
    if len(anys) == 2:
        return anys[place].at[t]
    return tile_of(anys[0], cores[place], base + t * width)


def mixer_scratch(weights):
    w = weights[0]
    blocks, rows = (w.shape[1], w.shape[2]) if len(weights) == 2 else (w.shape[0], w.shape[2])
    return [pltpu.VMEM((2, blocks, rows, blocks * rows), LOW)] * 2


def swap_halves(value):
    lane = lax.broadcasted_iota(jnp.int32, value.shape, 1)
    return jnp.where(
        lax.rem(lane, HD) < HD // 2,
        pltpu.roll(value, 128 - HD // 2, 1),
        pltpu.roll(value, HD // 2, 1),
    )


def ordered(first, own, other):
    return jnp.concatenate([jnp.where(first, own, other), jnp.where(first, other, own)], 1)


def head_mask(shape, head):
    lane = lax.broadcasted_iota(jnp.int32, shape, 1)
    return (lane < HD) if head == 0 else (lane >= HD)


def attention_forward_kernel(
    base, place_of, ins, anys, outs, w_a, w_b, mixed, bias, columns_of_lse, sems
):
    resid, seg_col, seg_row, cosine, sine, gains = ins
    middle, query, keys, values, lse, pack = outs
    width = resid.shape[1]
    half = width // 2
    cores = (place_of[0], 1 - place_of[0])
    copies = fetch(
        [mixer_tile(anys, cores, p, t, base, width) for t in range(2) for p in range(2)],
        [w.at[place] for w in (w_a, w_b) for place in range(2)],
        sems,
    )
    first = place_of[0] == 0
    normed, _, _ = normalize(resid[...], gains[0:1], gains[1:2])
    normed_low, attended = pack.at[0], pack.at[1]
    normed_low[...] = normed.astype(LOW)
    bias[...] = jnp.where(seg_col[...] == seg_row[...], 0.0, -1000000000.0)
    for place in range(2):
        copies[place].wait()
        mixed[...] = dot(normed_low[...], matrix(w_a, place))
        for p in range(half // 128):
            for part, target, scale in ((0, query, HD ** (-0.5)), (1, keys, 1.0)):
                x = mixed[:, part * half + p * 128 : part * half + (p + 1) * 128]
                x = x * cosine[...] + swap_halves(x) * sine[...]
                x = (x * scale if scale != 1.0 else x).astype(LOW)
                target[:, place * half + p * 128 : place * half + (p + 1) * 128] = x
    for place in range(2):
        copies[2 + place].wait()
        values[:, place * half : (place + 1) * half] = dot(
            normed_low[...], matrix(w_b, place, 0, half)
        ).astype(LOW)

    columns_of_lse[...] = jnp.zeros_like(columns_of_lse)

    for p in range(width // 128):
        columns = slice(p * 128, (p + 1) * 128)
        q, k, v = query[:, columns], keys[:, columns], values[:, columns]
        out = []
        for head in range(2):
            masked_q = jnp.where(head_mask(q.shape, head), q, jnp.zeros_like(q))
            scores = dot_nt(masked_q, k) + bias[...]
            top = jnp.max(scores, -1, keepdims=True)
            expo = jnp.exp(scores - top)
            total = jnp.sum(expo, -1, keepdims=True)
            probs = (expo * (1.0 / total)).astype(LOW)
            out.append(dot(probs, v))
            lane = lax.broadcasted_iota(jnp.int32, columns_of_lse.shape, 1)
            columns_of_lse[...] = jnp.where(
                lane == 2 * p + head, top + jnp.log(total), columns_of_lse[...]
            )
        attended[:, columns] = jnp.where(head_mask(out[0].shape, 0), out[0], out[1]).astype(LOW)
    lse[...] = columns_of_lse[...].T[: lse.shape[0]]
    attended[...] = ordered(first, attended[:, :half], attended[:, half:])
    out = ordered(
        first,
        dot(attended[...], matrix(w_b, 0, half, width)),
        dot(attended[...], matrix(w_b, 1, half, width)),
    )
    middle[...] = resid[...] + out


def attention_forward(place, resid, weights, base, gains, cosine, sine, segments):
    length, width = resid.shape
    one = (length, width)
    return call(
        functools.partial(attention_forward_kernel, base),
        place,
        [(one, FULL)] + [(one, LOW)] * 3 + [((16, length), FULL), ((2,) + one, LOW)],
        [resid, *segments, cosine, sine, gains],
        weights,
        mixer_scratch(weights)
        + [
            pltpu.VMEM(one, FULL),
            pltpu.VMEM((length, length), FULL),
            pltpu.VMEM((length, 128), FULL),
            pltpu.SemaphoreType.DMA((4,)),
        ],
        8 * length * width * width + 4 * length * length * width,
    )


GELU_SCALE = 0.7978845608028654
GELU_CUBE = 0.044715


def fetch_hidden(anys, base, cores, ups, downs, sems, between=lambda t: None, down_first=False):
    blocks, parts, rows, width = downs.shape
    half, some = width // 2, max(blocks // 4, 1)
    copies = {}

    def up_source(place, within):
        if len(anys) == 2:
            return anys[place].at[2 * within]
        return tile_of(anys[0], cores[place], base + (2 + within) * width)

    def down_source(place, first, j):
        if len(anys) == 2:
            return anys[place].at[1 + j // 2 * 2, pl.ds(first, some), :, j % 2 * half : (j % 2 + 1) * half]
        at = base + 4 * width + j * half
        return anys[0].at[pl.ds(first, some), cores[place], :, at : at + half]

    for t in range(4):
        up = lambda: fetch([up_source(t // 2, t % 2)], [ups.at[t]], sems, t)
        if not down_first:
            copies[0, t] = up()
        if blocks >= 4 or t == 0:
            sources, targets = [], []
            first = (2 * cores[t // 2] + t % 2) * some if blocks >= 4 else 0
            for place in range(2):
                columns = pl.ds(pl.multiple_of(cores[place] * half, 128), half)
                for j in range(4):
                    sources.append(down_source(place, first, j))
                    targets.append(downs.at[pl.ds(t * some, some), j, :, columns])
            copies[1, t] = fetch(sources, targets, sems, 4 + 8 * t)
        between(t)
        if down_first:
            copies[0, t] = up()

    def wait(which, t):
        for copy in copies.pop((which, t), []):
            copy.wait()

    return wait


def rows_of(downs, t, cores):
    blocks, parts, rows, width = downs.shape
    if blocks >= 4:
        some = blocks // 4
        return downs[t * some : (t + 1) * some].reshape(some * parts * rows, width)
    return downs[0, 2 * cores[t // 2] + t % 2]


def hidden_scratch(weights):
    w = weights[0]
    blocks, rows = (w.shape[1], w.shape[2]) if len(weights) == 2 else (w.shape[0], w.shape[2])
    return [
        pltpu.VMEM((4, blocks, rows, blocks * rows), LOW),
        pltpu.VMEM((blocks, 4, rows, blocks * rows), LOW),
        pltpu.SemaphoreType.DMA((36,)),
    ]


def hidden_forward_kernel(base, place_of, ins, anys, outs, ups, downs, sems):
    middle, gains = ins
    output, pack, hidden = outs
    cores = (place_of[0], 1 - place_of[0])
    wait = fetch_hidden(anys, base, cores, ups, downs, sems)
    normed, _, _ = normalize(middle[...], gains[0:1], gains[1:2])
    pack[0] = normed.astype(LOW)
    pack.send(0)
    for t in range(4):
        wait(0, t)
        index = 2 * cores[t // 2] + t % 2
        x = dot(pack[0], matrix(ups, t))
        hidden[index] = x
        hidden.send(index)
        inner = jnp.tanh(x * (GELU_SCALE + (GELU_SCALE * GELU_CUBE) * (x * x)))
        value = x * 0.5
        value = (value + value * inner).astype(LOW)
        pack[1 + index] = value
        pack.send(1 + index)
        wait(1, t)
        product = dot(value, rows_of(downs, t, cores))
        output[...] = (middle[...] if t == 0 else output[...]) + product


def hidden_forward(place, middle, weights, base, gains):
    length, width = middle.shape
    one = (length, width)
    return call(
        functools.partial(hidden_forward_kernel, base),
        place,
        [(one, FULL), ((5,) + one, LOW), ((4,) + one, FULL)],
        [middle, gains],
        weights,
        hidden_scratch(weights),
        16 * length * width * width,
        sent=(1, 2),
    )


def hidden_back_kernel(base, place_of, ins, anys, outs, ups, downs, sems, hidden_here, total, own_sems):
    branch, grad, middle, gains = ins
    hidden, *weights = anys
    grad_middle, grad_gains, grad_own, grad_other = outs
    cores = (place_of[0], 1 - place_of[0])
    copies = []

    def fetch_values(t):
        source = hidden.at[2 * cores[t // 2] + t % 2]
        copies.extend(fetch([source], [hidden_here.at[t]], own_sems, t))

    wait = fetch_hidden(weights, base, cores, ups, downs, sems, fetch_values, down_first=True)
    for t in range(4):
        wait(1, t)
        grad_active = dot_nt(branch[...], rows_of(downs, t, cores))
        copies[t].wait()
        x = hidden_here[t]
        square = x * x
        inner = jnp.tanh(x * (GELU_SCALE + (GELU_SCALE * GELU_CUBE) * square))
        slope = x * (GELU_SCALE + (3.0 * GELU_SCALE * GELU_CUBE) * square)
        slope = (0.5 + 0.5 * inner) * (1.0 + slope * (1.0 - inner))
        value = (grad_active * slope).astype(LOW)
        (grad_own if t < 2 else grad_other)[t % 2] = value
        wait(0, t)
        product = dot_nt(value, matrix(ups, t))
        total[...] = product if t == 0 else total[...] + product
    _, unit, inverse = normalize(middle[...], gains[0:1], gains[1:2])
    back, gain, bias = normalize_back(total[...], unit, inverse, gains[0:1])
    grad_middle[...] = grad[...] + back
    grad_gains[0:1] = gain
    grad_gains[1:2] = bias


def hidden_back(place, grad, branch, middle, hidden, weights, base, gains):
    length, width = middle.shape
    one = (length, width)
    return call(
        functools.partial(hidden_back_kernel, base),
        place,
        [(one, FULL), ((2, width), FULL), ((2,) + one, LOW), ((2,) + one, LOW)],
        [branch, grad, middle, gains],
        [hidden] + weights,
        hidden_scratch(weights)
        + [
            pltpu.VMEM((4,) + one, FULL),
            pltpu.VMEM(one, FULL),
            pltpu.SemaphoreType.DMA((4,)),
        ],
        16 * length * width * width,
    )


def attention_back_kernel(base, place_of, ins, anys, outs, w_a, w_b, bias, ga, gq, gk, gv, sems):
    grad_middle, query, keys, values, lse, seg_col, seg_row, cosine, sine, gains, resid = ins
    grad, branch, branch_own, branch_other, grad_gains, grad_own, grad_other = outs
    width = resid.shape[1]
    half = width // 2
    cores = (place_of[0], 1 - place_of[0])
    copies = fetch(
        [mixer_tile(anys, cores, p, t, base, width) for t in (1, 0) for p in range(2)],
        [w.at[place] for w in (w_b, w_a) for place in range(2)],
        sems,
    )
    first = place_of[0] == 0
    grads = (grad_own, grad_other)
    bias[...] = jnp.where(seg_col[...] == seg_row[...], 0.0, -1000000000.0)
    attn_grad = grad_middle[...].astype(LOW)
    left, right = attn_grad[:, :half], attn_grad[:, half:]
    grad_own[1, :, half:] = jnp.where(first, left, right)
    grad_other[1, :, half:] = jnp.where(first, right, left)
    copies[0].wait()
    copies[1].wait()
    natural = dot_nt(grad_own[1, :, half:], matrix(w_b, 0, half, width)) + dot_nt(
        grad_other[1, :, half:], matrix(w_b, 1, half, width)
    )
    natural = natural.astype(LOW)
    ga[:, :half] = jnp.where(first, natural[:, :half], natural[:, half:])
    ga[:, half:] = jnp.where(first, natural[:, half:], natural[:, :half])

    for p in range(width // 128):
        columns = slice(p * 128, (p + 1) * 128)
        q, k, v, g = query[:, columns], keys[:, columns], values[:, columns], ga[:, columns]
        flipped = k.T
        out_q, out_k, out_v = [], [], []
        for head in range(2):
            mask = head_mask(q.shape, head)
            zero = jnp.zeros_like(q)
            scores = dot_nt(k, jnp.where(mask, q, zero)) + bias[...]
            probs = jnp.exp(scores - lse[2 * p + head : 2 * p + head + 1, :])
            grad_probs = dot_nt(v, jnp.where(mask, g, zero))
            across = jnp.sum(probs * grad_probs, 0, keepdims=True)
            grad_scores = (probs * (grad_probs - across)).astype(LOW)
            out_k.append(dot(grad_scores, q))
            out_q.append(dot(flipped[head * HD : (head + 1) * HD], grad_scores))
            out_v.append(dot(probs.astype(LOW), g))
        out_q = jnp.concatenate(out_q, 0).T * HD ** (-0.5)
        out_k = jnp.where(head_mask(out_k[0].shape, 0), out_k[0], out_k[1])
        for x, target in ((out_q, gq), (out_k, gk)):
            x = x * cosine[...] - swap_halves(x) * sine[...]
            target[:, columns] = x.astype(LOW)
        gv[:, columns] = jnp.where(head_mask(out_v[0].shape, 0), out_v[0], out_v[1]).astype(LOW)
    for place in (1, 0):
        columns = slice(place * half, (place + 1) * half)
        grads[place][0, :, :half] = gq[:, columns]
        grads[place][0, :, half:] = gk[:, columns]
        grads[place][1, :, :half] = gv[:, columns]
    copies[2].wait()
    copies[3].wait()
    total = dot_nt(grad_own[0], matrix(w_a, 0)) + dot_nt(grad_other[0], matrix(w_a, 1))
    total = total + dot_nt(grad_own[1, :, :half], matrix(w_b, 0, 0, half))
    total = total + dot_nt(grad_other[1, :, :half], matrix(w_b, 1, 0, half))
    _, unit, inverse = normalize(resid[...], gains[0:1], gains[1:2])
    back, gain, bias_grad = normalize_back(total, unit, inverse, gains[0:1])
    back = grad_middle[...] + back
    grad[...] = back
    back = back.astype(LOW)
    branch[...] = back
    branch_own[...] = jnp.where(first, back[:, :half], back[:, half:])
    branch_other[...] = jnp.where(first, back[:, half:], back[:, :half])
    grad_gains[0:1] = gain
    grad_gains[1:2] = bias_grad


def attention_back(place, grad_middle, resid, weights, base, gains, cosine, sine, segments, query, keys, values, lse):
    length, width = resid.shape
    one = (length, width)
    return call(
        functools.partial(attention_back_kernel, base),
        place,
        [(one, FULL), (one, LOW)]
        + [((length, width // 2), LOW)] * 2
        + [((2, width), FULL)]
        + [((2,) + one, LOW)] * 2,
        [grad_middle, query, keys, values, lse]
        + [*segments, cosine, sine, gains, resid],
        weights,
        mixer_scratch(weights)
        + [
            pltpu.VMEM((length, length), FULL),
        ]
        + [pltpu.VMEM(one, LOW)] * 4
        + [pltpu.SemaphoreType.DMA((4,))],
        8 * length * width * width + 10 * length * length * width,
    )


def head_kernel(place_of, ins, anys, outs):
    resid, table, gains, codons, weight = ins
    grad, branch, branch_own, branch_other, head_in, grad_logits, grad_gains, sums = outs
    half = resid.shape[1] // 2
    normed, unit, inverse = normalize(resid[...], gains[0:1], gains[1:2])
    head_in[...] = normed.astype(LOW)
    logits = dot_nt(head_in[...], table[...])
    lane = lax.broadcasted_iota(jnp.int32, logits.shape, 1)
    logits = jnp.where(lane < V, logits, -1e30)
    top = jnp.max(logits, 1, keepdims=True)
    lse = top + jnp.log(jnp.sum(jnp.exp(logits - top), 1, keepdims=True))
    hot = jnp.where(lane == codons[...], 1.0, 0.0)
    picked = jnp.sum(logits * hot, 1, keepdims=True)
    loss = jnp.sum((lse - picked) * weight[...], 0, keepdims=True)
    count = jnp.sum(weight[...], 0, keepdims=True)
    lane = lax.broadcasted_iota(jnp.int32, sums.shape, 1)
    sums[...] = jnp.where(lane == 0, loss, jnp.where(lane == 1, count, 0.0))
    grad_logits[...] = ((jnp.exp(logits - lse) - hot) * weight[...]).astype(LOW)
    back, gain, bias = normalize_back(
        dot(grad_logits[...], table[...]), unit, inverse, gains[0:1]
    )
    grad[...] = back
    back = back.astype(LOW)
    branch[...] = back
    first = place_of[0] == 0
    branch_own[...] = jnp.where(first, back[:, :half], back[:, half:])
    branch_other[...] = jnp.where(first, back[:, half:], back[:, :half])
    grad_gains[0:1] = gain
    grad_gains[1:2] = bias


def head(place, resid, table, gains, codons, weight):
    length, width = resid.shape
    one, part = (length, width), (length, width // 2)
    return call(
        head_kernel,
        place,
        [(one, FULL), (one, LOW), (part, LOW), (part, LOW), (one, LOW)]
        + [((length, SMALL), LOW), ((2, width), FULL), ((1, SMALL), FULL)],
        [resid, table, gains, codons, weight],
        flops=4 * length * width * SMALL,
    )


def adam_step(master, grad, first, second, rate, decay):
    first = BETA_ONE * first + (1.0 - BETA_ONE) * grad
    second = BETA_TWO * second + (1.0 - BETA_TWO) * grad * grad
    fix_one = 1.0 / (1.0 - BETA_ONE**STEP)
    fix_two = 1.0 / (1.0 - BETA_TWO**STEP)
    update = first * fix_one / (jnp.sqrt(second * fix_two) + ADAM_EPS) + decay * master
    return (master - rate * update, first, second)


def scale_of(totals):
    count = totals[0:1, 1:2]
    grad_norm = jnp.sqrt(totals[0:1, 2:3]) / count
    return grad_norm, CLIP / jnp.maximum(grad_norm, CLIP) / count


def optimizer_kernel(chunks, place_of, ins, anys, outs, *scratch):
    *masters, sems = scratch
    copies = fetch(anys, masters, sems)
    totals, small_own, small_other, *rest = ins
    n = (len(rest) - 6) // 2
    own, other = rest[:n], rest[n : 2 * n]
    masters += rest[2 * n :]
    layers = len(chunks)
    first = place_of[0] == 0
    grad_norm, scale = scale_of(totals[...])
    outs[0][...] = grad_norm

    def step(which, at, grad, rate=RATE_MATRIX, decay=DECAY):
        master, moment, square = (masters[3 * which + i][at] for i in range(3))
        values = adam_step(master, grad * scale, moment, square, rate, decay)
        for i in range(3):
            outs[1 + 3 * which + i][at] = values[i]

    def tile(where, s, core):
        a, b = own[where[0]][where[1], s], other[where[0]][where[1], s]
        return jnp.where(first, a, b) if core == 0 else jnp.where(first, b, a)

    def arrive(*which):
        for copy in copies[3 * which[0] : 3 * which[-1] + 3]:
            copy.wait()

    def leave(which):
        for i in range(3):
            outs[1 + 3 * which + i].send()

    rows, width = own[0].shape[-2:]
    half = width // 2
    arrive(0, 1)
    for l in range(layers):
        for core in range(2):
            columns = lambda p: pl.ds(p * width + core * half, half)
            value = tile(chunks[l][0], 0, core)
            step(0, (l, slice(None), columns(0)), value[:, :half])
            step(0, (l, slice(None), columns(1)), value[:, half:])
            value = tile(chunks[l][0], 1, core)
            step(0, (l, slice(None), columns(2)), value[:, :half])
            step(1, (l, slice(None), columns(0)), value[:, half:])
    leave(0)
    leave(1)
    arrive(2)
    for l in range(layers):
        for core in range(2):
            for s in range(2):
                at = (l, slice(None), pl.ds((2 * core + s) * width, width))
                step(2, at, tile(chunks[l][1], s, core))
    leave(2)
    arrive(3)
    for l in range(layers):
        for core in range(2):
            for s in range(2):
                value = tile(chunks[l][2], s, core)
                for j in range(2):
                    at = (l, pl.ds((2 * s + j) * rows, rows), pl.ds(core * half, half))
                    step(3, at, value[:, j * half : (j + 1) * half])
    leave(3)
    small = jnp.where(first, small_own[...], small_other[...])
    step(4, (slice(None), slice(None)), small[:, :V])
    small = small.T
    for n in range(masters[15].shape[0]):
        step(5, n, small[V + 2 * n : V + 2 * n + 2], RATE_VECTOR, 0.0)


def optimizer(place, totals, small, chunks, own, other, masters):
    return call(
        functools.partial(optimizer_kernel, chunks),
        place,
        [((1, 1), FULL)] + [(m.shape, m.dtype) for m in masters],
        [totals, *small, *own, *other, *masters[12:]],
        masters[:12],
        [pltpu.VMEM(m.shape, m.dtype) for m in masters[:12]] + [pltpu.SemaphoreType.DMA((12,))],
        flops=20 * sum(m.size for m in masters),
        sent=range(1, 13),
    )


def pack_kernel(layers, place_of, ins, anys, outs):
    inward, outward, expand, shrink, small = ins
    out, *early = outs
    first = place_of[0] == 0
    rows = inward.shape[1]
    width = inward.shape[2] // 3
    half = width // 2
    at = 0
    if early:
        early[0][rows : rows + 16] = jnp.zeros((16, width), LOW)
        for q in range(rows // 16):
            early[0][rows : rows + 16, q * SMALL : (q + 1) * SMALL] = small[q * 16 : (q + 1) * 16]
    else:
        at = small.shape[1]
        out[:, :at] = small[...]
    for l in range(layers):
        sources = [inward[l, :, p * width : (p + 1) * width] for p in range(3)] + [outward[l]]
        sources.append(expand[l])
        sources += [shrink[l, j * rows : (j + 1) * rows] for j in range(shrink.shape[1] // rows)]
        for n, value in enumerate(sources):
            part = value.shape[1] // 2
            value = jnp.where(first, value[:, :part], value[:, part:]).astype(LOW)
            if early and l == 0 and n < 4:
                start = 0 if n < 2 else rows + 16
                early[0][start : start + rows, (n % 2) * half : (n % 2 + 1) * half] = value
            elif early and l == layers - 1 and n == 4:
                for t in range(2):
                    early[1][2 * t * rows : (2 * t + 1) * rows] = value[:, t * width : (t + 1) * width]
            elif early and l == layers - 1 and n > 4:
                start = (2 * ((n - 5) // 2) + 1) * rows
                lanes = (n - 5) % 2 * half
                early[1][start : start + rows, lanes : lanes + half] = value
            else:
                out[:, at : at + part] = value
                at += part


def swap_cores(value):
    return lax.ppermute(value, "dp", [(0, 1), (1, 0)])


def across(value, mask, size):
    return lax.ppermute(value, "fsdp", [(i, i ^ mask) for i in range(size)])


def tie(*values):
    return lax.optimization_barrier(values)


def total_of(value, size):
    value = value + swap_cores(value)
    bit = 1
    while bit < size:
        if 2 * bit < size:
            a, b, c = (across(value, m * bit, size) for m in (1, 2, 3))
            value = (value + a) + (b + c)
        else:
            value = value + across(value, bit, size)
        bit *= 4
    return value


def arrange_kernel(parts, place_of, ins, anys, outs, sems):
    copies, at = [], 0
    for h in range(2):
        for piece in anys:
            copies += fetch(
                [piece.at[h * parts[0] : h * parts[0] + parts[h]]],
                [outs[0].at[at : at + parts[h]]],
                sems,
                len(copies),
            )
            at += parts[h]
    for copy in copies:
        copy.wait()


def place_kernel(parts, rows, place_of, ins, anys, outs, sems):
    quarter, from_x, from_y, far_a, far_b = anys
    tiles, *small = outs
    count = tiles.shape[0] // 2
    x, y, z = place_of[1], place_of[2], place_of[3]
    for n in range(16):
        xor_z, xor_y, xor_x = n // 4, n // 2 % 2, n % 2
        index = jnp.bitwise_xor(z, xor_z) * 4 + jnp.bitwise_xor(y, xor_y) * 2 + jnp.bitwise_xor(x, xor_x)
        for h in range(2):
            at = xor_z * parts[h]
            if xor_x and xor_y:
                source = (far_a, far_b)[h]
            else:
                source = from_x if xor_x else from_y if xor_y else quarter
                at += h * 4 * parts[0]
            for t in range(count):
                here = source.at[at + t * rows : at + (t + 1) * rows]
                fetch([here], [tiles.at[h * count + t, index]], sems, h * count + t)
            if h == 0 and small:
                here = source.at[at + count * rows : at + parts[0]]
                fetch([here], [small[0].at[index]], sems, 2 * count)
    targets = [tiles.at[t] for t in range(2 * count)] + small
    for n, target in enumerate(targets):
        pltpu.make_async_copy(target, target, sems.at[n]).wait()


class Gather:
    def __init__(self, place, shard, parts, rows):
        self.place, self.shard, self.parts, self.rows = place, shard, parts, rows

    def along_z(self):
        self.got = [across(self.shard, mask, 16) for mask in Z]

    def in_plane(self):
        width = self.shard.shape[1]
        (quarter,) = call(
            functools.partial(arrange_kernel, self.parts),
            self.place,
            [((4 * sum(self.parts), width), LOW)],
            [],
            [self.shard] + self.got,
            [pltpu.SemaphoreType.DMA((8,))],
        )
        self.quarter, self.near = quarter, [across(quarter, X, 16), across(quarter, Y, 16)]

    def forward(self):
        cut = 4 * self.parts[0]
        from_x, from_y = self.near
        self.far = [across(from_y[:cut], X, 16), across(from_x[cut:], Y, 16)]

    def result(self):
        width = self.shard.shape[1]
        count, more = divmod(self.parts[0], self.rows)
        outs = [((2 * count, 16, self.rows, width), LOW)]
        if more:
            outs.append(((16, more, width), LOW))
        return call(
            functools.partial(place_kernel, self.parts, self.rows),
            self.place,
            outs,
            [],
            [self.quarter] + self.near + self.far,
            [pltpu.SemaphoreType.DMA((2 * count + 1,))],
        )


X, Y = 1, 2
Z = (4, 8, 12)


def round_kernel(jobs, small_job, n_ins, counts, smalls, last, place_of, ins, anys, outs, *scratch):
    new, once, twice, done = counts
    small_new, small_once, small_twice, small_done = smalls
    rest = list(ins[n_ins:]) + list(outs) + list(scratch)
    pop = lambda present, n=1: [rest.pop(0) for _ in range(n)] if present else [None] * n
    (keep_once,), (small_keep_once,) = pop(once), pop(small_once)
    (keep_twice,), (small_keep_twice,) = pop(twice), pop(small_twice)
    from_x, from_y = pop(once or twice, 2)
    (keep_done,), (small_keep_done,) = pop(done), pop(small_done)
    from_z = pop(done, 3)
    (squares_in,), (sums,) = pop(done), pop(last)
    to_x, to_y = pop(new or once, 2)
    (out_once,), (small_out_once,) = pop(new), pop(small_new)
    (out_twice,), (small_out_twice,) = pop(once), pop(small_once)
    (out_done,), (small_out_done,) = pop(twice), pop(small_twice)
    to_z = pop(twice, 3)
    (share,), (small_share,), (squares,) = pop(done), pop(small_done), pop(done)
    (totals,) = pop(last)
    (tile,), (unit,), (small_tile,) = pop(new), pop(new), pop(small_new)
    rows = (out_once if new else out_twice if once else out_done if twice else share).shape[-2]
    rows = rows // (8 if new else 4 if once else 1)
    bits, z = (place_of[1], place_of[2]), place_of[3]
    to, came = (to_x, to_y), (from_x, from_y)

    def block(index, size=rows):
        if isinstance(index, int):
            return pl.ds(index * size, size)
        return pl.ds(pl.multiple_of(index * size, 16), size)

    def factor(spec):
        which, index, low, high = spec
        ref = ins[which] if index is None else ins[which].at[index]
        return ref[...] if low is None else ref[:, low:high]

    def put_small(ref, start, group, side, value):
        for q in range(rows // 16):
            lanes = side * (rows // 16) + q
            ref[pl.ds(start + group * 16, 16), lanes * SMALL : (lanes + 1) * SMALL] = value[
                q * 16 : (q + 1) * 16
            ].astype(LOW)

    def take_small(ref, start, group, side):
        parts = []
        for q in range(rows // 16):
            lanes = side * (rows // 16) + q
            at = pl.ds(pl.multiple_of(start + group * 16, 16), 16)
            parts.append(ref[at, lanes * SMALL : (lanes + 1) * SMALL])
        return jnp.concatenate(parts, 0).astype(FULL)

    def summed(products):
        total = None
        for left, right in products:
            product = cross(factor(left), factor(right))
            total = product if total is None else total + product
        return total

    for p in range(new):
        if len(jobs[p]) == 4:
            for quarter, products in enumerate(jobs[p]):
                unit[...] = summed(products)
                half = unit.shape[1]
                for index in range(4):
                    for s in range(2):
                        for j in range(2):
                            tile[s, block(quarter * 4 + index), j * half : (j + 1) * half] = unit[
                                block(index * 4 + 2 * s + j), :
                            ]
        else:
            for s in range(2):
                for low, high, products in jobs[p][s]:
                    tile[s, :, low:high] = summed(products)
        for s in range(2):
            for zz in range(4):
                for other in range(2):
                    at = zz * 2 + other
                    index = lambda bit: zz * 4 + (other * 2 + bit if s == 0 else bit * 2 + other)
                    to[s][block(p * 8 + at), :] = tile[s, block(index(1 - bits[s])), :].astype(LOW)
                    out_once[p, s, block(at), :] = tile[s, block(index(bits[s])), :]
    if small_new:
        products, norms_at = small_job
        total = summed(products)
        norms = jnp.concatenate([ins[mine][...] + ins[theirs][...] for mine, theirs in norms_at], 0)
        high = norms.astype(LOW)
        shape = (norms.shape[0], SMALL)
        column = lax.broadcasted_iota(jnp.int32, shape, 1) - V
        pick = jnp.where(lax.broadcasted_iota(jnp.int32, shape, 0) == column, 1.0, 0.0).astype(LOW)
        total = total + (cross(high, pick) + cross((norms - high.astype(FULL)).astype(LOW), pick))
        small_tile[...] = total
        for zz in range(4):
            for other in range(2):
                index = lambda bit: zz * 4 + other * 2 + bit
                send = small_tile[block(index(1 - bits[0])), :]
                put_small(to_x, (new * 8 + once * 4) * rows, other * 2 + zz // 2, zz % 2, send)
                small_out_once[block(zz * 2 + other), :] = small_tile[block(index(bits[0])), :]
    for p in range(once):
        for s in range(2):
            for zz in range(4):
                for bit in range(2):
                    at = zz * 2 + (bits[1 - s] if bit else 1 - bits[1 - s])
                    value = keep_once[p, s, block(at), :] + came[s][block(p * 8 + at), :].astype(FULL)
                    if bit:
                        out_twice[p, s, block(zz), :] = value
                    else:
                        to[1 - s][block(new * 8 + p * 4 + zz), :] = value.astype(LOW)
    if small_once:
        start = (once * 8 + twice * 4) * rows
        for zz in range(4):
            for bit in range(2):
                other = bits[1] if bit else 1 - bits[1]
                value = small_keep_once[block(zz * 2 + other), :]
                value = value + take_small(from_x, start, other * 2 + zz // 2, zz % 2)
                if bit:
                    small_out_twice[block(zz), :] = value
                else:
                    put_small(to_y, (new * 8 + once * 4) * rows, zz, 0, value)
    for p in range(twice):
        for s in range(2):
            for xor in range(4):
                at = jnp.bitwise_xor(z, xor)
                value = keep_twice[p, s, block(at), :] + came[1 - s][
                    block(once * 8 + p * 4 + at), :
                ].astype(FULL)
                if xor == 0:
                    out_done[p, s] = value
                else:
                    to_z[xor - 1][block(2 * p + s), :] = value.astype(LOW)
    if small_twice:
        for xor in range(4):
            at = jnp.bitwise_xor(z, xor)
            value = small_keep_twice[block(at), :]
            value = value + take_small(from_y, (once * 8 + twice * 4) * rows, at, 0)
            if xor == 0:
                small_out_done[...] = value
            else:
                put_small(to_z[xor - 1], twice * 2 * rows, 0, 0, value)
    if done:
        squares[...] = squares_in[...]
    for p in range(done):
        for s in range(2):
            value = keep_done[p, s]
            for f in from_z:
                value = value + f[block(2 * p + s), :].astype(FULL)
            share[p, s] = value
            squares[...] += jnp.sum(value * value, 0, keepdims=True)
    if small_done:
        value = small_keep_done[...]
        for f in from_z:
            value = value + take_small(f, done * 2 * rows, 0, 0)
        small_share[...] = value
    if last:
        total = jnp.sum(squares[...], 1, keepdims=True)
        if small_done:
            square = jnp.sum(jnp.sum(value * value, 0, keepdims=True), 1, keepdims=True)
            total = total + jnp.where(place_of[0] == 0, square, jnp.zeros_like(square))
        lane = lax.broadcasted_iota(jnp.int32, sums.shape, 1)
        totals[...] = jnp.where(lane == 2, total, sums[...])


class Rounds:
    def __init__(self, place, rows, width, sums):
        self.place, self.rows, self.width, self.sums = place, rows, width, sums
        self.counts, self.smalls = (0,) * 4, (False,) * 4
        self.kept, self.small_kept = [None] * 3, [None] * 3
        self.came = self.came_z = self.totals = None
        self.shares, self.others, self.small_share = [], [], None
        self.squares = jnp.zeros((1, width), FULL)
        self.flying, self.swapping = [], 0

    def step(self, chunk, *ties, small=None):
        rows, width = self.rows, self.width
        new, once, twice, done = counts = (len(chunk),) + self.counts[:3]
        smalls = (small is not None,) + self.smalls[:3]
        last = not (new or once or twice)
        arrays, jobs = [], []

        def number(spec):
            array, *place = spec
            for i, known in enumerate(arrays):
                if known is array:
                    return (i, *place)
            arrays.append(array)
            return (len(arrays) - 1, *place)

        numbered = lambda products: [(number(l), number(r)) for l, r in products]
        for pair in chunk:
            if len(pair) == 4:
                jobs.append([numbered(products) for products in pair])
            else:
                jobs.append([[(a, b, numbered(ps)) for a, b, ps in tile] for tile in pair])
        small_job = None
        if small is not None:
            small_job = (
                [(number(l), number(r)) for l, r in small[0]],
                [(number((a,))[0], number((b,))[0]) for a, b in small[1]],
            )
        ins = list(arrays)
        for stage in range(2):
            ins += [self.kept[stage]] * (counts[1 + stage] > 0)
            ins += [self.small_kept[stage]] * smalls[1 + stage]
        if once or twice:
            ins += self.came
        if done:
            ins += [self.kept[2]] + [self.small_kept[2]] * smalls[3] + self.came_z + [self.squares]
        ins += [self.sums] * last
        outs = []
        if new or once:
            for added in (64 * smalls[0], 64 * smalls[1]):
                outs.append((((new * 8 + once * 4) * rows + added, width), LOW))
        for stage, blocks in enumerate((8, 4, 1)):
            if counts[stage]:
                outs.append(((counts[stage], 2, blocks * rows, width), FULL))
            if smalls[stage]:
                outs.append(((blocks * rows, SMALL), FULL))
        if twice:
            outs += [((twice * 2 * rows + 16 * smalls[2], width), LOW)] * 3
        if done:
            outs.append(((done, 2, rows, width), FULL))
            outs += [((rows, SMALL), FULL)] * smalls[3]
            outs.append(((1, width), FULL))
        outs += [((1, SMALL), FULL)] * last
        length = 2 * arrays[0].shape[-2] if new else 0
        scratch = []
        if new:
            scratch.append(pltpu.VMEM((2, 16 * rows, width), FULL))
            scratch.append(pltpu.VMEM((16 * rows, width // 2), FULL))
        scratch += [pltpu.VMEM((16 * rows, SMALL), FULL)] * smalls[0]
        got = list(
            call(
                functools.partial(
                    round_kernel, jobs, small_job, len(arrays), counts, smalls, last
                ),
                self.place,
                outs,
                ins,
                [],
                scratch,
                4 * new * length * width * width,
                limit=VMEM_LIMIT if new else 24 << 20,
            )
        )
        if last:
            self.totals = got.pop()
        if done:
            self.squares = got.pop()
            if smalls[3]:
                self.small_share = got.pop()
            self.shares.append(got.pop())
        self.counts, self.smalls = counts, smalls
        self.kept, self.small_kept = [None] * 3, [None] * 3
        if last:
            return ties
        got, ties, self.shares = tie(got, ties, self.shares)
        to = [got.pop(0) for _ in range(2)] if new or once else []
        for stage in range(3):
            if counts[stage]:
                self.kept[stage] = got.pop(0)
            if smalls[stage]:
                self.small_kept[stage] = got.pop(0)
        self.flying = [across(v, mask, 16) for v, mask in zip(to, (X, Y))]
        self.flying += [across(v, mask, 16) for v, mask in zip(got, Z)]
        self.swapping = 0
        while len(self.flying) < 5 and len(self.others) + self.swapping < len(self.shares):
            self.flying.append(swap_cores(self.shares[len(self.others) + self.swapping]))
            self.swapping += 1
        return ties

    def finish(self, *ties):
        flying, ties = tie(self.flying, ties)
        self.came = self.came_z = None
        if self.counts[0] or self.counts[1]:
            self.came, flying = flying[:2], flying[2:]
        if self.counts[2]:
            self.came_z, flying = flying[:3], flying[3:]
        self.others += flying
        return ties

    def left(self):
        return any(self.counts[:3])

    def swap_rest(self):
        self.others += [swap_cores(v) for v in self.shares[len(self.others) :]]


class PlainRounds:
    def __init__(self):
        self.shares, self.squares = [], []

    def step(self, chunk, *ties):
        def factor(spec):
            array, index, low, high = spec
            array = array if index is None else array[index]
            return array if low is None else array[:, low:high]

        summed = lambda products: sum(cross(factor(l), factor(r)) for l, r in products)
        scatter = lambda v: lax.psum_scatter(v, "fsdp", scatter_dimension=0, tiled=True)
        shares = []
        for pair in chunk:
            if len(pair) == 4:
                v = scatter(jnp.concatenate([summed(products) for products in pair], 0))
                v = v.reshape(2, 2, -1, v.shape[1])
                shares.append(jnp.concatenate([v[:, 0], v[:, 1]], 2))
            else:
                tiles = [jnp.concatenate([summed(ps) for _, _, ps in t], 1) for t in pair]
                shares.append(jnp.stack([scatter(t) for t in tiles]))
        share = jnp.stack(shares)
        self.shares.append((share, swap_cores(share)))
        self.squares.append(jnp.sum(share * share, (0, 1, 2))[None])
        return ties

    def finish(self, *ties):
        return ties

    def left(self):
        return False


def half_of(value, core):
    half = value.shape[1] // 2
    return lax.dynamic_slice_in_dim(value, core * half, half, 1)


def body(
    fsdp,
    codons,
    masked,
    segments,
    inward,
    outward,
    expand,
    shrink,
    codon_table,
    norm_params,
    inward_first,
    inward_second,
    outward_first,
    outward_second,
    expand_first,
    expand_second,
    shrink_first,
    shrink_second,
    table_first,
    table_second,
    norm_first,
    norm_second,
):
    layers = inward.shape[0]
    length = codons.shape[0]
    rows = inward.shape[1]
    width = rows * fsdp
    half = width // 2
    fast = fsdp == 16 and rows == 48 and layers > 1
    core, index = lax.axis_index("dp"), lax.axis_index("fsdp")
    bit = lambda b: lax.rem(lax.div(index, b), 2)
    place = jnp.stack([core, bit(1), bit(2), lax.div(index, 4)]).astype(jnp.int32)
    weight = masked.astype(FULL)
    inputs = jnp.where(masked == 1, V - 1, codons)

    norms = norm_params.shape[0] * 2
    small = jnp.concatenate(
        [codon_table.astype(LOW), norm_params.astype(LOW).reshape(norms, rows)], 0
    )
    small = jnp.pad(small.T, ((0, 0), (0, -small.shape[0] % 128)))
    columns = small.shape[1] + layers * 6 * width
    shapes = [(rows, columns)]
    if fast:
        shapes = [(rows, (layers - 1) * 6 * width), (2 * rows + 16, width), (4 * rows, width)]
    weights, *early = call(
        functools.partial(pack_kernel, layers),
        place,
        [(shape, LOW) for shape in shapes],
        [inward, outward, expand, shrink, small],
    )
    weights = lax.all_gather(weights, ("fsdp", "dp"), axis=0, tiled=True)
    weights = weights.reshape(fsdp, 2, rows, -1)
    if not fast:
        columns = [weights[:, :, :, : small.shape[1]]]
        for at in range(small.shape[1], weights.shape[3], 6 * width):
            columns.append(weights[:, :, :, at : at + 4 * width])
            quarter = weights[:, :, :, at + 4 * width : at + 6 * width]
            quarter = quarter.reshape(fsdp, 2, rows, 4, half).transpose(1, 0, 3, 2, 4)
            quarter = quarter.reshape(2, 4, width, half).transpose(0, 2, 1, 3)
            columns.append(quarter.reshape(2, fsdp, rows, 2 * width).transpose(1, 0, 2, 3))
        weights = jnp.concatenate(columns, 3).transpose(1, 0, 2, 3).reshape(1, 2, width, -1)
    mixers, hiddens = [[weights]] * layers, [[weights]] * layers
    if fast:
        first = Gather(place, early[0], (rows + 16, rows), rows)
        last = Gather(place, early[1], (2 * rows, 2 * rows), rows)
        first.along_z()
        columns = (codons[:, None], weight[:, None], segments[:, None])
        first.got, last.shard, columns = tie(first.got, last.shard, columns)
        first.in_plane()
        last.along_z()
        first.near, last.got = tie(first.near, last.got)
        first.forward()
        (first.far,) = tie(first.far)
        own, small = first.result()
        mixers[0] = [own, swap_cores(own)]
        own, last.got = tie(own, last.got)
        last.in_plane()
        small = small[:, :, : rows // 16 * SMALL].reshape(16, 16, rows // 16, SMALL)
        small = small.transpose(0, 2, 1, 3).reshape(width, SMALL).T
    else:
        columns = (codons[:, None], weight[:, None], segments[:, None])
        small = weights[:, 0, :, :SMALL].reshape(width, SMALL).T
    start = -2 * width if fast else weights.shape[3] - layers * 6 * width
    base = lambda l: start + l * 6 * width
    gains = small[V : V + norms].astype(FULL).reshape(-1, 2, width)

    cosine, sine = rotary_tables(length)
    chosen = (inputs[:, None] == jnp.arange(SMALL, dtype=jnp.int32)[None, :]).astype(LOW)
    resid = dot(chosen, small)
    kept = []
    for l in range(layers):
        gain = gains[2 * l : 2 * l + 2]
        middle, query, keys, values, lse, pack = attention_forward(
            place, resid, mixers[l], base(l), gain[0], cosine, sine, (columns[2], segments[None, :])
        )
        if fast and l == 0:
            middle, last.near = tie(middle, last.near)
            last.forward()
        output, pack_mid, hidden = hidden_forward(place, middle, hiddens[l], base(l), gain[1])
        if fast and l == 0:
            output, last.far = tie(output, last.far)
            (own,) = last.result()
            hiddens[-1] = [own, swap_cores(own)]
            output, hiddens[-1][0] = tie(output, own)
        kept.append((resid, query, keys, values, lse, pack, middle, hidden, pack_mid))
        resid = output
    grad, branch, branch_own, branch_other, head_in, grad_logits, grad_norms, sums = head(
        place, resid, small, gains[2 * layers], columns[0], columns[1]
    )
    grad_norms = [grad_norms]
    early = (head_in, grad_logits, chosen)
    early_came = [swap_cores(v) for v in early]
    mid_came = [swap_cores(saved[-1]) for saved in kept]
    pack_came = [swap_cores(saved[5]) for saved in kept]
    grad, branch, mid_came[-1] = tie(grad, branch, mid_came[-1])

    rounds = Rounds(place, rows, width, sums) if fast else PlainRounds()
    whole = lambda array, i=None: (array, i, None, None)
    tile = lambda left, right, other_left, other_right: [
        (0, width, [(left, right), (other_left, other_right)])
    ]
    chunk = []
    for l in reversed(range(layers)):
        resid, query, keys, values, lse, pack, middle, hidden, pack_mid = kept[l]
        gain = gains[2 * l : 2 * l + 2]
        branch_came = swap_cores(branch_other)
        chunk.append(
            [
                [
                    (whole(pack_mid, 1 + t), whole(branch_own)),
                    (whole(mid_came[l], 1 + t), whole(branch_came)),
                ]
                for t in range(4)
            ]
        )
        grad, branch = rounds.step(chunk, grad, branch)
        grad_middle, gains_mid, up_own, up_other = hidden_back(
            place, grad, branch, middle, hidden, hiddens[l], base(l), gain[1]
        )
        grad_middle, up_own, up_other, early_came = rounds.finish(
            grad_middle, up_own, up_other, early_came
        )
        up_came = swap_cores(up_other)
        if l == 0:
            norms_early = jnp.concatenate([gains_mid] + grad_norms, 0)
            norms_early = (norms_early, swap_cores(norms_early))
        (grad_middle,) = rounds.step(
            [
                [
                    tile(
                        whole(pack_mid, 0), whole(up_own, s), whole(mid_came[l], 0), whole(up_came, s)
                    )
                    for s in range(2)
                ]
            ],
            grad_middle,
        )
        grad, branch, branch_own, branch_other, gains_in, mix_own, mix_other = attention_back(
            place, grad_middle, resid, mixers[l], base(l), gain[0], cosine, sine,
            (columns[2], segments[None, :]),
            query, keys, values, lse,
        )
        grad_norms = [gains_in, gains_mid] + grad_norms
        grad, branch, branch_own, branch_other, mix_own, mix_other, mid_came, pack_came = (
            rounds.finish(
                grad, branch, branch_own, branch_other, mix_own, mix_other, mid_came, pack_came
            )
        )
        mix_came = swap_cores(mix_other)
        products = lambda i, a, b: [
            ((pack, i, None, None), (mix_own, 1, a, b)),
            ((pack_came[l], i, None, None), (mix_came, 1, a, b)),
        ]
        chunk = [
            [
                tile(whole(pack, 0), whole(mix_own, 0), whole(pack_came[l], 0), whole(mix_came, 0)),
                [(0, half, products(0, 0, half)), (half, width, products(1, half, width))],
            ]
        ]
    late = (grad_norms[0], swap_cores(grad_norms[0]))
    branch_came = swap_cores(branch)
    products = [(whole(early[0]), whole(early[1])), (whole(early_came[0]), whole(early_came[1]))]
    products += [(whole(branch), whole(early[2])), (whole(branch_came), whole(early_came[2]))]
    if fast:
        rounds.step(chunk, small=(products, [late, norms_early]))
        while rounds.left():
            rounds.finish()
            rounds.step([])
        rounds.swap_rest()
        share_small = rounds.small_share
        small_other = swap_cores(share_small)
        totals = rounds.totals
    else:
        rounds.step(chunk)
        table = sum(cross(l[0], r[0]) for l, r in products)
        table = table + jnp.pad(
            jnp.concatenate([a + b for a, b in (late, norms_early)], 0).T,
            ((0, 0), (V, SMALL - V - norms)),
        )
        table = jnp.where(core == 0, table, swap_cores(table))
        share_small = lax.psum_scatter(table, "fsdp", scatter_dimension=0, tiled=True)
        squares = jnp.sum(share_small * share_small) * (core == 0)
        for value in rounds.squares:
            squares = squares + jnp.sum(value)
        totals = sums + jnp.where(jnp.arange(SMALL) == 2, squares, 0.0)[None]
    totals = total_of(totals, fsdp)
    shares = list(zip(rounds.shares, rounds.others)) if fast else rounds.shares
    places = [(2 * (layers - 1 - l), 0 if l == layers - 1 else 1) for l in range(layers)]

    def tiles_at(chunk, pair):
        own, other = (v[pair] for v in shares[chunk])
        ordered = (jnp.where(core == 0, own, other), jnp.where(core == 0, other, own))
        return [v[s] for v in ordered for s in range(2)]

    if not fast:
        share_in, share_out, share_up, share_down = [], [], [], []
        side = lambda *values: jnp.concatenate(values, 1)
        for at, pair in places:
            a_0, b_0, a_1, b_1 = tiles_at(at + 2, 0)
            share_in.append(
                side(
                    a_0[:, :half], a_1[:, :half], a_0[:, half:],
                    a_1[:, half:], b_0[:, :half], b_1[:, :half],
                )
            )
            share_out.append(side(b_0[:, half:], b_1[:, half:]))
            share_up.append(side(*tiles_at(at + 1, 0)))
            a_0, b_0, a_1, b_1 = tiles_at(at, pair)
            share_down.append(
                jnp.concatenate(
                    [
                        side(x[:, j * half : (j + 1) * half], y[:, j * half : (j + 1) * half])
                        for x, y in ((a_0, a_1), (b_0, b_1))
                        for j in range(2)
                    ],
                    0,
                )
            )
        share_in, share_out, share_up, share_down = (
            jnp.stack(v) for v in (share_in, share_out, share_up, share_down)
        )
    masters = (inward, outward, expand, shrink, codon_table, norm_params)
    firsts = (inward_first, outward_first, expand_first, shrink_first, table_first, norm_first)
    seconds = (
        inward_second,
        outward_second,
        expand_second,
        shrink_second,
        table_second,
        norm_second,
    )
    if fast:
        chunks = [((at + 2, 0), (at + 1, 0), (at, pair)) for at, pair in places]
        own, other = zip(*shares)
        states = [v for group in zip(masters, firsts, seconds) for v in group]
        states[12:15] = [v.T for v in states[12:15]]
        grad_norm, *values = optimizer(
            place, totals, (share_small, small_other), chunks, own, other, states
        )
        values[12:15] = [v.T for v in values[12:15]]
    else:
        grad_norm, scale = scale_of(totals)
        share_small = share_small[:, : V + norms].T
        grads = (share_in, share_out, share_up, share_down)
        grads += (share_small[:V], share_small[V:].reshape(-1, 2, rows))
        values = []
        for index, grad in enumerate(grads):
            rate, decay = (RATE_VECTOR, 0.0) if index == 5 else (RATE_MATRIX, DECAY)
            values.extend(
                adam_step(masters[index], grad * scale.reshape(()), firsts[index], seconds[index], rate, decay)
            )
    return (totals[0, 0], totals[0, 1], grad_norm.reshape(()), *values)


def solution(mesh):
    in_specs = (
        P(("fsdp", "dp")),
        P(("fsdp", "dp")),
        P(("fsdp", "dp")),
        P(None, "fsdp", None),
        P(None, "fsdp", None),
        P(None, "fsdp", None),
        P(None, "fsdp", None),
        P(None, "fsdp"),
        P(None, None, "fsdp"),
        P(None, "fsdp", None),
        P(None, "fsdp", None),
        P(None, "fsdp", None),
        P(None, "fsdp", None),
        P(None, "fsdp", None),
        P(None, "fsdp", None),
        P(None, "fsdp", None),
        P(None, "fsdp", None),
        P(None, "fsdp"),
        P(None, "fsdp"),
        P(None, None, "fsdp"),
        P(None, None, "fsdp"),
    )
    out_specs = (
        P(),
        P(),
        P(),
        P(None, "fsdp", None),
        P(None, "fsdp", None),
        P(None, "fsdp", None),
        P(None, "fsdp", None),
        P(None, "fsdp", None),
        P(None, "fsdp", None),
        P(None, "fsdp", None),
        P(None, "fsdp", None),
        P(None, "fsdp", None),
        P(None, "fsdp", None),
        P(None, "fsdp", None),
        P(None, "fsdp", None),
        P(None, "fsdp"),
        P(None, "fsdp"),
        P(None, "fsdp"),
        P(None, None, "fsdp"),
        P(None, None, "fsdp"),
        P(None, None, "fsdp"),
    )
    step = functools.partial(body, mesh.shape["fsdp"])
    return jax.shard_map(step, mesh=mesh, in_specs=in_specs, out_specs=out_specs, check_vma=False)
```

```python
import functools

import jax
import jax.numpy as jnp
from jax import lax
from jax.experimental import pallas as pl
from jax.experimental.pallas import tpu as pltpu
from jax.sharding import PartitionSpec as P

HD = 64
V = 70
STEP = 10


NORM_EPS = 1e-05
BETA_ONE = 0.9
BETA_TWO = 0.95
ADAM_EPS = 1e-08
DECAY = 0.1
RATE_MATRIX = 0.05
RATE_VECTOR = 0.3
CLIP = 0.05


def rotary_tables(length):
    freq = 10000.0 ** (-jnp.arange(HD // 2, dtype=jnp.float32) * 2.0 / HD)
    angle = jnp.arange(length, dtype=jnp.float32)[:, None] * freq[None, :]
    cosine, sine = jnp.cos(angle), jnp.sin(angle)
    return (
        jnp.concatenate([cosine] * 4, 1),
        jnp.concatenate([-sine, sine] * 2, 1),
    )


def normalize(resid, gain, bias):
    mean = jnp.mean(resid, -1, keepdims=True)
    centred = resid - mean
    inverse = lax.rsqrt(jnp.mean(centred * centred, -1, keepdims=True) + NORM_EPS)
    unit = centred * inverse
    return (unit * gain + bias, unit, inverse)


def normalize_back(grad, unit, inverse, gain):
    scaled = grad * gain
    across = (
        scaled
        - jnp.mean(scaled, -1, keepdims=True)
        - unit * jnp.mean(scaled * unit, -1, keepdims=True)
    )
    return (across * inverse, jnp.sum(grad * unit, 0, keepdims=True), jnp.sum(grad, 0, keepdims=True))


def dot(left, right):
    return jnp.dot(left, right, preferred_element_type=jnp.float32)


def dot_nt(left, right):
    return lax.dot_general(
        left, right, (((1,), (1,)), ((), ())), preferred_element_type=jnp.float32
    )


def cross(left, right):
    return lax.dot_general(
        left, right, (((0,), (0,)), ((), ())), preferred_element_type=jnp.float32
    )


VMEM_LIMIT = 56 * 1024 * 1024
LOW, FULL = jnp.bfloat16, jnp.float32
SMALL = 128


class Sent:
    def __init__(self, here, there, sems):
        self.here, self.there, self.sems = here, there, sems
        self.shape, self.at = here.shape, here.at
        self.copies = []

    def __getitem__(self, at):
        return self.here[at]

    def __setitem__(self, at, value):
        self.here[at] = value

    def send(self, index=None):
        here, there = self.here, self.there
        if index is not None:
            here, there = here.at[index], there.at[index]
        copy = pltpu.make_async_copy(here, there, self.sems.at[len(self.copies)])
        copy.start()
        self.copies.append(copy)


def call(kernel, scalars, outs, ins, anys=(), scratch=(), flops=0, sent=(), limit=VMEM_LIMIT):
    whole = pl.BlockSpec(memory_space=pltpu.VMEM)
    left = pl.BlockSpec(memory_space=pl.ANY)

    def body(scalars, *refs):
        refs = list(refs)
        take = lambda n: [refs.pop(0) for _ in range(n)]
        in_refs, any_refs, out_refs = take(len(ins)), take(len(anys)), take(len(outs))
        here = take(len(sent))
        for n, i in enumerate(sent):
            out_refs[i] = Sent(here[n], out_refs[i], refs[-1].at[n])
        kernel(scalars, in_refs, any_refs, out_refs, *(refs[:-1] if sent else refs))
        for i in sent:
            for copy in out_refs[i].copies:
                copy.wait()

    return pl.pallas_call(
        body,
        out_shape=[jax.ShapeDtypeStruct(s, t) for s, t in outs],
        in_specs=[pl.BlockSpec(memory_space=pltpu.SMEM)]
        + [whole] * len(ins)
        + [left] * len(anys),
        out_specs=[left if i in sent else whole for i in range(len(outs))],
        scratch_shapes=[pltpu.VMEM(*outs[i]) for i in sent]
        + list(scratch)
        + [pltpu.SemaphoreType.DMA((len(sent), 5))] * (len(sent) > 0),
        compiler_params=pltpu.CompilerParams(vmem_limit_bytes=limit),
        cost_estimate=pl.CostEstimate(
            flops=flops,
            bytes_accessed=sum(x.size * x.dtype.itemsize for x in list(ins) + list(anys)),
            transcendentals=0,
        ),
    )(scalars, *ins, *anys)


def fetch(sources, targets, sems, first=0):
    copies = [
        pltpu.make_async_copy(s, t, sems.at[first + i])
        for i, (s, t) in enumerate(zip(sources, targets))
    ]
    for c in copies:
        c.start()
    return copies


def tile_of(ref, core, at):
    return ref.at[:, core, :, at : at + ref.shape[0] * ref.shape[2]]


def matrix(ref, place, low=None, high=None):
    value = ref[place] if low is None else ref[place, :, :, low:high]
    return value.reshape(-1, value.shape[-1])


def mixer_tile(anys, cores, place, t, base, width):
    if len(anys) == 2:
        return anys[place].at[t]
    return tile_of(anys[0], cores[place], base + t * width)


def mixer_scratch(weights):
    w = weights[0]
    blocks, rows = (w.shape[1], w.shape[2]) if len(weights) == 2 else (w.shape[0], w.shape[2])
    return [pltpu.VMEM((2, blocks, rows, blocks * rows), LOW)] * 2


def swap_halves(value):
    lane = lax.broadcasted_iota(jnp.int32, value.shape, 1)
    return jnp.where(
        lax.rem(lane, HD) < HD // 2,
        pltpu.roll(value, 128 - HD // 2, 1),
        pltpu.roll(value, HD // 2, 1),
    )


def ordered(first, own, other):
    return jnp.concatenate([jnp.where(first, own, other), jnp.where(first, other, own)], 1)


def head_mask(shape, head):
    lane = lax.broadcasted_iota(jnp.int32, shape, 1)
    return (lane < HD) if head == 0 else (lane >= HD)


def attention_forward_kernel(
    base, place_of, ins, anys, outs, w_a, w_b, mixed, bias, columns_of_lse, sems
):
    resid, seg_col, seg_row, cosine, sine, gains = ins
    middle, query, keys, values, lse, pack = outs
    width = resid.shape[1]
    half = width // 2
    cores = (place_of[0], 1 - place_of[0])
    copies = fetch(
        [mixer_tile(anys, cores, p, t, base, width) for t in range(2) for p in range(2)],
        [w.at[place] for w in (w_a, w_b) for place in range(2)],
        sems,
    )
    first = place_of[0] == 0
    normed, _, _ = normalize(resid[...], gains[0:1], gains[1:2])
    normed_low, attended = pack.at[0], pack.at[1]
    normed_low[...] = normed.astype(LOW)
    bias[...] = jnp.where(seg_col[...] == seg_row[...], 0.0, -1000000000.0)
    for place in range(2):
        copies[place].wait()
        mixed[...] = dot(normed_low[...], matrix(w_a, place))
        for p in range(half // 128):
            for part, target, scale in ((0, query, HD ** (-0.5)), (1, keys, 1.0)):
                x = mixed[:, part * half + p * 128 : part * half + (p + 1) * 128]
                x = x * cosine[...] + swap_halves(x) * sine[...]
                x = (x * scale if scale != 1.0 else x).astype(LOW)
                target[:, place * half + p * 128 : place * half + (p + 1) * 128] = x
    for place in range(2):
        copies[2 + place].wait()
        values[:, place * half : (place + 1) * half] = dot(
            normed_low[...], matrix(w_b, place, 0, half)
        ).astype(LOW)

    columns_of_lse[...] = jnp.zeros_like(columns_of_lse)

    for p in range(width // 128):
        columns = slice(p * 128, (p + 1) * 128)
        q, k, v = query[:, columns], keys[:, columns], values[:, columns]
        out = []
        for head in range(2):
            masked_q = jnp.where(head_mask(q.shape, head), q, jnp.zeros_like(q))
            scores = dot_nt(masked_q, k) + bias[...]
            top = jnp.max(scores, -1, keepdims=True)
            expo = jnp.exp(scores - top)
            total = jnp.sum(expo, -1, keepdims=True)
            probs = (expo * (1.0 / total)).astype(LOW)
            out.append(dot(probs, v))
            lane = lax.broadcasted_iota(jnp.int32, columns_of_lse.shape, 1)
            columns_of_lse[...] = jnp.where(
                lane == 2 * p + head, top + jnp.log(total), columns_of_lse[...]
            )
        attended[:, columns] = jnp.where(head_mask(out[0].shape, 0), out[0], out[1]).astype(LOW)
    lse[...] = columns_of_lse[...].T[: lse.shape[0]]
    attended[...] = ordered(first, attended[:, :half], attended[:, half:])
    out = ordered(
        first,
        dot(attended[...], matrix(w_b, 0, half, width)),
        dot(attended[...], matrix(w_b, 1, half, width)),
    )
    middle[...] = resid[...] + out


def attention_forward(place, resid, weights, base, gains, cosine, sine, segments):
    length, width = resid.shape
    one = (length, width)
    return call(
        functools.partial(attention_forward_kernel, base),
        place,
        [(one, FULL)] + [(one, LOW)] * 3 + [((16, length), FULL), ((2,) + one, LOW)],
        [resid, *segments, cosine, sine, gains],
        weights,
        mixer_scratch(weights)
        + [
            pltpu.VMEM(one, FULL),
            pltpu.VMEM((length, length), FULL),
            pltpu.VMEM((length, 128), FULL),
            pltpu.SemaphoreType.DMA((4,)),
        ],
        8 * length * width * width + 4 * length * length * width,
    )


GELU_SCALE = 0.7978845608028654
GELU_CUBE = 0.044715


def fetch_hidden(anys, base, cores, ups, downs, sems, between=lambda t: None, down_first=False):
    blocks, parts, rows, width = downs.shape
    half, some = width // 2, max(blocks // 4, 1)
    copies = {}

    def up_source(place, within):
        if len(anys) == 2:
            return anys[place].at[2 * within]
        return tile_of(anys[0], cores[place], base + (2 + within) * width)

    def down_source(place, first, j):
        if len(anys) == 2:
            return anys[place].at[1 + j // 2 * 2, pl.ds(first, some), :, j % 2 * half : (j % 2 + 1) * half]
        at = base + 4 * width + j * half
        return anys[0].at[pl.ds(first, some), cores[place], :, at : at + half]

    for t in range(4):
        up = lambda: fetch([up_source(t // 2, t % 2)], [ups.at[t]], sems, t)
        if not down_first:
            copies[0, t] = up()
        if blocks >= 4 or t == 0:
            sources, targets = [], []
            first = (2 * cores[t // 2] + t % 2) * some if blocks >= 4 else 0
            for place in range(2):
                columns = pl.ds(pl.multiple_of(cores[place] * half, 128), half)
                for j in range(4):
                    sources.append(down_source(place, first, j))
                    targets.append(downs.at[pl.ds(t * some, some), j, :, columns])
            copies[1, t] = fetch(sources, targets, sems, 4 + 8 * t)
        between(t)
        if down_first:
            copies[0, t] = up()

    def wait(which, t):
        for copy in copies.pop((which, t), []):
            copy.wait()

    return wait


def rows_of(downs, t, cores):
    blocks, parts, rows, width = downs.shape
    if blocks >= 4:
        some = blocks // 4
        return downs[t * some : (t + 1) * some].reshape(some * parts * rows, width)
    return downs[0, 2 * cores[t // 2] + t % 2]


def hidden_scratch(weights):
    w = weights[0]
    blocks, rows = (w.shape[1], w.shape[2]) if len(weights) == 2 else (w.shape[0], w.shape[2])
    return [
        pltpu.VMEM((4, blocks, rows, blocks * rows), LOW),
        pltpu.VMEM((blocks, 4, rows, blocks * rows), LOW),
        pltpu.SemaphoreType.DMA((36,)),
    ]


def hidden_forward_kernel(base, place_of, ins, anys, outs, ups, downs, sems):
    middle, gains = ins
    output, pack, hidden = outs
    cores = (place_of[0], 1 - place_of[0])
    wait = fetch_hidden(anys, base, cores, ups, downs, sems)
    normed, _, _ = normalize(middle[...], gains[0:1], gains[1:2])
    pack[0] = normed.astype(LOW)
    pack.send(0)
    for t in range(4):
        wait(0, t)
        index = 2 * cores[t // 2] + t % 2
        x = dot(pack[0], matrix(ups, t))
        hidden[index] = x
        hidden.send(index)
        inner = jnp.tanh(x * (GELU_SCALE + (GELU_SCALE * GELU_CUBE) * (x * x)))
        value = x * 0.5
        value = (value + value * inner).astype(LOW)
        pack[1 + index] = value
        pack.send(1 + index)
        wait(1, t)
        product = dot(value, rows_of(downs, t, cores))
        output[...] = (middle[...] if t == 0 else output[...]) + product


def hidden_forward(place, middle, weights, base, gains):
    length, width = middle.shape
    one = (length, width)
    return call(
        functools.partial(hidden_forward_kernel, base),
        place,
        [(one, FULL), ((5,) + one, LOW), ((4,) + one, FULL)],
        [middle, gains],
        weights,
        hidden_scratch(weights),
        16 * length * width * width,
        sent=(1, 2),
    )


def hidden_back_kernel(base, place_of, ins, anys, outs, ups, downs, sems, hidden_here, total, own_sems):
    branch, grad, middle, gains = ins
    hidden, *weights = anys
    grad_middle, grad_gains, grad_own, grad_other = outs
    cores = (place_of[0], 1 - place_of[0])
    copies = []

    def fetch_values(t):
        source = hidden.at[2 * cores[t // 2] + t % 2]
        copies.extend(fetch([source], [hidden_here.at[t]], own_sems, t))

    wait = fetch_hidden(weights, base, cores, ups, downs, sems, fetch_values, down_first=True)
    for t in range(4):
        wait(1, t)
        grad_active = dot_nt(branch[...], rows_of(downs, t, cores))
        copies[t].wait()
        x = hidden_here[t]
        square = x * x
        inner = jnp.tanh(x * (GELU_SCALE + (GELU_SCALE * GELU_CUBE) * square))
        slope = x * (GELU_SCALE + (3.0 * GELU_SCALE * GELU_CUBE) * square)
        slope = (0.5 + 0.5 * inner) * (1.0 + slope * (1.0 - inner))
        value = (grad_active * slope).astype(LOW)
        (grad_own if t < 2 else grad_other)[t % 2] = value
        wait(0, t)
        product = dot_nt(value, matrix(ups, t))
        total[...] = product if t == 0 else total[...] + product
    _, unit, inverse = normalize(middle[...], gains[0:1], gains[1:2])
    back, gain, bias = normalize_back(total[...], unit, inverse, gains[0:1])
    grad_middle[...] = grad[...] + back
    grad_gains[0:1] = gain
    grad_gains[1:2] = bias


def hidden_back(place, grad, branch, middle, hidden, weights, base, gains):
    length, width = middle.shape
    one = (length, width)
    return call(
        functools.partial(hidden_back_kernel, base),
        place,
        [(one, FULL), ((2, width), FULL), ((2,) + one, LOW), ((2,) + one, LOW)],
        [branch, grad, middle, gains],
        [hidden] + weights,
        hidden_scratch(weights)
        + [
            pltpu.VMEM((4,) + one, FULL),
            pltpu.VMEM(one, FULL),
            pltpu.SemaphoreType.DMA((4,)),
        ],
        16 * length * width * width,
    )


def attention_back_kernel(base, place_of, ins, anys, outs, w_a, w_b, bias, ga, gq, gk, gv, sems):
    grad_middle, query, keys, values, lse, seg_col, seg_row, cosine, sine, gains, resid = ins
    grad, branch, branch_own, branch_other, grad_gains, grad_own, grad_other = outs
    width = resid.shape[1]
    half = width // 2
    cores = (place_of[0], 1 - place_of[0])
    copies = fetch(
        [mixer_tile(anys, cores, p, t, base, width) for t in (1, 0) for p in range(2)],
        [w.at[place] for w in (w_b, w_a) for place in range(2)],
        sems,
    )
    first = place_of[0] == 0
    grads = (grad_own, grad_other)
    bias[...] = jnp.where(seg_col[...] == seg_row[...], 0.0, -1000000000.0)
    attn_grad = grad_middle[...].astype(LOW)
    left, right = attn_grad[:, :half], attn_grad[:, half:]
    grad_own[1, :, half:] = jnp.where(first, left, right)
    grad_other[1, :, half:] = jnp.where(first, right, left)
    copies[0].wait()
    copies[1].wait()
    natural = dot_nt(grad_own[1, :, half:], matrix(w_b, 0, half, width)) + dot_nt(
        grad_other[1, :, half:], matrix(w_b, 1, half, width)
    )
    natural = natural.astype(LOW)
    ga[:, :half] = jnp.where(first, natural[:, :half], natural[:, half:])
    ga[:, half:] = jnp.where(first, natural[:, half:], natural[:, :half])

    for p in range(width // 128):
        columns = slice(p * 128, (p + 1) * 128)
        q, k, v, g = query[:, columns], keys[:, columns], values[:, columns], ga[:, columns]
        flipped = k.T
        out_q, out_k, out_v = [], [], []
        for head in range(2):
            mask = head_mask(q.shape, head)
            zero = jnp.zeros_like(q)
            scores = dot_nt(k, jnp.where(mask, q, zero)) + bias[...]
            probs = jnp.exp(scores - lse[2 * p + head : 2 * p + head + 1, :])
            grad_probs = dot_nt(v, jnp.where(mask, g, zero))
            across = jnp.sum(probs * grad_probs, 0, keepdims=True)
            grad_scores = (probs * (grad_probs - across)).astype(LOW)
            out_k.append(dot(grad_scores, q))
            out_q.append(dot(flipped[head * HD : (head + 1) * HD], grad_scores))
            out_v.append(dot(probs.astype(LOW), g))
        out_q = jnp.concatenate(out_q, 0).T * HD ** (-0.5)
        out_k = jnp.where(head_mask(out_k[0].shape, 0), out_k[0], out_k[1])
        for x, target in ((out_q, gq), (out_k, gk)):
            x = x * cosine[...] - swap_halves(x) * sine[...]
            target[:, columns] = x.astype(LOW)
        gv[:, columns] = jnp.where(head_mask(out_v[0].shape, 0), out_v[0], out_v[1]).astype(LOW)
    for place in (1, 0):
        columns = slice(place * half, (place + 1) * half)
        grads[place][0, :, :half] = gq[:, columns]
        grads[place][0, :, half:] = gk[:, columns]
        grads[place][1, :, :half] = gv[:, columns]
    copies[2].wait()
    copies[3].wait()
    total = dot_nt(grad_own[0], matrix(w_a, 0)) + dot_nt(grad_other[0], matrix(w_a, 1))
    total = total + dot_nt(grad_own[1, :, :half], matrix(w_b, 0, 0, half))
    total = total + dot_nt(grad_other[1, :, :half], matrix(w_b, 1, 0, half))
    _, unit, inverse = normalize(resid[...], gains[0:1], gains[1:2])
    back, gain, bias_grad = normalize_back(total, unit, inverse, gains[0:1])
    back = grad_middle[...] + back
    grad[...] = back
    back = back.astype(LOW)
    branch[...] = back
    branch_own[...] = jnp.where(first, back[:, :half], back[:, half:])
    branch_other[...] = jnp.where(first, back[:, half:], back[:, :half])
    grad_gains[0:1] = gain
    grad_gains[1:2] = bias_grad


def attention_back(place, grad_middle, resid, weights, base, gains, cosine, sine, segments, query, keys, values, lse):
    length, width = resid.shape
    one = (length, width)
    return call(
        functools.partial(attention_back_kernel, base),
        place,
        [(one, FULL), (one, LOW)]
        + [((length, width // 2), LOW)] * 2
        + [((2, width), FULL)]
        + [((2,) + one, LOW)] * 2,
        [grad_middle, query, keys, values, lse]
        + [*segments, cosine, sine, gains, resid],
        weights,
        mixer_scratch(weights)
        + [
            pltpu.VMEM((length, length), FULL),
        ]
        + [pltpu.VMEM(one, LOW)] * 4
        + [pltpu.SemaphoreType.DMA((4,))],
        8 * length * width * width + 10 * length * length * width,
    )


def head_kernel(place_of, ins, anys, outs):
    resid, table, gains, hot, weight = ins
    grad, branch, branch_own, branch_other, head_in, grad_logits, grad_gains, sums = outs
    half = resid.shape[1] // 2
    normed, unit, inverse = normalize(resid[...], gains[0:1], gains[1:2])
    head_in[...] = normed.astype(LOW)
    logits = dot_nt(head_in[...], table[...])
    lane = lax.broadcasted_iota(jnp.int32, logits.shape, 1)
    logits = jnp.where(lane < V, logits, -1e30)
    top = jnp.max(logits, 1, keepdims=True)
    lse = top + jnp.log(jnp.sum(jnp.exp(logits - top), 1, keepdims=True))
    hot = hot[...].astype(FULL)
    weight = weight[:, 0:1]
    picked = jnp.sum(logits * hot, 1, keepdims=True)
    loss = jnp.sum((lse - picked) * weight, 0, keepdims=True)
    count = jnp.sum(weight, 0, keepdims=True)
    lane = lax.broadcasted_iota(jnp.int32, sums.shape, 1)
    sums[...] = jnp.where(lane == 0, loss, jnp.where(lane == 1, count, 0.0))
    grad_logits[...] = ((jnp.exp(logits - lse) - hot) * weight).astype(LOW)
    back, gain, bias = normalize_back(
        dot(grad_logits[...], table[...]), unit, inverse, gains[0:1]
    )
    grad[...] = back
    back = back.astype(LOW)
    branch[...] = back
    first = place_of[0] == 0
    branch_own[...] = jnp.where(first, back[:, :half], back[:, half:])
    branch_other[...] = jnp.where(first, back[:, half:], back[:, :half])
    grad_gains[0:1] = gain
    grad_gains[1:2] = bias


def head(place, resid, table, gains, hot, weight):
    length, width = resid.shape
    one, part = (length, width), (length, width // 2)
    return call(
        head_kernel,
        place,
        [(one, FULL), (one, LOW), (part, LOW), (part, LOW), (one, LOW)]
        + [((length, SMALL), LOW), ((2, width), FULL), ((1, SMALL), FULL)],
        [resid, table, gains, hot, weight],
        flops=4 * length * width * SMALL,
    )


def adam_step(master, grad, first, second, rate, decay):
    first = BETA_ONE * first + (1.0 - BETA_ONE) * grad
    second = BETA_TWO * second + (1.0 - BETA_TWO) * grad * grad
    fix_one = 1.0 / (1.0 - BETA_ONE**STEP)
    fix_two = 1.0 / (1.0 - BETA_TWO**STEP)
    update = first * fix_one / (jnp.sqrt(second * fix_two) + ADAM_EPS) + decay * master
    return (master - rate * update, first, second)


def scale_of(totals):
    count = totals[0:1, 1:2]
    grad_norm = jnp.sqrt(totals[0:1, 2:3]) / count
    return grad_norm, CLIP / jnp.maximum(grad_norm, CLIP) / count


def optimizer_kernel(chunks, place_of, ins, anys, outs, *scratch):
    *masters, sems = scratch
    copies = fetch(anys, masters, sems)
    totals, small_own, small_other, *rest = ins
    n = (len(rest) - 6) // 2
    own, other = rest[:n], rest[n : 2 * n]
    masters += rest[2 * n :]
    layers = len(chunks)
    first = place_of[0] == 0
    grad_norm, scale = scale_of(totals[...])
    outs[0][...] = grad_norm

    def step(which, at, grad, rate=RATE_MATRIX, decay=DECAY):
        master, moment, square = (masters[3 * which + i][at] for i in range(3))
        values = adam_step(master, grad * scale, moment, square, rate, decay)
        for i in range(3):
            outs[1 + 3 * which + i][at] = values[i]

    def tile(where, s, core):
        a, b = own[where[0]][where[1], s], other[where[0]][where[1], s]
        return jnp.where(first, a, b) if core == 0 else jnp.where(first, b, a)

    def arrive(*which):
        for copy in copies[3 * which[0] : 3 * which[-1] + 3]:
            copy.wait()

    def leave(which):
        for i in range(3):
            outs[1 + 3 * which + i].send()

    rows, width = own[0].shape[-2:]
    half = width // 2
    arrive(0, 1)
    for l in range(layers):
        for core in range(2):
            columns = lambda p: pl.ds(p * width + core * half, half)
            value = tile(chunks[l][0], 0, core)
            step(0, (l, slice(None), columns(0)), value[:, :half])
            step(0, (l, slice(None), columns(1)), value[:, half:])
            value = tile(chunks[l][0], 1, core)
            step(0, (l, slice(None), columns(2)), value[:, :half])
            step(1, (l, slice(None), columns(0)), value[:, half:])
    leave(0)
    leave(1)
    arrive(2)
    for l in range(layers):
        for core in range(2):
            for s in range(2):
                at = (l, slice(None), pl.ds((2 * core + s) * width, width))
                step(2, at, tile(chunks[l][1], s, core))
    leave(2)
    arrive(3)
    for l in range(layers):
        for core in range(2):
            for s in range(2):
                value = tile(chunks[l][2], s, core)
                for j in range(2):
                    at = (l, pl.ds((2 * s + j) * rows, rows), pl.ds(core * half, half))
                    step(3, at, value[:, j * half : (j + 1) * half])
    leave(3)
    small = jnp.where(first, small_own[...], small_other[...])
    step(4, (slice(None), slice(None)), small[:, :V])
    small = small.T
    for n in range(masters[15].shape[0]):
        step(5, n, small[V + 2 * n : V + 2 * n + 2], RATE_VECTOR, 0.0)


def optimizer(place, totals, small, chunks, own, other, masters):
    return call(
        functools.partial(optimizer_kernel, chunks),
        place,
        [((1, 1), FULL)] + [(m.shape, m.dtype) for m in masters],
        [totals, *small, *own, *other, *masters[12:]],
        masters[:12],
        [pltpu.VMEM(m.shape, m.dtype) for m in masters[:12]] + [pltpu.SemaphoreType.DMA((12,))],
        flops=20 * sum(m.size for m in masters),
        sent=range(1, 13),
    )


def pack_kernel(layers, place_of, ins, anys, outs):
    inward, outward, expand, shrink, small = ins
    out, *early = outs
    first = place_of[0] == 0
    rows = inward.shape[1]
    width = inward.shape[2] // 3
    half = width // 2
    at = 0
    if early:
        early[0][rows : rows + 16] = jnp.zeros((16, width), LOW)
        for q in range(rows // 16):
            early[0][rows : rows + 16, q * SMALL : (q + 1) * SMALL] = small[q * 16 : (q + 1) * 16]
    else:
        at = small.shape[1]
        out[:, :at] = small[...]
    for l in range(layers):
        sources = [inward[l, :, p * width : (p + 1) * width] for p in range(3)] + [outward[l]]
        sources.append(expand[l])
        sources += [shrink[l, j * rows : (j + 1) * rows] for j in range(shrink.shape[1] // rows)]
        for n, value in enumerate(sources):
            part = value.shape[1] // 2
            value = jnp.where(first, value[:, :part], value[:, part:]).astype(LOW)
            if early and l == 0 and n < 4:
                start = 0 if n < 2 else rows + 16
                early[0][start : start + rows, (n % 2) * half : (n % 2 + 1) * half] = value
            elif early and l == layers - 1 and n == 4:
                for t in range(2):
                    early[1][2 * t * rows : (2 * t + 1) * rows] = value[:, t * width : (t + 1) * width]
            elif early and l == layers - 1 and n > 4:
                start = (2 * ((n - 5) // 2) + 1) * rows
                lanes = (n - 5) % 2 * half
                early[1][start : start + rows, lanes : lanes + half] = value
            else:
                out[:, at : at + part] = value
                at += part


def swap_cores(value):
    return lax.ppermute(value, "dp", [(0, 1), (1, 0)])


def across(value, mask, size):
    return lax.ppermute(value, "fsdp", [(i, i ^ mask) for i in range(size)])


def tie(*values):
    return lax.optimization_barrier(values)


def total_of(value, size):
    value = value + swap_cores(value)
    bit = 1
    while bit < size:
        if 2 * bit < size:
            a, b, c = (across(value, m * bit, size) for m in (1, 2, 3))
            value = (value + a) + (b + c)
        else:
            value = value + across(value, bit, size)
        bit *= 4
    return value


def arrange_kernel(parts, place_of, ins, anys, outs, sems):
    copies, at = [], 0
    for h in range(2):
        for piece in anys:
            copies += fetch(
                [piece.at[h * parts[0] : h * parts[0] + parts[h]]],
                [outs[0].at[at : at + parts[h]]],
                sems,
                len(copies),
            )
            at += parts[h]
    for copy in copies:
        copy.wait()


def place_kernel(parts, rows, place_of, ins, anys, outs, sems):
    quarter, from_x, from_y, far_a, far_b = anys
    tiles, *small = outs
    count = tiles.shape[0] // 2
    x, y, z = place_of[1], place_of[2], place_of[3]
    for n in range(16):
        xor_z, xor_y, xor_x = n // 4, n // 2 % 2, n % 2
        index = jnp.bitwise_xor(z, xor_z) * 4 + jnp.bitwise_xor(y, xor_y) * 2 + jnp.bitwise_xor(x, xor_x)
        for h in range(2):
            at = xor_z * parts[h]
            if xor_x and xor_y:
                source = (far_a, far_b)[h]
            else:
                source = from_x if xor_x else from_y if xor_y else quarter
                at += h * 4 * parts[0]
            for t in range(count):
                here = source.at[at + t * rows : at + (t + 1) * rows]
                fetch([here], [tiles.at[h * count + t, index]], sems, h * count + t)
            if h == 0 and small:
                here = source.at[at + count * rows : at + parts[0]]
                fetch([here], [small[0].at[index]], sems, 2 * count)
    targets = [tiles.at[t] for t in range(2 * count)] + small
    for n, target in enumerate(targets):
        pltpu.make_async_copy(target, target, sems.at[n]).wait()


class Gather:
    def __init__(self, place, shard, parts, rows):
        self.place, self.shard, self.parts, self.rows = place, shard, parts, rows

    def along_z(self):
        self.got = [across(self.shard, mask, 16) for mask in Z]

    def in_plane(self):
        width = self.shard.shape[1]
        (quarter,) = call(
            functools.partial(arrange_kernel, self.parts),
            self.place,
            [((4 * sum(self.parts), width), LOW)],
            [],
            [self.shard] + self.got,
            [pltpu.SemaphoreType.DMA((8,))],
        )
        self.quarter, self.near = quarter, [across(quarter, X, 16), across(quarter, Y, 16)]

    def forward(self):
        cut = 4 * self.parts[0]
        from_x, from_y = self.near
        self.far = [across(from_y[:cut], X, 16), across(from_x[cut:], Y, 16)]

    def result(self):
        width = self.shard.shape[1]
        count, more = divmod(self.parts[0], self.rows)
        outs = [((2 * count, 16, self.rows, width), LOW)]
        if more:
            outs.append(((16, more, width), LOW))
        return call(
            functools.partial(place_kernel, self.parts, self.rows),
            self.place,
            outs,
            [],
            [self.quarter] + self.near + self.far,
            [pltpu.SemaphoreType.DMA((2 * count + 1,))],
        )


X, Y = 1, 2
Z = (4, 8, 12)


def round_kernel(jobs, small_job, n_ins, counts, smalls, last, place_of, ins, anys, outs, *scratch):
    new, once, twice, done = counts
    small_new, small_once, small_twice, small_done = smalls
    rest = list(ins[n_ins:]) + list(outs) + list(scratch)
    pop = lambda present, n=1: [rest.pop(0) for _ in range(n)] if present else [None] * n
    (keep_once,), (small_keep_once,) = pop(once), pop(small_once)
    (keep_twice,), (small_keep_twice,) = pop(twice), pop(small_twice)
    from_x, from_y = pop(once or twice, 2)
    (keep_done,), (small_keep_done,) = pop(done), pop(small_done)
    from_z = pop(done, 3)
    (squares_in,), (sums,) = pop(done), pop(last)
    to_x, to_y = pop(new or once, 2)
    (out_once,), (small_out_once,) = pop(new), pop(small_new)
    (out_twice,), (small_out_twice,) = pop(once), pop(small_once)
    (out_done,), (small_out_done,) = pop(twice), pop(small_twice)
    to_z = pop(twice, 3)
    (share,), (small_share,), (squares,) = pop(done), pop(small_done), pop(done)
    (totals,) = pop(last)
    (tile,), (unit,), (small_tile,), (flat,) = pop(new), pop(new), pop(small_new), pop(small_new)
    rows = (out_once if new else out_twice if once else out_done if twice else share).shape[-2]
    rows = rows // (8 if new else 4 if once else 1)
    bits, z = (place_of[1], place_of[2]), place_of[3]
    to, came = (to_x, to_y), (from_x, from_y)

    def block(index, size=rows):
        if isinstance(index, int):
            return pl.ds(index * size, size)
        return pl.ds(pl.multiple_of(index * size, 16), size)

    def factor(spec):
        which, index, low, high = spec
        ref = ins[which] if index is None else ins[which].at[index]
        return ref[...] if low is None else ref[:, low:high]

    def put_small(ref, start, group, side, value):
        for q in range(rows // 16):
            lanes = side * (rows // 16) + q
            ref[pl.ds(start + group * 16, 16), lanes * SMALL : (lanes + 1) * SMALL] = value[
                q * 16 : (q + 1) * 16
            ].astype(LOW)

    def take_small(ref, start, group, side):
        parts = []
        for q in range(rows // 16):
            lanes = side * (rows // 16) + q
            at = pl.ds(pl.multiple_of(start + group * 16, 16), 16)
            parts.append(ref[at, lanes * SMALL : (lanes + 1) * SMALL])
        return jnp.concatenate(parts, 0).astype(FULL)

    def summed(products):
        total = None
        for left, right in products:
            product = cross(factor(left), factor(right))
            total = product if total is None else total + product
        return total

    for p in range(new):
        if len(jobs[p]) == 4:
            for quarter, products in enumerate(jobs[p]):
                unit[...] = summed(products)
                half = unit.shape[1]
                for index in range(4):
                    for s in range(2):
                        for j in range(2):
                            tile[s, block(quarter * 4 + index), j * half : (j + 1) * half] = unit[
                                block(index * 4 + 2 * s + j), :
                            ]
        else:
            for s in range(2):
                for low, high, products in jobs[p][s]:
                    tile[s, :, low:high] = summed(products)
        for s in range(2):
            for zz in range(4):
                for other in range(2):
                    at = zz * 2 + other
                    index = lambda bit: zz * 4 + (other * 2 + bit if s == 0 else bit * 2 + other)
                    to[s][block(p * 8 + at), :] = tile[s, block(index(1 - bits[s])), :].astype(LOW)
                    out_once[p, s, block(at), :] = tile[s, block(index(bits[s])), :]
    if small_new:
        products, norms_at = small_job
        flat[...] = summed([(right, left) for left, right in products])
        at = V
        for mine, theirs in norms_at:
            count = ins[mine].shape[0]
            flat[at : at + count] += ins[mine][...] + ins[theirs][...]
            at += count
        total = flat[...].T
        small_tile[...] = total
        for zz in range(4):
            for other in range(2):
                index = lambda bit: zz * 4 + other * 2 + bit
                send = small_tile[block(index(1 - bits[0])), :]
                put_small(to_x, (new * 8 + once * 4) * rows, other * 2 + zz // 2, zz % 2, send)
                small_out_once[block(zz * 2 + other), :] = small_tile[block(index(bits[0])), :]
    for p in range(once):
        for s in range(2):
            for zz in range(4):
                for bit in range(2):
                    at = zz * 2 + (bits[1 - s] if bit else 1 - bits[1 - s])
                    value = keep_once[p, s, block(at), :] + came[s][block(p * 8 + at), :].astype(FULL)
                    if bit:
                        out_twice[p, s, block(zz), :] = value
                    else:
                        to[1 - s][block(new * 8 + p * 4 + zz), :] = value.astype(LOW)
    if small_once:
        start = (once * 8 + twice * 4) * rows
        for zz in range(4):
            for bit in range(2):
                other = bits[1] if bit else 1 - bits[1]
                value = small_keep_once[block(zz * 2 + other), :]
                value = value + take_small(from_x, start, other * 2 + zz // 2, zz % 2)
                if bit:
                    small_out_twice[block(zz), :] = value
                else:
                    put_small(to_y, (new * 8 + once * 4) * rows, zz, 0, value)
    for p in range(twice):
        for s in range(2):
            for xor in range(4):
                at = jnp.bitwise_xor(z, xor)
                value = keep_twice[p, s, block(at), :] + came[1 - s][
                    block(once * 8 + p * 4 + at), :
                ].astype(FULL)
                if xor == 0:
                    out_done[p, s] = value
                else:
                    to_z[xor - 1][block(2 * p + s), :] = value.astype(LOW)
    if small_twice:
        for xor in range(4):
            at = jnp.bitwise_xor(z, xor)
            value = small_keep_twice[block(at), :]
            value = value + take_small(from_y, (once * 8 + twice * 4) * rows, at, 0)
            if xor == 0:
                small_out_done[...] = value
            else:
                put_small(to_z[xor - 1], twice * 2 * rows, 0, 0, value)
    if done:
        squares[...] = squares_in[...]
    for p in range(done):
        for s in range(2):
            value = keep_done[p, s]
            for f in from_z:
                value = value + f[block(2 * p + s), :].astype(FULL)
            share[p, s] = value
            squares[...] += jnp.sum(value * value, 0, keepdims=True)
    if small_done:
        value = small_keep_done[...]
        for f in from_z:
            value = value + take_small(f, done * 2 * rows, 0, 0)
        small_share[...] = value
    if last:
        total = jnp.sum(squares[...], 1, keepdims=True)
        if small_done:
            square = jnp.sum(jnp.sum(value * value, 0, keepdims=True), 1, keepdims=True)
            total = total + jnp.where(place_of[0] == 0, square, jnp.zeros_like(square))
        lane = lax.broadcasted_iota(jnp.int32, sums.shape, 1)
        totals[...] = jnp.where(lane == 2, total, sums[...])


class Rounds:
    def __init__(self, place, rows, width, sums):
        self.place, self.rows, self.width, self.sums = place, rows, width, sums
        self.counts, self.smalls = (0,) * 4, (False,) * 4
        self.kept, self.small_kept = [None] * 3, [None] * 3
        self.came = self.came_z = self.totals = None
        self.shares, self.others, self.small_share = [], [], None
        self.squares = jnp.zeros((1, width), FULL)
        self.flying, self.swapping = [], 0

    def step(self, chunk, *ties, small=None):
        rows, width = self.rows, self.width
        new, once, twice, done = counts = (len(chunk),) + self.counts[:3]
        smalls = (small is not None,) + self.smalls[:3]
        last = not (new or once or twice)
        arrays, jobs = [], []

        def number(spec):
            array, *place = spec
            for i, known in enumerate(arrays):
                if known is array:
                    return (i, *place)
            arrays.append(array)
            return (len(arrays) - 1, *place)

        numbered = lambda products: [(number(l), number(r)) for l, r in products]
        for pair in chunk:
            if len(pair) == 4:
                jobs.append([numbered(products) for products in pair])
            else:
                jobs.append([[(a, b, numbered(ps)) for a, b, ps in tile] for tile in pair])
        small_job = None
        if small is not None:
            small_job = (
                [(number(l), number(r)) for l, r in small[0]],
                [(number((a,))[0], number((b,))[0]) for a, b in small[1]],
            )
        ins = list(arrays)
        for stage in range(2):
            ins += [self.kept[stage]] * (counts[1 + stage] > 0)
            ins += [self.small_kept[stage]] * smalls[1 + stage]
        if once or twice:
            ins += self.came
        if done:
            ins += [self.kept[2]] + [self.small_kept[2]] * smalls[3] + self.came_z + [self.squares]
        ins += [self.sums] * last
        outs = []
        if new or once:
            for added in (64 * smalls[0], 64 * smalls[1]):
                outs.append((((new * 8 + once * 4) * rows + added, width), LOW))
        for stage, blocks in enumerate((8, 4, 1)):
            if counts[stage]:
                outs.append(((counts[stage], 2, blocks * rows, width), FULL))
            if smalls[stage]:
                outs.append(((blocks * rows, SMALL), FULL))
        if twice:
            outs += [((twice * 2 * rows + 16 * smalls[2], width), LOW)] * 3
        if done:
            outs.append(((done, 2, rows, width), FULL))
            outs += [((rows, SMALL), FULL)] * smalls[3]
            outs.append(((1, width), FULL))
        outs += [((1, SMALL), FULL)] * last
        length = 2 * arrays[0].shape[-2] if new else 0
        scratch = []
        if new:
            scratch.append(pltpu.VMEM((2, 16 * rows, width), FULL))
            scratch.append(pltpu.VMEM((16 * rows, width // 2), FULL))
        if smalls[0]:
            scratch.append(pltpu.VMEM((16 * rows, SMALL), FULL))
            scratch.append(pltpu.VMEM((SMALL, width), FULL))
        got = list(
            call(
                functools.partial(
                    round_kernel, jobs, small_job, len(arrays), counts, smalls, last
                ),
                self.place,
                outs,
                ins,
                [],
                scratch,
                4 * new * length * width * width,
                limit=VMEM_LIMIT if new or once else 24 << 20,
            )
        )
        if last:
            self.totals = got.pop()
        if done:
            self.squares = got.pop()
            if smalls[3]:
                self.small_share = got.pop()
            self.shares.append(got.pop())
        self.counts, self.smalls = counts, smalls
        self.kept, self.small_kept = [None] * 3, [None] * 3
        if last:
            return ties
        got, ties, self.shares = tie(got, ties, self.shares)
        to = [got.pop(0) for _ in range(2)] if new or once else []
        for stage in range(3):
            if counts[stage]:
                self.kept[stage] = got.pop(0)
            if smalls[stage]:
                self.small_kept[stage] = got.pop(0)
        self.flying = [across(v, mask, 16) for v, mask in zip(to, (X, Y))]
        self.flying += [across(v, mask, 16) for v, mask in zip(got, Z)]
        self.swapping = 0
        while len(self.flying) < 5 and len(self.others) + self.swapping < len(self.shares):
            self.flying.append(swap_cores(self.shares[len(self.others) + self.swapping]))
            self.swapping += 1
        return ties

    def finish(self, *ties):
        flying, ties = tie(self.flying, ties)
        self.came = self.came_z = None
        if self.counts[0] or self.counts[1]:
            self.came, flying = flying[:2], flying[2:]
        if self.counts[2]:
            self.came_z, flying = flying[:3], flying[3:]
        self.others += flying
        return ties

    def left(self):
        return any(self.counts[:3])

    def swap_rest(self):
        self.others += [swap_cores(v) for v in self.shares[len(self.others) :]]


class PlainRounds:
    def __init__(self):
        self.shares, self.squares = [], []

    def step(self, chunk, *ties):
        def factor(spec):
            array, index, low, high = spec
            array = array if index is None else array[index]
            return array if low is None else array[:, low:high]

        summed = lambda products: sum(cross(factor(l), factor(r)) for l, r in products)
        scatter = lambda v: lax.psum_scatter(v, "fsdp", scatter_dimension=0, tiled=True)
        shares = []
        for pair in chunk:
            if len(pair) == 4:
                v = scatter(jnp.concatenate([summed(products) for products in pair], 0))
                v = v.reshape(2, 2, -1, v.shape[1])
                shares.append(jnp.concatenate([v[:, 0], v[:, 1]], 2))
            else:
                tiles = [jnp.concatenate([summed(ps) for _, _, ps in t], 1) for t in pair]
                shares.append(jnp.stack([scatter(t) for t in tiles]))
        share = jnp.stack(shares)
        self.shares.append((share, swap_cores(share)))
        self.squares.append(jnp.sum(share * share, (0, 1, 2))[None])
        return ties

    def finish(self, *ties):
        return ties

    def left(self):
        return False


def half_of(value, core):
    half = value.shape[1] // 2
    return lax.dynamic_slice_in_dim(value, core * half, half, 1)


def body(
    fsdp,
    codons,
    masked,
    segments,
    inward,
    outward,
    expand,
    shrink,
    codon_table,
    norm_params,
    inward_first,
    inward_second,
    outward_first,
    outward_second,
    expand_first,
    expand_second,
    shrink_first,
    shrink_second,
    table_first,
    table_second,
    norm_first,
    norm_second,
):
    layers = inward.shape[0]
    length = codons.shape[0]
    rows = inward.shape[1]
    width = rows * fsdp
    half = width // 2
    fast = fsdp == 16 and rows == 48 and layers > 1
    core, index = lax.axis_index("dp"), lax.axis_index("fsdp")
    bit = lambda b: lax.rem(lax.div(index, b), 2)
    place = jnp.stack([core, bit(1), bit(2), lax.div(index, 4)]).astype(jnp.int32)
    weight = masked.astype(FULL)
    inputs = jnp.where(masked == 1, V - 1, codons)

    norms = norm_params.shape[0] * 2
    small = jnp.concatenate(
        [codon_table.astype(LOW), norm_params.astype(LOW).reshape(norms, rows)], 0
    )
    small = jnp.pad(small.T, ((0, 0), (0, -small.shape[0] % 128)))
    columns = small.shape[1] + layers * 6 * width
    shapes = [(rows, columns)]
    if fast:
        shapes = [(rows, (layers - 1) * 6 * width), (2 * rows + 16, width), (4 * rows, width)]
    weights, *early = call(
        functools.partial(pack_kernel, layers),
        place,
        [(shape, LOW) for shape in shapes],
        [inward, outward, expand, shrink, small],
    )
    weights = lax.all_gather(weights, ("fsdp", "dp"), axis=0, tiled=True)
    weights = weights.reshape(fsdp, 2, rows, -1)
    if not fast:
        columns = [weights[:, :, :, : small.shape[1]]]
        for at in range(small.shape[1], weights.shape[3], 6 * width):
            columns.append(weights[:, :, :, at : at + 4 * width])
            quarter = weights[:, :, :, at + 4 * width : at + 6 * width]
            quarter = quarter.reshape(fsdp, 2, rows, 4, half).transpose(1, 0, 3, 2, 4)
            quarter = quarter.reshape(2, 4, width, half).transpose(0, 2, 1, 3)
            columns.append(quarter.reshape(2, fsdp, rows, 2 * width).transpose(1, 0, 2, 3))
        weights = jnp.concatenate(columns, 3).transpose(1, 0, 2, 3).reshape(1, 2, width, -1)
    hot = (codons[:, None] == jnp.arange(SMALL, dtype=jnp.int32)[None, :]).astype(LOW)
    columns = (hot, jnp.broadcast_to(weight[:, None], (length, SMALL)), segments[:, None])
    mixers, hiddens = [[weights]] * layers, [[weights]] * layers
    if fast:
        first = Gather(place, early[0], (rows + 16, rows), rows)
        last = Gather(place, early[1], (2 * rows, 2 * rows), rows)
        first.along_z()
        first.got, last.shard, columns = tie(first.got, last.shard, columns)
        first.in_plane()
        last.along_z()
        (first.near,) = tie(first.near)
        first.forward()
        first.far, last.got = tie(first.far, last.got)
        own, small = first.result()
        mixers[0] = [own, swap_cores(own)]
        last.in_plane()
        small = small[:, :, : rows // 16 * SMALL].reshape(16, 16, rows // 16, SMALL)
        small = small.transpose(0, 2, 1, 3).reshape(width, SMALL).T
    else:
        small = weights[:, 0, :, :SMALL].reshape(width, SMALL).T
    start = -2 * width if fast else weights.shape[3] - layers * 6 * width
    base = lambda l: start + l * 6 * width
    gains = small[V : V + norms].astype(FULL).reshape(-1, 2, width)

    cosine, sine = rotary_tables(length)
    chosen = (inputs[:, None] == jnp.arange(SMALL, dtype=jnp.int32)[None, :]).astype(LOW)
    resid = dot(chosen, small)
    kept = []
    for l in range(layers):
        gain = gains[2 * l : 2 * l + 2]
        middle, query, keys, values, lse, pack = attention_forward(
            place, resid, mixers[l], base(l), gain[0], cosine, sine, (columns[2], segments[None, :])
        )
        if fast and l == 0:
            middle, last.near = tie(middle, last.near)
            last.forward()
        output, pack_mid, hidden = hidden_forward(place, middle, hiddens[l], base(l), gain[1])
        if fast and l == 0:
            output, last.far = tie(output, last.far)
            (own,) = last.result()
            hiddens[-1] = [own, swap_cores(own)]
            output, hiddens[-1][0] = tie(output, own)
        kept.append((resid, query, keys, values, lse, pack, middle, hidden, pack_mid))
        resid = output
    grad, branch, branch_own, branch_other, head_in, grad_logits, grad_norms, sums = head(
        place, resid, small, gains[2 * layers], columns[0], columns[1]
    )
    grad_norms = [grad_norms]
    early = (head_in, grad_logits, chosen)
    early_came = [swap_cores(v) for v in early]
    mid_came = [swap_cores(saved[-1]) for saved in kept]
    pack_came = [swap_cores(saved[5]) for saved in kept]
    grad, branch, mid_came[-1] = tie(grad, branch, mid_came[-1])

    rounds = Rounds(place, rows, width, sums) if fast else PlainRounds()
    whole = lambda array, i=None: (array, i, None, None)
    tile = lambda left, right, other_left, other_right: [
        (0, width, [(left, right), (other_left, other_right)])
    ]
    chunk = []
    for l in reversed(range(layers)):
        resid, query, keys, values, lse, pack, middle, hidden, pack_mid = kept[l]
        gain = gains[2 * l : 2 * l + 2]
        branch_came = swap_cores(branch_other)
        chunk.append(
            [
                [
                    (whole(pack_mid, 1 + t), whole(branch_own)),
                    (whole(mid_came[l], 1 + t), whole(branch_came)),
                ]
                for t in range(4)
            ]
        )
        grad, branch = rounds.step(chunk, grad, branch)
        grad_middle, gains_mid, up_own, up_other = hidden_back(
            place, grad, branch, middle, hidden, hiddens[l], base(l), gain[1]
        )
        grad_middle, up_own, up_other, early_came = rounds.finish(
            grad_middle, up_own, up_other, early_came
        )
        up_came = swap_cores(up_other)
        if l == 0:
            norms_early = jnp.concatenate([gains_mid] + grad_norms, 0)
            norms_early = (norms_early, swap_cores(norms_early))
        (grad_middle,) = rounds.step(
            [
                [
                    tile(
                        whole(pack_mid, 0), whole(up_own, s), whole(mid_came[l], 0), whole(up_came, s)
                    )
                    for s in range(2)
                ]
            ],
            grad_middle,
        )
        grad, branch, branch_own, branch_other, gains_in, mix_own, mix_other = attention_back(
            place, grad_middle, resid, mixers[l], base(l), gain[0], cosine, sine,
            (columns[2], segments[None, :]),
            query, keys, values, lse,
        )
        grad_norms = [gains_in, gains_mid] + grad_norms
        grad, branch, branch_own, branch_other, mix_own, mix_other, mid_came, pack_came = (
            rounds.finish(
                grad, branch, branch_own, branch_other, mix_own, mix_other, mid_came, pack_came
            )
        )
        mix_came = swap_cores(mix_other)
        products = lambda i, a, b: [
            ((pack, i, None, None), (mix_own, 1, a, b)),
            ((pack_came[l], i, None, None), (mix_came, 1, a, b)),
        ]
        chunk = [
            [
                tile(whole(pack, 0), whole(mix_own, 0), whole(pack_came[l], 0), whole(mix_came, 0)),
                [(0, half, products(0, 0, half)), (half, width, products(1, half, width))],
            ]
        ]
    late = (grad_norms[0], swap_cores(grad_norms[0]))
    branch_came = swap_cores(branch)
    products = [(whole(early[0]), whole(early[1])), (whole(early_came[0]), whole(early_came[1]))]
    products += [(whole(branch), whole(early[2])), (whole(branch_came), whole(early_came[2]))]
    if fast:
        rounds.step(chunk, small=(products, [late, norms_early]))
        while rounds.left():
            rounds.finish()
            rounds.step([])
        rounds.swap_rest()
        share_small = rounds.small_share
        small_other = swap_cores(share_small)
        totals = rounds.totals
    else:
        rounds.step(chunk)
        table = sum(cross(l[0], r[0]) for l, r in products)
        table = table + jnp.pad(
            jnp.concatenate([a + b for a, b in (late, norms_early)], 0).T,
            ((0, 0), (V, SMALL - V - norms)),
        )
        table = jnp.where(core == 0, table, swap_cores(table))
        share_small = lax.psum_scatter(table, "fsdp", scatter_dimension=0, tiled=True)
        squares = jnp.sum(share_small * share_small) * (core == 0)
        for value in rounds.squares:
            squares = squares + jnp.sum(value)
        totals = sums + jnp.where(jnp.arange(SMALL) == 2, squares, 0.0)[None]
    totals = total_of(totals, fsdp)
    shares = list(zip(rounds.shares, rounds.others)) if fast else rounds.shares
    places = [(2 * (layers - 1 - l), 0 if l == layers - 1 else 1) for l in range(layers)]

    def tiles_at(chunk, pair):
        own, other = (v[pair] for v in shares[chunk])
        ordered = (jnp.where(core == 0, own, other), jnp.where(core == 0, other, own))
        return [v[s] for v in ordered for s in range(2)]

    if not fast:
        share_in, share_out, share_up, share_down = [], [], [], []
        side = lambda *values: jnp.concatenate(values, 1)
        for at, pair in places:
            a_0, b_0, a_1, b_1 = tiles_at(at + 2, 0)
            share_in.append(
                side(
                    a_0[:, :half], a_1[:, :half], a_0[:, half:],
                    a_1[:, half:], b_0[:, :half], b_1[:, :half],
                )
            )
            share_out.append(side(b_0[:, half:], b_1[:, half:]))
            share_up.append(side(*tiles_at(at + 1, 0)))
            a_0, b_0, a_1, b_1 = tiles_at(at, pair)
            share_down.append(
                jnp.concatenate(
                    [
                        side(x[:, j * half : (j + 1) * half], y[:, j * half : (j + 1) * half])
                        for x, y in ((a_0, a_1), (b_0, b_1))
                        for j in range(2)
                    ],
                    0,
                )
            )
        share_in, share_out, share_up, share_down = (
            jnp.stack(v) for v in (share_in, share_out, share_up, share_down)
        )
    masters = (inward, outward, expand, shrink, codon_table, norm_params)
    firsts = (inward_first, outward_first, expand_first, shrink_first, table_first, norm_first)
    seconds = (
        inward_second,
        outward_second,
        expand_second,
        shrink_second,
        table_second,
        norm_second,
    )
    if fast:
        chunks = [((at + 2, 0), (at + 1, 0), (at, pair)) for at, pair in places]
        own, other = zip(*shares)
        states = [v for group in zip(masters, firsts, seconds) for v in group]
        states[12:15] = [v.T for v in states[12:15]]
        grad_norm, *values = optimizer(
            place, totals, (share_small, small_other), chunks, own, other, states
        )
        values[12:15] = [v.T for v in values[12:15]]
    else:
        grad_norm, scale = scale_of(totals)
        share_small = share_small[:, : V + norms].T
        grads = (share_in, share_out, share_up, share_down)
        grads += (share_small[:V], share_small[V:].reshape(-1, 2, rows))
        values = []
        for index, grad in enumerate(grads):
            rate, decay = (RATE_VECTOR, 0.0) if index == 5 else (RATE_MATRIX, DECAY)
            values.extend(
                adam_step(masters[index], grad * scale.reshape(()), firsts[index], seconds[index], rate, decay)
            )
    return (totals[0, 0], totals[0, 1], grad_norm.reshape(()), *values)


def solution(mesh):
    in_specs = (
        P(("fsdp", "dp")),
        P(("fsdp", "dp")),
        P(("fsdp", "dp")),
        P(None, "fsdp", None),
        P(None, "fsdp", None),
        P(None, "fsdp", None),
        P(None, "fsdp", None),
        P(None, "fsdp"),
        P(None, None, "fsdp"),
        P(None, "fsdp", None),
        P(None, "fsdp", None),
        P(None, "fsdp", None),
        P(None, "fsdp", None),
        P(None, "fsdp", None),
        P(None, "fsdp", None),
        P(None, "fsdp", None),
        P(None, "fsdp", None),
        P(None, "fsdp"),
        P(None, "fsdp"),
        P(None, None, "fsdp"),
        P(None, None, "fsdp"),
    )
    out_specs = (
        P(),
        P(),
        P(),
        P(None, "fsdp", None),
        P(None, "fsdp", None),
        P(None, "fsdp", None),
        P(None, "fsdp", None),
        P(None, "fsdp", None),
        P(None, "fsdp", None),
        P(None, "fsdp", None),
        P(None, "fsdp", None),
        P(None, "fsdp", None),
        P(None, "fsdp", None),
        P(None, "fsdp", None),
        P(None, "fsdp", None),
        P(None, "fsdp"),
        P(None, "fsdp"),
        P(None, "fsdp"),
        P(None, None, "fsdp"),
        P(None, None, "fsdp"),
        P(None, None, "fsdp"),
    )
    step = functools.partial(body, mesh.shape["fsdp"])
    return jax.shard_map(step, mesh=mesh, in_specs=in_specs, out_specs=out_specs, check_vma=False)
```

```python
import functools

import jax
import jax.numpy as jnp
from jax import lax
from jax.experimental import pallas as pl
from jax.experimental.pallas import tpu as pltpu
from jax.sharding import PartitionSpec as P

HD = 64
V = 70
STEP = 10


NORM_EPS = 1e-05
BETA_ONE = 0.9
BETA_TWO = 0.95
ADAM_EPS = 1e-08
DECAY = 0.1
RATE_MATRIX = 0.05
RATE_VECTOR = 0.3
CLIP = 0.05


def rotary_tables(length):
    freq = 10000.0 ** (-jnp.arange(HD // 2, dtype=jnp.float32) * 2.0 / HD)
    angle = jnp.arange(length, dtype=jnp.float32)[:, None] * freq[None, :]
    cosine, sine = jnp.cos(angle), jnp.sin(angle)
    return (
        jnp.concatenate([cosine] * 4, 1),
        jnp.concatenate([-sine, sine] * 2, 1),
    )


def normalize(resid, gain, bias):
    mean = jnp.mean(resid, -1, keepdims=True)
    centred = resid - mean
    inverse = lax.rsqrt(jnp.mean(centred * centred, -1, keepdims=True) + NORM_EPS)
    unit = centred * inverse
    return (unit * gain + bias, unit, inverse)


def normalize_back(grad, unit, inverse, gain):
    scaled = grad * gain
    across = (
        scaled
        - jnp.mean(scaled, -1, keepdims=True)
        - unit * jnp.mean(scaled * unit, -1, keepdims=True)
    )
    return (across * inverse, jnp.sum(grad * unit, 0, keepdims=True), jnp.sum(grad, 0, keepdims=True))


def dot(left, right):
    return jnp.dot(left, right, preferred_element_type=jnp.float32)


def dot_nt(left, right):
    return lax.dot_general(
        left, right, (((1,), (1,)), ((), ())), preferred_element_type=jnp.float32
    )


def cross(left, right):
    return lax.dot_general(
        left, right, (((0,), (0,)), ((), ())), preferred_element_type=jnp.float32
    )


VMEM_LIMIT = 56 * 1024 * 1024
LOW, FULL = jnp.bfloat16, jnp.float32
SMALL = 128


class Sent:
    def __init__(self, here, there, sems):
        self.here, self.there, self.sems = here, there, sems
        self.shape, self.at = here.shape, here.at
        self.copies = []

    def __getitem__(self, at):
        return self.here[at]

    def __setitem__(self, at, value):
        self.here[at] = value

    def send(self, index=None):
        here, there = self.here, self.there
        if index is not None:
            here, there = here.at[index], there.at[index]
        copy = pltpu.make_async_copy(here, there, self.sems.at[len(self.copies)])
        copy.start()
        self.copies.append(copy)


def call(kernel, scalars, outs, ins, anys=(), scratch=(), flops=0, sent=(), limit=VMEM_LIMIT):
    whole = pl.BlockSpec(memory_space=pltpu.VMEM)
    left = pl.BlockSpec(memory_space=pl.ANY)

    def body(scalars, *refs):
        refs = list(refs)
        take = lambda n: [refs.pop(0) for _ in range(n)]
        in_refs, any_refs, out_refs = take(len(ins)), take(len(anys)), take(len(outs))
        here = take(len(sent))
        for n, i in enumerate(sent):
            out_refs[i] = Sent(here[n], out_refs[i], refs[-1].at[n])
        kernel(scalars, in_refs, any_refs, out_refs, *(refs[:-1] if sent else refs))
        for i in sent:
            for copy in out_refs[i].copies:
                copy.wait()

    return pl.pallas_call(
        body,
        out_shape=[jax.ShapeDtypeStruct(s, t) for s, t in outs],
        in_specs=[pl.BlockSpec(memory_space=pltpu.SMEM)]
        + [whole] * len(ins)
        + [left] * len(anys),
        out_specs=[left if i in sent else whole for i in range(len(outs))],
        scratch_shapes=[pltpu.VMEM(*outs[i]) for i in sent]
        + list(scratch)
        + [pltpu.SemaphoreType.DMA((len(sent), 5))] * (len(sent) > 0),
        compiler_params=pltpu.CompilerParams(vmem_limit_bytes=limit),
        cost_estimate=pl.CostEstimate(
            flops=flops,
            bytes_accessed=sum(x.size * x.dtype.itemsize for x in list(ins) + list(anys)),
            transcendentals=0,
        ),
    )(scalars, *ins, *anys)


def fetch(sources, targets, sems, first=0):
    copies = [
        pltpu.make_async_copy(s, t, sems.at[first + i])
        for i, (s, t) in enumerate(zip(sources, targets))
    ]
    for c in copies:
        c.start()
    return copies


def tile_of(ref, core, at):
    return ref.at[:, core, :, at : at + ref.shape[0] * ref.shape[2]]


def matrix(ref, place, low=None, high=None):
    value = ref[place] if low is None else ref[place, :, :, low:high]
    return value.reshape(-1, value.shape[-1])


def mixer_tile(anys, cores, place, t, base, width):
    if len(anys) == 2:
        return anys[place].at[t]
    return tile_of(anys[0], cores[place], base + t * width)


def mixer_scratch(weights):
    w = weights[0]
    blocks, rows = (w.shape[1], w.shape[2]) if len(weights) == 2 else (w.shape[0], w.shape[2])
    return [pltpu.VMEM((2, blocks, rows, blocks * rows), LOW)] * 2


def swap_halves(value):
    lane = lax.broadcasted_iota(jnp.int32, value.shape, 1)
    return jnp.where(
        lax.rem(lane, HD) < HD // 2,
        pltpu.roll(value, 128 - HD // 2, 1),
        pltpu.roll(value, HD // 2, 1),
    )


def ordered(first, own, other):
    return jnp.concatenate([jnp.where(first, own, other), jnp.where(first, other, own)], 1)


def head_mask(shape, head):
    lane = lax.broadcasted_iota(jnp.int32, shape, 1)
    return (lane < HD) if head == 0 else (lane >= HD)


def attention_forward_kernel(
    base, place_of, ins, anys, outs, w_a, w_b, mixed, bias, columns_of_lse, sems
):
    resid, seg_col, seg_row, cosine, sine, gains = ins
    middle, query, keys, values, lse, pack = outs
    width = resid.shape[1]
    half = width // 2
    cores = (place_of[0], 1 - place_of[0])
    copies = fetch(
        [mixer_tile(anys, cores, p, t, base, width) for t in range(2) for p in range(2)],
        [w.at[place] for w in (w_a, w_b) for place in range(2)],
        sems,
    )
    first = place_of[0] == 0
    normed, _, _ = normalize(resid[...], gains[0:1], gains[1:2])
    normed_low, attended = pack.at[0], pack.at[1]
    normed_low[...] = normed.astype(LOW)
    bias[...] = jnp.where(seg_col[...] == seg_row[...], 0.0, -1000000000.0)
    for place in range(2):
        copies[place].wait()
        mixed[...] = dot(normed_low[...], matrix(w_a, place))
        for p in range(half // 128):
            for part, target, scale in ((0, query, HD ** (-0.5)), (1, keys, 1.0)):
                x = mixed[:, part * half + p * 128 : part * half + (p + 1) * 128]
                x = x * cosine[...] + swap_halves(x) * sine[...]
                x = (x * scale if scale != 1.0 else x).astype(LOW)
                target[:, place * half + p * 128 : place * half + (p + 1) * 128] = x
    for place in range(2):
        copies[2 + place].wait()
        values[:, place * half : (place + 1) * half] = dot(
            normed_low[...], matrix(w_b, place, 0, half)
        ).astype(LOW)

    columns_of_lse[...] = jnp.zeros_like(columns_of_lse)

    for p in range(width // 128):
        columns = slice(p * 128, (p + 1) * 128)
        q, k, v = query[:, columns], keys[:, columns], values[:, columns]
        out = []
        for head in range(2):
            masked_q = jnp.where(head_mask(q.shape, head), q, jnp.zeros_like(q))
            scores = dot_nt(masked_q, k) + bias[...]
            top = jnp.max(scores, -1, keepdims=True)
            expo = jnp.exp(scores - top)
            total = jnp.sum(expo, -1, keepdims=True)
            probs = (expo * (1.0 / total)).astype(LOW)
            out.append(dot(probs, v))
            lane = lax.broadcasted_iota(jnp.int32, columns_of_lse.shape, 1)
            columns_of_lse[...] = jnp.where(
                lane == 2 * p + head, top + jnp.log(total), columns_of_lse[...]
            )
        attended[:, columns] = jnp.where(head_mask(out[0].shape, 0), out[0], out[1]).astype(LOW)
    lse[...] = columns_of_lse[...].T[: lse.shape[0]]
    attended[...] = ordered(first, attended[:, :half], attended[:, half:])
    out = ordered(
        first,
        dot(attended[...], matrix(w_b, 0, half, width)),
        dot(attended[...], matrix(w_b, 1, half, width)),
    )
    middle[...] = resid[...] + out


def attention_forward(place, resid, weights, base, gains, cosine, sine, segments):
    length, width = resid.shape
    one = (length, width)
    return call(
        functools.partial(attention_forward_kernel, base),
        place,
        [(one, FULL)] + [(one, LOW)] * 3 + [((16, length), FULL), ((2,) + one, LOW)],
        [resid, *segments, cosine, sine, gains],
        weights,
        mixer_scratch(weights)
        + [
            pltpu.VMEM(one, FULL),
            pltpu.VMEM((length, length), FULL),
            pltpu.VMEM((length, 128), FULL),
            pltpu.SemaphoreType.DMA((4,)),
        ],
        8 * length * width * width + 4 * length * length * width,
    )


GELU_SCALE = 0.7978845608028654
GELU_CUBE = 0.044715


def fetch_hidden(anys, base, cores, ups, downs, sems, between=lambda t: None, down_first=False):
    blocks, parts, rows, width = downs.shape
    half, some = width // 2, max(blocks // 4, 1)
    copies = {}

    def up_source(place, within):
        if len(anys) == 2:
            return anys[place].at[2 * within]
        return tile_of(anys[0], cores[place], base + (2 + within) * width)

    def down_source(place, first, j):
        if len(anys) == 2:
            return anys[place].at[1 + j // 2 * 2, pl.ds(first, some), :, j % 2 * half : (j % 2 + 1) * half]
        at = base + 4 * width + j * half
        return anys[0].at[pl.ds(first, some), cores[place], :, at : at + half]

    for t in range(4):
        up = lambda: fetch([up_source(t // 2, t % 2)], [ups.at[t]], sems, t)
        if not down_first:
            copies[0, t] = up()
        if blocks >= 4 or t == 0:
            sources, targets = [], []
            first = (2 * cores[t // 2] + t % 2) * some if blocks >= 4 else 0
            for place in range(2):
                columns = pl.ds(pl.multiple_of(cores[place] * half, 128), half)
                for j in range(4):
                    sources.append(down_source(place, first, j))
                    targets.append(downs.at[pl.ds(t * some, some), j, :, columns])
            copies[1, t] = fetch(sources, targets, sems, 4 + 8 * t)
        between(t)
        if down_first:
            copies[0, t] = up()

    def wait(which, t):
        for copy in copies.pop((which, t), []):
            copy.wait()

    return wait


def rows_of(downs, t, cores):
    blocks, parts, rows, width = downs.shape
    if blocks >= 4:
        some = blocks // 4
        return downs[t * some : (t + 1) * some].reshape(some * parts * rows, width)
    return downs[0, 2 * cores[t // 2] + t % 2]


def hidden_scratch(weights):
    w = weights[0]
    blocks, rows = (w.shape[1], w.shape[2]) if len(weights) == 2 else (w.shape[0], w.shape[2])
    return [
        pltpu.VMEM((4, blocks, rows, blocks * rows), LOW),
        pltpu.VMEM((blocks, 4, rows, blocks * rows), LOW),
        pltpu.SemaphoreType.DMA((36,)),
    ]


def hidden_forward_kernel(base, place_of, ins, anys, outs, ups, downs, sems):
    middle, gains = ins
    output, pack, hidden = outs
    cores = (place_of[0], 1 - place_of[0])
    wait = fetch_hidden(anys, base, cores, ups, downs, sems)
    normed, _, _ = normalize(middle[...], gains[0:1], gains[1:2])
    pack[0] = normed.astype(LOW)
    pack.send(0)
    for t in range(4):
        wait(0, t)
        index = 2 * cores[t // 2] + t % 2
        x = dot(pack[0], matrix(ups, t))
        hidden[index] = x
        hidden.send(index)
        inner = jnp.tanh(x * (GELU_SCALE + (GELU_SCALE * GELU_CUBE) * (x * x)))
        value = x * 0.5
        value = (value + value * inner).astype(LOW)
        pack[1 + index] = value
        pack.send(1 + index)
        wait(1, t)
        product = dot(value, rows_of(downs, t, cores))
        output[...] = (middle[...] if t == 0 else output[...]) + product


def hidden_forward(place, middle, weights, base, gains):
    length, width = middle.shape
    one = (length, width)
    return call(
        functools.partial(hidden_forward_kernel, base),
        place,
        [(one, FULL), ((5,) + one, LOW), ((4,) + one, FULL)],
        [middle, gains],
        weights,
        hidden_scratch(weights),
        16 * length * width * width,
        sent=(1, 2),
    )


def hidden_back_kernel(base, place_of, ins, anys, outs, ups, downs, sems, hidden_here, total, own_sems):
    branch, grad, middle, gains = ins
    hidden, *weights = anys
    grad_middle, grad_gains, grad_own, grad_other = outs
    cores = (place_of[0], 1 - place_of[0])
    copies = []

    def fetch_values(t):
        source = hidden.at[2 * cores[t // 2] + t % 2]
        copies.extend(fetch([source], [hidden_here.at[t]], own_sems, t))

    wait = fetch_hidden(weights, base, cores, ups, downs, sems, fetch_values, down_first=True)
    for t in range(4):
        wait(1, t)
        grad_active = dot_nt(branch[...], rows_of(downs, t, cores))
        copies[t].wait()
        x = hidden_here[t]
        square = x * x
        inner = jnp.tanh(x * (GELU_SCALE + (GELU_SCALE * GELU_CUBE) * square))
        slope = x * (GELU_SCALE + (3.0 * GELU_SCALE * GELU_CUBE) * square)
        slope = (0.5 + 0.5 * inner) * (1.0 + slope * (1.0 - inner))
        value = (grad_active * slope).astype(LOW)
        (grad_own if t < 2 else grad_other)[t % 2] = value
        wait(0, t)
        product = dot_nt(value, matrix(ups, t))
        total[...] = product if t == 0 else total[...] + product
    _, unit, inverse = normalize(middle[...], gains[0:1], gains[1:2])
    back, gain, bias = normalize_back(total[...], unit, inverse, gains[0:1])
    grad_middle[...] = grad[...] + back
    grad_gains[0:1] = gain
    grad_gains[1:2] = bias


def hidden_back(place, grad, branch, middle, hidden, weights, base, gains):
    length, width = middle.shape
    one = (length, width)
    return call(
        functools.partial(hidden_back_kernel, base),
        place,
        [(one, FULL), ((2, width), FULL), ((2,) + one, LOW), ((2,) + one, LOW)],
        [branch, grad, middle, gains],
        [hidden] + weights,
        hidden_scratch(weights)
        + [
            pltpu.VMEM((4,) + one, FULL),
            pltpu.VMEM(one, FULL),
            pltpu.SemaphoreType.DMA((4,)),
        ],
        16 * length * width * width,
    )


def attention_back_kernel(base, place_of, ins, anys, outs, w_a, w_b, bias, ga, gq, gk, gv, sems):
    grad_middle, query, keys, values, lse, seg_col, seg_row, cosine, sine, gains, resid = ins
    grad, branch, branch_own, branch_other, grad_gains, grad_own, grad_other = outs
    width = resid.shape[1]
    half = width // 2
    cores = (place_of[0], 1 - place_of[0])
    copies = fetch(
        [mixer_tile(anys, cores, p, t, base, width) for t in (1, 0) for p in range(2)],
        [w.at[place] for w in (w_b, w_a) for place in range(2)],
        sems,
    )
    first = place_of[0] == 0
    grads = (grad_own, grad_other)
    bias[...] = jnp.where(seg_col[...] == seg_row[...], 0.0, -1000000000.0)
    attn_grad = grad_middle[...].astype(LOW)
    left, right = attn_grad[:, :half], attn_grad[:, half:]
    grad_own[1, :, half:] = jnp.where(first, left, right)
    grad_other[1, :, half:] = jnp.where(first, right, left)
    copies[0].wait()
    copies[1].wait()
    natural = dot_nt(grad_own[1, :, half:], matrix(w_b, 0, half, width)) + dot_nt(
        grad_other[1, :, half:], matrix(w_b, 1, half, width)
    )
    natural = natural.astype(LOW)
    ga[:, :half] = jnp.where(first, natural[:, :half], natural[:, half:])
    ga[:, half:] = jnp.where(first, natural[:, half:], natural[:, :half])

    for p in range(width // 128):
        columns = slice(p * 128, (p + 1) * 128)
        q, k, v, g = query[:, columns], keys[:, columns], values[:, columns], ga[:, columns]
        flipped = k.T
        out_q, out_k, out_v = [], [], []
        for head in range(2):
            mask = head_mask(q.shape, head)
            zero = jnp.zeros_like(q)
            scores = dot_nt(k, jnp.where(mask, q, zero)) + bias[...]
            probs = jnp.exp(scores - lse[2 * p + head : 2 * p + head + 1, :])
            grad_probs = dot_nt(v, jnp.where(mask, g, zero))
            across = jnp.sum(probs * grad_probs, 0, keepdims=True)
            grad_scores = (probs * (grad_probs - across)).astype(LOW)
            out_k.append(dot(grad_scores, q))
            out_q.append(dot(flipped[head * HD : (head + 1) * HD], grad_scores))
            out_v.append(dot(probs.astype(LOW), g))
        out_q = jnp.concatenate(out_q, 0).T * HD ** (-0.5)
        out_k = jnp.where(head_mask(out_k[0].shape, 0), out_k[0], out_k[1])
        for x, target in ((out_q, gq), (out_k, gk)):
            x = x * cosine[...] - swap_halves(x) * sine[...]
            target[:, columns] = x.astype(LOW)
        gv[:, columns] = jnp.where(head_mask(out_v[0].shape, 0), out_v[0], out_v[1]).astype(LOW)
    for place in (1, 0):
        columns = slice(place * half, (place + 1) * half)
        grads[place][0, :, :half] = gq[:, columns]
        grads[place][0, :, half:] = gk[:, columns]
        grads[place][1, :, :half] = gv[:, columns]
    copies[2].wait()
    copies[3].wait()
    total = dot_nt(grad_own[0], matrix(w_a, 0)) + dot_nt(grad_other[0], matrix(w_a, 1))
    total = total + dot_nt(grad_own[1, :, :half], matrix(w_b, 0, 0, half))
    total = total + dot_nt(grad_other[1, :, :half], matrix(w_b, 1, 0, half))
    _, unit, inverse = normalize(resid[...], gains[0:1], gains[1:2])
    back, gain, bias_grad = normalize_back(total, unit, inverse, gains[0:1])
    back = grad_middle[...] + back
    grad[...] = back
    back = back.astype(LOW)
    branch[...] = back
    branch_own[...] = jnp.where(first, back[:, :half], back[:, half:])
    branch_other[...] = jnp.where(first, back[:, half:], back[:, :half])
    grad_gains[0:1] = gain
    grad_gains[1:2] = bias_grad


def attention_back(place, grad_middle, resid, weights, base, gains, cosine, sine, segments, query, keys, values, lse):
    length, width = resid.shape
    one = (length, width)
    return call(
        functools.partial(attention_back_kernel, base),
        place,
        [(one, FULL), (one, LOW)]
        + [((length, width // 2), LOW)] * 2
        + [((2, width), FULL)]
        + [((2,) + one, LOW)] * 2,
        [grad_middle, query, keys, values, lse]
        + [*segments, cosine, sine, gains, resid],
        weights,
        mixer_scratch(weights)
        + [
            pltpu.VMEM((length, length), FULL),
        ]
        + [pltpu.VMEM(one, LOW)] * 4
        + [pltpu.SemaphoreType.DMA((4,))],
        8 * length * width * width + 10 * length * length * width,
    )


def head_kernel(place_of, ins, anys, outs):
    resid, table, gains, hot, weight = ins
    grad, branch, branch_own, branch_other, head_in, grad_logits, grad_gains, sums = outs
    half = resid.shape[1] // 2
    normed, unit, inverse = normalize(resid[...], gains[0:1], gains[1:2])
    head_in[...] = normed.astype(LOW)
    logits = dot_nt(head_in[...], table[...])
    lane = lax.broadcasted_iota(jnp.int32, logits.shape, 1)
    logits = jnp.where(lane < V, logits, -1e30)
    top = jnp.max(logits, 1, keepdims=True)
    lse = top + jnp.log(jnp.sum(jnp.exp(logits - top), 1, keepdims=True))
    hot = hot[...].astype(FULL)
    weight = weight[:, 0:1]
    picked = jnp.sum(logits * hot, 1, keepdims=True)
    loss = jnp.sum((lse - picked) * weight, 0, keepdims=True)
    count = jnp.sum(weight, 0, keepdims=True)
    lane = lax.broadcasted_iota(jnp.int32, sums.shape, 1)
    sums[...] = jnp.where(lane == 0, loss, jnp.where(lane == 1, count, 0.0))
    grad_logits[...] = ((jnp.exp(logits - lse) - hot) * weight).astype(LOW)
    back, gain, bias = normalize_back(
        dot(grad_logits[...], table[...]), unit, inverse, gains[0:1]
    )
    grad[...] = back
    back = back.astype(LOW)
    branch[...] = back
    first = place_of[0] == 0
    branch_own[...] = jnp.where(first, back[:, :half], back[:, half:])
    branch_other[...] = jnp.where(first, back[:, half:], back[:, :half])
    grad_gains[0:1] = gain
    grad_gains[1:2] = bias


def head(place, resid, table, gains, hot, weight):
    length, width = resid.shape
    one, part = (length, width), (length, width // 2)
    return call(
        head_kernel,
        place,
        [(one, FULL), (one, LOW), (part, LOW), (part, LOW), (one, LOW)]
        + [((length, SMALL), LOW), ((2, width), FULL), ((1, SMALL), FULL)],
        [resid, table, gains, hot, weight],
        flops=4 * length * width * SMALL,
    )


def adam_step(master, grad, first, second, rate, decay):
    first = BETA_ONE * first + (1.0 - BETA_ONE) * grad
    second = BETA_TWO * second + (1.0 - BETA_TWO) * grad * grad
    fix_one = 1.0 / (1.0 - BETA_ONE**STEP)
    fix_two = 1.0 / (1.0 - BETA_TWO**STEP)
    update = first * fix_one / (jnp.sqrt(second * fix_two) + ADAM_EPS) + decay * master
    return (master - rate * update, first, second)


def scale_of(totals):
    count = totals[0:1, 1:2]
    grad_norm = jnp.sqrt(totals[0:1, 2:3]) / count
    return grad_norm, CLIP / jnp.maximum(grad_norm, CLIP) / count


def optimizer_kernel(chunks, place_of, ins, anys, outs, *scratch):
    *masters, sems = scratch
    copies = fetch(anys, masters, sems)
    totals, small_own, small_other, *rest = ins
    n = (len(rest) - 6) // 2
    own, other = rest[:n], rest[n : 2 * n]
    masters += rest[2 * n :]
    layers = len(chunks)
    first = place_of[0] == 0
    grad_norm, scale = scale_of(totals[...])
    outs[0][...] = grad_norm

    def step(which, at, grad, rate=RATE_MATRIX, decay=DECAY):
        master, moment, square = (masters[3 * which + i][at] for i in range(3))
        values = adam_step(master, grad * scale, moment, square, rate, decay)
        for i in range(3):
            outs[1 + 3 * which + i][at] = values[i]

    def tile(where, s, core):
        a, b = own[where[0]][where[1], s], other[where[0]][where[1], s]
        return jnp.where(first, a, b) if core == 0 else jnp.where(first, b, a)

    def arrive(*which):
        for copy in copies[3 * which[0] : 3 * which[-1] + 3]:
            copy.wait()

    def leave(which):
        for i in range(3):
            outs[1 + 3 * which + i].send()

    rows, width = own[0].shape[-2:]
    half = width // 2
    arrive(0, 1)
    for l in range(layers):
        for core in range(2):
            columns = lambda p: pl.ds(p * width + core * half, half)
            value = tile(chunks[l][0], 0, core)
            step(0, (l, slice(None), columns(0)), value[:, :half])
            step(0, (l, slice(None), columns(1)), value[:, half:])
            value = tile(chunks[l][0], 1, core)
            step(0, (l, slice(None), columns(2)), value[:, :half])
            step(1, (l, slice(None), columns(0)), value[:, half:])
    leave(0)
    leave(1)
    arrive(2)
    for l in range(layers):
        for core in range(2):
            for s in range(2):
                at = (l, slice(None), pl.ds((2 * core + s) * width, width))
                step(2, at, tile(chunks[l][1], s, core))
    leave(2)
    arrive(3)
    for l in range(layers):
        for core in range(2):
            for s in range(2):
                value = tile(chunks[l][2], s, core)
                for j in range(2):
                    at = (l, pl.ds((2 * s + j) * rows, rows), pl.ds(core * half, half))
                    step(3, at, value[:, j * half : (j + 1) * half])
    leave(3)
    small = jnp.where(first, small_own[...], small_other[...])
    step(4, (slice(None), slice(None)), small[:, :V])
    small = small.T
    for n in range(masters[15].shape[0]):
        step(5, n, small[V + 2 * n : V + 2 * n + 2], RATE_VECTOR, 0.0)


def optimizer(place, totals, small, chunks, own, other, masters):
    return call(
        functools.partial(optimizer_kernel, chunks),
        place,
        [((1, 1), FULL)] + [(m.shape, m.dtype) for m in masters],
        [totals, *small, *own, *other, *masters[12:]],
        masters[:12],
        [pltpu.VMEM(m.shape, m.dtype) for m in masters[:12]] + [pltpu.SemaphoreType.DMA((12,))],
        flops=20 * sum(m.size for m in masters),
        sent=range(1, 13),
    )


def pack_kernel(layers, place_of, ins, anys, outs):
    inward, outward, expand, shrink, small = ins
    out, *early = outs
    first = place_of[0] == 0
    rows = inward.shape[1]
    width = inward.shape[2] // 3
    half = width // 2
    at = 0
    if early:
        early[0][rows : rows + 16] = jnp.zeros((16, width), LOW)
        for q in range(rows // 16):
            early[0][rows : rows + 16, q * SMALL : (q + 1) * SMALL] = small[q * 16 : (q + 1) * 16]
    else:
        at = small.shape[1]
        out[:, :at] = small[...]
    for l in range(layers):
        sources = [inward[l, :, p * width : (p + 1) * width] for p in range(3)] + [outward[l]]
        sources.append(expand[l])
        sources += [shrink[l, j * rows : (j + 1) * rows] for j in range(shrink.shape[1] // rows)]
        for n, value in enumerate(sources):
            part = value.shape[1] // 2
            value = jnp.where(first, value[:, :part], value[:, part:]).astype(LOW)
            if early and l == 0 and n < 4:
                start = 0 if n < 2 else rows + 16
                early[0][start : start + rows, (n % 2) * half : (n % 2 + 1) * half] = value
            elif early and l == layers - 1 and n == 4:
                for t in range(2):
                    early[1][2 * t * rows : (2 * t + 1) * rows] = value[:, t * width : (t + 1) * width]
            elif early and l == layers - 1 and n > 4:
                start = (2 * ((n - 5) // 2) + 1) * rows
                lanes = (n - 5) % 2 * half
                early[1][start : start + rows, lanes : lanes + half] = value
            else:
                out[:, at : at + part] = value
                at += part


def swap_cores(value):
    return lax.ppermute(value, "dp", [(0, 1), (1, 0)])


def across(value, mask, size):
    return lax.ppermute(value, "fsdp", [(i, i ^ mask) for i in range(size)])


def tie(*values):
    return lax.optimization_barrier(values)


def total_of(value, size):
    value = value + swap_cores(value)
    bit = 1
    while bit < size:
        if 2 * bit < size:
            a, b, c = (across(value, m * bit, size) for m in (1, 2, 3))
            value = (value + a) + (b + c)
        else:
            value = value + across(value, bit, size)
        bit *= 4
    return value


def arrange_kernel(parts, place_of, ins, anys, outs, sems):
    copies, at = [], 0
    for h in range(2):
        for piece in anys:
            copies += fetch(
                [piece.at[h * parts[0] : h * parts[0] + parts[h]]],
                [outs[0].at[at : at + parts[h]]],
                sems,
                len(copies),
            )
            at += parts[h]
    for copy in copies:
        copy.wait()


def place_kernel(parts, rows, place_of, ins, anys, outs, sems):
    quarter, from_x, from_y, far_a, far_b = anys
    tiles, *small = outs
    count = tiles.shape[0] // 2
    x, y, z = place_of[1], place_of[2], place_of[3]
    for n in range(16):
        xor_z, xor_y, xor_x = n // 4, n // 2 % 2, n % 2
        index = jnp.bitwise_xor(z, xor_z) * 4 + jnp.bitwise_xor(y, xor_y) * 2 + jnp.bitwise_xor(x, xor_x)
        for h in range(2):
            at = xor_z * parts[h]
            if xor_x and xor_y:
                source = (far_a, far_b)[h]
            else:
                source = from_x if xor_x else from_y if xor_y else quarter
                at += h * 4 * parts[0]
            for t in range(count):
                here = source.at[at + t * rows : at + (t + 1) * rows]
                fetch([here], [tiles.at[h * count + t, index]], sems, h * count + t)
            if h == 0 and small:
                here = source.at[at + count * rows : at + parts[0]]
                fetch([here], [small[0].at[index]], sems, 2 * count)
    targets = [tiles.at[t] for t in range(2 * count)] + small
    for n, target in enumerate(targets):
        pltpu.make_async_copy(target, target, sems.at[n]).wait()


class Gather:
    def __init__(self, place, shard, parts, rows):
        self.place, self.shard, self.parts, self.rows = place, shard, parts, rows

    def along_z(self):
        self.got = [across(self.shard, mask, 16) for mask in Z]

    def in_plane(self):
        width = self.shard.shape[1]
        (quarter,) = call(
            functools.partial(arrange_kernel, self.parts),
            self.place,
            [((4 * sum(self.parts), width), LOW)],
            [],
            [self.shard] + self.got,
            [pltpu.SemaphoreType.DMA((8,))],
        )
        self.quarter, self.near = quarter, [across(quarter, X, 16), across(quarter, Y, 16)]

    def forward(self):
        cut = 4 * self.parts[0]
        from_x, from_y = self.near
        self.far = [across(from_y[:cut], X, 16), across(from_x[cut:], Y, 16)]

    def result(self):
        width = self.shard.shape[1]
        count, more = divmod(self.parts[0], self.rows)
        outs = [((2 * count, 16, self.rows, width), LOW)]
        if more:
            outs.append(((16, more, width), LOW))
        return call(
            functools.partial(place_kernel, self.parts, self.rows),
            self.place,
            outs,
            [],
            [self.quarter] + self.near + self.far,
            [pltpu.SemaphoreType.DMA((2 * count + 1,))],
        )


X, Y = 1, 2
Z = (4, 8, 12)


def round_kernel(jobs, small_job, n_ins, counts, smalls, last, split, place_of, ins, anys, outs, *scratch):
    new, once, twice, done = counts
    small_new, small_once, small_twice, small_done = smalls
    rest = list(ins[n_ins:]) + list(outs) + list(scratch)
    pop = lambda present, n=1: [rest.pop(0) for _ in range(n)] if present else [None] * n
    (keep_once,), (small_keep_once,) = pop(once), pop(small_once)
    (keep_twice,), (small_keep_twice,) = pop(twice), pop(small_twice)
    from_x, from_y = pop(once or twice, 2)
    again_x, again_y = pop(split and twice, 2)
    (keep_done,), (small_keep_done,) = pop(done), pop(small_done)
    from_z = pop(done, 3)
    (squares_in,), (sums,) = pop(done), pop(last)
    to_x, to_y = pop(new or once, 2)
    (out_once,), (small_out_once,) = pop(new), pop(small_new)
    (out_twice,), (small_out_twice,) = pop(once), pop(small_once)
    (out_done,), (small_out_done,) = pop(twice), pop(small_twice)
    to_z = pop(twice, 3)
    (share,), (small_share,), (squares,) = pop(done), pop(small_done), pop(done)
    (totals,) = pop(last)
    (tile,), (unit,), (small_tile,), (flat,) = pop(new), pop(new), pop(small_new), pop(small_new)
    rows = (out_once if new else out_twice if once else out_done if twice else share).shape[-2]
    rows = rows // (8 if new else 4 if once else 1)
    bits, z = (place_of[1], place_of[2]), place_of[3]
    to, came = (to_x, to_y), (from_x, from_y)
    again, behind = (came, once * 8)
    if split:
        again, behind = (again_x, again_y), 0

    def block(index, size=rows):
        if isinstance(index, int):
            return pl.ds(index * size, size)
        return pl.ds(pl.multiple_of(index * size, 16), size)

    def factor(spec):
        which, index, low, high = spec
        ref = ins[which] if index is None else ins[which].at[index]
        return ref[...] if low is None else ref[:, low:high]

    def put_small(ref, start, group, side, value):
        for q in range(rows // 16):
            lanes = side * (rows // 16) + q
            ref[pl.ds(start + group * 16, 16), lanes * SMALL : (lanes + 1) * SMALL] = value[
                q * 16 : (q + 1) * 16
            ].astype(LOW)

    def take_small(ref, start, group, side):
        parts = []
        for q in range(rows // 16):
            lanes = side * (rows // 16) + q
            at = pl.ds(pl.multiple_of(start + group * 16, 16), 16)
            parts.append(ref[at, lanes * SMALL : (lanes + 1) * SMALL])
        return jnp.concatenate(parts, 0).astype(FULL)

    def summed(products):
        total = None
        for left, right in products:
            product = cross(factor(left), factor(right))
            total = product if total is None else total + product
        return total

    for p in range(new):
        if len(jobs[p]) == 4:
            for quarter, products in enumerate(jobs[p]):
                unit[...] = summed(products)
                half = unit.shape[1]
                for index in range(4):
                    for s in range(2):
                        for j in range(2):
                            tile[s, block(quarter * 4 + index), j * half : (j + 1) * half] = unit[
                                block(index * 4 + 2 * s + j), :
                            ]
        else:
            for s in range(2):
                for low, high, products in jobs[p][s]:
                    tile[s, :, low:high] = summed(products)
        for s in range(2):
            for zz in range(4):
                for other in range(2):
                    at = zz * 2 + other
                    index = lambda bit: zz * 4 + (other * 2 + bit if s == 0 else bit * 2 + other)
                    to[s][block(p * 8 + at), :] = tile[s, block(index(1 - bits[s])), :].astype(LOW)
                    out_once[p, s, block(at), :] = tile[s, block(index(bits[s])), :]
    if small_new:
        products, norms_at = small_job
        flat[...] = summed([(right, left) for left, right in products])
        at = V
        for mine, theirs in norms_at:
            count = ins[mine].shape[0]
            flat[at : at + count] += ins[mine][...] + ins[theirs][...]
            at += count
        total = flat[...].T
        small_tile[...] = total
        for zz in range(4):
            for other in range(2):
                index = lambda bit: zz * 4 + other * 2 + bit
                send = small_tile[block(index(1 - bits[0])), :]
                put_small(to_x, (new * 8 + once * 4) * rows, other * 2 + zz // 2, zz % 2, send)
                small_out_once[block(zz * 2 + other), :] = small_tile[block(index(bits[0])), :]
    for p in range(once):
        for s in range(2):
            for zz in range(4):
                for bit in range(2):
                    at = zz * 2 + (bits[1 - s] if bit else 1 - bits[1 - s])
                    value = keep_once[p, s, block(at), :] + came[s][block(p * 8 + at), :].astype(FULL)
                    if bit:
                        out_twice[p, s, block(zz), :] = value
                    else:
                        to[1 - s][block(new * 8 + p * 4 + zz), :] = value.astype(LOW)
    if small_once:
        start = (once * 8 + (0 if split else twice * 4)) * rows
        for zz in range(4):
            for bit in range(2):
                other = bits[1] if bit else 1 - bits[1]
                value = small_keep_once[block(zz * 2 + other), :]
                value = value + take_small(from_x, start, other * 2 + zz // 2, zz % 2)
                if bit:
                    small_out_twice[block(zz), :] = value
                else:
                    put_small(to_y, (new * 8 + once * 4) * rows, zz, 0, value)
    for p in range(twice):
        for s in range(2):
            for xor in range(4):
                at = jnp.bitwise_xor(z, xor)
                value = keep_twice[p, s, block(at), :] + again[1 - s][
                    block(behind + p * 4 + at), :
                ].astype(FULL)
                if xor == 0:
                    out_done[p, s] = value
                else:
                    to_z[xor - 1][block(2 * p + s), :] = value.astype(LOW)
    if small_twice:
        for xor in range(4):
            at = jnp.bitwise_xor(z, xor)
            value = small_keep_twice[block(at), :]
            value = value + take_small(from_y, (once * 8 + twice * 4) * rows, at, 0)
            if xor == 0:
                small_out_done[...] = value
            else:
                put_small(to_z[xor - 1], twice * 2 * rows, 0, 0, value)
    if done:
        squares[...] = squares_in[...]
    for p in range(done):
        for s in range(2):
            value = keep_done[p, s]
            for f in from_z:
                value = value + f[block(2 * p + s), :].astype(FULL)
            share[p, s] = value
            squares[...] += jnp.sum(value * value, 0, keepdims=True)
    if small_done:
        value = small_keep_done[...]
        for f in from_z:
            value = value + take_small(f, done * 2 * rows, 0, 0)
        small_share[...] = value
    if last:
        total = jnp.sum(squares[...], 1, keepdims=True)
        if small_done:
            square = jnp.sum(jnp.sum(value * value, 0, keepdims=True), 1, keepdims=True)
            total = total + jnp.where(place_of[0] == 0, square, jnp.zeros_like(square))
        lane = lax.broadcasted_iota(jnp.int32, sums.shape, 1)
        totals[...] = jnp.where(lane == 2, total, sums[...])


class Rounds:
    def __init__(self, place, rows, width, sums):
        self.place, self.rows, self.width, self.sums = place, rows, width, sums
        self.counts, self.smalls = (0,) * 4, (False,) * 4
        self.kept, self.small_kept = [None] * 3, [None] * 3
        self.came = self.came_z = self.totals = self.again = None
        self.shares, self.others, self.small_share = [], [], None
        self.squares = jnp.zeros((1, width), FULL)
        self.flying, self.swapping = [], 0

    def run(self, chunk, small, counts, smalls, limit):
        rows, width = self.rows, self.width
        new, once, twice, done = counts
        last = not (new or once or twice)
        split = self.again is not None
        arrays, jobs = [], []

        def number(spec):
            array, *place = spec
            for i, known in enumerate(arrays):
                if known is array:
                    return (i, *place)
            arrays.append(array)
            return (len(arrays) - 1, *place)

        numbered = lambda products: [(number(l), number(r)) for l, r in products]
        for pair in chunk:
            if len(pair) == 4:
                jobs.append([numbered(products) for products in pair])
            else:
                jobs.append([[(a, b, numbered(ps)) for a, b, ps in tile] for tile in pair])
        small_job = None
        if small is not None:
            small_job = (
                [(number(l), number(r)) for l, r in small[0]],
                [(number((a,))[0], number((b,))[0]) for a, b in small[1]],
            )
        ins = list(arrays)
        for stage in range(2):
            ins += [self.kept[stage]] * (counts[1 + stage] > 0)
            ins += [self.small_kept[stage]] * smalls[1 + stage]
        if once or twice:
            ins += self.came
        if split and twice:
            ins += self.again
        if done:
            ins += [self.kept[2]] + [self.small_kept[2]] * smalls[3] + self.came_z + [self.squares]
        ins += [self.sums] * last
        outs = []
        if new or once:
            for added in (64 * smalls[0], 64 * smalls[1]):
                outs.append((((new * 8 + once * 4) * rows + added, width), LOW))
        for stage, blocks in enumerate((8, 4, 1)):
            if counts[stage]:
                outs.append(((counts[stage], 2, blocks * rows, width), FULL))
            if smalls[stage]:
                outs.append(((blocks * rows, SMALL), FULL))
        if twice:
            outs += [((twice * 2 * rows + 16 * smalls[2], width), LOW)] * 3
        if done:
            outs.append(((done, 2, rows, width), FULL))
            outs += [((rows, SMALL), FULL)] * smalls[3]
            outs.append(((1, width), FULL))
        outs += [((1, SMALL), FULL)] * last
        length = 2 * arrays[0].shape[-2] if new else 0
        scratch = []
        if new:
            scratch.append(pltpu.VMEM((2, 16 * rows, width), FULL))
            scratch.append(pltpu.VMEM((16 * rows, width // 2), FULL))
        if smalls[0]:
            scratch.append(pltpu.VMEM((16 * rows, SMALL), FULL))
            scratch.append(pltpu.VMEM((SMALL, width), FULL))
        got = list(
            call(
                functools.partial(
                    round_kernel, jobs, small_job, len(arrays), counts, smalls, last, split
                ),
                self.place,
                outs,
                ins,
                [],
                scratch,
                4 * new * length * width * width,
                limit=limit,
            )
        )
        if last:
            self.totals = got.pop()
        if done:
            self.squares = got.pop()
            if smalls[3]:
                self.small_share = got.pop()
            self.shares.append(got.pop())
        to = [got.pop(0) for _ in range(2)] if new or once else []
        kept, small_kept = [None] * 3, [None] * 3
        for stage in range(3):
            if counts[stage]:
                kept[stage] = got.pop(0)
            if smalls[stage]:
                small_kept[stage] = got.pop(0)
        return to, kept, small_kept, got

    def step(self, chunk, *ties, small=None, split=False):
        counts = (len(chunk),) + self.counts[:3]
        smalls = (small is not None,) + self.smalls[:3]
        again = None
        plane = lambda to: [across(v, mask, 16) for v, mask in zip(to, (X, Y))]
        line = lambda to: [across(v, mask, 16) for v, mask in zip(to, Z)]
        if split:
            to, kept, small_kept, to_z = self.run(
                [], None, (0,) + counts[1:], (False,) + smalls[1:], VMEM_LIMIT
            )
            again, along_z = plane(to), line(to_z)
            to, new_kept, new_small, _ = self.run(
                chunk, small, (counts[0], 0, 0, 0), (smalls[0],) + (False,) * 3, VMEM_LIMIT
            )
            kept[0], small_kept[0] = new_kept[0], new_small[0]
            again, to, kept, small_kept, ties, self.shares = tie(
                again, to, kept, small_kept, ties, self.shares
            )
            self.flying = plane(to) + along_z
        else:
            limit = VMEM_LIMIT if chunk else 24 << 20
            to, kept, small_kept, to_z = self.run(chunk, small, counts, smalls, limit)
            if any(counts[:3]):
                to, kept, small_kept, to_z, ties, self.shares = tie(
                    to, kept, small_kept, to_z, ties, self.shares
                )
            self.flying = plane(to) + line(to_z)
        self.again = again
        self.counts, self.smalls = counts, smalls
        self.kept, self.small_kept = kept, small_kept
        if not any(counts[:3]):
            return ties
        self.swapping = 0
        while len(self.flying) < 5 and len(self.others) + self.swapping < len(self.shares):
            self.flying.append(swap_cores(self.shares[len(self.others) + self.swapping]))
            self.swapping += 1
        return ties

    def finish(self, *ties):
        flying, ties = tie(self.flying, ties)
        self.came = self.came_z = None
        if self.counts[0] or self.counts[1]:
            self.came, flying = flying[:2], flying[2:]
        if self.counts[2]:
            self.came_z, flying = flying[:3], flying[3:]
        self.others += flying
        return ties

    def left(self):
        return any(self.counts[:3])

    def swap_rest(self):
        self.others += [swap_cores(v) for v in self.shares[len(self.others) :]]


class PlainRounds:
    def __init__(self):
        self.shares, self.squares = [], []

    def step(self, chunk, *ties, split=False):
        def factor(spec):
            array, index, low, high = spec
            array = array if index is None else array[index]
            return array if low is None else array[:, low:high]

        summed = lambda products: sum(cross(factor(l), factor(r)) for l, r in products)
        scatter = lambda v: lax.psum_scatter(v, "fsdp", scatter_dimension=0, tiled=True)
        shares = []
        for pair in chunk:
            if len(pair) == 4:
                v = scatter(jnp.concatenate([summed(products) for products in pair], 0))
                v = v.reshape(2, 2, -1, v.shape[1])
                shares.append(jnp.concatenate([v[:, 0], v[:, 1]], 2))
            else:
                tiles = [jnp.concatenate([summed(ps) for _, _, ps in t], 1) for t in pair]
                shares.append(jnp.stack([scatter(t) for t in tiles]))
        share = jnp.stack(shares)
        self.shares.append((share, swap_cores(share)))
        self.squares.append(jnp.sum(share * share, (0, 1, 2))[None])
        return ties

    def finish(self, *ties):
        return ties

    def left(self):
        return False


def half_of(value, core):
    half = value.shape[1] // 2
    return lax.dynamic_slice_in_dim(value, core * half, half, 1)


def body(
    fsdp,
    codons,
    masked,
    segments,
    inward,
    outward,
    expand,
    shrink,
    codon_table,
    norm_params,
    inward_first,
    inward_second,
    outward_first,
    outward_second,
    expand_first,
    expand_second,
    shrink_first,
    shrink_second,
    table_first,
    table_second,
    norm_first,
    norm_second,
):
    layers = inward.shape[0]
    length = codons.shape[0]
    rows = inward.shape[1]
    width = rows * fsdp
    half = width // 2
    fast = fsdp == 16 and rows == 48 and layers > 1
    core, index = lax.axis_index("dp"), lax.axis_index("fsdp")
    bit = lambda b: lax.rem(lax.div(index, b), 2)
    place = jnp.stack([core, bit(1), bit(2), lax.div(index, 4)]).astype(jnp.int32)
    weight = masked.astype(FULL)
    inputs = jnp.where(masked == 1, V - 1, codons)

    norms = norm_params.shape[0] * 2
    small = jnp.concatenate(
        [codon_table.astype(LOW), norm_params.astype(LOW).reshape(norms, rows)], 0
    )
    small = jnp.pad(small.T, ((0, 0), (0, -small.shape[0] % 128)))
    columns = small.shape[1] + layers * 6 * width
    shapes = [(rows, columns)]
    if fast:
        shapes = [(rows, (layers - 1) * 6 * width), (2 * rows + 16, width), (4 * rows, width)]
    weights, *early = call(
        functools.partial(pack_kernel, layers),
        place,
        [(shape, LOW) for shape in shapes],
        [inward, outward, expand, shrink, small],
    )
    weights = lax.all_gather(weights, ("fsdp", "dp"), axis=0, tiled=True)
    weights = weights.reshape(fsdp, 2, rows, -1)
    if not fast:
        columns = [weights[:, :, :, : small.shape[1]]]
        for at in range(small.shape[1], weights.shape[3], 6 * width):
            columns.append(weights[:, :, :, at : at + 4 * width])
            quarter = weights[:, :, :, at + 4 * width : at + 6 * width]
            quarter = quarter.reshape(fsdp, 2, rows, 4, half).transpose(1, 0, 3, 2, 4)
            quarter = quarter.reshape(2, 4, width, half).transpose(0, 2, 1, 3)
            columns.append(quarter.reshape(2, fsdp, rows, 2 * width).transpose(1, 0, 2, 3))
        weights = jnp.concatenate(columns, 3).transpose(1, 0, 2, 3).reshape(1, 2, width, -1)
    hot = (codons[:, None] == jnp.arange(SMALL, dtype=jnp.int32)[None, :]).astype(LOW)
    columns = (hot, jnp.broadcast_to(weight[:, None], (length, SMALL)), segments[:, None])
    mixers, hiddens = [[weights]] * layers, [[weights]] * layers
    if fast:
        first = Gather(place, early[0], (rows + 16, rows), rows)
        last = Gather(place, early[1], (2 * rows, 2 * rows), rows)
        first.along_z()
        first.got, last.shard, columns = tie(first.got, last.shard, columns)
        first.in_plane()
        last.along_z()
        first.near, last.got = tie(first.near, last.got)
        first.forward()
        (first.far,) = tie(first.far)
        own, small = first.result()
        mixers[0] = [own, swap_cores(own)]
        own, last.got = tie(own, last.got)
        last.in_plane()
        small = small[:, :, : rows // 16 * SMALL].reshape(16, 16, rows // 16, SMALL)
        small = small.transpose(0, 2, 1, 3).reshape(width, SMALL).T
    else:
        small = weights[:, 0, :, :SMALL].reshape(width, SMALL).T
    start = -2 * width if fast else weights.shape[3] - layers * 6 * width
    base = lambda l: start + l * 6 * width
    gains = small[V : V + norms].astype(FULL).reshape(-1, 2, width)

    cosine, sine = rotary_tables(length)
    chosen = (inputs[:, None] == jnp.arange(SMALL, dtype=jnp.int32)[None, :]).astype(LOW)
    resid = dot(chosen, small)
    kept = []
    for l in range(layers):
        gain = gains[2 * l : 2 * l + 2]
        middle, query, keys, values, lse, pack = attention_forward(
            place, resid, mixers[l], base(l), gain[0], cosine, sine, (columns[2], segments[None, :])
        )
        if fast and l == 0:
            middle, last.near = tie(middle, last.near)
            last.forward()
        output, pack_mid, hidden = hidden_forward(place, middle, hiddens[l], base(l), gain[1])
        if fast and l == 0:
            output, last.far = tie(output, last.far)
            (own,) = last.result()
            hiddens[-1] = [own, swap_cores(own)]
            output, hiddens[-1][0] = tie(output, own)
        kept.append((resid, query, keys, values, lse, pack, middle, hidden, pack_mid))
        resid = output
    grad, branch, branch_own, branch_other, head_in, grad_logits, grad_norms, sums = head(
        place, resid, small, gains[2 * layers], columns[0], columns[1]
    )
    grad_norms = [grad_norms]
    early = (head_in, grad_logits, chosen)
    early_came = [swap_cores(v) for v in early]
    mid_came = [swap_cores(saved[-1]) for saved in kept]
    pack_came = [swap_cores(saved[5]) for saved in kept]
    grad, branch, mid_came[-1] = tie(grad, branch, mid_came[-1])

    rounds = Rounds(place, rows, width, sums) if fast else PlainRounds()
    whole = lambda array, i=None: (array, i, None, None)
    tile = lambda left, right, other_left, other_right: [
        (0, width, [(left, right), (other_left, other_right)])
    ]
    chunk = []
    for l in reversed(range(layers)):
        resid, query, keys, values, lse, pack, middle, hidden, pack_mid = kept[l]
        gain = gains[2 * l : 2 * l + 2]
        branch_came = swap_cores(branch_other)
        chunk.append(
            [
                [
                    (whole(pack_mid, 1 + t), whole(branch_own)),
                    (whole(mid_came[l], 1 + t), whole(branch_came)),
                ]
                for t in range(4)
            ]
        )
        grad, branch = rounds.step(chunk, grad, branch, split=l == 0)
        grad_middle, gains_mid, up_own, up_other = hidden_back(
            place, grad, branch, middle, hidden, hiddens[l], base(l), gain[1]
        )
        grad_middle, up_own, up_other, early_came = rounds.finish(
            grad_middle, up_own, up_other, early_came
        )
        up_came = swap_cores(up_other)
        if l == 0:
            norms_early = jnp.concatenate([gains_mid] + grad_norms, 0)
            norms_early = (norms_early, swap_cores(norms_early))
        (grad_middle,) = rounds.step(
            [
                [
                    tile(
                        whole(pack_mid, 0), whole(up_own, s), whole(mid_came[l], 0), whole(up_came, s)
                    )
                    for s in range(2)
                ]
            ],
            grad_middle,
        )
        grad, branch, branch_own, branch_other, gains_in, mix_own, mix_other = attention_back(
            place, grad_middle, resid, mixers[l], base(l), gain[0], cosine, sine,
            (columns[2], segments[None, :]),
            query, keys, values, lse,
        )
        grad_norms = [gains_in, gains_mid] + grad_norms
        grad, branch, branch_own, branch_other, mix_own, mix_other, mid_came, pack_came = (
            rounds.finish(
                grad, branch, branch_own, branch_other, mix_own, mix_other, mid_came, pack_came
            )
        )
        mix_came = swap_cores(mix_other)
        products = lambda i, a, b: [
            ((pack, i, None, None), (mix_own, 1, a, b)),
            ((pack_came[l], i, None, None), (mix_came, 1, a, b)),
        ]
        chunk = [
            [
                tile(whole(pack, 0), whole(mix_own, 0), whole(pack_came[l], 0), whole(mix_came, 0)),
                [(0, half, products(0, 0, half)), (half, width, products(1, half, width))],
            ]
        ]
    late = (grad_norms[0], swap_cores(grad_norms[0]))
    branch_came = swap_cores(branch)
    products = [(whole(early[0]), whole(early[1])), (whole(early_came[0]), whole(early_came[1]))]
    products += [(whole(branch), whole(early[2])), (whole(branch_came), whole(early_came[2]))]
    if fast:
        rounds.step(chunk, small=(products, [late, norms_early]), split=True)
        while rounds.left():
            rounds.finish()
            rounds.step([])
        rounds.swap_rest()
        share_small = rounds.small_share
        small_other = swap_cores(share_small)
        totals = rounds.totals
    else:
        rounds.step(chunk)
        table = sum(cross(l[0], r[0]) for l, r in products)
        table = table + jnp.pad(
            jnp.concatenate([a + b for a, b in (late, norms_early)], 0).T,
            ((0, 0), (V, SMALL - V - norms)),
        )
        table = jnp.where(core == 0, table, swap_cores(table))
        share_small = lax.psum_scatter(table, "fsdp", scatter_dimension=0, tiled=True)
        squares = jnp.sum(share_small * share_small) * (core == 0)
        for value in rounds.squares:
            squares = squares + jnp.sum(value)
        totals = sums + jnp.where(jnp.arange(SMALL) == 2, squares, 0.0)[None]
    totals = total_of(totals, fsdp)
    shares = list(zip(rounds.shares, rounds.others)) if fast else rounds.shares
    places = [(2 * (layers - 1 - l), 0 if l == layers - 1 else 1) for l in range(layers)]

    def tiles_at(chunk, pair):
        own, other = (v[pair] for v in shares[chunk])
        ordered = (jnp.where(core == 0, own, other), jnp.where(core == 0, other, own))
        return [v[s] for v in ordered for s in range(2)]

    if not fast:
        share_in, share_out, share_up, share_down = [], [], [], []
        side = lambda *values: jnp.concatenate(values, 1)
        for at, pair in places:
            a_0, b_0, a_1, b_1 = tiles_at(at + 2, 0)
            share_in.append(
                side(
                    a_0[:, :half], a_1[:, :half], a_0[:, half:],
                    a_1[:, half:], b_0[:, :half], b_1[:, :half],
                )
            )
            share_out.append(side(b_0[:, half:], b_1[:, half:]))
            share_up.append(side(*tiles_at(at + 1, 0)))
            a_0, b_0, a_1, b_1 = tiles_at(at, pair)
            share_down.append(
                jnp.concatenate(
                    [
                        side(x[:, j * half : (j + 1) * half], y[:, j * half : (j + 1) * half])
                        for x, y in ((a_0, a_1), (b_0, b_1))
                        for j in range(2)
                    ],
                    0,
                )
            )
        share_in, share_out, share_up, share_down = (
            jnp.stack(v) for v in (share_in, share_out, share_up, share_down)
        )
    masters = (inward, outward, expand, shrink, codon_table, norm_params)
    firsts = (inward_first, outward_first, expand_first, shrink_first, table_first, norm_first)
    seconds = (
        inward_second,
        outward_second,
        expand_second,
        shrink_second,
        table_second,
        norm_second,
    )
    if fast:
        chunks = [((at + 2, 0), (at + 1, 0), (at, pair)) for at, pair in places]
        own, other = zip(*shares)
        states = [v for group in zip(masters, firsts, seconds) for v in group]
        states[12:15] = [v.T for v in states[12:15]]
        grad_norm, *values = optimizer(
            place, totals, (share_small, small_other), chunks, own, other, states
        )
        values[12:15] = [v.T for v in values[12:15]]
    else:
        grad_norm, scale = scale_of(totals)
        share_small = share_small[:, : V + norms].T
        grads = (share_in, share_out, share_up, share_down)
        grads += (share_small[:V], share_small[V:].reshape(-1, 2, rows))
        values = []
        for index, grad in enumerate(grads):
            rate, decay = (RATE_VECTOR, 0.0) if index == 5 else (RATE_MATRIX, DECAY)
            values.extend(
                adam_step(masters[index], grad * scale.reshape(()), firsts[index], seconds[index], rate, decay)
            )
    return (totals[0, 0], totals[0, 1], grad_norm.reshape(()), *values)


def solution(mesh):
    in_specs = (
        P(("fsdp", "dp")),
        P(("fsdp", "dp")),
        P(("fsdp", "dp")),
        P(None, "fsdp", None),
        P(None, "fsdp", None),
        P(None, "fsdp", None),
        P(None, "fsdp", None),
        P(None, "fsdp"),
        P(None, None, "fsdp"),
        P(None, "fsdp", None),
        P(None, "fsdp", None),
        P(None, "fsdp", None),
        P(None, "fsdp", None),
        P(None, "fsdp", None),
        P(None, "fsdp", None),
        P(None, "fsdp", None),
        P(None, "fsdp", None),
        P(None, "fsdp"),
        P(None, "fsdp"),
        P(None, None, "fsdp"),
        P(None, None, "fsdp"),
    )
    out_specs = (
        P(),
        P(),
        P(),
        P(None, "fsdp", None),
        P(None, "fsdp", None),
        P(None, "fsdp", None),
        P(None, "fsdp", None),
        P(None, "fsdp", None),
        P(None, "fsdp", None),
        P(None, "fsdp", None),
        P(None, "fsdp", None),
        P(None, "fsdp", None),
        P(None, "fsdp", None),
        P(None, "fsdp", None),
        P(None, "fsdp", None),
        P(None, "fsdp"),
        P(None, "fsdp"),
        P(None, "fsdp"),
        P(None, None, "fsdp"),
        P(None, None, "fsdp"),
        P(None, None, "fsdp"),
    )
    step = functools.partial(body, mesh.shape["fsdp"])
    return jax.shard_map(step, mesh=mesh, in_specs=in_specs, out_specs=out_specs, check_vma=False)
```

```python
import functools

import jax
import jax.numpy as jnp
from jax import lax
from jax.experimental import pallas as pl
from jax.experimental.pallas import tpu as pltpu
from jax.sharding import PartitionSpec as P

HD = 64
V = 70
STEP = 10


NORM_EPS = 1e-05
BETA_ONE = 0.9
BETA_TWO = 0.95
ADAM_EPS = 1e-08
DECAY = 0.1
RATE_MATRIX = 0.05
RATE_VECTOR = 0.3
CLIP = 0.05


def rotary_tables(length):
    freq = 10000.0 ** (-jnp.arange(HD // 2, dtype=jnp.float32) * 2.0 / HD)
    angle = jnp.arange(length, dtype=jnp.float32)[:, None] * freq[None, :]
    cosine, sine = jnp.cos(angle), jnp.sin(angle)
    return (
        jnp.concatenate([cosine] * 4, 1),
        jnp.concatenate([-sine, sine] * 2, 1),
    )


def normalize(resid, gain, bias):
    mean = jnp.mean(resid, -1, keepdims=True)
    centred = resid - mean
    inverse = lax.rsqrt(jnp.mean(centred * centred, -1, keepdims=True) + NORM_EPS)
    unit = centred * inverse
    return (unit * gain + bias, unit, inverse)


def normalize_back(grad, unit, inverse, gain):
    scaled = grad * gain
    across = (
        scaled
        - jnp.mean(scaled, -1, keepdims=True)
        - unit * jnp.mean(scaled * unit, -1, keepdims=True)
    )
    return (across * inverse, jnp.sum(grad * unit, 0, keepdims=True), jnp.sum(grad, 0, keepdims=True))


def dot(left, right):
    return jnp.dot(left, right, preferred_element_type=jnp.float32)


def dot_nt(left, right):
    return lax.dot_general(
        left, right, (((1,), (1,)), ((), ())), preferred_element_type=jnp.float32
    )


def cross(left, right):
    return lax.dot_general(
        left, right, (((0,), (0,)), ((), ())), preferred_element_type=jnp.float32
    )


VMEM_LIMIT = 56 * 1024 * 1024
LOW, FULL = jnp.bfloat16, jnp.float32
SMALL = 128


class Sent:
    def __init__(self, here, there, sems):
        self.here, self.there, self.sems = here, there, sems
        self.shape, self.at = here.shape, here.at
        self.copies = []

    def __getitem__(self, at):
        return self.here[at]

    def __setitem__(self, at, value):
        self.here[at] = value

    def send(self, index=None):
        here, there = self.here, self.there
        if index is not None:
            here, there = here.at[index], there.at[index]
        copy = pltpu.make_async_copy(here, there, self.sems.at[len(self.copies)])
        copy.start()
        self.copies.append(copy)


def call(kernel, scalars, outs, ins, anys=(), scratch=(), flops=0, sent=(), limit=VMEM_LIMIT):
    whole = pl.BlockSpec(memory_space=pltpu.VMEM)
    left = pl.BlockSpec(memory_space=pl.ANY)

    def body(scalars, *refs):
        refs = list(refs)
        take = lambda n: [refs.pop(0) for _ in range(n)]
        in_refs, any_refs, out_refs = take(len(ins)), take(len(anys)), take(len(outs))
        here = take(len(sent))
        for n, i in enumerate(sent):
            out_refs[i] = Sent(here[n], out_refs[i], refs[-1].at[n])
        kernel(scalars, in_refs, any_refs, out_refs, *(refs[:-1] if sent else refs))
        for i in sent:
            for copy in out_refs[i].copies:
                copy.wait()

    return pl.pallas_call(
        body,
        out_shape=[jax.ShapeDtypeStruct(s, t) for s, t in outs],
        in_specs=[pl.BlockSpec(memory_space=pltpu.SMEM)]
        + [whole] * len(ins)
        + [left] * len(anys),
        out_specs=[left if i in sent else whole for i in range(len(outs))],
        scratch_shapes=[pltpu.VMEM(*outs[i]) for i in sent]
        + list(scratch)
        + [pltpu.SemaphoreType.DMA((len(sent), 5))] * (len(sent) > 0),
        compiler_params=pltpu.CompilerParams(vmem_limit_bytes=limit),
        cost_estimate=pl.CostEstimate(
            flops=flops,
            bytes_accessed=sum(x.size * x.dtype.itemsize for x in list(ins) + list(anys)),
            transcendentals=0,
        ),
    )(scalars, *ins, *anys)


def fetch(sources, targets, sems, first=0):
    copies = [
        pltpu.make_async_copy(s, t, sems.at[first + i])
        for i, (s, t) in enumerate(zip(sources, targets))
    ]
    for c in copies:
        c.start()
    return copies


def tile_of(ref, core, at):
    return ref.at[:, core, :, at : at + ref.shape[0] * ref.shape[2]]


def matrix(ref, place, low=None, high=None):
    value = ref[place] if low is None else ref[place, :, :, low:high]
    return value.reshape(-1, value.shape[-1])


def mixer_tile(anys, cores, place, t, base, width):
    if len(anys) == 2:
        return anys[place].at[t]
    return tile_of(anys[0], cores[place], base + t * width)


def mixer_scratch(weights):
    w = weights[0]
    blocks, rows = (w.shape[1], w.shape[2]) if len(weights) == 2 else (w.shape[0], w.shape[2])
    return [pltpu.VMEM((2, blocks, rows, blocks * rows), LOW)] * 2


def swap_halves(value):
    lane = lax.broadcasted_iota(jnp.int32, value.shape, 1)
    return jnp.where(
        lax.rem(lane, HD) < HD // 2,
        pltpu.roll(value, 128 - HD // 2, 1),
        pltpu.roll(value, HD // 2, 1),
    )


def ordered(first, own, other):
    return jnp.concatenate([jnp.where(first, own, other), jnp.where(first, other, own)], 1)


def head_mask(shape, head):
    lane = lax.broadcasted_iota(jnp.int32, shape, 1)
    return (lane < HD) if head == 0 else (lane >= HD)


def attention_forward_kernel(
    base, place_of, ins, anys, outs, w_a, w_b, mixed, bias, columns_of_lse, sems
):
    resid, seg_col, seg_row, cosine, sine, gains = ins
    middle, query, keys, values, lse, pack = outs
    width = resid.shape[1]
    half = width // 2
    cores = (place_of[0], 1 - place_of[0])
    copies = fetch(
        [mixer_tile(anys, cores, p, t, base, width) for t in range(2) for p in range(2)],
        [w.at[place] for w in (w_a, w_b) for place in range(2)],
        sems,
    )
    first = place_of[0] == 0
    normed, _, _ = normalize(resid[...], gains[0:1], gains[1:2])
    normed_low, attended = pack.at[0], pack.at[1]
    normed_low[...] = normed.astype(LOW)
    bias[...] = jnp.where(seg_col[...] == seg_row[...], 0.0, -1000000000.0)
    for place in range(2):
        copies[place].wait()
        mixed[...] = dot(normed_low[...], matrix(w_a, place))
        for p in range(half // 128):
            for part, target, scale in ((0, query, HD ** (-0.5)), (1, keys, 1.0)):
                x = mixed[:, part * half + p * 128 : part * half + (p + 1) * 128]
                x = x * cosine[...] + swap_halves(x) * sine[...]
                x = (x * scale if scale != 1.0 else x).astype(LOW)
                target[:, place * half + p * 128 : place * half + (p + 1) * 128] = x
    for place in range(2):
        copies[2 + place].wait()
        values[:, place * half : (place + 1) * half] = dot(
            normed_low[...], matrix(w_b, place, 0, half)
        ).astype(LOW)

    columns_of_lse[...] = jnp.zeros_like(columns_of_lse)

    for p in range(width // 128):
        columns = slice(p * 128, (p + 1) * 128)
        q, k, v = query[:, columns], keys[:, columns], values[:, columns]
        out = []
        for head in range(2):
            masked_q = jnp.where(head_mask(q.shape, head), q, jnp.zeros_like(q))
            scores = dot_nt(masked_q, k) + bias[...]
            top = jnp.max(scores, -1, keepdims=True)
            expo = jnp.exp(scores - top)
            total = jnp.sum(expo, -1, keepdims=True)
            probs = (expo * (1.0 / total)).astype(LOW)
            out.append(dot(probs, v))
            lane = lax.broadcasted_iota(jnp.int32, columns_of_lse.shape, 1)
            columns_of_lse[...] = jnp.where(
                lane == 2 * p + head, top + jnp.log(total), columns_of_lse[...]
            )
        attended[:, columns] = jnp.where(head_mask(out[0].shape, 0), out[0], out[1]).astype(LOW)
    lse[...] = columns_of_lse[...].T[: lse.shape[0]]
    attended[...] = ordered(first, attended[:, :half], attended[:, half:])
    out = ordered(
        first,
        dot(attended[...], matrix(w_b, 0, half, width)),
        dot(attended[...], matrix(w_b, 1, half, width)),
    )
    middle[...] = resid[...] + out


def attention_forward(place, resid, weights, base, gains, cosine, sine, segments):
    length, width = resid.shape
    one = (length, width)
    return call(
        functools.partial(attention_forward_kernel, base),
        place,
        [(one, FULL)] + [(one, LOW)] * 3 + [((16, length), FULL), ((2,) + one, LOW)],
        [resid, *segments, cosine, sine, gains],
        weights,
        mixer_scratch(weights)
        + [
            pltpu.VMEM(one, FULL),
            pltpu.VMEM((length, length), FULL),
            pltpu.VMEM((length, 128), FULL),
            pltpu.SemaphoreType.DMA((4,)),
        ],
        8 * length * width * width + 4 * length * length * width,
    )


GELU_SCALE = 0.7978845608028654
GELU_CUBE = 0.044715


def fetch_hidden(anys, base, cores, ups, downs, sems, between=lambda t: None, down_first=False):
    blocks, parts, rows, width = downs.shape
    half, some = width // 2, max(blocks // 4, 1)
    copies = {}

    def up_source(place, within):
        if len(anys) == 2:
            return anys[place].at[2 * within]
        return tile_of(anys[0], cores[place], base + (2 + within) * width)

    def down_source(place, first, j):
        if len(anys) == 2:
            return anys[place].at[1 + j // 2 * 2, pl.ds(first, some), :, j % 2 * half : (j % 2 + 1) * half]
        at = base + 4 * width + j * half
        return anys[0].at[pl.ds(first, some), cores[place], :, at : at + half]

    for t in range(4):
        up = lambda: fetch([up_source(t // 2, t % 2)], [ups.at[t]], sems, t)
        if not down_first:
            copies[0, t] = up()
        if blocks >= 4 or t == 0:
            sources, targets = [], []
            first = (2 * cores[t // 2] + t % 2) * some if blocks >= 4 else 0
            for place in range(2):
                columns = pl.ds(pl.multiple_of(cores[place] * half, 128), half)
                for j in range(4):
                    sources.append(down_source(place, first, j))
                    targets.append(downs.at[pl.ds(t * some, some), j, :, columns])
            copies[1, t] = fetch(sources, targets, sems, 4 + 8 * t)
        between(t)
        if down_first:
            copies[0, t] = up()

    def wait(which, t):
        for copy in copies.pop((which, t), []):
            copy.wait()

    return wait


def rows_of(downs, t, cores):
    blocks, parts, rows, width = downs.shape
    if blocks >= 4:
        some = blocks // 4
        return downs[t * some : (t + 1) * some].reshape(some * parts * rows, width)
    return downs[0, 2 * cores[t // 2] + t % 2]


def hidden_scratch(weights):
    w = weights[0]
    blocks, rows = (w.shape[1], w.shape[2]) if len(weights) == 2 else (w.shape[0], w.shape[2])
    return [
        pltpu.VMEM((4, blocks, rows, blocks * rows), LOW),
        pltpu.VMEM((blocks, 4, rows, blocks * rows), LOW),
        pltpu.SemaphoreType.DMA((36,)),
    ]


def hidden_forward_kernel(base, place_of, ins, anys, outs, ups, downs, sems):
    middle, gains = ins
    output, pack, hidden = outs
    cores = (place_of[0], 1 - place_of[0])
    wait = fetch_hidden(anys, base, cores, ups, downs, sems)
    normed, _, _ = normalize(middle[...], gains[0:1], gains[1:2])
    pack[0] = normed.astype(LOW)
    pack.send(0)
    for t in range(4):
        wait(0, t)
        index = 2 * cores[t // 2] + t % 2
        x = dot(pack[0], matrix(ups, t))
        hidden[index] = x
        hidden.send(index)
        inner = jnp.tanh(x * (GELU_SCALE + (GELU_SCALE * GELU_CUBE) * (x * x)))
        value = x * 0.5
        value = (value + value * inner).astype(LOW)
        pack[1 + index] = value
        pack.send(1 + index)
        wait(1, t)
        product = dot(value, rows_of(downs, t, cores))
        output[...] = (middle[...] if t == 0 else output[...]) + product


def hidden_forward(place, middle, weights, base, gains):
    length, width = middle.shape
    one = (length, width)
    return call(
        functools.partial(hidden_forward_kernel, base),
        place,
        [(one, FULL), ((5,) + one, LOW), ((4,) + one, FULL)],
        [middle, gains],
        weights,
        hidden_scratch(weights),
        16 * length * width * width,
        sent=(1, 2),
    )


def hidden_back_kernel(base, place_of, ins, anys, outs, ups, downs, sems, hidden_here, total, own_sems):
    branch, grad, middle, gains = ins
    hidden, *weights = anys
    grad_middle, grad_gains, grad_own, grad_other = outs
    cores = (place_of[0], 1 - place_of[0])
    copies = []

    def fetch_values(t):
        source = hidden.at[2 * cores[t // 2] + t % 2]
        copies.extend(fetch([source], [hidden_here.at[t]], own_sems, t))

    wait = fetch_hidden(weights, base, cores, ups, downs, sems, fetch_values, down_first=True)
    for t in range(4):
        wait(1, t)
        grad_active = dot_nt(branch[...], rows_of(downs, t, cores))
        copies[t].wait()
        x = hidden_here[t]
        square = x * x
        inner = jnp.tanh(x * (GELU_SCALE + (GELU_SCALE * GELU_CUBE) * square))
        slope = x * (GELU_SCALE + (3.0 * GELU_SCALE * GELU_CUBE) * square)
        slope = (0.5 + 0.5 * inner) * (1.0 + slope * (1.0 - inner))
        value = (grad_active * slope).astype(LOW)
        (grad_own if t < 2 else grad_other)[t % 2] = value
        wait(0, t)
        product = dot_nt(value, matrix(ups, t))
        total[...] = product if t == 0 else total[...] + product
    _, unit, inverse = normalize(middle[...], gains[0:1], gains[1:2])
    back, gain, bias = normalize_back(total[...], unit, inverse, gains[0:1])
    grad_middle[...] = grad[...] + back
    grad_gains[0:1] = gain
    grad_gains[1:2] = bias


def hidden_back(place, grad, branch, middle, hidden, weights, base, gains):
    length, width = middle.shape
    one = (length, width)
    return call(
        functools.partial(hidden_back_kernel, base),
        place,
        [(one, FULL), ((2, width), FULL), ((2,) + one, LOW), ((2,) + one, LOW)],
        [branch, grad, middle, gains],
        [hidden] + weights,
        hidden_scratch(weights)
        + [
            pltpu.VMEM((4,) + one, FULL),
            pltpu.VMEM(one, FULL),
            pltpu.SemaphoreType.DMA((4,)),
        ],
        16 * length * width * width,
    )


def attention_back_kernel(base, place_of, ins, anys, outs, w_a, w_b, bias, ga, gq, gk, gv, sems):
    grad_middle, query, keys, values, lse, seg_col, seg_row, cosine, sine, gains, resid = ins
    grad, branch, branch_own, branch_other, grad_gains, grad_own, grad_other = outs
    width = resid.shape[1]
    half = width // 2
    cores = (place_of[0], 1 - place_of[0])
    copies = fetch(
        [mixer_tile(anys, cores, p, t, base, width) for t in (1, 0) for p in range(2)],
        [w.at[place] for w in (w_b, w_a) for place in range(2)],
        sems,
    )
    first = place_of[0] == 0
    grads = (grad_own, grad_other)
    bias[...] = jnp.where(seg_col[...] == seg_row[...], 0.0, -1000000000.0)
    attn_grad = grad_middle[...].astype(LOW)
    left, right = attn_grad[:, :half], attn_grad[:, half:]
    grad_own[1, :, half:] = jnp.where(first, left, right)
    grad_other[1, :, half:] = jnp.where(first, right, left)
    copies[0].wait()
    copies[1].wait()
    natural = dot_nt(grad_own[1, :, half:], matrix(w_b, 0, half, width)) + dot_nt(
        grad_other[1, :, half:], matrix(w_b, 1, half, width)
    )
    natural = natural.astype(LOW)
    ga[:, :half] = jnp.where(first, natural[:, :half], natural[:, half:])
    ga[:, half:] = jnp.where(first, natural[:, half:], natural[:, :half])

    for p in range(width // 128):
        columns = slice(p * 128, (p + 1) * 128)
        q, k, v, g = query[:, columns], keys[:, columns], values[:, columns], ga[:, columns]
        flipped = k.T
        out_q, out_k, out_v = [], [], []
        for head in range(2):
            mask = head_mask(q.shape, head)
            zero = jnp.zeros_like(q)
            scores = dot_nt(k, jnp.where(mask, q, zero)) + bias[...]
            probs = jnp.exp(scores - lse[2 * p + head : 2 * p + head + 1, :])
            grad_probs = dot_nt(v, jnp.where(mask, g, zero))
            across = jnp.sum(probs * grad_probs, 0, keepdims=True)
            grad_scores = (probs * (grad_probs - across)).astype(LOW)
            out_k.append(dot(grad_scores, q))
            out_q.append(dot(flipped[head * HD : (head + 1) * HD], grad_scores))
            out_v.append(dot(probs.astype(LOW), g))
        out_q = jnp.concatenate(out_q, 0).T * HD ** (-0.5)
        out_k = jnp.where(head_mask(out_k[0].shape, 0), out_k[0], out_k[1])
        for x, target in ((out_q, gq), (out_k, gk)):
            x = x * cosine[...] - swap_halves(x) * sine[...]
            target[:, columns] = x.astype(LOW)
        gv[:, columns] = jnp.where(head_mask(out_v[0].shape, 0), out_v[0], out_v[1]).astype(LOW)
    for place in (1, 0):
        columns = slice(place * half, (place + 1) * half)
        grads[place][0, :, :half] = gq[:, columns]
        grads[place][0, :, half:] = gk[:, columns]
        grads[place][1, :, :half] = gv[:, columns]
    copies[2].wait()
    copies[3].wait()
    total = dot_nt(grad_own[0], matrix(w_a, 0)) + dot_nt(grad_other[0], matrix(w_a, 1))
    total = total + dot_nt(grad_own[1, :, :half], matrix(w_b, 0, 0, half))
    total = total + dot_nt(grad_other[1, :, :half], matrix(w_b, 1, 0, half))
    _, unit, inverse = normalize(resid[...], gains[0:1], gains[1:2])
    back, gain, bias_grad = normalize_back(total, unit, inverse, gains[0:1])
    back = grad_middle[...] + back
    grad[...] = back
    back = back.astype(LOW)
    branch[...] = back
    branch_own[...] = jnp.where(first, back[:, :half], back[:, half:])
    branch_other[...] = jnp.where(first, back[:, half:], back[:, :half])
    grad_gains[0:1] = gain
    grad_gains[1:2] = bias_grad


def attention_back(place, grad_middle, resid, weights, base, gains, cosine, sine, segments, query, keys, values, lse):
    length, width = resid.shape
    one = (length, width)
    return call(
        functools.partial(attention_back_kernel, base),
        place,
        [(one, FULL), (one, LOW)]
        + [((length, width // 2), LOW)] * 2
        + [((2, width), FULL)]
        + [((2,) + one, LOW)] * 2,
        [grad_middle, query, keys, values, lse]
        + [*segments, cosine, sine, gains, resid],
        weights,
        mixer_scratch(weights)
        + [
            pltpu.VMEM((length, length), FULL),
        ]
        + [pltpu.VMEM(one, LOW)] * 4
        + [pltpu.SemaphoreType.DMA((4,))],
        8 * length * width * width + 10 * length * length * width,
    )


def head_kernel(place_of, ins, anys, outs):
    resid, table, gains, hot, weight = ins
    grad, branch, branch_own, branch_other, head_in, grad_logits, grad_gains, sums = outs
    half = resid.shape[1] // 2
    normed, unit, inverse = normalize(resid[...], gains[0:1], gains[1:2])
    head_in[...] = normed.astype(LOW)
    logits = dot_nt(head_in[...], table[...])
    lane = lax.broadcasted_iota(jnp.int32, logits.shape, 1)
    logits = jnp.where(lane < V, logits, -1e30)
    top = jnp.max(logits, 1, keepdims=True)
    lse = top + jnp.log(jnp.sum(jnp.exp(logits - top), 1, keepdims=True))
    hot = hot[...].astype(FULL)
    weight = weight[:, 0:1]
    picked = jnp.sum(logits * hot, 1, keepdims=True)
    loss = jnp.sum((lse - picked) * weight, 0, keepdims=True)
    count = jnp.sum(weight, 0, keepdims=True)
    lane = lax.broadcasted_iota(jnp.int32, sums.shape, 1)
    sums[...] = jnp.where(lane == 0, loss, jnp.where(lane == 1, count, 0.0))
    grad_logits[...] = ((jnp.exp(logits - lse) - hot) * weight).astype(LOW)
    back, gain, bias = normalize_back(
        dot(grad_logits[...], table[...]), unit, inverse, gains[0:1]
    )
    grad[...] = back
    back = back.astype(LOW)
    branch[...] = back
    first = place_of[0] == 0
    branch_own[...] = jnp.where(first, back[:, :half], back[:, half:])
    branch_other[...] = jnp.where(first, back[:, half:], back[:, :half])
    grad_gains[0:1] = gain
    grad_gains[1:2] = bias


def head(place, resid, table, gains, hot, weight):
    length, width = resid.shape
    one, part = (length, width), (length, width // 2)
    return call(
        head_kernel,
        place,
        [(one, FULL), (one, LOW), (part, LOW), (part, LOW), (one, LOW)]
        + [((length, SMALL), LOW), ((2, width), FULL), ((1, SMALL), FULL)],
        [resid, table, gains, hot, weight],
        flops=4 * length * width * SMALL,
    )


def adam_step(master, grad, first, second, rate, decay):
    first = BETA_ONE * first + (1.0 - BETA_ONE) * grad
    second = BETA_TWO * second + (1.0 - BETA_TWO) * grad * grad
    fix_one = 1.0 / (1.0 - BETA_ONE**STEP)
    fix_two = 1.0 / (1.0 - BETA_TWO**STEP)
    update = first * fix_one / (jnp.sqrt(second * fix_two) + ADAM_EPS) + decay * master
    return (master - rate * update, first, second)


def scale_of(totals):
    count = totals[0:1, 1:2]
    grad_norm = jnp.sqrt(totals[0:1, 2:3]) / count
    return grad_norm, CLIP / jnp.maximum(grad_norm, CLIP) / count


def optimizer_kernel(chunks, place_of, ins, anys, outs, *scratch):
    *masters, sems = scratch
    copies = fetch(anys, masters, sems)
    totals, small_own, small_other, *rest = ins
    n = (len(rest) - 6) // 2
    own, other = rest[:n], rest[n : 2 * n]
    masters += rest[2 * n :]
    layers = len(chunks)
    first = place_of[0] == 0
    grad_norm, scale = scale_of(totals[...])
    outs[0][...] = grad_norm

    def step(which, at, grad, rate=RATE_MATRIX, decay=DECAY):
        master, moment, square = (masters[3 * which + i][at] for i in range(3))
        values = adam_step(master, grad * scale, moment, square, rate, decay)
        for i in range(3):
            outs[1 + 3 * which + i][at] = values[i]

    def tile(where, s, core):
        a, b = own[where[0]][where[1], s], other[where[0]][where[1], s]
        return jnp.where(first, a, b) if core == 0 else jnp.where(first, b, a)

    def arrive(*which):
        for copy in copies[3 * which[0] : 3 * which[-1] + 3]:
            copy.wait()

    def leave(which):
        for i in range(3):
            outs[1 + 3 * which + i].send()

    rows, width = own[0].shape[-2:]
    half = width // 2
    arrive(0, 1)
    for l in range(layers):
        for core in range(2):
            columns = lambda p: pl.ds(p * width + core * half, half)
            value = tile(chunks[l][0], 0, core)
            step(0, (l, slice(None), columns(0)), value[:, :half])
            step(0, (l, slice(None), columns(1)), value[:, half:])
            value = tile(chunks[l][0], 1, core)
            step(0, (l, slice(None), columns(2)), value[:, :half])
            step(1, (l, slice(None), columns(0)), value[:, half:])
    leave(0)
    leave(1)
    arrive(2)
    for l in range(layers):
        for core in range(2):
            for s in range(2):
                at = (l, slice(None), pl.ds((2 * core + s) * width, width))
                step(2, at, tile(chunks[l][1], s, core))
    leave(2)
    arrive(3)
    for l in range(layers):
        for core in range(2):
            for s in range(2):
                value = tile(chunks[l][2], s, core)
                for j in range(2):
                    at = (l, pl.ds((2 * s + j) * rows, rows), pl.ds(core * half, half))
                    step(3, at, value[:, j * half : (j + 1) * half])
    leave(3)
    small = jnp.where(first, small_own[...], small_other[...])
    step(4, (slice(None), slice(None)), small[:, :V])
    small = small.T
    for n in range(masters[15].shape[0]):
        step(5, n, small[V + 2 * n : V + 2 * n + 2], RATE_VECTOR, 0.0)


def optimizer(place, totals, small, chunks, own, other, masters):
    return call(
        functools.partial(optimizer_kernel, chunks),
        place,
        [((1, 1), FULL)] + [(m.shape, m.dtype) for m in masters],
        [totals, *small, *own, *other, *masters[12:]],
        masters[:12],
        [pltpu.VMEM(m.shape, m.dtype) for m in masters[:12]] + [pltpu.SemaphoreType.DMA((12,))],
        flops=20 * sum(m.size for m in masters),
        sent=range(1, 13),
    )


def pack_kernel(layers, place_of, ins, anys, outs):
    inward, outward, expand, shrink, small = ins
    out, *early = outs
    first = place_of[0] == 0
    rows = inward.shape[1]
    width = inward.shape[2] // 3
    half = width // 2
    at = 0
    if early:
        early[0][rows : rows + 16] = jnp.zeros((16, width), LOW)
        for q in range(rows // 16):
            early[0][rows : rows + 16, q * SMALL : (q + 1) * SMALL] = small[q * 16 : (q + 1) * 16]
    else:
        at = small.shape[1]
        out[:, :at] = small[...]
    for l in range(layers):
        sources = [inward[l, :, p * width : (p + 1) * width] for p in range(3)] + [outward[l]]
        sources.append(expand[l])
        sources += [shrink[l, j * rows : (j + 1) * rows] for j in range(shrink.shape[1] // rows)]
        for n, value in enumerate(sources):
            part = value.shape[1] // 2
            value = jnp.where(first, value[:, :part], value[:, part:]).astype(LOW)
            if early and l == 0 and n < 4:
                start = 0 if n < 2 else rows + 16
                early[0][start : start + rows, (n % 2) * half : (n % 2 + 1) * half] = value
            elif early and l == layers - 1 and n == 4:
                for t in range(2):
                    early[1][2 * t * rows : (2 * t + 1) * rows] = value[:, t * width : (t + 1) * width]
            elif early and l == layers - 1 and n > 4:
                start = (2 * ((n - 5) // 2) + 1) * rows
                lanes = (n - 5) % 2 * half
                early[1][start : start + rows, lanes : lanes + half] = value
            else:
                out[:, at : at + part] = value
                at += part


def swap_cores(value):
    return lax.ppermute(value, "dp", [(0, 1), (1, 0)])


def across(value, mask, size):
    return lax.ppermute(value, "fsdp", [(i, i ^ mask) for i in range(size)])


def tie(*values):
    return lax.optimization_barrier(values)


def total_of(value, size):
    value = value + swap_cores(value)
    bit = 1
    while bit < size:
        if 2 * bit < size:
            a, b, c = (across(value, m * bit, size) for m in (1, 2, 3))
            value = (value + a) + (b + c)
        else:
            value = value + across(value, bit, size)
        bit *= 4
    return value


def arrange_kernel(parts, place_of, ins, anys, outs, sems):
    copies, at = [], 0
    for h in range(2):
        for piece in anys:
            copies += fetch(
                [piece.at[h * parts[0] : h * parts[0] + parts[h]]],
                [outs[0].at[at : at + parts[h]]],
                sems,
                len(copies),
            )
            at += parts[h]
    for copy in copies:
        copy.wait()


def place_kernel(parts, rows, place_of, ins, anys, outs, sems):
    quarter, from_x, from_y, far_a, far_b = anys
    tiles, *small = outs
    count = tiles.shape[0] // 2
    x, y, z = place_of[1], place_of[2], place_of[3]
    for n in range(16):
        xor_z, xor_y, xor_x = n // 4, n // 2 % 2, n % 2
        index = jnp.bitwise_xor(z, xor_z) * 4 + jnp.bitwise_xor(y, xor_y) * 2 + jnp.bitwise_xor(x, xor_x)
        for h in range(2):
            at = xor_z * parts[h]
            if xor_x and xor_y:
                source = (far_a, far_b)[h]
            else:
                source = from_x if xor_x else from_y if xor_y else quarter
                at += h * 4 * parts[0]
            for t in range(count):
                here = source.at[at + t * rows : at + (t + 1) * rows]
                fetch([here], [tiles.at[h * count + t, index]], sems, h * count + t)
            if h == 0 and small:
                here = source.at[at + count * rows : at + parts[0]]
                fetch([here], [small[0].at[index]], sems, 2 * count)
    targets = [tiles.at[t] for t in range(2 * count)] + small
    for n, target in enumerate(targets):
        pltpu.make_async_copy(target, target, sems.at[n]).wait()
        if n < 2 * count:
            tiles.send(n)


class Gather:
    def __init__(self, place, shard, parts, rows):
        self.place, self.shard, self.parts, self.rows = place, shard, parts, rows

    def along_z(self):
        self.got = [across(self.shard, mask, 16) for mask in Z]

    def in_plane(self):
        width = self.shard.shape[1]
        (quarter,) = call(
            functools.partial(arrange_kernel, self.parts),
            self.place,
            [((4 * sum(self.parts), width), LOW)],
            [],
            [self.shard] + self.got,
            [pltpu.SemaphoreType.DMA((8,))],
        )
        self.quarter, self.near = quarter, [across(quarter, X, 16), across(quarter, Y, 16)]

    def forward(self):
        cut = 4 * self.parts[0]
        from_x, from_y = self.near
        self.far = [across(from_y[:cut], X, 16), across(from_x[cut:], Y, 16)]

    def result(self):
        width = self.shard.shape[1]
        count, more = divmod(self.parts[0], self.rows)
        outs = [((2 * count, 16, self.rows, width), LOW)]
        if more:
            outs.append(((16, more, width), LOW))
        return call(
            functools.partial(place_kernel, self.parts, self.rows),
            self.place,
            outs,
            [],
            [self.quarter] + self.near + self.far,
            [pltpu.SemaphoreType.DMA((2 * count + 1,))],
            sent=(0,),
        )


X, Y = 1, 2
Z = (4, 8, 12)


def round_kernel(jobs, small_job, n_ins, counts, smalls, last, split, place_of, ins, anys, outs, *scratch):
    new, once, twice, done = counts
    small_new, small_once, small_twice, small_done = smalls
    rest = list(ins[n_ins:]) + list(outs) + list(scratch)
    pop = lambda present, n=1: [rest.pop(0) for _ in range(n)] if present else [None] * n
    (keep_once,), (small_keep_once,) = pop(once), pop(small_once)
    (keep_twice,), (small_keep_twice,) = pop(twice), pop(small_twice)
    from_x, from_y = pop(once or twice, 2)
    again_x, again_y = pop(split and twice, 2)
    (keep_done,), (small_keep_done,) = pop(done), pop(small_done)
    from_z = pop(done, 3)
    (squares_in,), (sums,) = pop(done), pop(last)
    to_x, to_y = pop(new or once, 2)
    (out_once,), (small_out_once,) = pop(new), pop(small_new)
    (out_twice,), (small_out_twice,) = pop(once), pop(small_once)
    (out_done,), (small_out_done,) = pop(twice), pop(small_twice)
    to_z = pop(twice, 3)
    (share,), (small_share,), (squares,) = pop(done), pop(small_done), pop(done)
    (totals,) = pop(last)
    (tile,), (unit,), (small_tile,), (flat,) = pop(new), pop(new), pop(small_new), pop(small_new)
    rows = (out_once if new else out_twice if once else out_done if twice else share).shape[-2]
    rows = rows // (8 if new else 4 if once else 1)
    bits, z = (place_of[1], place_of[2]), place_of[3]
    to, came = (to_x, to_y), (from_x, from_y)
    again, behind = (came, once * 8)
    if split:
        again, behind = (again_x, again_y), 0

    def block(index, size=rows):
        if isinstance(index, int):
            return pl.ds(index * size, size)
        return pl.ds(pl.multiple_of(index * size, 16), size)

    def factor(spec):
        which, index, low, high = spec
        ref = ins[which] if index is None else ins[which].at[index]
        return ref[...] if low is None else ref[:, low:high]

    def put_small(ref, start, group, side, value):
        for q in range(rows // 16):
            lanes = side * (rows // 16) + q
            ref[pl.ds(start + group * 16, 16), lanes * SMALL : (lanes + 1) * SMALL] = value[
                q * 16 : (q + 1) * 16
            ].astype(LOW)

    def take_small(ref, start, group, side):
        parts = []
        for q in range(rows // 16):
            lanes = side * (rows // 16) + q
            at = pl.ds(pl.multiple_of(start + group * 16, 16), 16)
            parts.append(ref[at, lanes * SMALL : (lanes + 1) * SMALL])
        return jnp.concatenate(parts, 0).astype(FULL)

    def summed(products):
        total = None
        for left, right in products:
            product = cross(factor(left), factor(right))
            total = product if total is None else total + product
        return total

    for p in range(new):
        if len(jobs[p]) == 4:
            for quarter, products in enumerate(jobs[p]):
                unit[...] = summed(products)
                half = unit.shape[1]
                for index in range(4):
                    for s in range(2):
                        for j in range(2):
                            tile[s, block(quarter * 4 + index), j * half : (j + 1) * half] = unit[
                                block(index * 4 + 2 * s + j), :
                            ]
        else:
            for s in range(2):
                for low, high, products in jobs[p][s]:
                    tile[s, :, low:high] = summed(products)
        for s in range(2):
            for zz in range(4):
                for other in range(2):
                    at = zz * 2 + other
                    index = lambda bit: zz * 4 + (other * 2 + bit if s == 0 else bit * 2 + other)
                    to[s][block(p * 8 + at), :] = tile[s, block(index(1 - bits[s])), :].astype(LOW)
                    out_once[p, s, block(at), :] = tile[s, block(index(bits[s])), :]
            out_once.send((p, s))
    if small_new:
        products, norms_at = small_job
        flat[...] = summed([(right, left) for left, right in products])
        at = V
        for mine, theirs in norms_at:
            count = ins[mine].shape[0]
            flat[at : at + count] += ins[mine][...] + ins[theirs][...]
            at += count
        total = flat[...].T
        small_tile[...] = total
        for zz in range(4):
            for other in range(2):
                index = lambda bit: zz * 4 + other * 2 + bit
                send = small_tile[block(index(1 - bits[0])), :]
                put_small(to_x, (new * 8 + once * 4) * rows, other * 2 + zz // 2, zz % 2, send)
                small_out_once[block(zz * 2 + other), :] = small_tile[block(index(bits[0])), :]
    for p in range(once):
        for s in range(2):
            for zz in range(4):
                for bit in range(2):
                    at = zz * 2 + (bits[1 - s] if bit else 1 - bits[1 - s])
                    value = keep_once[p, s, block(at), :] + came[s][block(p * 8 + at), :].astype(FULL)
                    if bit:
                        out_twice[p, s, block(zz), :] = value
                    else:
                        to[1 - s][block(new * 8 + p * 4 + zz), :] = value.astype(LOW)
    if small_once:
        start = (once * 8 + (0 if split else twice * 4)) * rows
        for zz in range(4):
            for bit in range(2):
                other = bits[1] if bit else 1 - bits[1]
                value = small_keep_once[block(zz * 2 + other), :]
                value = value + take_small(from_x, start, other * 2 + zz // 2, zz % 2)
                if bit:
                    small_out_twice[block(zz), :] = value
                else:
                    put_small(to_y, (new * 8 + once * 4) * rows, zz, 0, value)
    for p in range(twice):
        for s in range(2):
            for xor in range(4):
                at = jnp.bitwise_xor(z, xor)
                value = keep_twice[p, s, block(at), :] + again[1 - s][
                    block(behind + p * 4 + at), :
                ].astype(FULL)
                if xor == 0:
                    out_done[p, s] = value
                else:
                    to_z[xor - 1][block(2 * p + s), :] = value.astype(LOW)
    if small_twice:
        for xor in range(4):
            at = jnp.bitwise_xor(z, xor)
            value = small_keep_twice[block(at), :]
            value = value + take_small(from_y, (once * 8 + twice * 4) * rows, at, 0)
            if xor == 0:
                small_out_done[...] = value
            else:
                put_small(to_z[xor - 1], twice * 2 * rows, 0, 0, value)
    if done:
        squares[...] = squares_in[...]
    for p in range(done):
        for s in range(2):
            value = keep_done[p, s]
            for f in from_z:
                value = value + f[block(2 * p + s), :].astype(FULL)
            share[p, s] = value
            squares[...] += jnp.sum(value * value, 0, keepdims=True)
    if small_done:
        value = small_keep_done[...]
        for f in from_z:
            value = value + take_small(f, done * 2 * rows, 0, 0)
        small_share[...] = value
    if last:
        total = jnp.sum(squares[...], 1, keepdims=True)
        if small_done:
            square = jnp.sum(jnp.sum(value * value, 0, keepdims=True), 1, keepdims=True)
            total = total + jnp.where(place_of[0] == 0, square, jnp.zeros_like(square))
        lane = lax.broadcasted_iota(jnp.int32, sums.shape, 1)
        totals[...] = jnp.where(lane == 2, total, sums[...])


class Rounds:
    def __init__(self, place, rows, width, sums):
        self.place, self.rows, self.width, self.sums = place, rows, width, sums
        self.counts, self.smalls = (0,) * 4, (False,) * 4
        self.kept, self.small_kept = [None] * 3, [None] * 3
        self.came = self.came_z = self.totals = self.again = None
        self.shares, self.others, self.small_share = [], [], None
        self.squares = jnp.zeros((1, width), FULL)
        self.flying, self.swapping = [], 0

    def run(self, chunk, small, counts, smalls, limit):
        rows, width = self.rows, self.width
        new, once, twice, done = counts
        last = not (new or once or twice)
        split = self.again is not None
        arrays, jobs = [], []

        def number(spec):
            array, *place = spec
            for i, known in enumerate(arrays):
                if known is array:
                    return (i, *place)
            arrays.append(array)
            return (len(arrays) - 1, *place)

        numbered = lambda products: [(number(l), number(r)) for l, r in products]
        for pair in chunk:
            if len(pair) == 4:
                jobs.append([numbered(products) for products in pair])
            else:
                jobs.append([[(a, b, numbered(ps)) for a, b, ps in tile] for tile in pair])
        small_job = None
        if small is not None:
            small_job = (
                [(number(l), number(r)) for l, r in small[0]],
                [(number((a,))[0], number((b,))[0]) for a, b in small[1]],
            )
        ins = list(arrays)
        for stage in range(2):
            ins += [self.kept[stage]] * (counts[1 + stage] > 0)
            ins += [self.small_kept[stage]] * smalls[1 + stage]
        if once or twice:
            ins += self.came
        if split and twice:
            ins += self.again
        if done:
            ins += [self.kept[2]] + [self.small_kept[2]] * smalls[3] + self.came_z + [self.squares]
        ins += [self.sums] * last
        outs = []
        if new or once:
            for added in (64 * smalls[0], 64 * smalls[1]):
                outs.append((((new * 8 + once * 4) * rows + added, width), LOW))
        for stage, blocks in enumerate((8, 4, 1)):
            if counts[stage]:
                outs.append(((counts[stage], 2, blocks * rows, width), FULL))
            if smalls[stage]:
                outs.append(((blocks * rows, SMALL), FULL))
        if twice:
            outs += [((twice * 2 * rows + 16 * smalls[2], width), LOW)] * 3
        if done:
            outs.append(((done, 2, rows, width), FULL))
            outs += [((rows, SMALL), FULL)] * smalls[3]
            outs.append(((1, width), FULL))
        outs += [((1, SMALL), FULL)] * last
        length = 2 * arrays[0].shape[-2] if new else 0
        scratch = []
        if new:
            scratch.append(pltpu.VMEM((2, 16 * rows, width), FULL))
            scratch.append(pltpu.VMEM((16 * rows, width // 2), FULL))
        if smalls[0]:
            scratch.append(pltpu.VMEM((16 * rows, SMALL), FULL))
            scratch.append(pltpu.VMEM((SMALL, width), FULL))
        got = list(
            call(
                functools.partial(
                    round_kernel, jobs, small_job, len(arrays), counts, smalls, last, split
                ),
                self.place,
                outs,
                ins,
                [],
                scratch,
                4 * new * length * width * width,
                sent=(2,) if new else (),
                limit=limit,
            )
        )
        if last:
            self.totals = got.pop()
        if done:
            self.squares = got.pop()
            if smalls[3]:
                self.small_share = got.pop()
            self.shares.append(got.pop())
        to = [got.pop(0) for _ in range(2)] if new or once else []
        kept, small_kept = [None] * 3, [None] * 3
        for stage in range(3):
            if counts[stage]:
                kept[stage] = got.pop(0)
            if smalls[stage]:
                small_kept[stage] = got.pop(0)
        return to, kept, small_kept, got

    def step(self, chunk, *ties, small=None, split=False):
        counts = (len(chunk),) + self.counts[:3]
        smalls = (small is not None,) + self.smalls[:3]
        again = None
        plane = lambda to: [across(v, mask, 16) for v, mask in zip(to, (X, Y))]
        line = lambda to: [across(v, mask, 16) for v, mask in zip(to, Z)]
        if split:
            to, kept, small_kept, to_z = self.run(
                [], None, (0,) + counts[1:], (False,) + smalls[1:], VMEM_LIMIT
            )
            again, along_z = plane(to), line(to_z)
            to, new_kept, new_small, _ = self.run(
                chunk, small, (counts[0], 0, 0, 0), (smalls[0],) + (False,) * 3, VMEM_LIMIT
            )
            kept[0], small_kept[0] = new_kept[0], new_small[0]
            again, to, kept, small_kept, ties, self.shares = tie(
                again, to, kept, small_kept, ties, self.shares
            )
            self.flying = plane(to) + along_z
        else:
            limit = VMEM_LIMIT if chunk else 24 << 20
            to, kept, small_kept, to_z = self.run(chunk, small, counts, smalls, limit)
            if any(counts[:3]):
                to, kept, small_kept, to_z, ties, self.shares = tie(
                    to, kept, small_kept, to_z, ties, self.shares
                )
            self.flying = plane(to) + line(to_z)
        self.again = again
        self.counts, self.smalls = counts, smalls
        self.kept, self.small_kept = kept, small_kept
        if not any(counts[:3]):
            return ties
        self.swapping = 0
        while len(self.flying) < 5 and len(self.others) + self.swapping < len(self.shares):
            self.flying.append(swap_cores(self.shares[len(self.others) + self.swapping]))
            self.swapping += 1
        return ties

    def finish(self, *ties):
        flying, ties = tie(self.flying, ties)
        self.came = self.came_z = None
        if self.counts[0] or self.counts[1]:
            self.came, flying = flying[:2], flying[2:]
        if self.counts[2]:
            self.came_z, flying = flying[:3], flying[3:]
        self.others += flying
        return ties

    def left(self):
        return any(self.counts[:3])

    def swap_rest(self):
        self.others += [swap_cores(v) for v in self.shares[len(self.others) :]]


class PlainRounds:
    def __init__(self):
        self.shares, self.squares = [], []

    def step(self, chunk, *ties, split=False):
        def factor(spec):
            array, index, low, high = spec
            array = array if index is None else array[index]
            return array if low is None else array[:, low:high]

        summed = lambda products: sum(cross(factor(l), factor(r)) for l, r in products)
        scatter = lambda v: lax.psum_scatter(v, "fsdp", scatter_dimension=0, tiled=True)
        shares = []
        for pair in chunk:
            if len(pair) == 4:
                v = scatter(jnp.concatenate([summed(products) for products in pair], 0))
                v = v.reshape(2, 2, -1, v.shape[1])
                shares.append(jnp.concatenate([v[:, 0], v[:, 1]], 2))
            else:
                tiles = [jnp.concatenate([summed(ps) for _, _, ps in t], 1) for t in pair]
                shares.append(jnp.stack([scatter(t) for t in tiles]))
        share = jnp.stack(shares)
        self.shares.append((share, swap_cores(share)))
        self.squares.append(jnp.sum(share * share, (0, 1, 2))[None])
        return ties

    def finish(self, *ties):
        return ties

    def left(self):
        return False


def half_of(value, core):
    half = value.shape[1] // 2
    return lax.dynamic_slice_in_dim(value, core * half, half, 1)


def body(
    fsdp,
    codons,
    masked,
    segments,
    inward,
    outward,
    expand,
    shrink,
    codon_table,
    norm_params,
    inward_first,
    inward_second,
    outward_first,
    outward_second,
    expand_first,
    expand_second,
    shrink_first,
    shrink_second,
    table_first,
    table_second,
    norm_first,
    norm_second,
):
    layers = inward.shape[0]
    length = codons.shape[0]
    rows = inward.shape[1]
    width = rows * fsdp
    half = width // 2
    fast = fsdp == 16 and rows == 48 and layers > 1
    core, index = lax.axis_index("dp"), lax.axis_index("fsdp")
    bit = lambda b: lax.rem(lax.div(index, b), 2)
    place = jnp.stack([core, bit(1), bit(2), lax.div(index, 4)]).astype(jnp.int32)
    weight = masked.astype(FULL)
    inputs = jnp.where(masked == 1, V - 1, codons)

    norms = norm_params.shape[0] * 2
    small = jnp.concatenate(
        [codon_table.astype(LOW), norm_params.astype(LOW).reshape(norms, rows)], 0
    )
    small = jnp.pad(small.T, ((0, 0), (0, -small.shape[0] % 128)))
    columns = small.shape[1] + layers * 6 * width
    shapes = [(rows, columns)]
    if fast:
        shapes = [(rows, (layers - 1) * 6 * width), (2 * rows + 16, width), (4 * rows, width)]
    weights, *early = call(
        functools.partial(pack_kernel, layers),
        place,
        [(shape, LOW) for shape in shapes],
        [inward, outward, expand, shrink, small],
    )
    weights = lax.all_gather(weights, ("fsdp", "dp"), axis=0, tiled=True)
    weights = weights.reshape(fsdp, 2, rows, -1)
    if not fast:
        columns = [weights[:, :, :, : small.shape[1]]]
        for at in range(small.shape[1], weights.shape[3], 6 * width):
            columns.append(weights[:, :, :, at : at + 4 * width])
            quarter = weights[:, :, :, at + 4 * width : at + 6 * width]
            quarter = quarter.reshape(fsdp, 2, rows, 4, half).transpose(1, 0, 3, 2, 4)
            quarter = quarter.reshape(2, 4, width, half).transpose(0, 2, 1, 3)
            columns.append(quarter.reshape(2, fsdp, rows, 2 * width).transpose(1, 0, 2, 3))
        weights = jnp.concatenate(columns, 3).transpose(1, 0, 2, 3).reshape(1, 2, width, -1)
    hot = (codons[:, None] == jnp.arange(SMALL, dtype=jnp.int32)[None, :]).astype(LOW)
    columns = (hot, jnp.broadcast_to(weight[:, None], (length, SMALL)), segments[:, None])
    mixers, hiddens = [[weights]] * layers, [[weights]] * layers
    if fast:
        first = Gather(place, early[0], (rows + 16, rows), rows)
        last = Gather(place, early[1], (2 * rows, 2 * rows), rows)
        first.along_z()
        first.got, last.shard, columns = tie(first.got, last.shard, columns)
        first.in_plane()
        last.along_z()
        first.near, last.got = tie(first.near, last.got)
        first.forward()
        (first.far,) = tie(first.far)
        own, small = first.result()
        mixers[0] = [own, swap_cores(own)]
        own, last.got = tie(own, last.got)
        last.in_plane()
        small = small[:, :, : rows // 16 * SMALL].reshape(16, 16, rows // 16, SMALL)
        small = small.transpose(0, 2, 1, 3).reshape(width, SMALL).T
    else:
        small = weights[:, 0, :, :SMALL].reshape(width, SMALL).T
    start = -2 * width if fast else weights.shape[3] - layers * 6 * width
    base = lambda l: start + l * 6 * width
    gains = small[V : V + norms].astype(FULL).reshape(-1, 2, width)

    cosine, sine = rotary_tables(length)
    chosen = (inputs[:, None] == jnp.arange(SMALL, dtype=jnp.int32)[None, :]).astype(LOW)
    resid = dot(chosen, small)
    kept = []
    for l in range(layers):
        gain = gains[2 * l : 2 * l + 2]
        middle, query, keys, values, lse, pack = attention_forward(
            place, resid, mixers[l], base(l), gain[0], cosine, sine, (columns[2], segments[None, :])
        )
        if fast and l == 0:
            middle, last.near = tie(middle, last.near)
            last.forward()
        output, pack_mid, hidden = hidden_forward(place, middle, hiddens[l], base(l), gain[1])
        if fast and l == 0:
            output, last.far = tie(output, last.far)
            (own,) = last.result()
            hiddens[-1] = [own, swap_cores(own)]
            output, hiddens[-1][0] = tie(output, own)
        kept.append((resid, query, keys, values, lse, pack, middle, hidden, pack_mid))
        resid = output
    grad, branch, branch_own, branch_other, head_in, grad_logits, grad_norms, sums = head(
        place, resid, small, gains[2 * layers], columns[0], columns[1]
    )
    grad_norms = [grad_norms]
    early = (head_in, grad_logits, chosen)
    early_came = [swap_cores(v) for v in early]
    mid_came = [swap_cores(saved[-1]) for saved in kept]
    pack_came = [swap_cores(saved[5]) for saved in kept]
    grad, branch, mid_came[-1] = tie(grad, branch, mid_came[-1])

    rounds = Rounds(place, rows, width, sums) if fast else PlainRounds()
    whole = lambda array, i=None: (array, i, None, None)
    tile = lambda left, right, other_left, other_right: [
        (0, width, [(left, right), (other_left, other_right)])
    ]
    chunk = []
    for l in reversed(range(layers)):
        resid, query, keys, values, lse, pack, middle, hidden, pack_mid = kept[l]
        gain = gains[2 * l : 2 * l + 2]
        branch_came = swap_cores(branch_other)
        chunk.append(
            [
                [
                    (whole(pack_mid, 1 + t), whole(branch_own)),
                    (whole(mid_came[l], 1 + t), whole(branch_came)),
                ]
                for t in range(4)
            ]
        )
        grad, branch = rounds.step(chunk, grad, branch, split=l == 0)
        grad_middle, gains_mid, up_own, up_other = hidden_back(
            place, grad, branch, middle, hidden, hiddens[l], base(l), gain[1]
        )
        grad_middle, up_own, up_other, early_came = rounds.finish(
            grad_middle, up_own, up_other, early_came
        )
        up_came = swap_cores(up_other)
        if l == 0:
            norms_early = jnp.concatenate([gains_mid] + grad_norms, 0)
            norms_early = (norms_early, swap_cores(norms_early))
        (grad_middle,) = rounds.step(
            [
                [
                    tile(
                        whole(pack_mid, 0), whole(up_own, s), whole(mid_came[l], 0), whole(up_came, s)
                    )
                    for s in range(2)
                ]
            ],
            grad_middle,
        )
        grad, branch, branch_own, branch_other, gains_in, mix_own, mix_other = attention_back(
            place, grad_middle, resid, mixers[l], base(l), gain[0], cosine, sine,
            (columns[2], segments[None, :]),
            query, keys, values, lse,
        )
        grad_norms = [gains_in, gains_mid] + grad_norms
        grad, branch, branch_own, branch_other, mix_own, mix_other, mid_came, pack_came = (
            rounds.finish(
                grad, branch, branch_own, branch_other, mix_own, mix_other, mid_came, pack_came
            )
        )
        mix_came = swap_cores(mix_other)
        products = lambda i, a, b: [
            ((pack, i, None, None), (mix_own, 1, a, b)),
            ((pack_came[l], i, None, None), (mix_came, 1, a, b)),
        ]
        chunk = [
            [
                tile(whole(pack, 0), whole(mix_own, 0), whole(pack_came[l], 0), whole(mix_came, 0)),
                [(0, half, products(0, 0, half)), (half, width, products(1, half, width))],
            ]
        ]
    late = (grad_norms[0], swap_cores(grad_norms[0]))
    branch_came = swap_cores(branch)
    products = [(whole(early[0]), whole(early[1])), (whole(early_came[0]), whole(early_came[1]))]
    products += [(whole(branch), whole(early[2])), (whole(branch_came), whole(early_came[2]))]
    if fast:
        rounds.step(chunk, small=(products, [late, norms_early]), split=True)
        while rounds.left():
            rounds.finish()
            rounds.step([])
        rounds.swap_rest()
        share_small = rounds.small_share
        small_other = swap_cores(share_small)
        totals = rounds.totals
    else:
        rounds.step(chunk)
        table = sum(cross(l[0], r[0]) for l, r in products)
        table = table + jnp.pad(
            jnp.concatenate([a + b for a, b in (late, norms_early)], 0).T,
            ((0, 0), (V, SMALL - V - norms)),
        )
        table = jnp.where(core == 0, table, swap_cores(table))
        share_small = lax.psum_scatter(table, "fsdp", scatter_dimension=0, tiled=True)
        squares = jnp.sum(share_small * share_small) * (core == 0)
        for value in rounds.squares:
            squares = squares + jnp.sum(value)
        totals = sums + jnp.where(jnp.arange(SMALL) == 2, squares, 0.0)[None]
    totals = total_of(totals, fsdp)
    shares = list(zip(rounds.shares, rounds.others)) if fast else rounds.shares
    places = [(2 * (layers - 1 - l), 0 if l == layers - 1 else 1) for l in range(layers)]

    def tiles_at(chunk, pair):
        own, other = (v[pair] for v in shares[chunk])
        ordered = (jnp.where(core == 0, own, other), jnp.where(core == 0, other, own))
        return [v[s] for v in ordered for s in range(2)]

    if not fast:
        share_in, share_out, share_up, share_down = [], [], [], []
        side = lambda *values: jnp.concatenate(values, 1)
        for at, pair in places:
            a_0, b_0, a_1, b_1 = tiles_at(at + 2, 0)
            share_in.append(
                side(
                    a_0[:, :half], a_1[:, :half], a_0[:, half:],
                    a_1[:, half:], b_0[:, :half], b_1[:, :half],
                )
            )
            share_out.append(side(b_0[:, half:], b_1[:, half:]))
            share_up.append(side(*tiles_at(at + 1, 0)))
            a_0, b_0, a_1, b_1 = tiles_at(at, pair)
            share_down.append(
                jnp.concatenate(
                    [
                        side(x[:, j * half : (j + 1) * half], y[:, j * half : (j + 1) * half])
                        for x, y in ((a_0, a_1), (b_0, b_1))
                        for j in range(2)
                    ],
                    0,
                )
            )
        share_in, share_out, share_up, share_down = (
            jnp.stack(v) for v in (share_in, share_out, share_up, share_down)
        )
    masters = (inward, outward, expand, shrink, codon_table, norm_params)
    firsts = (inward_first, outward_first, expand_first, shrink_first, table_first, norm_first)
    seconds = (
        inward_second,
        outward_second,
        expand_second,
        shrink_second,
        table_second,
        norm_second,
    )
    if fast:
        chunks = [((at + 2, 0), (at + 1, 0), (at, pair)) for at, pair in places]
        own, other = zip(*shares)
        states = [v for group in zip(masters, firsts, seconds) for v in group]
        states[12:15] = [v.T for v in states[12:15]]
        grad_norm, *values = optimizer(
            place, totals, (share_small, small_other), chunks, own, other, states
        )
        values[12:15] = [v.T for v in values[12:15]]
    else:
        grad_norm, scale = scale_of(totals)
        share_small = share_small[:, : V + norms].T
        grads = (share_in, share_out, share_up, share_down)
        grads += (share_small[:V], share_small[V:].reshape(-1, 2, rows))
        values = []
        for index, grad in enumerate(grads):
            rate, decay = (RATE_VECTOR, 0.0) if index == 5 else (RATE_MATRIX, DECAY)
            values.extend(
                adam_step(masters[index], grad * scale.reshape(()), firsts[index], seconds[index], rate, decay)
            )
    return (totals[0, 0], totals[0, 1], grad_norm.reshape(()), *values)


def solution(mesh):
    in_specs = (
        P(("fsdp", "dp")),
        P(("fsdp", "dp")),
        P(("fsdp", "dp")),
        P(None, "fsdp", None),
        P(None, "fsdp", None),
        P(None, "fsdp", None),
        P(None, "fsdp", None),
        P(None, "fsdp"),
        P(None, None, "fsdp"),
        P(None, "fsdp", None),
        P(None, "fsdp", None),
        P(None, "fsdp", None),
        P(None, "fsdp", None),
        P(None, "fsdp", None),
        P(None, "fsdp", None),
        P(None, "fsdp", None),
        P(None, "fsdp", None),
        P(None, "fsdp"),
        P(None, "fsdp"),
        P(None, None, "fsdp"),
        P(None, None, "fsdp"),
    )
    out_specs = (
        P(),
        P(),
        P(),
        P(None, "fsdp", None),
        P(None, "fsdp", None),
        P(None, "fsdp", None),
        P(None, "fsdp", None),
        P(None, "fsdp", None),
        P(None, "fsdp", None),
        P(None, "fsdp", None),
        P(None, "fsdp", None),
        P(None, "fsdp", None),
        P(None, "fsdp", None),
        P(None, "fsdp", None),
        P(None, "fsdp", None),
        P(None, "fsdp"),
        P(None, "fsdp"),
        P(None, "fsdp"),
        P(None, None, "fsdp"),
        P(None, None, "fsdp"),
        P(None, None, "fsdp"),
    )
    step = functools.partial(body, mesh.shape["fsdp"])
    return jax.shard_map(step, mesh=mesh, in_specs=in_specs, out_specs=out_specs, check_vma=False)
```
